32 devices in a mesh: replica: 8 (over y, x, core), shard: 4 (over z).
Axes of the slice: x: 2, y: 2, z: 4, core: 2. Of those that a mesh axis runs over, the one named last changes fastest.
Arguments:
- hidden_in: bfloat16 [6144, 2048], P(('replica', 'shard')), may hold values from -6 to 6
- attention_gain: bfloat16 [2048], P('shard'), may hold values from 0.5 to 1.5
- query_weight: bfloat16 [2048, 2048], P('shard'), may hold values from -0.1875 to 0.1875
- key_weight: bfloat16 [2048, 256], P('shard'), may hold values from -0.1875 to 0.1875
- value_weight: bfloat16 [2048, 256], P('shard'), may hold values from -0.125 to 0.125
- output_weight: bfloat16 [2048, 2048], P('shard'), may hold values from -0.75 to 0.75
- feedforward_gain: bfloat16 [2048], P('shard'), may hold values from 0.5 to 1.5
- gate_weight: bfloat16 [2048, 5632], P('shard'), may hold values from -0.125 to 0.125
- up_weight: bfloat16 [2048, 5632], P('shard'), may hold values from -0.125 to 0.125
- down_weight: bfloat16 [5632, 2048], P('shard'), may hold values from -0.078125 to 0.078125
- out_grad: bfloat16 [6144, 2048], P(('replica', 'shard')), may hold values from -6 to 6
Outputs:
- output: bfloat16 [6144, 2048], P(('replica', 'shard'))
- grad_input: bfloat16 [6144, 2048], P(('replica', 'shard'))
- grad_attention_gain: float32 [2048], P('shard')
- grad_query_weight: float32 [2048, 2048], P('shard')
- grad_key_weight: float32 [2048, 256], P('shard')
- grad_value_weight: float32 [2048, 256], P('shard')
- grad_output_weight: float32 [2048, 2048], P('shard')
- grad_feedforward_gain: float32 [2048], P('shard')
- grad_gate_weight: float32 [2048, 5632], P('shard')
- grad_up_weight: float32 [2048, 5632], P('shard')
- grad_down_weight: float32 [5632, 2048], P('shard')
The draws below stay inside these ranges and needn't reach their ends.
All inputs are finite; a program needn't handle non-finite values.
Results may differ from the reference program's by a relative error of at most 0.022.
Values may be sent and summed in bfloat16 or wider, within the bound.
No kernel may reach another device: no remote copies, remote signals or barrier semaphores. Data moves between devices by JAX's collectives and lax.ppermute only.
A program may use at most 448 MiB of HBM per device.

```python
import math
import jax
import jax.numpy as jnp
from jax import lax

D = 2048
HEADS = 32
KV_HEADS = 4
HEAD = 64
FF = 5632
SEQ = 768
TOKENS = 6144
N_REPLICA = 8


def levels(rng, shape, cuts, least, largest):
    level = 1.0
    for dim, blocks in cuts:
        steps = jax.random.uniform(jax.random.fold_in(jax.random.fold_in(rng, 6), dim), (blocks,), jnp.float32, least / len(cuts), largest / len(cuts))
        level = level * jnp.repeat(jnp.exp(steps), shape[dim] // blocks).reshape((-1,) + (1,) * (len(shape) - 1 - dim))
    return level


def scatter_about(own_key, dims, scale, most, cuts=(), kind=jnp.bfloat16):
    level = levels(own_key, dims, cuts, -0.22, 0.18) if cuts else 1.0
    entries = jax.random.normal(own_key, dims, jnp.float32) * scale * level
    return jnp.minimum(jnp.maximum(entries, -most), most).astype(kind)


def setup_inputs(seed: int = 0) -> dict:
    streams_of = jax.random.split(jax.random.key(seed), 12)
    hidden_in = scatter_about(streams_of[0], (TOKENS, D), 1.0, 6.0, ((0, 32),))
    attention_gain = jnp.clip(1.0 + 0.1 * jax.random.normal(streams_of[1], (D,), jnp.float32), 0.5, 1.5).astype(jnp.bfloat16)
    query_weight = scatter_about(streams_of[2], (D, D), (D // 2) ** -0.5, 0.1875, ((0, 4),))
    key_weight = scatter_about(streams_of[3], (D, KV_HEADS * HEAD), (D // 2) ** -0.5, 0.1875, ((0, 4),))
    value_weight = scatter_about(streams_of[4], (D, KV_HEADS * HEAD), D ** -0.5, 0.125, ((0, 4),))
    output_weight = scatter_about(streams_of[5], (D, D), HEAD ** -0.5, 0.75, ((0, 4),))
    feedforward_gain = jnp.clip(1.0 + 0.1 * jax.random.normal(streams_of[6], (D,), jnp.float32), 0.5, 1.5).astype(jnp.bfloat16)
    gate_weight = scatter_about(streams_of[7], (D, FF), D ** -0.5, 0.125, ((0, 4),))
    up_weight = scatter_about(streams_of[8], (D, FF), D ** -0.5, 0.125, ((0, 4),))
    down_weight = scatter_about(streams_of[9], (FF, D), FF ** -0.5, 0.078125, ((0, 4),))
    out_grad = scatter_about(streams_of[10], (TOKENS, D), 1.0, 6.0, ((0, 32),))
    return dict(hidden_in=hidden_in, attention_gain=attention_gain, query_weight=query_weight, key_weight=key_weight, value_weight=value_weight, output_weight=output_weight, feedforward_gain=feedforward_gain, gate_weight=gate_weight, up_weight=up_weight, down_weight=down_weight, out_grad=out_grad)


@jax.custom_vjp
def low(v):
    return lax.optimization_barrier(v.astype(jnp.bfloat16)).astype(jnp.float32)

@jax.custom_vjp
def low_back(v):
    return v

def low_keep(v):
    return (low(v), None)

def low_pass(kept, grad):
    return (grad,)

def back_keep(v):
    return (v, None)

def back_low(kept, grad):
    return (low(grad),)
low.defvjp(low_keep, low_pass)
low_back.defvjp(back_keep, back_low)
norm_eps = 1e-05
rope_base = 10000.0
masked_score = -1e+30
highest = lax.Precision.HIGHEST

def product(left, right):
    return jnp.dot(left, right, precision=highest)

def rms_norm(values, gain):
    inverse = lax.rsqrt(lax.optimization_barrier(jnp.mean(values * values, axis=-1, keepdims=True)) + norm_eps)
    return values * inverse * gain

def rotary_tables(places, width):
    inverse = rope_base ** (-jnp.arange(0, width, 2, dtype=jnp.float32) / width)
    angles = places.astype(jnp.float32)[:, None] * inverse[None, :]
    angles = jnp.concatenate([angles, angles], axis=1)
    return (jnp.cos(angles), jnp.sin(angles))

def rotate_half(values):
    middle = values.shape[-1] // 2
    return jnp.concatenate([-values[..., middle:], values[..., :middle]], axis=-1)

def apply_rotary(values, cosine_table, sine_table):
    return values * cosine_table[:, None, :] + rotate_half(values) * sine_table[:, None, :]

def attend_block(query_block, keys, values, first_row):
    group_size = HEADS // KV_HEADS
    block_rows = query_block.shape[0]
    grouped = query_block.reshape(block_rows, KV_HEADS, group_size, HEAD)
    scores = jnp.einsum('tcmd,scd->tcms', grouped, keys, precision=highest) * HEAD ** (-0.5)
    scores = low_back(scores)
    query_places = first_row + jnp.arange(block_rows, dtype=jnp.int32)
    key_places = jnp.arange(keys.shape[0], dtype=jnp.int32)
    allowed = key_places[None, :] <= query_places[:, None]
    scores = jnp.where(allowed[:, None, None, :], scores, masked_score)
    row_max = lax.optimization_barrier(jnp.max(scores, axis=-1, keepdims=True))
    exponent_terms = jnp.exp(scores - row_max)
    probs = exponent_terms / lax.optimization_barrier(jnp.sum(exponent_terms, axis=-1, keepdims=True))
    probs_low = low(probs)
    mixed = jnp.einsum('tcms,scd->tcmd', probs_low, values, precision=highest)
    return mixed.reshape(block_rows, HEADS * HEAD)

def attend(queries, keys, values):
    query_rows = math.gcd(SEQ, 256)
    block_count = SEQ // query_rows

    def one_block(block_index):
        first_row = block_index * query_rows
        query_block = lax.dynamic_slice_in_dim(queries, first_row, query_rows, 0)
        return attend_block(query_block, keys, values, first_row)
    outputs = lax.map(jax.checkpoint(one_block), jnp.arange(block_count, dtype=jnp.int32))
    return outputs.reshape(SEQ, HEADS * HEAD)

def layer(params, hidden_seq):
    attention_gain, query_weight, key_weight, value_weight, output_weight, feedforward_gain, gate_weight, up_weight, down_weight = params
    cosine_table, sine_table = rotary_tables(jnp.arange(SEQ, dtype=jnp.int32), HEAD)
    normed_one = low(rms_norm(hidden_seq, attention_gain))
    query_raw = low_back(product(normed_one, query_weight)).reshape(SEQ, HEADS, HEAD)
    queries = low(apply_rotary(query_raw, cosine_table, sine_table))
    key_raw = low_back(product(normed_one, key_weight)).reshape(SEQ, KV_HEADS, HEAD)
    keys = low(apply_rotary(key_raw, cosine_table, sine_table))
    values = low(low_back(product(normed_one, value_weight))).reshape(SEQ, KV_HEADS, HEAD)
    attended = low(low_back(attend(queries, keys, values)))
    middle = hidden_seq + low_back(product(attended, output_weight))
    normed_two = low(rms_norm(middle, feedforward_gain))
    gate_proj = low_back(product(normed_two, gate_weight))
    up_proj = low_back(product(normed_two, up_weight))
    hidden_act = low(gate_proj * jax.nn.sigmoid(gate_proj) * up_proj)
    return middle + low_back(product(hidden_act, down_weight))

def reference(hidden_in, attention_gain, query_weight, key_weight, value_weight, output_weight, feedforward_gain, gate_weight, up_weight, down_weight, out_grad):
    params = tuple((matrix.astype(jnp.float32) for matrix in (attention_gain, query_weight, key_weight, value_weight, output_weight, feedforward_gain, gate_weight, up_weight, down_weight)))
    inputs = hidden_in.astype(jnp.float32).reshape(N_REPLICA, SEQ, D)
    cotangent = out_grad.astype(jnp.float32).reshape(N_REPLICA, SEQ, D)
    starting = jax.tree.map(jnp.zeros_like, params)

    def per_sequence(totals, seq_pair):
        sequence, tangent = seq_pair
        result, pullback = jax.vjp(layer, params, sequence)
        param_grads, input_grad = pullback(tangent)
        totals = jax.tree.map(jnp.add, totals, param_grads)
        return (totals, (result, input_grad))
    totals, (results, input_grads) = lax.scan(per_sequence, starting, (inputs, cotangent))
    output = results.reshape(TOKENS, D).astype(jnp.bfloat16)
    grad_input = input_grads.reshape(TOKENS, D).astype(jnp.bfloat16)
    return (output, grad_input, totals[0], totals[1], totals[2], totals[3], totals[4], totals[5], totals[6], totals[7], totals[8])
```

```python
import jax
import jax.numpy as jnp
from jax import lax
from jax.sharding import PartitionSpec as P

HEADS = 32
KV_HEADS = 4
HEAD = 64
GROUP = HEADS // KV_HEADS
CHIPS = 4
PIECES = 2 * CHIPS

norm_eps = 1e-05
rope_base = 10000.0
masked_score = -1e30

f32 = jnp.float32
bf16 = jnp.bfloat16


def matmul(left, right):
    return jnp.dot(left, right, preferred_element_type=f32)


def left_transposed(left, right):
    return lax.dot_general(left, right, (((0,), (0,)), ((), ())), preferred_element_type=f32)


def right_transposed(left, right):
    return lax.dot_general(left, right, (((1,), (1,)), ((), ())), preferred_element_type=f32)


def rotary_tables(places, width):
    inverse = rope_base ** (-jnp.arange(0, width, 2, dtype=f32) / width)
    angles = places.astype(f32)[:, None] * inverse[None, :]
    angles = jnp.concatenate([angles, angles], axis=1)
    return (jnp.cos(angles), jnp.sin(angles))


def rotate_half(values):
    middle = values.shape[-1] // 2
    return jnp.concatenate([-values[..., middle:], values[..., :middle]], axis=-1)


def swap(value, mask):
    size = lax.axis_size("replica")
    return lax.ppermute(value, "replica", [(i, i ^ mask) for i in range(size)])


def shift(value, step):
    size = lax.axis_size("shard")
    pairs = [(i, i + step) for i in range(size) if 0 <= i + step < size]
    return lax.ppermute(value, "shard", pairs)


def plane_gather(value):
    return [value] + [swap(value, 2 * m) for m in range(1, CHIPS)]


def plane_sum(parts):
    sent = [swap(parts[m].astype(bf16), 2 * m) for m in range(1, CHIPS)]
    total = parts[0]
    for part in sent:
        total = total + part.astype(f32)
    return total


def scaled(weight, gain):
    return (weight.astype(f32) * gain[:, None]).astype(bf16)


def per_device(
    hidden_in,
    attention_gain,
    query_weight,
    key_weight,
    value_weight,
    output_weight,
    feedforward_gain,
    gate_weight,
    up_weight,
    down_weight,
    out_grad,
):
    rows, width = hidden_in.shape
    shards = lax.axis_size("shard")
    replicas = lax.axis_size("replica")
    place = lax.axis_index("replica")
    depth = lax.axis_index("shard")
    core = place % 2
    chip = (place // 2) % CHIPS
    piece = place % PIECES
    local = width // shards
    ff_local = down_weight.shape[0]
    ff_cut = ff_local // PIECES
    ff_half = ff_cut * shards
    q_width = GROUP * HEAD
    q_half = q_width // 2
    scale = HEAD ** (-0.5)
    gain_one = attention_gain.astype(f32)
    gain_two = feedforward_gain.astype(f32)

    def ff_columns(weight):
        return jnp.concatenate(
            [
                lax.dynamic_slice_in_dim(weight, s * ff_local + piece * ff_cut, ff_cut, 1)
                for s in range(shards)
            ],
            axis=1,
        )

    def natural(pieces, count):
        stacked = jnp.stack(pieces)
        mine = place % count
        return [lax.dynamic_index_in_dim(stacked, mine ^ i, 0, keepdims=False) for i in range(count)]

    qkv_block = scaled(
        jnp.concatenate(
            [
                lax.dynamic_slice_in_dim(query_weight, chip * q_width + core * q_half, q_half, 1),
                lax.dynamic_slice_in_dim(key_weight, chip * HEAD, HEAD, 1),
                lax.dynamic_slice_in_dim(value_weight, chip * HEAD, HEAD, 1),
            ],
            axis=1,
        ),
        gain_one,
    )
    qkv_own = lax.all_gather(qkv_block, "shard", axis=0, tiled=True)
    qkv_other = swap(qkv_own, 1)
    out_cut = local // PIECES
    out_own = lax.all_gather(
        lax.dynamic_slice_in_dim(output_weight, piece * out_cut, out_cut, 0), "shard", axis=0
    )
    gu_block = scaled(
        jnp.concatenate([ff_columns(gate_weight), ff_columns(up_weight)], axis=1), gain_two
    )
    gu_own = lax.all_gather(gu_block, "shard", axis=0, tiled=True)
    down_own = lax.all_gather(
        lax.dynamic_slice_in_dim(down_weight, piece * ff_cut, ff_cut, 0), "shard", axis=0, tiled=True
    )

    x_blocks = plane_gather(hidden_in)
    g_blocks = plane_gather(out_grad)

    inputs = hidden_in.astype(f32)

    def normed(block):
        wide = block.astype(f32)
        inverse = lax.rsqrt(jnp.mean(wide * wide, axis=1, keepdims=True) + norm_eps)
        return ((wide * inverse).astype(bf16), inverse)

    inv_one = normed(hidden_in)[1]
    one_all = jnp.concatenate([normed(block)[0] for block in x_blocks], axis=0)
    g_all = jnp.concatenate(g_blocks, axis=0)

    first = core == 0
    wq = jnp.concatenate(
        [
            jnp.where(first, qkv_own[:, :q_half], qkv_other[:, :q_half]),
            jnp.where(first, qkv_other[:, :q_half], qkv_own[:, :q_half]),
            qkv_own[:, q_half:],
        ],
        axis=1,
    )
    cosine, sine = rotary_tables(depth * rows + jnp.arange(rows, dtype=jnp.int32), HEAD)
    cosine = jnp.tile(cosine, (CHIPS, 1))[:, None, :]
    sine = jnp.tile(sine, (CHIPS, 1))[:, None, :]

    def rot(values):
        return values * cosine + rotate_half(values) * sine

    def rot_t(values):
        return values * cosine - rotate_half(values * sine)

    tokens = CHIPS * rows
    qkv = matmul(one_all, wq)
    qk = rot(qkv[:, : q_width + HEAD].reshape(tokens, GROUP + 1, HEAD)).astype(bf16)
    queries = qk[:, :GROUP].reshape(CHIPS, rows, GROUP, HEAD)
    kv = jnp.concatenate([qk[:, GROUP], qkv[:, q_width + HEAD :].astype(bf16)], axis=1)
    kv_all = jnp.stack([kv] + [shift(kv, d) for d in range(1, shards)])
    kv_all = kv_all.reshape(shards, CHIPS, rows, 2 * HEAD).transpose(1, 0, 2, 3)
    kv_all = kv_all.reshape(CHIPS, shards * rows, 2 * HEAD)
    keys = kv_all[..., :HEAD]
    values = kv_all[..., HEAD:]

    back = jnp.arange(shards * rows, dtype=jnp.int32) // rows
    inside = jnp.arange(shards * rows, dtype=jnp.int32) % rows
    mine = jnp.arange(rows, dtype=jnp.int32)
    allowed = jnp.where(
        back[None, :] == 0, inside[None, :] <= mine[:, None], back[None, :] <= depth
    )
    scores = jnp.einsum("btmd,bsd->bmts", queries, keys, preferred_element_type=f32) * scale
    scores = jnp.where(allowed[None, None], scores, masked_score)
    probs = jax.nn.softmax(scores, axis=-1)
    probs_low = probs.astype(bf16)
    attended = jnp.einsum("bmts,bsd->btmd", probs_low, values, preferred_element_type=f32)
    attended = attended.astype(bf16).reshape(tokens, q_width)

    group_shards = shards // CHIPS

    def for_chip(mask):
        return lax.dynamic_slice_in_dim(out_own, (chip ^ mask) * group_shards, group_shards, 0)

    out_mine = jnp.stack([for_chip(0)] + [swap(for_chip(m), 2 * m) for m in range(1, CHIPS)])
    out_theirs = swap(out_mine, 1)
    out_pieces = []
    for m in range(CHIPS):
        out_pieces += [out_mine[m], out_theirs[m]]
    wo = jnp.stack(natural(out_pieces, PIECES), axis=1).reshape(q_width, width)

    def split(whole):
        return [whole[m * rows : (m + 1) * rows] for m in range(CHIPS)]

    middle = inputs + plane_sum(split(matmul(attended, wo)))
    two, inv_two = normed(middle)
    two_all = jnp.concatenate(plane_gather(two), axis=0)

    gu_other = swap(gu_own, 1)
    down_other = swap(down_own, 1)
    out_part = jnp.zeros((tokens, width), f32)
    e_part = jnp.zeros((tokens, width), f32)
    gu_terms = []
    down_terms = []
    for gu, down in ((gu_own, down_own), (gu_other, down_other)):
        both = matmul(two_all, gu)
        gate, up = both[:, :ff_half], both[:, ff_half:]
        sig = jax.nn.sigmoid(gate)
        act = (gate * sig * up).astype(bf16)
        out_part = out_part + matmul(act, down)
        down_terms.append(left_transposed(act, g_all))
        grad_hidden = right_transposed(g_all, down)
        grad_gate = grad_hidden * up * sig * (1.0 + gate * (1.0 - sig))
        grad_up = grad_hidden * gate * sig
        grads = jnp.concatenate([grad_gate, grad_up], axis=1).astype(bf16)
        gu_terms.append(left_transposed(two_all, grads))
        e_part = e_part + right_transposed(grads, gu)

    def reduced(own, other):
        both = (own + swap(other.astype(bf16), 1).astype(f32)).astype(bf16)
        kept = lax.psum_scatter(both, "shard", scatter_dimension=0, tiled=True)
        if replicas > PIECES:
            groups = [
                [e * PIECES + i for e in range(replicas // PIECES)] for i in range(PIECES)
            ]
            kept = lax.psum(kept, "replica", axis_index_groups=groups)
        return kept

    def plane_pieces(kept):
        mine = plane_gather(kept)
        theirs = [swap(part, 1) for part in mine]
        pieces = []
        for m in range(CHIPS):
            pieces += [mine[m], theirs[m]]
        return natural(pieces, PIECES)

    down_kept = reduced(*down_terms)
    gu_kept = reduced(*gu_terms)

    output = (middle + plane_sum(split(out_part))).astype(bf16)

    def norm_back(e, values, inverse):
        mean_term = jnp.mean(e * values, axis=1, keepdims=True)
        return inverse * e - values * (inverse * inverse * inverse) * mean_term

    grad_middle = out_grad.astype(f32) + norm_back(plane_sum(split(e_part)), middle, inv_two)
    branch_all = jnp.concatenate(plane_gather(grad_middle.astype(bf16)), axis=0)
    wo_term = left_transposed(attended, branch_all)
    grad_attended = right_transposed(branch_all, wo).astype(bf16).reshape(CHIPS, rows, GROUP, HEAD)

    grad_probs = jnp.einsum("btmd,bsd->bmts", grad_attended, values, preferred_element_type=f32)
    row_delta = jnp.sum(probs * grad_probs, axis=-1, keepdims=True)
    grad_scores = (probs * (grad_probs - row_delta)).astype(bf16)
    grad_q = jnp.einsum("bmts,bsd->btmd", grad_scores, keys, preferred_element_type=f32) * scale
    grad_k = jnp.einsum("bmts,btmd->bsd", grad_scores, queries, preferred_element_type=f32) * scale
    grad_v = jnp.einsum("bmts,btmd->bsd", probs_low, grad_attended, preferred_element_type=f32)
    grad_kv = jnp.concatenate([grad_k, grad_v], axis=-1)
    grad_kv = grad_kv.reshape(CHIPS, shards, rows, 2 * HEAD).transpose(1, 0, 2, 3)
    grad_kv = grad_kv.reshape(shards, tokens, 2 * HEAD)
    kv_sum = grad_kv[0]
    for d in range(1, shards):
        kv_sum = kv_sum + shift(grad_kv[d].astype(bf16), -d).astype(f32)
    grad_q = grad_q.reshape(tokens, GROUP, HEAD)
    grad_qk = rot_t(jnp.concatenate([grad_q, kv_sum[:, None, :HEAD]], axis=1))
    grad_qkv = jnp.concatenate(
        [grad_qk.reshape(tokens, q_width + HEAD), kv_sum[:, HEAD:]], axis=1
    ).astype(bf16)
    qkv_term = left_transposed(one_all, grad_qkv)
    e_one = plane_sum(split(right_transposed(grad_qkv, wq)))
    grad_input = (grad_middle + norm_back(e_one, inputs, inv_one)).astype(bf16)

    def qkv_side(side):
        return jnp.concatenate(
            [
                lax.dynamic_slice_in_dim(qkv_term, side * q_half, q_half, 1),
                qkv_term[:, q_width:],
            ],
            axis=1,
        )

    wo_cut = wo_term.reshape(group_shards, CHIPS, 2, out_cut, width)

    def wo_side(side):
        return lax.dynamic_index_in_dim(wo_cut, side, 2, keepdims=False)

    wo_mine = (wo_side(core) + swap(wo_side(1 - core).astype(bf16), 1).astype(f32)).astype(bf16)

    def wo_for(mask):
        return lax.dynamic_index_in_dim(wo_mine, chip ^ mask, 1, keepdims=False)

    wo_chips = [wo_for(0)] + [swap(wo_for(m), 2 * m) for m in range(1, CHIPS)]
    wo_stack = jnp.stack(wo_chips)
    wo_block = jnp.concatenate(
        [lax.dynamic_index_in_dim(wo_stack, chip ^ i, 0, keepdims=False) for i in range(CHIPS)],
        axis=0,
    ).reshape(shards * out_cut, width)

    def over_groups(kept):
        if replicas > PIECES:
            groups = [
                [e * PIECES + i for e in range(replicas // PIECES)] for i in range(PIECES)
            ]
            kept = lax.psum(kept, "replica", axis_index_groups=groups)
        return kept

    wo_kept = over_groups(lax.psum_scatter(wo_block, "shard", scatter_dimension=0, tiled=True))
    qkv_kept = reduced(qkv_side(core), qkv_side(1 - core))

    down_out = jnp.concatenate(plane_pieces(down_kept), axis=0).astype(f32)
    wo_out = jnp.concatenate(plane_pieces(wo_kept), axis=0).astype(f32)
    gu_parts = [
        part.reshape(local, 2, shards, ff_cut) for part in plane_pieces(gu_kept)
    ]
    gu_all = jnp.stack(gu_parts, axis=3).reshape(local, 2, shards * ff_local).astype(f32)
    qkv_parts = plane_pieces(qkv_kept)
    q_all = jnp.concatenate([part[:, :q_half] for part in qkv_parts], axis=1).astype(f32)
    k_all = jnp.concatenate(
        [part[:, q_half : q_half + HEAD] for part in qkv_parts[::2]], axis=1
    ).astype(f32)
    v_all = jnp.concatenate([part[:, q_half + HEAD :] for part in qkv_parts[::2]], axis=1).astype(
        f32
    )

    def gain_grad(pairs):
        return sum(jnp.sum(term * weight.astype(f32), axis=1) for term, weight in pairs)

    gain_one_out = gain_grad(((q_all, query_weight), (k_all, key_weight), (v_all, value_weight)))
    gain_two_out = gain_grad(((gu_all[:, 0], gate_weight), (gu_all[:, 1], up_weight)))
    return (
        output,
        grad_input,
        gain_one_out,
        q_all * gain_one[:, None],
        k_all * gain_one[:, None],
        v_all * gain_one[:, None],
        wo_out,
        gain_two_out,
        gu_all[:, 0] * gain_two[:, None],
        gu_all[:, 1] * gain_two[:, None],
        down_out,
    )


def solution(mesh):
    return jax.shard_map(
        per_device,
        mesh=mesh,
        in_specs=(
            P(("replica", "shard"), None),
            P("shard"),
            P("shard", None),
            P("shard", None),
            P("shard", None),
            P("shard", None),
            P("shard"),
            P("shard", None),
            P("shard", None),
            P("shard", None),
            P(("replica", "shard"), None),
        ),
        out_specs=(
            P(("replica", "shard"), None),
            P(("replica", "shard"), None),
            P("shard"),
            P("shard", None),
            P("shard", None),
            P("shard", None),
            P("shard", None),
            P("shard"),
            P("shard", None),
            P("shard", None),
            P("shard", None),
        ),
        check_vma=False,
    )
```

```python
import functools

import jax
import jax.numpy as jnp
from jax import lax
from jax.experimental import pallas as pl
from jax.experimental.pallas import tpu as pltpu
from jax.sharding import PartitionSpec as P

HEADS = 32
KV_HEADS = 4
HEAD = 64
GROUP = HEADS // KV_HEADS
CHIPS = 4
PIECES = 2 * CHIPS
LANES = 128

norm_eps = 1e-05
rope_base = 10000.0
masked_score = -1e30

f32 = jnp.float32
bf16 = jnp.bfloat16
VMEM = pltpu.VMEM
NT = (((1,), (1,)), ((), ()))
TN = (((0,), (0,)), ((), ()))


def dot(left, right):
    return jnp.dot(left, right, preferred_element_type=f32)


def dot_nt(left, right):
    return lax.dot_general(left, right, NT, preferred_element_type=f32)


def dot_tn(left, right):
    return lax.dot_general(left, right, TN, preferred_element_type=f32)


def shape(dims, kind):
    return jax.ShapeDtypeStruct(dims, kind)


def whole():
    return pl.BlockSpec(memory_space=VMEM)


def kernel_call(body, out_shape, in_specs, out_specs, operands, *, index=None, grid=(), scratch=(),
                flops=0, moved=0, exps=0, aliases=None, name=None):
    params = pltpu.CompilerParams(
        vmem_limit_bytes=52 * 2**20, dimension_semantics=("arbitrary",) * len(grid)
    )
    cost = pl.CostEstimate(flops=int(flops), bytes_accessed=int(moved), transcendentals=int(exps))
    common = dict(
        out_shape=out_shape,
        compiler_params=params,
        cost_estimate=cost,
        input_output_aliases=aliases or {},
        name=name,
    )
    if index is None:
        spec = pl.GridSpec(grid=grid, in_specs=in_specs, out_specs=out_specs, scratch_shapes=scratch)
        return pl.pallas_call(body, grid_spec=spec, **common)(*operands)
    spec = pltpu.PrefetchScalarGridSpec(
        num_scalar_prefetch=1, grid=grid, in_specs=in_specs, out_specs=out_specs,
        scratch_shapes=scratch,
    )
    return pl.pallas_call(body, grid_spec=spec, **common)(index, *operands)


def swap(value, mask):
    size = lax.axis_size("replica")
    return lax.ppermute(value, "replica", [(i, i ^ mask) for i in range(size)])


def shift(value, step):
    size = lax.axis_size("shard")
    pairs = [(i, i + step) for i in range(size) if 0 <= i + step < size]
    return lax.ppermute(value, "shard", pairs)


def plane_gather(value):
    return [value] + [swap(value, 2 * m) for m in range(1, CHIPS)]


def plane_sum(parts):
    sent = [swap(parts[m], 2 * m) for m in range(1, CHIPS)]
    total = parts[0]
    for part in sent:
        total = total + part.astype(f32)
    return total


def attention_block_body(local, group_shards, index, q, k, v, o, gain, out):
    scale = gain[:, :1]
    q_width = GROUP * HEAD
    cut = local // CHIPS
    for chip in range(CHIPS):

        @pl.when(index[0] == chip)
        def _():
            parts = []
            for m in range(CHIPS):
                for s in range(group_shards):
                    start = chip * q_width + s * local + (m ^ chip) * cut
                    parts.append(q[:, start : start + cut])
            parts.append(k[:, chip * HEAD : (chip + 1) * HEAD])
            parts.append(v[:, chip * HEAD : (chip + 1) * HEAD])
            wide = jnp.concatenate([part.astype(f32) for part in parts], axis=1)
            out[:, : q_width + 2 * HEAD] = (wide * scale).astype(bf16)

    half = local // 2
    shards = o.shape[1] // local
    for core in range(2):

        @pl.when(index[1] == core)
        def _():
            base = q_width + 2 * HEAD
            for s in range(shards):
                piece = o[:, s * local + core * half : s * local + (core + 1) * half]
                spot = s * half
                row, column = (0, spot) if spot < 512 else (cut, spot - 512)
                out[row : row + cut, base + column : base + column + half] = piece


def attention_block(index, query, key, value, output, gain):
    local, width = query.shape
    half = local // 2
    shards = width // local
    return kernel_call(
        functools.partial(attention_block_body, local, shards // CHIPS),
        shape((half, GROUP * HEAD + 2 * HEAD + 512), bf16),
        [
            pl.BlockSpec((half, width), lambda i, n: (n[1], 0)),
            pl.BlockSpec((half, key.shape[1]), lambda i, n: (n[1], 0)),
            pl.BlockSpec((half, key.shape[1]), lambda i, n: (n[1], 0)),
            pl.BlockSpec((local // CHIPS, width), lambda i, n: (n[0], 0)),
            pl.BlockSpec((half, LANES), lambda i, n: (n[1], 0)),
        ],
        pl.BlockSpec((half, GROUP * HEAD + 2 * HEAD + 512), lambda i, n: (0, 0)),
        (query, key, value, output, gain),
        index=index,
        grid=(1,),
        moved=3e6,
        name="attention_block",
    )


def feedforward_block_body(ff_local, cut, index, gate, up, gain, out):
    scale = gain[:, :1]
    shards = gate.shape[1] // ff_local
    width = shards * cut
    for chip in range(CHIPS):

        @pl.when(index[0] == chip)
        def _():
            for n, source in enumerate((gate, up)):
                parts = [
                    source[:, s * ff_local + chip * cut : s * ff_local + (chip + 1) * cut].astype(f32)
                    for s in range(shards)
                ]
                wide = jnp.concatenate(parts, axis=1)
                out[:, n * width : (n + 1) * width] = (wide * scale).astype(bf16)


def feedforward_block(index, gate, up, gain, ff_local):
    local, ff = gate.shape
    half = local // 2
    rows = 64
    steps = half // rows
    cut = ff_local // CHIPS
    width = 2 * (ff // CHIPS)
    return kernel_call(
        functools.partial(feedforward_block_body, ff_local, cut),
        shape((half, width), bf16),
        [
            pl.BlockSpec((rows, ff), lambda i, n: (n[1] * steps + i, 0)),
            pl.BlockSpec((rows, ff), lambda i, n: (n[1] * steps + i, 0)),
            pl.BlockSpec((rows, LANES), lambda i, n: (n[1] * steps + i, 0)),
        ],
        pl.BlockSpec((rows, width), lambda i, n: (i, 0)),
        (gate, up, gain),
        index=index,
        grid=(steps,),
        moved=4 * half * ff + 2 * half * width,
        name="feedforward_block",
    )


def half_rotated(values):
    middle = values.shape[0] // 2
    return jnp.concatenate([-values[middle:], values[:middle]], axis=0)


def qkv_body(*refs):
    xs, (own, other, cosine, sine), (xhat, queries, kv) = refs[:CHIPS], refs[CHIPS : CHIPS + 4], refs[CHIPS + 4 :]
    rows, width = xs[0].shape
    for m in range(CHIPS):
        x = xs[m][...].astype(f32)
        inverse = lax.rsqrt(jnp.mean(x * x, axis=1, keepdims=True) + norm_eps)
        xhat[m * rows : (m + 1) * rows, :] = (x * inverse).astype(bf16)
    cos, sin = cosine[...], sine[...]
    for m in range(CHIPS):
        block = xhat[m * rows : (m + 1) * rows, :]
        total = dot(block[:, : width // 2], own[...]) + dot(block[:, width // 2 :], other[...])
        turned = total.T
        for h in range(GROUP + 1):
            u = turned[h * HEAD : (h + 1) * HEAD]
            u = u * cos + half_rotated(u) * sin
            if h < GROUP:
                queries[m, h * HEAD : (h + 1) * HEAD, :] = (u * HEAD ** (-0.5)).astype(bf16)
            else:
                both = jnp.concatenate([u, turned[(h + 1) * HEAD :]], axis=0)
                kv[m * rows : (m + 1) * rows, :] = both.T.astype(bf16)


def qkv_call(xs, own, other, cosine, sine):
    rows, width = xs[0].shape
    tokens = CHIPS * rows
    return kernel_call(
        qkv_body,
        (
            shape((tokens, width), bf16),
            shape((CHIPS, GROUP * HEAD, rows), bf16),
            shape((tokens, 2 * HEAD), bf16),
        ),
        [whole()] * (CHIPS + 4),
        (whole(), whole(), whole()),
        (*xs, own, other, cosine, sine),
        flops=2 * tokens * width * own.shape[1],
        moved=10e6,
        name="qkv",
    )


def set_bias(bias, depth, shards):
    rows = bias.shape[1]
    key = lax.broadcasted_iota(jnp.int32, bias.shape, 0)
    mine = lax.broadcasted_iota(jnp.int32, bias.shape, 1)
    limit = jnp.where(key < rows, mine, (depth + 1) * rows - 1)
    bias[...] = jnp.where(key <= limit, 0.0, masked_score)


def attention_body(shards, index, queries, *refs):
    kvs = refs[:shards]
    turned_out, out, stats, bias, kv_all, out_turned = refs[shards:]
    rows = queries.shape[2]

    @pl.when(pl.program_id(0) == 0)
    def _():
        set_bias(bias, index[2], shards)

    for d in range(shards):
        kv_all[d * rows : (d + 1) * rows, :] = kvs[d][...]
    kv = kv_all[...]
    v_turned = kv.astype(f32).T[HEAD:].astype(bf16)
    zeros = jnp.zeros((HEAD, rows), bf16)
    for h in range(GROUP):
        q = jnp.concatenate([queries[0, h * HEAD : (h + 1) * HEAD, :], zeros], axis=0)
        scores = dot(kv, q) + bias[...]
        top = jnp.max(scores, axis=0, keepdims=True)
        terms = jnp.exp(scores - top)
        total = jnp.sum(terms, axis=0, keepdims=True)
        mixed = dot(v_turned, terms.astype(bf16)) / total
        out_turned[h * HEAD : (h + 1) * HEAD, :] = mixed
        stats[0, h : h + 1, :] = top + jnp.log(total)
    turned_out[0] = out_turned[...].astype(bf16)
    out[...] = out_turned[...].T.astype(bf16)


def attention_call(index, queries, kvs):
    chips, width, rows = queries.shape
    shards = len(kvs)
    keys = shards * rows
    return kernel_call(
        functools.partial(attention_body, shards),
        (
            shape((chips, width, rows), bf16),
            shape((chips * rows, width), bf16),
            shape((chips, GROUP, rows), f32),
        ),
        [pl.BlockSpec((1, width, rows), lambda i, n: (i, 0, 0))]
        + [pl.BlockSpec((rows, 2 * HEAD), lambda i, n: (i, 0))] * shards,
        (
            pl.BlockSpec((1, width, rows), lambda i, n: (i, 0, 0)),
            pl.BlockSpec((rows, width), lambda i, n: (i, 0)),
            pl.BlockSpec((1, GROUP, rows), lambda i, n: (i, 0, 0)),
        ),
        (queries, *kvs),
        index=index,
        grid=(chips,),
        scratch=(
            VMEM((keys, rows), f32),
            VMEM((keys, 2 * HEAD), bf16),
            VMEM((width, rows), f32),
        ),
        flops=chips * GROUP * 4 * keys * rows * 2 * HEAD,
        exps=chips * GROUP * keys * rows,
        moved=4e6,
        name="attention",
    )


def attention_back_body(shards, index, branch, wo_own, wo_other, queries, turned_out, stats, cosine, sine, *refs):
    kvs = refs[:shards]
    grad_q, grad_first, grad_rest, bias, kv_all, q_turned, total = refs[-7:]
    rows = queries.shape[2]
    width = branch.shape[1]
    set_bias(bias, index[2], shards)
    for d in range(shards):
        kv_all[d * rows : (d + 1) * rows, :] = kvs[d][...]
    kv = kv_all[...]
    k_turned = kv.astype(f32).T[:HEAD].astype(bf16)
    grad_out = dot_nt(wo_own[...], branch[:, : width // 2])
    grad_out = (grad_out + dot_nt(wo_other[...], branch[:, width // 2 :])).astype(bf16)
    zeros = jnp.zeros((HEAD, rows), bf16)
    cos, sin = cosine[...], sine[...]
    for h in range(GROUP):
        span = slice(h * HEAD, (h + 1) * HEAD)
        q = jnp.concatenate([queries[0, span, :], zeros], axis=0)
        mine = grad_out[span]
        padded = jnp.concatenate([zeros, mine], axis=0)
        probs = jnp.exp(dot(kv, q) + bias[...] - stats[0, h : h + 1, :])
        delta = jnp.sum(
            mine.astype(f32) * turned_out[0, span, :].astype(f32), axis=0, keepdims=True
        )
        grad_scores = (probs * (dot(kv, padded) - delta)).astype(bf16)
        u = dot(k_turned, grad_scores) * HEAD ** (-0.5)
        q_turned[span, :] = u * cos - half_rotated(u) * sin
        term = dot_nt(grad_scores, q) + dot_nt(probs.astype(bf16), padded)
        if h == 0:
            total[...] = term
        else:
            total[...] += term
    grad_q[...] = q_turned[...].T.astype(bf16)
    grad_first[...] = total[:rows, :]
    for d in range(1, shards):
        grad_rest[d - 1] = total[d * rows : (d + 1) * rows, :].astype(bf16)


def attention_back_call(index, m, branch, wo_own, wo_other, queries, turned_out, stats, cosine, sine, kvs, before):
    chips, width, rows = queries.shape
    shards = len(kvs)
    keys = shards * rows
    tokens = chips * rows
    fixed = pl.BlockSpec((1, width, rows), lambda i, n: (m, 0, 0))
    in_specs = [
        whole(), whole(), whole(), fixed, fixed,
        pl.BlockSpec((1, GROUP, rows), lambda i, n: (m, 0, 0)), whole(), whole(),
    ] + [pl.BlockSpec((rows, 2 * HEAD), lambda i, n: (m, 0))] * shards
    operands = (branch, wo_own, wo_other, queries, turned_out, stats, cosine, sine, *kvs)
    aliases = {}
    if before is not None:
        aliases = {1 + len(operands) + n: n for n in range(3)}
        in_specs = in_specs + [pl.BlockSpec(memory_space=pl.ANY)] * 3
        operands = operands + tuple(before)
    return kernel_call(
        functools.partial(attention_back_body, shards),
        (
            shape((tokens, width), bf16),
            shape((tokens, 2 * HEAD), f32),
            shape((shards - 1, tokens, 2 * HEAD), bf16),
        ),
        in_specs,
        (
            pl.BlockSpec((rows, width), lambda i, n: (m, 0)),
            pl.BlockSpec((rows, 2 * HEAD), lambda i, n: (m, 0)),
            pl.BlockSpec((shards - 1, rows, 2 * HEAD), lambda i, n: (0, m, 0)),
        ),
        operands,
        index=index,
        grid=(1,),
        scratch=(
            VMEM((keys, rows), f32),
            VMEM((keys, 2 * HEAD), bf16),
            VMEM((width, rows), f32),
            VMEM((keys, 2 * HEAD), f32),
        ),
        flops=GROUP * 10 * keys * rows * 2 * HEAD + 2 * rows * width * branch.shape[1],
        exps=GROUP * keys * rows,
        moved=5e6,
        aliases=aliases,
        name="attention_back",
    )


def parts_body(steps, transposed, widths, *refs):
    count = len(widths)
    lefts, (own, other), outs = refs[:count], refs[count : count + 2], refs[count + 2 :]
    rows = outs[0].shape[0]
    step = pl.program_id(0)

    def run(weight):
        start = 0
        total = None
        for left, wide in zip(lefts, widths):
            if transposed:
                term = dot_nt(left[...], weight[:, start : start + wide])
            else:
                term = dot(left[...], weight[start : start + wide, :])
            total = term if total is None else total + term
            start += wide
        for m in range(CHIPS):
            outs[m][...] = total[m * rows : (m + 1) * rows, :].astype(outs[m].dtype)

    @pl.when(step < steps)
    def _():
        run(own)

    @pl.when(step >= steps)
    def _():
        run(other)


def parts_call(lefts, own, other, transposed, name):
    tokens = lefts[0].shape[0]
    rows = tokens // CHIPS
    widths = tuple(left.shape[1] for left in lefts)
    depth = sum(widths)
    half = own.shape[0] if transposed else own.shape[1]
    tile = 256
    steps = half // tile
    last = steps - 1
    if transposed:
        weight_specs = [
            pl.BlockSpec((tile, depth), lambda j: (jnp.minimum(j, last), 0)),
            pl.BlockSpec((tile, depth), lambda j: (jnp.maximum(j - steps, 0), 0)),
        ]
    else:
        weight_specs = [
            pl.BlockSpec((depth, tile), lambda j: (0, jnp.minimum(j, last))),
            pl.BlockSpec((depth, tile), lambda j: (0, jnp.maximum(j - steps, 0))),
        ]
    return kernel_call(
        functools.partial(parts_body, steps, transposed, widths),
        tuple(shape((rows, 2 * half), f32 if m == 0 else bf16) for m in range(CHIPS)),
        [pl.BlockSpec((tokens, wide), lambda j: (0, 0)) for wide in widths] + weight_specs,
        tuple(pl.BlockSpec((rows, tile), lambda j: (0, j)) for _ in range(CHIPS)),
        (*lefts, own, other),
        grid=(2 * steps,),
        flops=4 * tokens * depth * half,
        moved=2 * tokens * depth + 4 * depth * half + 4 * tokens * half,
        name=name,
    )


def gate_body(*refs):
    twos = refs[:CHIPS]
    gate_own, up_own, gate_other, up_other, act, for_gate, for_up, two_all = refs[CHIPS:]
    rows, width = twos[0].shape
    half = width // 2

    @pl.when(pl.program_id(0) == 0)
    def _():
        for m in range(CHIPS):
            two_all[m * rows : (m + 1) * rows, :] = twos[m][...]

    own = jnp.concatenate([gate_own[...], up_own[...]], axis=1)
    other = jnp.concatenate([gate_other[...], up_other[...]], axis=1)
    both = dot(two_all[:, :half], own) + dot(two_all[:, half:], other)
    wide = gate_own.shape[1]
    gate, up = both[:, :wide], both[:, wide:]
    sig = 1.0 / (1.0 + jnp.exp(-gate))
    silu = gate * sig
    act[...] = (silu * up).astype(bf16)
    for_gate[...] = (up * sig * (1.0 + gate * (1.0 - sig))).astype(bf16)
    for_up[...] = silu.astype(bf16)


def gate_call(twos, own, other):
    rows, width = twos[0].shape
    tokens = CHIPS * rows
    half = width // 2
    ff = own.shape[1] // 2
    tile = LANES
    steps = ff // tile
    weight = [
        pl.BlockSpec((half, tile), lambda j: (0, j)),
        pl.BlockSpec((half, tile), lambda j: (0, j + steps)),
    ]
    column = pl.BlockSpec((tokens, tile), lambda j: (0, j))
    return kernel_call(
        gate_body,
        tuple(shape((tokens, ff), bf16) for _ in range(3)) + (shape((tokens, width), bf16),),
        [pl.BlockSpec((rows, width), lambda j: (0, 0))] * CHIPS + weight + weight,
        (column, column, column, pl.BlockSpec((tokens, width), lambda j: (0, 0))),
        (*twos, own, own, other, other),
        grid=(steps,),
        flops=4 * tokens * width * ff,
        moved=4 * tokens * width + 4 * width * ff + 6 * tokens * ff,
        exps=tokens * ff,
        name="gate",
    )


def hidden_back_body(g, own, other, for_gate, for_up, grads):
    half = g.shape[1] // 2
    ff = own.shape[0]
    hidden = dot_nt(g[:, :half], own[...]) + dot_nt(g[:, half:], other[...])
    grads[:, :ff] = (hidden * for_gate[...].astype(f32)).astype(bf16)
    grads[:, ff:] = (hidden * for_up[...].astype(f32)).astype(bf16)


def hidden_back_call(g, own, other, for_gate, for_up):
    tokens, width = g.shape
    ff, half = own.shape
    block = tokens // 2
    row = lambda i: (i, 0)
    fixed = lambda i: (0, 0)
    return kernel_call(
        hidden_back_body,
        shape((tokens, 2 * ff), bf16),
        [
            pl.BlockSpec((block, width), row),
            pl.BlockSpec((ff, half), fixed),
            pl.BlockSpec((ff, half), fixed),
            pl.BlockSpec((block, ff), row),
            pl.BlockSpec((block, ff), row),
        ],
        pl.BlockSpec((block, 2 * ff), row),
        (g, own, other, for_gate, for_up),
        grid=(2,),
        flops=2 * tokens * width * ff,
        moved=2 * tokens * width + 4 * ff * half + 8 * tokens * ff,
        name="hidden_back",
    )


def weight_grad_body(count, added, left, *refs):
    rights, out = refs[:count], refs[-1]
    start = 0
    for right in rights:
        wide = right.shape[1]
        term = dot_tn(left[...], right[...])
        if added:
            term = term + refs[count][:, start : start + wide].astype(f32)
        out[:, start : start + wide] = term.astype(bf16)
        start += wide


def weight_grad(left, left_side, rights, right_side, added, name):
    tokens = left.shape[0]
    rows = left.shape[1] // (1 if left_side is None else 2)
    tile = 256 if rows % 256 == 0 else LANES
    steps = rows // tile
    first = 0 if left_side is None else left_side * steps
    wides = [right.shape[1] // (1 if right_side is None else 2) for right in rights]
    spot = 0 if right_side is None else right_side
    width = sum(wides)
    in_specs = [pl.BlockSpec((tokens, tile), lambda i: (0, first + i))]
    in_specs += [pl.BlockSpec((tokens, wide), lambda i: (0, spot)) for wide in wides]
    operands = (left, *rights)
    if added is not None:
        in_specs.append(pl.BlockSpec((tile, width), lambda i: (i, 0)))
        operands = operands + (added,)
    return kernel_call(
        functools.partial(weight_grad_body, len(rights), added is not None),
        shape((rows, width), bf16),
        in_specs,
        pl.BlockSpec((tile, width), lambda i: (i, 0)),
        operands,
        grid=(steps,),
        flops=2 * tokens * rows * width,
        moved=2 * tokens * (rows + width) + 4 * rows * width,
        name=name,
    )


def rows_result_body(local, index, *refs):
    pieces, out = refs[:PIECES], refs[PIECES]
    half = local // 2
    shards = out.shape[1] // local
    for m in range(CHIPS):
        for core in range(2):

            @pl.when((pl.program_id(0) == m) & (index[1] == core))
            def _():
                for side in range(2):
                    piece = pieces[2 * m + side]
                    for s in range(shards):
                        spot = s * local + (core ^ side) * half
                        out[:, spot : spot + half] = piece[:, s * half : (s + 1) * half].astype(f32)


def rows_result(index, pieces, local, name):
    cut, half_width = pieces[0].shape
    return kernel_call(
        functools.partial(rows_result_body, local),
        shape((CHIPS * cut, 2 * half_width), f32),
        [pl.BlockSpec((cut, half_width), lambda i, n: (0, 0))] * PIECES,
        pl.BlockSpec((cut, 2 * half_width), lambda i, n: (n[0] ^ i, 0)),
        tuple(pieces),
        index=index,
        grid=(CHIPS,),
        moved=PIECES * cut * half_width * 6,
        name=name,
    )


def lane_sum(value):
    total = value[:, :LANES]
    for n in range(1, value.shape[1] // LANES):
        total = total + value[:, n * LANES : (n + 1) * LANES]
    return total


def feedforward_result_body(ff_local, cut, index, *refs):
    pieces = refs[:CHIPS]
    gate_weight, up_weight, gain = refs[CHIPS : CHIPS + 3]
    gate_out, up_out, gain_out = refs[-3:]
    shards = gate_weight.shape[1] // ff_local
    width = shards * cut
    for chip in range(CHIPS):

        @pl.when(index[0] == chip)
        def _():
            @pl.loop(0, gate_out.shape[0] // 16)
            def _(n):
                rows = pl.ds(pl.multiple_of(n * 16, 16), 16)
                scale = gain[rows, :1]
                total = jnp.zeros((16, LANES), f32)
                for base, weight, out in ((0, gate_weight, gate_out), (width, up_weight, up_out)):
                    parts = []
                    for s in range(shards):
                        for owner in range(CHIPS):
                            start = base + s * cut
                            parts.append(pieces[owner ^ chip][rows, start : start + cut].astype(f32))
                    wide = jnp.concatenate(parts, axis=1)
                    total = total + lane_sum(wide * weight[rows, :].astype(f32))
                    out[rows, :] = wide * scale
                gain_out[rows, :] = total


def feedforward_result(index, side, pieces, gate_weight, up_weight, gain, ff_local, before):
    local, ff = gate_weight.shape
    half = local // 2
    rows = 64
    steps = half // rows
    row = lambda i, n: ((n[1] ^ side) * steps + i, 0)
    in_specs = [pl.BlockSpec((rows, pieces[0].shape[1]), lambda i, n: (i, 0))] * CHIPS
    in_specs += [pl.BlockSpec((rows, ff), row)] * 2 + [pl.BlockSpec((rows, LANES), row)]
    operands = (*pieces, gate_weight, up_weight, gain)
    aliases = {}
    if before is not None:
        aliases = {1 + len(operands) + n: n for n in range(3)}
        in_specs = in_specs + [pl.BlockSpec(memory_space=pl.ANY)] * 3
        operands = operands + tuple(before)
    return kernel_call(
        functools.partial(feedforward_result_body, ff_local, ff_local // CHIPS),
        (shape((local, ff), f32), shape((local, ff), f32), shape((local, LANES), f32)),
        in_specs,
        (pl.BlockSpec((rows, ff), row), pl.BlockSpec((rows, ff), row), pl.BlockSpec((rows, LANES), row)),
        operands,
        index=index,
        grid=(steps,),
        moved=half * ff * 16,
        aliases=aliases,
        name="feedforward_result",
    )


def qkv_result_body(local, group_shards, index, *refs):
    pieces = refs[:PIECES]
    weights, gain = refs[PIECES : PIECES + 3], refs[PIECES + 3]
    outs, gain_out = refs[PIECES + 4 : PIECES + 7], refs[PIECES + 7]
    q_width = GROUP * HEAD
    cut = local // CHIPS
    scale = gain[:, :1]
    for chip in range(CHIPS):
        for side in range(2):

            @pl.when((index[0] == chip) & (pl.program_id(0) == side))
            def _():
                parts, k_parts, v_parts = [], [], []
                for owner in range(CHIPS):
                    piece = pieces[2 * (owner ^ chip) + side]
                    for s in range(group_shards):
                        for j in range(CHIPS):
                            start = ((j ^ owner) * group_shards + s) * cut
                            parts.append(piece[:, start : start + cut].astype(f32))
                    k_parts.append(piece[:, q_width : q_width + HEAD].astype(f32))
                    v_parts.append(piece[:, q_width + HEAD :].astype(f32))
                total = jnp.zeros((gain.shape[0], LANES), f32)
                for part, weight, out in zip((parts, k_parts, v_parts), weights, outs):
                    wide = jnp.concatenate(part, axis=1)
                    total = total + lane_sum(wide * weight[...].astype(f32))
                    out[...] = wide * scale
                gain_out[...] = total


def qkv_result(index, pieces, query, key, value, gain):
    local, width = query.shape
    half = local // 2
    group_shards = width // local // CHIPS
    row = lambda i, n: (n[1] ^ i, 0)
    kv_width = key.shape[1]
    return kernel_call(
        functools.partial(qkv_result_body, local, group_shards),
        (
            shape((local, width), f32),
            shape((local, kv_width), f32),
            shape((local, kv_width), f32),
            shape((local, LANES), f32),
        ),
        [pl.BlockSpec(pieces[0].shape, lambda i, n: (0, 0))] * PIECES
        + [
            pl.BlockSpec((half, width), row),
            pl.BlockSpec((half, kv_width), row),
            pl.BlockSpec((half, kv_width), row),
            pl.BlockSpec((half, LANES), row),
        ],
        (
            pl.BlockSpec((half, width), row),
            pl.BlockSpec((half, kv_width), row),
            pl.BlockSpec((half, kv_width), row),
            pl.BlockSpec((half, LANES), row),
        ),
        (*pieces, query, key, value, gain),
        index=index,
        grid=(2,),
        moved=local * width * 10,
        name="qkv_result",
    )


def per_device(
    hidden_in,
    attention_gain,
    query_weight,
    key_weight,
    value_weight,
    output_weight,
    feedforward_gain,
    gate_weight,
    up_weight,
    down_weight,
    out_grad,
):
    rows, width = hidden_in.shape
    shards = lax.axis_size("shard")
    replicas = lax.axis_size("replica")
    place = lax.axis_index("replica")
    depth = lax.axis_index("shard")
    core = place % 2
    chip = (place // 2) % CHIPS
    local = width // shards
    half = local // 2
    ff_local = down_weight.shape[0]
    cut = ff_local // CHIPS
    tokens = CHIPS * rows
    group_shards = shards // CHIPS
    q_width = GROUP * HEAD
    qkv_width = q_width + 2 * HEAD
    index = jnp.stack([chip, core, depth]).astype(jnp.int32)
    first = core == 0

    def own_first(value):
        cut_up = value.reshape(value.shape[0], shards, 2, half)
        even = cut_up[:, :, 0].reshape(value.shape[0], width // 2)
        odd = cut_up[:, :, 1].reshape(value.shape[0], width // 2)
        return jnp.concatenate([jnp.where(first, even, odd), jnp.where(first, odd, even)], axis=1)

    def in_order(value):
        left, right = value[:, : width // 2], value[:, width // 2 :]
        even = jnp.where(first, left, right).reshape(value.shape[0], shards, half)
        odd = jnp.where(first, right, left).reshape(value.shape[0], shards, half)
        return jnp.stack([even, odd], axis=2).reshape(value.shape[0], width)

    gain_one = jnp.broadcast_to(attention_gain.astype(f32)[:, None], (local, LANES))
    gain_two = jnp.broadcast_to(feedforward_gain.astype(f32)[:, None], (local, LANES))

    x = own_first(hidden_in)
    xs = plane_gather(x)

    at_block = attention_block(index, query_weight, key_weight, value_weight, output_weight, gain_one)
    at_own = lax.all_gather(at_block, "shard", axis=0, tiled=True)
    gu_own = lax.all_gather(
        feedforward_block(index, gate_weight, up_weight, gain_two, ff_local), "shard", axis=0, tiled=True
    )
    down_cut = lax.dynamic_slice_in_dim(down_weight, chip * cut, cut, 0)
    down_own = lax.all_gather(own_first(down_cut)[:, : width // 2], "shard", axis=0, tiled=True)

    g = own_first(out_grad)

    qkv_own = at_own[:, :qkv_width]
    qkv_other = swap(qkv_own, 1)
    inverse = rope_base ** (-jnp.arange(0, HEAD, 2, dtype=f32) / HEAD)
    places = (depth * rows + jnp.arange(rows, dtype=jnp.int32)).astype(f32)
    angles = inverse[:, None] * places[None, :]
    angles = jnp.concatenate([angles, angles], axis=0)
    cosine, sine = jnp.cos(angles), jnp.sin(angles)

    xhat, queries, kv = qkv_call(xs, qkv_own, qkv_other, cosine, sine)
    kvs = [kv] + [shift(kv, d) for d in range(1, shards)]
    turned, attended, stats = attention_call(index, queries, kvs)

    def out_for(mask):
        start = (chip ^ mask) * group_shards * half
        return lax.dynamic_slice(at_own, (start, qkv_width), (group_shards * half, 512))

    out_pieces = [out_for(0)] + [swap(out_for(m), 2 * m) for m in range(1, CHIPS)]
    out_rows = []
    for piece in out_pieces:
        split = piece.reshape(group_shards, 2, half // 2, 512)
        out_rows.append(
            jnp.concatenate([split[:, 0], split[:, 1]], axis=-1).reshape(-1, width // 2)
        )
    wo_own = jnp.concatenate(out_rows, axis=0)
    wo_other = swap(wo_own, 1)

    def normed(block):
        inverse = lax.rsqrt(jnp.mean(block * block, axis=1, keepdims=True) + norm_eps)
        return ((block * inverse).astype(bf16), inverse)

    wide_x = x.astype(f32)
    middle = wide_x + plane_sum(parts_call((attended,), wo_own, wo_other, False, "attention_out"))
    two, inv_two = normed(middle)
    twos = plane_gather(two)

    gu_other = swap(gu_own, 1)
    down_other = swap(down_own, 1)
    act, for_gate, for_up, two_all = gate_call(twos, gu_own, gu_other)

    g_all = jnp.concatenate(plane_gather(g), axis=0)

    def over_groups(kept):
        if replicas > PIECES:
            groups = [
                [e * PIECES + i for e in range(replicas // PIECES)] for i in range(PIECES)
            ]
            kept = lax.psum(kept, "replica", axis_index_groups=groups)
        return kept

    def reduced(term):
        kept = lax.psum_scatter(term, "shard", scatter_dimension=0, tiled=True)
        return over_groups(kept)

    def plane_pieces(kept):
        mine = plane_gather(kept)
        return mine, [swap(part, 1) for part in mine]

    def mixed(mine, theirs):
        return [part for pair in zip(mine, theirs) for part in pair]

    down_sent = swap(weight_grad(act, None, (g_all,), 1, None, "down_grad_other"), 1)
    down_kept = reduced(weight_grad(act, None, (g_all,), 0, down_sent, "down_grad"))

    grads = hidden_back_call(g_all, down_own, down_other, for_gate, for_up)
    e_two = plane_sum(parts_call((grads,), gu_own, gu_other, True, "feedforward_back"))
    gu_sent = swap(weight_grad(two_all, 1, (grads,), None, None, "gate_grad_other"), 1)
    gu_kept = reduced(weight_grad(two_all, 0, (grads,), None, gu_sent, "gate_grad"))

    def norm_back(e, values, inverse):
        mean_term = jnp.mean(e * values, axis=1, keepdims=True)
        return inverse * e - values * (inverse * inverse * inverse) * mean_term

    grad_middle = g.astype(f32) + norm_back(e_two, middle, inv_two)
    branches = plane_gather(grad_middle.astype(bf16))
    before = None
    for m in range(CHIPS):
        before = attention_back_call(
            index, m, branches[m], wo_own, wo_other, queries, turned, stats, cosine, sine, kvs, before
        )
    grad_q, grad_first, grad_rest = before

    kv_sum = grad_first
    for d in range(1, shards):
        kv_sum = kv_sum + shift(grad_rest[d - 1], -d).astype(f32)
    cos_rows = jnp.tile(cosine.T, (CHIPS, 1))
    sin_rows = jnp.tile(sine.T, (CHIPS, 1))
    k_sum = kv_sum[:, :HEAD]
    k_turned = jnp.concatenate([-k_sum[:, HEAD // 2 :], k_sum[:, : HEAD // 2]], axis=1)
    grad_kv = jnp.concatenate([k_sum * cos_rows - k_turned * sin_rows, kv_sum[:, HEAD:]], axis=1)
    grad_kv = grad_kv.astype(bf16)

    branch_all = jnp.concatenate(branches, axis=0)
    wo_sent = swap(weight_grad(attended, None, (branch_all,), 1, None, "out_grad_other"), 1)
    wo_term = weight_grad(attended, None, (branch_all,), 0, wo_sent, "out_grad")
    wo_cut = q_width // CHIPS
    wo_chips = [wo_term[:wo_cut]] + [
        swap(wo_term[m * wo_cut : (m + 1) * wo_cut], 2 * m) for m in range(1, CHIPS)
    ]
    wo_stack = jnp.stack(wo_chips)
    wo_block = jnp.concatenate(
        [lax.dynamic_index_in_dim(wo_stack, chip ^ i, 0, keepdims=False) for i in range(CHIPS)],
        axis=0,
    )
    wo_kept = reduced(wo_block)

    pair = (grad_q, grad_kv)
    qkv_sent = swap(weight_grad(xhat, 1, pair, None, None, "qkv_grad_other"), 1)
    qkv_kept = reduced(weight_grad(xhat, 0, pair, None, qkv_sent, "qkv_grad"))
    e_one = plane_sum(parts_call(pair, qkv_own, qkv_other, True, "qkv_back"))
    inv_one = normed(wide_x)[1]
    grad_input = in_order((grad_middle + norm_back(e_one, wide_x, inv_one)).astype(bf16))

    out_parts = parts_call((act,), down_own, down_other, False, "feedforward_out")
    output = in_order((middle + plane_sum(out_parts)).astype(bf16))

    down_out = rows_result(index, mixed(*plane_pieces(down_kept)), local, "down_result")
    gu_mine, gu_theirs = plane_pieces(gu_kept)
    gu_out = feedforward_result(index, 0, gu_mine, gate_weight, up_weight, gain_two, ff_local, None)
    gu_out = feedforward_result(index, 1, gu_theirs, gate_weight, up_weight, gain_two, ff_local, gu_out)
    wo_out = rows_result(index, mixed(*plane_pieces(wo_kept)), local, "out_result")
    q_out, k_out, v_out, gain_one_sums = qkv_result(
        index, mixed(*plane_pieces(qkv_kept)), query_weight, key_weight, value_weight, gain_one
    )
    return (
        output,
        grad_input,
        jnp.sum(gain_one_sums, axis=1),
        q_out,
        k_out,
        v_out,
        wo_out,
        jnp.sum(gu_out[2], axis=1),
        gu_out[0],
        gu_out[1],
        down_out,
    )


def solution(mesh):
    return jax.shard_map(
        per_device,
        mesh=mesh,
        in_specs=(
            P(("replica", "shard"), None),
            P("shard"),
            P("shard", None),
            P("shard", None),
            P("shard", None),
            P("shard", None),
            P("shard"),
            P("shard", None),
            P("shard", None),
            P("shard", None),
            P(("replica", "shard"), None),
        ),
        out_specs=(
            P(("replica", "shard"), None),
            P(("replica", "shard"), None),
            P("shard"),
            P("shard", None),
            P("shard", None),
            P("shard", None),
            P("shard", None),
            P("shard"),
            P("shard", None),
            P("shard", None),
            P("shard", None),
        ),
        check_vma=False,
    )
```

```python
import functools

import jax
import jax.numpy as jnp
from jax import lax
from jax.experimental import pallas as pl
from jax.experimental.pallas import tpu as pltpu
from jax.sharding import PartitionSpec as P

HEADS = 32
KV_HEADS = 4
HEAD = 64
GROUP = HEADS // KV_HEADS
CHIPS = 4
PIECES = 2 * CHIPS
LANES = 128

norm_eps = 1e-05
rope_base = 10000.0
masked_score = -1e30

f32 = jnp.float32
bf16 = jnp.bfloat16
VMEM = pltpu.VMEM
NT = (((1,), (1,)), ((), ()))
TN = (((0,), (0,)), ((), ()))


def dot(left, right):
    return jnp.dot(left, right, preferred_element_type=f32)


def dot_nt(left, right):
    return lax.dot_general(left, right, NT, preferred_element_type=f32)


def dot_tn(left, right):
    return lax.dot_general(left, right, TN, preferred_element_type=f32)


def shape(dims, kind):
    return jax.ShapeDtypeStruct(dims, kind)


def whole():
    return pl.BlockSpec(memory_space=VMEM)


def kernel_call(body, out_shape, in_specs, out_specs, operands, *, index=None, grid=(), scratch=(),
                flops=0, moved=0, exps=0, aliases=None, name=None):
    params = pltpu.CompilerParams(
        vmem_limit_bytes=52 * 2**20, dimension_semantics=("arbitrary",) * len(grid)
    )
    cost = pl.CostEstimate(flops=0, bytes_accessed=0, transcendentals=0)
    common = dict(
        out_shape=out_shape,
        compiler_params=params,
        cost_estimate=cost,
        input_output_aliases=aliases or {},
        name=name,
    )
    if index is None:
        spec = pl.GridSpec(grid=grid, in_specs=in_specs, out_specs=out_specs, scratch_shapes=scratch)
        return pl.pallas_call(body, grid_spec=spec, **common)(*operands)
    spec = pltpu.PrefetchScalarGridSpec(
        num_scalar_prefetch=1, grid=grid, in_specs=in_specs, out_specs=out_specs,
        scratch_shapes=scratch,
    )
    return pl.pallas_call(body, grid_spec=spec, **common)(index, *operands)


def swap(value, mask):
    size = lax.axis_size("replica")
    return lax.ppermute(value, "replica", [(i, i ^ mask) for i in range(size)])


def shift(value, step):
    size = lax.axis_size("shard")
    pairs = [(i, i + step) for i in range(size) if 0 <= i + step < size]
    return lax.ppermute(value, "shard", pairs)


def plane_gather(value):
    return [value] + [swap(value, 2 * m) for m in range(1, CHIPS)]


def plane_send(parts):
    return [parts[0]] + [swap(parts[m], 2 * m) for m in range(1, CHIPS)]


def after(value, *others):
    return lax.optimization_barrier((value, *others))[0]


def attention_block_body(local, group_shards, index, q, k, v, o, gain, out):
    scale = gain[:, :1]
    q_width = GROUP * HEAD
    cut = local // CHIPS
    for chip in range(CHIPS):

        @pl.when(index[0] == chip)
        def _():
            parts = []
            for m in range(CHIPS):
                for s in range(group_shards):
                    start = chip * q_width + s * local + (m ^ chip) * cut
                    parts.append(q[:, start : start + cut])
            parts.append(k[:, chip * HEAD : (chip + 1) * HEAD])
            parts.append(v[:, chip * HEAD : (chip + 1) * HEAD])
            wide = jnp.concatenate([part.astype(f32) for part in parts], axis=1)
            out[:, : q_width + 2 * HEAD] = (wide * scale).astype(bf16)

    half = local // 2
    shards = o.shape[1] // local
    for core in range(2):

        @pl.when(index[1] == core)
        def _():
            base = q_width + 2 * HEAD
            for s in range(shards):
                piece = o[:, s * local + core * half : s * local + (core + 1) * half]
                spot = s * half
                row, column = (0, spot) if spot < 512 else (cut, spot - 512)
                out[row : row + cut, base + column : base + column + half] = piece


def attention_block(index, query, key, value, output, gain):
    local, width = query.shape
    half = local // 2
    shards = width // local
    return kernel_call(
        functools.partial(attention_block_body, local, shards // CHIPS),
        shape((half, GROUP * HEAD + 2 * HEAD + 512), bf16),
        [
            pl.BlockSpec((half, width), lambda i, n: (n[1], 0)),
            pl.BlockSpec((half, key.shape[1]), lambda i, n: (n[1], 0)),
            pl.BlockSpec((half, key.shape[1]), lambda i, n: (n[1], 0)),
            pl.BlockSpec((local // CHIPS, width), lambda i, n: (n[0], 0)),
            pl.BlockSpec((half, LANES), lambda i, n: (n[1], 0)),
        ],
        pl.BlockSpec((half, GROUP * HEAD + 2 * HEAD + 512), lambda i, n: (0, 0)),
        (query, key, value, output, gain),
        index=index,
        grid=(1,),
        moved=3e6,
        name="attention_block",
    )


def feedforward_block_body(ff_local, cut, index, gate, up, gain, out):
    scale = gain[:, :1]
    shards = gate.shape[1] // ff_local
    width = shards * cut
    for chip in range(CHIPS):

        @pl.when(index[0] == chip)
        def _():
            for n, source in enumerate((gate, up)):
                parts = [
                    source[:, s * ff_local + chip * cut : s * ff_local + (chip + 1) * cut].astype(f32)
                    for s in range(shards)
                ]
                wide = jnp.concatenate(parts, axis=1)
                out[:, n * width : (n + 1) * width] = (wide * scale).astype(bf16)


def feedforward_block(index, gate, up, gain, ff_local):
    local, ff = gate.shape
    half = local // 2
    rows = 64
    steps = half // rows
    cut = ff_local // CHIPS
    width = 2 * (ff // CHIPS)
    return kernel_call(
        functools.partial(feedforward_block_body, ff_local, cut),
        shape((half, width), bf16),
        [
            pl.BlockSpec((rows, ff), lambda i, n: (n[1] * steps + i, 0)),
            pl.BlockSpec((rows, ff), lambda i, n: (n[1] * steps + i, 0)),
            pl.BlockSpec((rows, LANES), lambda i, n: (n[1] * steps + i, 0)),
        ],
        pl.BlockSpec((rows, width), lambda i, n: (i, 0)),
        (gate, up, gain),
        index=index,
        grid=(steps,),
        moved=4 * half * ff + 2 * half * width,
        name="feedforward_block",
    )


def own_first_body(local, index, *refs):
    count = len(refs) // 2
    half = local // 2
    for core in range(2):

        @pl.when(index[1] == core)
        def _():
            for source, out in zip(refs[:count], refs[count:]):
                shards = source.shape[1] // local
                sides = out.shape[1] // (shards * half)
                for side in range(sides):
                    for s in range(shards):
                        start = s * local + (core ^ side) * half
                        spot = (side * shards + s) * half
                        out[:, spot : spot + half] = source[:, start : start + half]


def own_first(index, sources, local, halves=2):
    return kernel_call(
        functools.partial(own_first_body, local),
        tuple(shape((v.shape[0], v.shape[1] * halves // 2), bf16) for v in sources),
        [pl.BlockSpec(v.shape, lambda i, n: (0, 0)) for v in sources],
        tuple(
            pl.BlockSpec((v.shape[0], v.shape[1] * halves // 2), lambda i, n: (0, 0)) for v in sources
        ),
        tuple(sources),
        index=index,
        grid=(1,),
        name="own_first",
    )


def down_block_body(local, index, source, out):
    own_first_body(local, index, source, out)


def down_block(index, down, local):
    ff_local, width = down.shape
    cut = ff_local // CHIPS
    return kernel_call(
        functools.partial(down_block_body, local),
        shape((cut, width // 2), bf16),
        [pl.BlockSpec((cut, width), lambda i, n: (n[0], 0))],
        pl.BlockSpec((cut, width // 2), lambda i, n: (0, 0)),
        (down,),
        index=index,
        grid=(1,),
        name="down_block",
    )


def part_sum(parts):
    total = parts[0][...]
    for part in parts[1:]:
        total = total + part[...].astype(f32)
    return total


def mean_of(values):
    return jnp.mean(values, axis=1, keepdims=True)


def middle_body(*refs):
    parts, (x, middle, two) = refs[:CHIPS], refs[CHIPS:]
    total = x[...].astype(f32) + part_sum(parts)
    middle[...] = total
    two[...] = (total * lax.rsqrt(mean_of(total * total) + norm_eps)).astype(bf16)


def middle_call(parts, x):
    return kernel_call(
        middle_body,
        (shape(x.shape, f32), shape(x.shape, bf16)),
        [whole()] * (CHIPS + 1),
        (whole(), whole()),
        (*parts, x),
        name="middle",
    )


def norm_back(e, values):
    inverse = lax.rsqrt(mean_of(values * values) + norm_eps)
    return inverse * e - values * (inverse * inverse * inverse) * mean_of(e * values)


def grad_middle_body(*refs):
    parts, (middle, g, grad, low) = refs[:CHIPS], refs[CHIPS:]
    total = g[...].astype(f32) + norm_back(part_sum(parts), middle[...])
    grad[...] = total
    low[...] = total.astype(bf16)


def grad_middle_call(parts, middle, g):
    return kernel_call(
        grad_middle_body,
        (shape(g.shape, f32), shape(g.shape, bf16)),
        [whole()] * (CHIPS + 2),
        (whole(), whole()),
        (*parts, middle, g),
        name="grad_middle",
    )


def store_in_order(local, index, value, out):
    half = local // 2
    shards = out.shape[1] // local
    for core in range(2):

        @pl.when(index[1] == core)
        def _():
            for side in range(2):
                for s in range(shards):
                    spot = s * local + (core ^ side) * half
                    start = (side * shards + s) * half
                    out[:, spot : spot + half] = value[:, start : start + half].astype(bf16)


def output_body(local, index, *refs):
    parts, (middle, out) = refs[:CHIPS], refs[CHIPS:]
    store_in_order(local, index, middle[...] + part_sum(parts), out)


def output_call(index, parts, middle, local):
    spec = pl.BlockSpec(middle.shape, lambda i, n: (0, 0))
    return kernel_call(
        functools.partial(output_body, local),
        shape(middle.shape, bf16),
        [spec] * (CHIPS + 1),
        spec,
        (*parts, middle),
        index=index,
        grid=(1,),
        name="output",
    )


def grad_input_body(local, index, *refs):
    parts, (x, grad, out) = refs[:CHIPS], refs[CHIPS:]
    total = grad[...] + norm_back(part_sum(parts), x[...].astype(f32))
    store_in_order(local, index, total, out)


def grad_input_call(index, parts, x, grad, local):
    spec = pl.BlockSpec(x.shape, lambda i, n: (0, 0))
    return kernel_call(
        functools.partial(grad_input_body, local),
        shape(x.shape, bf16),
        [spec] * (CHIPS + 2),
        spec,
        (*parts, x, grad),
        index=index,
        grid=(1,),
        name="grad_input",
    )


def grad_kv_body(shards, *refs):
    first, rest, (cosine, sine, out) = refs[0], refs[1:shards], refs[shards:]
    total = first[...]
    for term in rest:
        total = total + term[...].astype(f32)
    rows = cosine.shape[1]
    cos, sin = cosine[...], sine[...]
    for m in range(CHIPS):
        turned = total[m * rows : (m + 1) * rows, :].T
        k = turned[:HEAD]
        k = k * cos - half_rotated(k) * sin
        both = jnp.concatenate([k, turned[HEAD:]], axis=0)
        out[m * rows : (m + 1) * rows, :] = both.T.astype(bf16)


def grad_kv_call(first, rest, cosine, sine):
    return kernel_call(
        functools.partial(grad_kv_body, len(rest) + 1),
        shape(first.shape, bf16),
        [whole()] * (len(rest) + 3),
        whole(),
        (first, *rest, cosine, sine),
        name="grad_kv",
    )


def half_rotated(values):
    middle = values.shape[0] // 2
    return jnp.concatenate([-values[middle:], values[:middle]], axis=0)


def qkv_body(*refs):
    xs, (own, other, cosine, sine), (xhat, queries, kv) = refs[:CHIPS], refs[CHIPS : CHIPS + 4], refs[CHIPS + 4 :]
    rows, width = xs[0].shape
    for m in range(CHIPS):
        x = xs[m][...].astype(f32)
        inverse = lax.rsqrt(jnp.mean(x * x, axis=1, keepdims=True) + norm_eps)
        xhat[m * rows : (m + 1) * rows, :] = (x * inverse).astype(bf16)
    cos, sin = cosine[...], sine[...]
    for m in range(CHIPS):
        block = xhat[m * rows : (m + 1) * rows, :]
        total = dot(block[:, : width // 2], own[...]) + dot(block[:, width // 2 :], other[...])
        turned = total.T
        for h in range(GROUP + 1):
            u = turned[h * HEAD : (h + 1) * HEAD]
            u = u * cos + half_rotated(u) * sin
            if h < GROUP:
                queries[m, h * HEAD : (h + 1) * HEAD, :] = (u * HEAD ** (-0.5)).astype(bf16)
            else:
                both = jnp.concatenate([u, turned[(h + 1) * HEAD :]], axis=0)
                kv[m * rows : (m + 1) * rows, :] = both.T.astype(bf16)


def qkv_call(xs, own, other, cosine, sine):
    rows, width = xs[0].shape
    tokens = CHIPS * rows
    return kernel_call(
        qkv_body,
        (
            shape((tokens, width), bf16),
            shape((CHIPS, GROUP * HEAD, rows), bf16),
            shape((tokens, 2 * HEAD), bf16),
        ),
        [whole()] * (CHIPS + 4),
        (whole(), whole(), whole()),
        (*xs, own, other, cosine, sine),
        flops=2 * tokens * width * own.shape[1],
        moved=10e6,
        name="qkv",
    )


def set_bias(bias, depth, shards):
    rows = bias.shape[1]
    key = lax.broadcasted_iota(jnp.int32, bias.shape, 0)
    mine = lax.broadcasted_iota(jnp.int32, bias.shape, 1)
    limit = jnp.where(key < rows, mine, (depth + 1) * rows - 1)
    bias[...] = jnp.where(key <= limit, 0.0, masked_score)


def attention_body(shards, index, queries, *refs):
    kvs = refs[:shards]
    turned_out, out, stats, bias, kv_all, out_turned = refs[shards:]
    rows = queries.shape[2]

    @pl.when(pl.program_id(0) == 0)
    def _():
        set_bias(bias, index[2], shards)

    for d in range(shards):
        kv_all[d * rows : (d + 1) * rows, :] = kvs[d][...]
    kv = kv_all[...]
    v_turned = kv.astype(f32).T[HEAD:].astype(bf16)
    zeros = jnp.zeros((HEAD, rows), bf16)
    for h in range(GROUP):
        q = jnp.concatenate([queries[0, h * HEAD : (h + 1) * HEAD, :], zeros], axis=0)
        scores = dot(kv, q) + bias[...]
        top = jnp.max(scores, axis=0, keepdims=True)
        terms = jnp.exp(scores - top)
        total = jnp.sum(terms, axis=0, keepdims=True)
        mixed = dot(v_turned, terms.astype(bf16)) / total
        out_turned[h * HEAD : (h + 1) * HEAD, :] = mixed
        stats[0, h : h + 1, :] = top + jnp.log(total)
    turned_out[0] = out_turned[...].astype(bf16)
    out[...] = out_turned[...].T.astype(bf16)


def attention_call(index, queries, kvs):
    chips, width, rows = queries.shape
    shards = len(kvs)
    keys = shards * rows
    return kernel_call(
        functools.partial(attention_body, shards),
        (
            shape((chips, width, rows), bf16),
            shape((chips * rows, width), bf16),
            shape((chips, GROUP, rows), f32),
        ),
        [pl.BlockSpec((1, width, rows), lambda i, n: (i, 0, 0))]
        + [pl.BlockSpec((rows, 2 * HEAD), lambda i, n: (i, 0))] * shards,
        (
            pl.BlockSpec((1, width, rows), lambda i, n: (i, 0, 0)),
            pl.BlockSpec((rows, width), lambda i, n: (i, 0)),
            pl.BlockSpec((1, GROUP, rows), lambda i, n: (i, 0, 0)),
        ),
        (queries, *kvs),
        index=index,
        grid=(chips,),
        scratch=(
            VMEM((keys, rows), f32),
            VMEM((keys, 2 * HEAD), bf16),
            VMEM((width, rows), f32),
        ),
        flops=chips * GROUP * 4 * keys * rows * 2 * HEAD,
        exps=chips * GROUP * keys * rows,
        moved=4e6,
        name="attention",
    )


def attention_back_body(shards, index, branch, wo_own, wo_other, queries, turned_out, stats, cosine, sine, *refs):
    kvs = refs[:shards]
    grad_q, grad_first, grad_rest, bias, kv_all, q_turned, total = refs[-7:]
    rows = queries.shape[2]
    width = branch.shape[1]
    set_bias(bias, index[2], shards)
    for d in range(shards):
        kv_all[d * rows : (d + 1) * rows, :] = kvs[d][...]
    kv = kv_all[...]
    k_turned = kv.astype(f32).T[:HEAD].astype(bf16)
    grad_out = dot_nt(wo_own[...], branch[:, : width // 2])
    grad_out = (grad_out + dot_nt(wo_other[...], branch[:, width // 2 :])).astype(bf16)
    zeros = jnp.zeros((HEAD, rows), bf16)
    cos, sin = cosine[...], sine[...]
    for h in range(GROUP):
        span = slice(h * HEAD, (h + 1) * HEAD)
        q = jnp.concatenate([queries[0, span, :], zeros], axis=0)
        mine = grad_out[span]
        padded = jnp.concatenate([zeros, mine], axis=0)
        probs = jnp.exp(dot(kv, q) + bias[...] - stats[0, h : h + 1, :])
        delta = jnp.sum(
            mine.astype(f32) * turned_out[0, span, :].astype(f32), axis=0, keepdims=True
        )
        grad_scores = (probs * (dot(kv, padded) - delta)).astype(bf16)
        u = dot(k_turned, grad_scores) * HEAD ** (-0.5)
        q_turned[span, :] = u * cos - half_rotated(u) * sin
        term = dot_nt(grad_scores, q) + dot_nt(probs.astype(bf16), padded)
        if h == 0:
            total[...] = term
        else:
            total[...] += term
    grad_q[...] = q_turned[...].T.astype(bf16)
    grad_first[...] = total[:rows, :]
    for d in range(1, shards):
        grad_rest[d - 1] = total[d * rows : (d + 1) * rows, :].astype(bf16)


def attention_back_call(index, m, branch, wo_own, wo_other, queries, turned_out, stats, cosine, sine, kvs, before):
    chips, width, rows = queries.shape
    shards = len(kvs)
    keys = shards * rows
    tokens = chips * rows
    fixed = pl.BlockSpec((1, width, rows), lambda i, n: (m, 0, 0))
    in_specs = [
        whole(), whole(), whole(), fixed, fixed,
        pl.BlockSpec((1, GROUP, rows), lambda i, n: (m, 0, 0)), whole(), whole(),
    ] + [pl.BlockSpec((rows, 2 * HEAD), lambda i, n: (m, 0))] * shards
    operands = (branch, wo_own, wo_other, queries, turned_out, stats, cosine, sine, *kvs)
    aliases = {}
    if before is not None:
        aliases = {1 + len(operands) + n: n for n in range(3)}
        in_specs = in_specs + [pl.BlockSpec(memory_space=pl.ANY)] * 3
        operands = operands + tuple(before)
    return kernel_call(
        functools.partial(attention_back_body, shards),
        (
            shape((tokens, width), bf16),
            shape((tokens, 2 * HEAD), f32),
            shape((shards - 1, tokens, 2 * HEAD), bf16),
        ),
        in_specs,
        (
            pl.BlockSpec((rows, width), lambda i, n: (m, 0)),
            pl.BlockSpec((rows, 2 * HEAD), lambda i, n: (m, 0)),
            pl.BlockSpec((shards - 1, rows, 2 * HEAD), lambda i, n: (0, m, 0)),
        ),
        operands,
        index=index,
        grid=(1,),
        scratch=(
            VMEM((keys, rows), f32),
            VMEM((keys, 2 * HEAD), bf16),
            VMEM((width, rows), f32),
            VMEM((keys, 2 * HEAD), f32),
        ),
        flops=GROUP * 10 * keys * rows * 2 * HEAD + 2 * rows * width * branch.shape[1],
        exps=GROUP * keys * rows,
        moved=5e6,
        aliases=aliases,
        name="attention_back",
    )


def parts_body(steps, transposed, widths, *refs):
    count = len(widths)
    lefts, (own, other), outs = refs[:count], refs[count : count + 2], refs[count + 2 :]
    rows = outs[0].shape[0]
    step = pl.program_id(0)

    def run(weight):
        start = 0
        total = None
        for left, wide in zip(lefts, widths):
            if transposed:
                term = dot_nt(left[...], weight[:, start : start + wide])
            else:
                term = dot(left[...], weight[start : start + wide, :])
            total = term if total is None else total + term
            start += wide
        for m in range(CHIPS):
            outs[m][...] = total[m * rows : (m + 1) * rows, :].astype(outs[m].dtype)

    @pl.when(step < steps)
    def _():
        run(own)

    @pl.when(step >= steps)
    def _():
        run(other)


def parts_call(lefts, own, other, transposed, name):
    tokens = lefts[0].shape[0]
    rows = tokens // CHIPS
    widths = tuple(left.shape[1] for left in lefts)
    depth = sum(widths)
    half = own.shape[0] if transposed else own.shape[1]
    tile = 256
    steps = half // tile
    last = steps - 1
    if transposed:
        weight_specs = [
            pl.BlockSpec((tile, depth), lambda j: (jnp.minimum(j, last), 0)),
            pl.BlockSpec((tile, depth), lambda j: (jnp.maximum(j - steps, 0), 0)),
        ]
    else:
        weight_specs = [
            pl.BlockSpec((depth, tile), lambda j: (0, jnp.minimum(j, last))),
            pl.BlockSpec((depth, tile), lambda j: (0, jnp.maximum(j - steps, 0))),
        ]
    return kernel_call(
        functools.partial(parts_body, steps, transposed, widths),
        tuple(shape((rows, 2 * half), f32 if m == 0 else bf16) for m in range(CHIPS)),
        [pl.BlockSpec((tokens, wide), lambda j: (0, 0)) for wide in widths] + weight_specs,
        tuple(pl.BlockSpec((rows, tile), lambda j: (0, j)) for _ in range(CHIPS)),
        (*lefts, own, other),
        grid=(2 * steps,),
        flops=4 * tokens * depth * half,
        moved=2 * tokens * depth + 4 * depth * half + 4 * tokens * half,
        name=name,
    )


def gate_body(*refs):
    twos = refs[:CHIPS]
    gate_own, up_own, gate_other, up_other, act, for_gate, for_up, two_all = refs[CHIPS:]
    rows, width = twos[0].shape
    half = width // 2

    @pl.when(pl.program_id(0) == 0)
    def _():
        for m in range(CHIPS):
            two_all[m * rows : (m + 1) * rows, :] = twos[m][...]

    own = jnp.concatenate([gate_own[...], up_own[...]], axis=1)
    other = jnp.concatenate([gate_other[...], up_other[...]], axis=1)
    both = dot(two_all[:, :half], own) + dot(two_all[:, half:], other)
    wide = gate_own.shape[1]
    gate, up = both[:, :wide], both[:, wide:]
    sig = 1.0 / (1.0 + jnp.exp(-gate))
    silu = gate * sig
    act[...] = (silu * up).astype(bf16)
    for_gate[...] = (up * sig * (1.0 + gate * (1.0 - sig))).astype(bf16)
    for_up[...] = silu.astype(bf16)


def gate_call(twos, own, other):
    rows, width = twos[0].shape
    tokens = CHIPS * rows
    half = width // 2
    ff = own.shape[1] // 2
    tile = LANES
    steps = ff // tile
    weight = [
        pl.BlockSpec((half, tile), lambda j: (0, j)),
        pl.BlockSpec((half, tile), lambda j: (0, j + steps)),
    ]
    column = pl.BlockSpec((tokens, tile), lambda j: (0, j))
    return kernel_call(
        gate_body,
        tuple(shape((tokens, ff), bf16) for _ in range(3)) + (shape((tokens, width), bf16),),
        [pl.BlockSpec((rows, width), lambda j: (0, 0))] * CHIPS + weight + weight,
        (column, column, column, pl.BlockSpec((tokens, width), lambda j: (0, 0))),
        (*twos, own, own, other, other),
        grid=(steps,),
        flops=4 * tokens * width * ff,
        moved=4 * tokens * width + 4 * width * ff + 6 * tokens * ff,
        exps=tokens * ff,
        name="gate",
    )


def hidden_back_body(g, own, other, for_gate, for_up, grads):
    half = g.shape[1] // 2
    ff = own.shape[0]
    hidden = dot_nt(g[:, :half], own[...]) + dot_nt(g[:, half:], other[...])
    grads[:, :ff] = (hidden * for_gate[...].astype(f32)).astype(bf16)
    grads[:, ff:] = (hidden * for_up[...].astype(f32)).astype(bf16)


def hidden_back_call(g, own, other, for_gate, for_up):
    tokens, width = g.shape
    ff, half = own.shape
    block = tokens // 2
    row = lambda i: (i, 0)
    fixed = lambda i: (0, 0)
    return kernel_call(
        hidden_back_body,
        shape((tokens, 2 * ff), bf16),
        [
            pl.BlockSpec((block, width), row),
            pl.BlockSpec((ff, half), fixed),
            pl.BlockSpec((ff, half), fixed),
            pl.BlockSpec((block, ff), row),
            pl.BlockSpec((block, ff), row),
        ],
        pl.BlockSpec((block, 2 * ff), row),
        (g, own, other, for_gate, for_up),
        grid=(2,),
        flops=2 * tokens * width * ff,
        moved=2 * tokens * width + 4 * ff * half + 8 * tokens * ff,
        name="hidden_back",
    )


def weight_grad_body(count, added, left, *refs):
    rights, out = refs[:count], refs[-1]
    start = 0
    for right in rights:
        wide = right.shape[1]
        term = dot_tn(left[...], right[...])
        if added:
            term = term + refs[count][:, start : start + wide].astype(f32)
        out[:, start : start + wide] = term.astype(bf16)
        start += wide


def weight_grad(left, left_side, rights, right_side, added, name):
    tokens = left.shape[0]
    rows = left.shape[1] // (1 if left_side is None else 2)
    tile = 256 if rows % 256 == 0 else LANES
    steps = rows // tile
    first = 0 if left_side is None else left_side * steps
    wides = [right.shape[1] // (1 if right_side is None else 2) for right in rights]
    spot = 0 if right_side is None else right_side
    width = sum(wides)
    in_specs = [pl.BlockSpec((tokens, tile), lambda i: (0, first + i))]
    in_specs += [pl.BlockSpec((tokens, wide), lambda i: (0, spot)) for wide in wides]
    operands = (left, *rights)
    if added is not None:
        in_specs.append(pl.BlockSpec((tile, width), lambda i: (i, 0)))
        operands = operands + (added,)
    return kernel_call(
        functools.partial(weight_grad_body, len(rights), added is not None),
        shape((rows, width), bf16),
        in_specs,
        pl.BlockSpec((tile, width), lambda i: (i, 0)),
        operands,
        grid=(steps,),
        flops=2 * tokens * rows * width,
        moved=2 * tokens * (rows + width) + 4 * rows * width,
        name=name,
    )


def rows_result_body(local, index, *refs):
    pieces, out = refs[:PIECES], refs[PIECES]
    half = local // 2
    shards = out.shape[1] // local
    for m in range(CHIPS):
        for core in range(2):

            @pl.when((pl.program_id(0) == m) & (index[1] == core))
            def _():
                for side in range(2):
                    piece = pieces[2 * m + side]
                    for s in range(shards):
                        spot = s * local + (core ^ side) * half
                        out[:, spot : spot + half] = piece[:, s * half : (s + 1) * half].astype(f32)


def rows_result(index, pieces, local, name):
    cut, half_width = pieces[0].shape
    return kernel_call(
        functools.partial(rows_result_body, local),
        shape((CHIPS * cut, 2 * half_width), f32),
        [pl.BlockSpec((cut, half_width), lambda i, n: (0, 0))] * PIECES,
        pl.BlockSpec((cut, 2 * half_width), lambda i, n: (n[0] ^ i, 0)),
        tuple(pieces),
        index=index,
        grid=(CHIPS,),
        moved=PIECES * cut * half_width * 6,
        name=name,
    )


def out_result_body(local, base, index, *refs):
    pieces, out = refs[:PIECES], refs[PIECES]
    half = local // 2
    cut = local // CHIPS
    shards = out.shape[1] // local
    for m in range(CHIPS):
        for core in range(2):

            @pl.when((pl.program_id(0) == m) & (index[1] == core))
            def _():
                for side in range(2):
                    piece = pieces[2 * m + side]
                    for s in range(shards):
                        spot = s * local + (core ^ side) * half
                        row, column = (0, s * half) if s * half < 512 else (cut, s * half - 512)
                        column += base
                        out[:, spot : spot + half] = piece[row : row + cut, column : column + half].astype(f32)


def out_result(index, pieces, local, width, base):
    cut = local // CHIPS
    return kernel_call(
        functools.partial(out_result_body, local, base),
        shape((local, width), f32),
        [pl.BlockSpec(pieces[0].shape, lambda i, n: (0, 0))] * PIECES,
        pl.BlockSpec((cut, width), lambda i, n: (n[0] ^ i, 0)),
        tuple(pieces),
        index=index,
        grid=(CHIPS,),
        name="out_result",
    )


def lane_sum(value):
    total = value[:, :LANES]
    for n in range(1, value.shape[1] // LANES):
        total = total + value[:, n * LANES : (n + 1) * LANES]
    return total


def feedforward_result_body(ff_local, cut, index, *refs):
    pieces = refs[:CHIPS]
    gate_weight, up_weight, gain = refs[CHIPS : CHIPS + 3]
    gate_out, up_out, gain_out = refs[-3:]
    shards = gate_weight.shape[1] // ff_local
    width = shards * cut
    for chip in range(CHIPS):

        @pl.when(index[0] == chip)
        def _():
            @pl.loop(0, gate_out.shape[0] // 16)
            def _(n):
                rows = pl.ds(pl.multiple_of(n * 16, 16), 16)
                scale = gain[rows, :1]
                total = jnp.zeros((16, LANES), f32)
                for base, weight, out in ((0, gate_weight, gate_out), (width, up_weight, up_out)):
                    parts = []
                    for s in range(shards):
                        for owner in range(CHIPS):
                            start = base + s * cut
                            parts.append(pieces[owner ^ chip][rows, start : start + cut].astype(f32))
                    wide = jnp.concatenate(parts, axis=1)
                    total = total + lane_sum(wide * weight[rows, :].astype(f32))
                    out[rows, :] = wide * scale
                gain_out[rows, :] = total


def feedforward_result(index, side, pieces, gate_weight, up_weight, gain, ff_local, before):
    local, ff = gate_weight.shape
    half = local // 2
    rows = 64
    steps = half // rows
    row = lambda i, n: ((n[1] ^ side) * steps + i, 0)
    in_specs = [pl.BlockSpec((rows, pieces[0].shape[1]), lambda i, n: (i, 0))] * CHIPS
    in_specs += [pl.BlockSpec((rows, ff), row)] * 2 + [pl.BlockSpec((rows, LANES), row)]
    operands = (*pieces, gate_weight, up_weight, gain)
    aliases = {}
    if before is not None:
        aliases = {1 + len(operands) + n: n for n in range(3)}
        in_specs = in_specs + [pl.BlockSpec(memory_space=pl.ANY)] * 3
        operands = operands + tuple(before)
    return kernel_call(
        functools.partial(feedforward_result_body, ff_local, ff_local // CHIPS),
        (shape((local, ff), f32), shape((local, ff), f32), shape((local, LANES), f32)),
        in_specs,
        (pl.BlockSpec((rows, ff), row), pl.BlockSpec((rows, ff), row), pl.BlockSpec((rows, LANES), row)),
        operands,
        index=index,
        grid=(steps,),
        moved=half * ff * 16,
        aliases=aliases,
        name="feedforward_result",
    )


def qkv_result_body(local, group_shards, index, *refs):
    pieces = refs[:PIECES]
    weights, gain = refs[PIECES : PIECES + 3], refs[PIECES + 3]
    outs, gain_out = refs[PIECES + 4 : PIECES + 7], refs[PIECES + 7]
    q_width = GROUP * HEAD
    cut = local // CHIPS
    scale = gain[:, :1]
    for chip in range(CHIPS):
        for side in range(2):

            @pl.when((index[0] == chip) & (pl.program_id(0) == side))
            def _():
                parts, k_parts, v_parts = [], [], []
                for owner in range(CHIPS):
                    piece = pieces[2 * (owner ^ chip) + side]
                    for s in range(group_shards):
                        for j in range(CHIPS):
                            start = ((j ^ owner) * group_shards + s) * cut
                            parts.append(piece[:, start : start + cut].astype(f32))
                    k_parts.append(piece[:, q_width : q_width + HEAD].astype(f32))
                    v_parts.append(piece[:, q_width + HEAD : q_width + 2 * HEAD].astype(f32))
                total = jnp.zeros((gain.shape[0], LANES), f32)
                for part, weight, out in zip((parts, k_parts, v_parts), weights, outs):
                    wide = jnp.concatenate(part, axis=1)
                    total = total + lane_sum(wide * weight[...].astype(f32))
                    out[...] = wide * scale
                gain_out[...] = total


def qkv_result(index, pieces, query, key, value, gain):
    local, width = query.shape
    half = local // 2
    group_shards = width // local // CHIPS
    row = lambda i, n: (n[1] ^ i, 0)
    kv_width = key.shape[1]
    return kernel_call(
        functools.partial(qkv_result_body, local, group_shards),
        (
            shape((local, width), f32),
            shape((local, kv_width), f32),
            shape((local, kv_width), f32),
            shape((local, LANES), f32),
        ),
        [pl.BlockSpec(pieces[0].shape, lambda i, n: (0, 0))] * PIECES
        + [
            pl.BlockSpec((half, width), row),
            pl.BlockSpec((half, kv_width), row),
            pl.BlockSpec((half, kv_width), row),
            pl.BlockSpec((half, LANES), row),
        ],
        (
            pl.BlockSpec((half, width), row),
            pl.BlockSpec((half, kv_width), row),
            pl.BlockSpec((half, kv_width), row),
            pl.BlockSpec((half, LANES), row),
        ),
        (*pieces, query, key, value, gain),
        index=index,
        grid=(2,),
        moved=local * width * 10,
        name="qkv_result",
    )


def per_device(
    hidden_in,
    attention_gain,
    query_weight,
    key_weight,
    value_weight,
    output_weight,
    feedforward_gain,
    gate_weight,
    up_weight,
    down_weight,
    out_grad,
):
    rows, width = hidden_in.shape
    shards = lax.axis_size("shard")
    replicas = lax.axis_size("replica")
    place = lax.axis_index("replica")
    depth = lax.axis_index("shard")
    core = place & 1
    chip = (place >> 1) & (CHIPS - 1)
    local = width // shards
    half = local // 2
    ff_local = down_weight.shape[0]
    group_shards = shards // CHIPS
    q_width = GROUP * HEAD
    qkv_width = q_width + 2 * HEAD
    index = jnp.stack([chip, core, depth]).astype(jnp.int32)

    gain_one = jnp.broadcast_to(attention_gain.astype(f32)[:, None], (local, LANES))
    gain_two = jnp.broadcast_to(feedforward_gain.astype(f32)[:, None], (local, LANES))

    x = own_first(index, (hidden_in,), local)[0]
    xs = plane_gather(x)

    at_block = attention_block(index, query_weight, key_weight, value_weight, output_weight, after(gain_one, x))
    at_own = lax.all_gather(at_block, "shard", axis=0, tiled=True)
    gu_block = feedforward_block(index, gate_weight, up_weight, after(gain_two, at_block), ff_local)
    gu_own = lax.all_gather(gu_block, "shard", axis=0, tiled=True)
    down_own = lax.all_gather(down_block(index, down_weight, local), "shard", axis=0, tiled=True)
    at_own = after(at_own, gu_block, *xs[1:])
    g = own_first(index, (out_grad,), local)[0]

    qkv_own = at_own[:, :qkv_width]
    qkv_other = swap(qkv_own, 1)
    inverse = rope_base ** (-jnp.arange(0, HEAD, 2, dtype=f32) / HEAD)
    places = (depth * rows + jnp.arange(rows, dtype=jnp.int32)).astype(f32)
    angles = inverse[:, None] * places[None, :]
    angles = jnp.concatenate([angles, angles], axis=0)
    cosine, sine = jnp.cos(angles), jnp.sin(angles)

    xhat, queries, kv = qkv_call(xs, qkv_own, qkv_other, cosine, sine)
    kvs = [kv] + [shift(kv, d) for d in range(1, shards)]
    g_all = jnp.concatenate(plane_gather(after(g, kv)), axis=0)
    turned, attended, stats = attention_call(index, queries, kvs)

    at_late = after(at_own, kv)

    def out_for(mask):
        start = (chip ^ mask) * group_shards * half
        return lax.dynamic_slice(at_late, (start, qkv_width), (group_shards * half, 512))

    out_pieces = [out_for(0)] + [swap(out_for(m), 2 * m) for m in range(1, CHIPS)]
    out_rows = []
    for piece in out_pieces:
        split = piece.reshape(group_shards, 2, half // 2, 512)
        out_rows.append(
            jnp.concatenate([split[:, 0], split[:, 1]], axis=-1).reshape(-1, width // 2)
        )
    wo_own = jnp.concatenate(out_rows, axis=0)
    wo_other = swap(wo_own, 1)

    attended_late = after(attended, g_all)
    mid_parts = plane_send(parts_call((attended_late,), wo_own, wo_other, False, "attention_out"))
    middle, two = middle_call(mid_parts, x)
    twos = plane_gather(two)

    gu_own = after(gu_own, *twos[1:])
    gu_other = swap(gu_own, 1)
    down_own = after(down_own, gu_other)
    down_other = swap(down_own, 1)
    act, for_gate, for_up, two_all = gate_call(twos, gu_own, gu_other)

    def over_groups(kept):
        if replicas > PIECES:
            groups = [
                [e * PIECES + i for e in range(replicas // PIECES)] for i in range(PIECES)
            ]
            kept = lax.psum(kept, "replica", axis_index_groups=groups)
        return kept

    def reduced(term):
        kept = lax.psum_scatter(term, "shard", scatter_dimension=0, tiled=True)
        return over_groups(kept)

    def plane_pieces(kept):
        mine = plane_gather(kept)
        return mine, [swap(part, 1) for part in mine]

    def mixed(mine, theirs):
        return [part for pair in zip(mine, theirs) for part in pair]

    down_sent = swap(weight_grad(act, None, (g_all,), 1, None, "down_grad_other"), 1)
    down_term = weight_grad(act, None, (g_all,), 0, down_sent, "down_grad")
    down_kept = reduced(down_term)

    grads = hidden_back_call(after(g_all, down_term), down_own, down_other, for_gate, for_up)
    e_parts = plane_send(parts_call((grads,), gu_own, gu_other, True, "feedforward_back"))
    gu_sent = swap(weight_grad(after(two_all, *e_parts[:1]), 1, (grads,), None, None, "gate_grad_other"), 1)
    gu_term = weight_grad(two_all, 0, (grads,), None, gu_sent, "gate_grad")
    gu_kept = reduced(gu_term)

    middle_late = after(middle, down_kept, gu_term)
    grad_middle, branch = grad_middle_call(e_parts, middle_late, g)
    branches = plane_gather(branch)

    act_late = after(act, branches[3])
    out_parts = plane_send(parts_call((act_late,), down_own, down_other, False, "feedforward_out"))
    output = output_call(index, out_parts, middle, local)

    before = None
    for m in range(CHIPS):
        before = attention_back_call(
            index, m, branches[m], wo_own, wo_other, queries, turned, stats, cosine, sine, kvs, before
        )
    grad_q, grad_first, grad_rest = before

    branch_all = jnp.concatenate(branches, axis=0)
    wo_sent = swap(weight_grad(attended, None, (branch_all,), 1, None, "out_grad_other"), 1)
    wo_term = weight_grad(attended, None, (branch_all,), 0, wo_sent, "out_grad")
    wo_cut = q_width // CHIPS
    wo_chips = [wo_term[:wo_cut]] + [
        swap(wo_term[m * wo_cut : (m + 1) * wo_cut], 2 * m) for m in range(1, CHIPS)
    ]
    wo_stack = jnp.stack(wo_chips)
    wo_block = jnp.concatenate(
        [lax.dynamic_index_in_dim(wo_stack, chip ^ i, 0, keepdims=False) for i in range(CHIPS)],
        axis=0,
    )

    kv_rest = [shift(grad_rest[d - 1], -d) for d in range(1, shards)]
    grad_kv = grad_kv_call(grad_first, kv_rest, cosine, sine)
    pair = (grad_q, grad_kv)
    qkv_sent = swap(weight_grad(xhat, 1, pair, None, None, "qkv_grad_other"), 1)
    qkv_term = weight_grad(xhat, 0, pair, None, qkv_sent, "qkv_grad")
    wo_wide = wo_block.reshape(shards, half // 2, 2, 512).transpose(0, 2, 1, 3).reshape(-1, 512)
    at_kept = reduced(jnp.concatenate([qkv_term, wo_wide], axis=1))

    e_one = plane_send(parts_call((grad_q, after(grad_kv, qkv_term)), qkv_own, qkv_other, True, "qkv_back"))
    grad_input = grad_input_call(index, e_one, x, grad_middle, local)

    down_kept = after(down_kept, *branches)
    down_out = rows_result(index, mixed(*plane_pieces(down_kept)), local, "down_result")
    gu_mine, gu_theirs = plane_pieces(gu_kept)
    gu_out = feedforward_result(index, 0, gu_mine, gate_weight, up_weight, gain_two, ff_local, None)
    gu_out = feedforward_result(index, 1, gu_theirs, gate_weight, up_weight, gain_two, ff_local, gu_out)
    at_pieces = mixed(*plane_pieces(at_kept))
    wo_out = out_result(index, at_pieces, local, width, qkv_width)
    q_out, k_out, v_out, gain_one_sums = qkv_result(
        index, at_pieces, query_weight, key_weight, value_weight, gain_one
    )
    return (
        output,
        grad_input,
        jnp.sum(gain_one_sums, axis=1),
        q_out,
        k_out,
        v_out,
        wo_out,
        jnp.sum(gu_out[2], axis=1),
        gu_out[0],
        gu_out[1],
        down_out,
    )


def solution(mesh):
    return jax.shard_map(
        per_device,
        mesh=mesh,
        in_specs=(
            P(("replica", "shard"), None),
            P("shard"),
            P("shard", None),
            P("shard", None),
            P("shard", None),
            P("shard", None),
            P("shard"),
            P("shard", None),
            P("shard", None),
            P("shard", None),
            P(("replica", "shard"), None),
        ),
        out_specs=(
            P(("replica", "shard"), None),
            P(("replica", "shard"), None),
            P("shard"),
            P("shard", None),
            P("shard", None),
            P("shard", None),
            P("shard", None),
            P("shard"),
            P("shard", None),
            P("shard", None),
            P("shard", None),
        ),
        check_vma=False,
    )
```

```python
import functools

import jax
import jax.numpy as jnp
from jax import lax
from jax.experimental import pallas as pl
from jax.experimental.pallas import tpu as pltpu
from jax.sharding import PartitionSpec as P

HEADS = 32
KV_HEADS = 4
HEAD = 64
GROUP = HEADS // KV_HEADS
CHIPS = 4
PIECES = 2 * CHIPS
LANES = 128

norm_eps = 1e-05
rope_base = 10000.0
masked_score = -1e30

f32 = jnp.float32
bf16 = jnp.bfloat16
VMEM = pltpu.VMEM
NT = (((1,), (1,)), ((), ()))
TN = (((0,), (0,)), ((), ()))


def dot(left, right):
    return jnp.dot(left, right, preferred_element_type=f32)


def dot_nt(left, right):
    return lax.dot_general(left, right, NT, preferred_element_type=f32)


def dot_tn(left, right):
    return lax.dot_general(left, right, TN, preferred_element_type=f32)


def shape(dims, kind):
    return jax.ShapeDtypeStruct(dims, kind)


def whole():
    return pl.BlockSpec(memory_space=VMEM)


def kernel_call(body, out_shape, in_specs, out_specs, operands, *, index=None, grid=(), scratch=(),
                moved=0, aliases=None, name=None):
    params = pltpu.CompilerParams(
        vmem_limit_bytes=52 * 2**20, dimension_semantics=("arbitrary",) * len(grid)
    )
    cost = pl.CostEstimate(flops=0, bytes_accessed=int(moved), transcendentals=0)
    common = dict(
        out_shape=out_shape,
        compiler_params=params,
        cost_estimate=cost,
        input_output_aliases=aliases or {},
        name=name,
    )
    if index is None:
        spec = pl.GridSpec(grid=grid, in_specs=in_specs, out_specs=out_specs, scratch_shapes=scratch)
        return pl.pallas_call(body, grid_spec=spec, **common)(*operands)
    spec = pltpu.PrefetchScalarGridSpec(
        num_scalar_prefetch=1, grid=grid, in_specs=in_specs, out_specs=out_specs,
        scratch_shapes=scratch,
    )
    return pl.pallas_call(body, grid_spec=spec, **common)(index, *operands)


def swap(value, mask):
    size = lax.axis_size("replica")
    return lax.ppermute(value, "replica", [(i, i ^ mask) for i in range(size)])


def shift(value, step):
    size = lax.axis_size("shard")
    pairs = [(i, i + step) for i in range(size) if 0 <= i + step < size]
    return lax.ppermute(value, "shard", pairs)


def plane_gather(value):
    return [value] + [swap(value, 2 * m) for m in range(1, CHIPS)]


def plane_send(parts):
    return [parts[0]] + [swap(parts[m], 2 * m) for m in range(1, CHIPS)]


def after(value, *others):
    return lax.optimization_barrier((value, *others))[0]


def attention_block_body(local, group_shards, index, q, k, v, o, gain, out):
    scale = gain[:, :1]
    q_width = GROUP * HEAD
    cut = local // CHIPS
    for chip in range(CHIPS):

        @pl.when(index[0] == chip)
        def _():
            parts = []
            for m in range(CHIPS):
                for s in range(group_shards):
                    start = chip * q_width + s * local + (m ^ chip) * cut
                    parts.append(q[:, start : start + cut])
            parts.append(k[:, chip * HEAD : (chip + 1) * HEAD])
            parts.append(v[:, chip * HEAD : (chip + 1) * HEAD])
            wide = jnp.concatenate([part.astype(f32) for part in parts], axis=1)
            out[:, : q_width + 2 * HEAD] = (wide * scale).astype(bf16)

    half = local // 2
    shards = o.shape[1] // local
    for core in range(2):

        @pl.when(index[1] == core)
        def _():
            base = q_width + 2 * HEAD
            for s in range(shards):
                piece = o[:, s * local + core * half : s * local + (core + 1) * half]
                spot = s * half
                row, column = (0, spot) if spot < 512 else (cut, spot - 512)
                out[row : row + cut, base + column : base + column + half] = piece


def attention_block(index, query, key, value, output, gain):
    local, width = query.shape
    half = local // 2
    shards = width // local
    return kernel_call(
        functools.partial(attention_block_body, local, shards // CHIPS),
        shape((half, GROUP * HEAD + 2 * HEAD + 512), bf16),
        [
            pl.BlockSpec((half, width), lambda i, n: (n[1], 0)),
            pl.BlockSpec((half, key.shape[1]), lambda i, n: (n[1], 0)),
            pl.BlockSpec((half, key.shape[1]), lambda i, n: (n[1], 0)),
            pl.BlockSpec((local // CHIPS, width), lambda i, n: (n[0], 0)),
            pl.BlockSpec((half, LANES), lambda i, n: (n[1], 0)),
        ],
        pl.BlockSpec((half, GROUP * HEAD + 2 * HEAD + 512), lambda i, n: (0, 0)),
        (query, key, value, output, gain),
        index=index,
        grid=(1,),
        name="attention_block",
    )


def feedforward_block_body(ff_local, cut, index, gate, up, gain, out):
    scale = gain[:, :1]
    shards = gate.shape[1] // ff_local
    width = shards * cut
    for chip in range(CHIPS):

        @pl.when(index[0] == chip)
        def _():
            for n, source in enumerate((gate, up)):
                parts = [
                    source[:, s * ff_local + chip * cut : s * ff_local + (chip + 1) * cut].astype(f32)
                    for s in range(shards)
                ]
                wide = jnp.concatenate(parts, axis=1)
                out[:, n * width : (n + 1) * width] = (wide * scale).astype(bf16)


def feedforward_block(index, gate, up, gain, ff_local):
    local, ff = gate.shape
    half = local // 2
    rows = 64
    steps = half // rows
    cut = ff_local // CHIPS
    width = 2 * (ff // CHIPS)
    return kernel_call(
        functools.partial(feedforward_block_body, ff_local, cut),
        shape((half, width), bf16),
        [
            pl.BlockSpec((rows, ff), lambda i, n: (n[1] * steps + i, 0)),
            pl.BlockSpec((rows, ff), lambda i, n: (n[1] * steps + i, 0)),
            pl.BlockSpec((rows, LANES), lambda i, n: (n[1] * steps + i, 0)),
        ],
        pl.BlockSpec((rows, width), lambda i, n: (i, 0)),
        (gate, up, gain),
        index=index,
        grid=(steps,),
        name="feedforward_block",
    )


def own_first_body(local, index, *refs):
    count = len(refs) // 2
    half = local // 2
    for core in range(2):

        @pl.when(index[1] == core)
        def _():
            for source, out in zip(refs[:count], refs[count:]):
                shards = source.shape[1] // local
                sides = out.shape[1] // (shards * half)
                for side in range(sides):
                    for s in range(shards):
                        start = s * local + (core ^ side) * half
                        spot = (side * shards + s) * half
                        out[:, spot : spot + half] = source[:, start : start + half]


def own_first(index, sources, local, halves=2):
    return kernel_call(
        functools.partial(own_first_body, local),
        tuple(shape((v.shape[0], v.shape[1] * halves // 2), bf16) for v in sources),
        [pl.BlockSpec(v.shape, lambda i, n: (0, 0)) for v in sources],
        tuple(
            pl.BlockSpec((v.shape[0], v.shape[1] * halves // 2), lambda i, n: (0, 0)) for v in sources
        ),
        tuple(sources),
        index=index,
        grid=(1,),
        name="own_first",
    )


def down_block_body(local, index, source, out):
    own_first_body(local, index, source, out)


def down_block(index, down, local):
    ff_local, width = down.shape
    cut = ff_local // CHIPS
    return kernel_call(
        functools.partial(down_block_body, local),
        shape((cut, width // 2), bf16),
        [pl.BlockSpec((cut, width), lambda i, n: (n[0], 0))],
        pl.BlockSpec((cut, width // 2), lambda i, n: (0, 0)),
        (down,),
        index=index,
        grid=(1,),
        name="down_block",
    )


def part_sum(parts):
    total = parts[0][...]
    for part in parts[1:]:
        total = total + part[...].astype(f32)
    return total


def mean_of(values):
    return jnp.mean(values, axis=1, keepdims=True)


def middle_body(*refs):
    parts, (x, middle, two) = refs[:CHIPS], refs[CHIPS:]
    total = x[...].astype(f32) + part_sum(parts)
    middle[...] = total
    two[...] = (total * lax.rsqrt(mean_of(total * total) + norm_eps)).astype(bf16)


def middle_call(parts, x):
    return kernel_call(
        middle_body,
        (shape(x.shape, f32), shape(x.shape, bf16)),
        [whole()] * (CHIPS + 1),
        (whole(), whole()),
        (*parts, x),
        name="middle",
    )


def norm_back(e, values):
    inverse = lax.rsqrt(mean_of(values * values) + norm_eps)
    return inverse * e - values * (inverse * inverse * inverse) * mean_of(e * values)


def grad_middle_body(*refs):
    parts, (middle, g, grad, low) = refs[:CHIPS], refs[CHIPS:]
    total = g[...].astype(f32) + norm_back(part_sum(parts), middle[...])
    grad[...] = total
    low[...] = total.astype(bf16)


def grad_middle_call(parts, middle, g):
    return kernel_call(
        grad_middle_body,
        (shape(g.shape, f32), shape(g.shape, bf16)),
        [whole()] * (CHIPS + 2),
        (whole(), whole()),
        (*parts, middle, g),
        name="grad_middle",
    )


def store_in_order(local, index, value, out):
    half = local // 2
    shards = out.shape[1] // local
    for core in range(2):

        @pl.when(index[1] == core)
        def _():
            for side in range(2):
                for s in range(shards):
                    spot = s * local + (core ^ side) * half
                    start = (side * shards + s) * half
                    out[:, spot : spot + half] = value[:, start : start + half].astype(bf16)


def output_body(local, index, *refs):
    parts, (middle, out) = refs[:CHIPS], refs[CHIPS:]
    store_in_order(local, index, middle[...] + part_sum(parts), out)


def output_call(index, parts, middle, local):
    spec = pl.BlockSpec(middle.shape, lambda i, n: (0, 0))
    return kernel_call(
        functools.partial(output_body, local),
        shape(middle.shape, bf16),
        [spec] * (CHIPS + 1),
        spec,
        (*parts, middle),
        index=index,
        grid=(1,),
        name="output",
    )


def grad_input_body(local, index, *refs):
    parts, (x, grad, out) = refs[:CHIPS], refs[CHIPS:]
    total = grad[...] + norm_back(part_sum(parts), x[...].astype(f32))
    store_in_order(local, index, total, out)


def grad_input_call(index, parts, x, grad, local):
    spec = pl.BlockSpec(x.shape, lambda i, n: (0, 0))
    return kernel_call(
        functools.partial(grad_input_body, local),
        shape(x.shape, bf16),
        [spec] * (CHIPS + 2),
        spec,
        (*parts, x, grad),
        index=index,
        grid=(1,),
        name="grad_input",
    )


def grad_kv_body(shards, *refs):
    first, rest, (cosine, sine, out) = refs[0], refs[1:shards], refs[shards:]
    total = first[...]
    for term in rest:
        total = total + term[...].astype(f32)
    rows = cosine.shape[1]
    cos, sin = cosine[...], sine[...]
    for m in range(CHIPS):
        turned = total[m * rows : (m + 1) * rows, :].T
        k = turned[:HEAD]
        k = k * cos - half_rotated(k) * sin
        both = jnp.concatenate([k, turned[HEAD:]], axis=0)
        out[m * rows : (m + 1) * rows, :] = both.T.astype(bf16)


def grad_kv_call(first, rest, cosine, sine):
    return kernel_call(
        functools.partial(grad_kv_body, len(rest) + 1),
        shape(first.shape, bf16),
        [whole()] * (len(rest) + 3),
        whole(),
        (first, *rest, cosine, sine),
        name="grad_kv",
    )


def half_rotated(values):
    middle = values.shape[0] // 2
    return jnp.concatenate([-values[middle:], values[:middle]], axis=0)


def qkv_body(*refs):
    xs, (own, other, cosine, sine), (xhat, queries, kv) = refs[:CHIPS], refs[CHIPS : CHIPS + 4], refs[CHIPS + 4 :]
    rows, width = xs[0].shape
    for m in range(CHIPS):
        x = xs[m][...].astype(f32)
        inverse = lax.rsqrt(jnp.mean(x * x, axis=1, keepdims=True) + norm_eps)
        xhat[m * rows : (m + 1) * rows, :] = (x * inverse).astype(bf16)
    cos, sin = cosine[...], sine[...]
    for m in range(CHIPS):
        block = xhat[m * rows : (m + 1) * rows, :]
        total = dot(block[:, : width // 2], own[...]) + dot(block[:, width // 2 :], other[...])
        turned = total.T
        for h in range(GROUP + 1):
            u = turned[h * HEAD : (h + 1) * HEAD]
            u = u * cos + half_rotated(u) * sin
            if h < GROUP:
                queries[m, h * HEAD : (h + 1) * HEAD, :] = (u * HEAD ** (-0.5)).astype(bf16)
            else:
                both = jnp.concatenate([u, turned[(h + 1) * HEAD :]], axis=0)
                kv[m * rows : (m + 1) * rows, :] = both.T.astype(bf16)


def qkv_call(xs, own, other, cosine, sine):
    rows, width = xs[0].shape
    tokens = CHIPS * rows
    return kernel_call(
        qkv_body,
        (
            shape((tokens, width), bf16),
            shape((CHIPS, GROUP * HEAD, rows), bf16),
            shape((tokens, 2 * HEAD), bf16),
        ),
        [whole()] * (CHIPS + 4),
        (whole(), whole(), whole()),
        (*xs, own, other, cosine, sine),
        name="qkv",
    )


def set_bias(bias, depth, shards):
    rows = bias.shape[1]
    key = lax.broadcasted_iota(jnp.int32, bias.shape, 0)
    mine = lax.broadcasted_iota(jnp.int32, bias.shape, 1)
    limit = jnp.where(key < rows, mine, (depth + 1) * rows - 1)
    bias[...] = jnp.where(key <= limit, 0.0, masked_score)


def attention_body(shards, index, queries, *refs):
    kvs = refs[:shards]
    turned_out, out, stats, bias, kv_all, out_turned = refs[shards:]
    rows = queries.shape[2]

    @pl.when(pl.program_id(0) == 0)
    def _():
        set_bias(bias, index[2], shards)

    for d in range(shards):
        kv_all[d * rows : (d + 1) * rows, :] = kvs[d][...]
    kv = kv_all[...]
    v_turned = kv.astype(f32).T[HEAD:].astype(bf16)
    zeros = jnp.zeros((HEAD, rows), bf16)
    for h in range(GROUP):
        q = jnp.concatenate([queries[0, h * HEAD : (h + 1) * HEAD, :], zeros], axis=0)
        scores = dot(kv, q) + bias[...]
        top = jnp.max(scores, axis=0, keepdims=True)
        terms = jnp.exp(scores - top)
        total = jnp.sum(terms, axis=0, keepdims=True)
        mixed = dot(v_turned, terms.astype(bf16)) / total
        out_turned[h * HEAD : (h + 1) * HEAD, :] = mixed
        stats[0, h : h + 1, :] = top + jnp.log(total)
    turned_out[0] = out_turned[...].astype(bf16)
    out[...] = out_turned[...].T.astype(bf16)


def attention_call(index, queries, kvs):
    chips, width, rows = queries.shape
    shards = len(kvs)
    keys = shards * rows
    return kernel_call(
        functools.partial(attention_body, shards),
        (
            shape((chips, width, rows), bf16),
            shape((chips * rows, width), bf16),
            shape((chips, GROUP, rows), f32),
        ),
        [pl.BlockSpec((1, width, rows), lambda i, n: (i, 0, 0))]
        + [pl.BlockSpec((rows, 2 * HEAD), lambda i, n: (i, 0))] * shards,
        (
            pl.BlockSpec((1, width, rows), lambda i, n: (i, 0, 0)),
            pl.BlockSpec((rows, width), lambda i, n: (i, 0)),
            pl.BlockSpec((1, GROUP, rows), lambda i, n: (i, 0, 0)),
        ),
        (queries, *kvs),
        index=index,
        grid=(chips,),
        scratch=(
            VMEM((keys, rows), f32),
            VMEM((keys, 2 * HEAD), bf16),
            VMEM((width, rows), f32),
        ),
        name="attention",
    )


def attention_back_body(shards, index, branch, wo_own, wo_other, queries, turned_out, stats, cosine, sine, *refs):
    kvs = refs[:shards]
    grad_q, grad_first, grad_rest, bias, kv_all, q_turned, total = refs[-7:]
    rows = queries.shape[2]
    width = branch.shape[1]
    set_bias(bias, index[2], shards)
    for d in range(shards):
        kv_all[d * rows : (d + 1) * rows, :] = kvs[d][...]
    kv = kv_all[...]
    k_turned = kv.astype(f32).T[:HEAD].astype(bf16)
    grad_out = dot_nt(wo_own[...], branch[:, : width // 2])
    grad_out = (grad_out + dot_nt(wo_other[...], branch[:, width // 2 :])).astype(bf16)
    zeros = jnp.zeros((HEAD, rows), bf16)
    cos, sin = cosine[...], sine[...]
    for h in range(GROUP):
        span = slice(h * HEAD, (h + 1) * HEAD)
        q = jnp.concatenate([queries[0, span, :], zeros], axis=0)
        mine = grad_out[span]
        padded = jnp.concatenate([zeros, mine], axis=0)
        probs = jnp.exp(dot(kv, q) + bias[...] - stats[0, h : h + 1, :])
        delta = jnp.sum(
            mine.astype(f32) * turned_out[0, span, :].astype(f32), axis=0, keepdims=True
        )
        grad_scores = (probs * (dot(kv, padded) - delta)).astype(bf16)
        u = dot(k_turned, grad_scores) * HEAD ** (-0.5)
        q_turned[span, :] = u * cos - half_rotated(u) * sin
        term = dot_nt(grad_scores, q) + dot_nt(probs.astype(bf16), padded)
        if h == 0:
            total[...] = term
        else:
            total[...] += term
    grad_q[...] = q_turned[...].T.astype(bf16)
    grad_first[...] = total[:rows, :]
    for d in range(1, shards):
        grad_rest[d - 1] = total[d * rows : (d + 1) * rows, :].astype(bf16)


def attention_back_call(index, m, branch, wo_own, wo_other, queries, turned_out, stats, cosine, sine, kvs, before):
    chips, width, rows = queries.shape
    shards = len(kvs)
    keys = shards * rows
    tokens = chips * rows
    fixed = pl.BlockSpec((1, width, rows), lambda i, n: (m, 0, 0))
    in_specs = [
        whole(), whole(), whole(), fixed, fixed,
        pl.BlockSpec((1, GROUP, rows), lambda i, n: (m, 0, 0)), whole(), whole(),
    ] + [pl.BlockSpec((rows, 2 * HEAD), lambda i, n: (m, 0))] * shards
    operands = (branch, wo_own, wo_other, queries, turned_out, stats, cosine, sine, *kvs)
    aliases = {}
    if before is not None:
        aliases = {1 + len(operands) + n: n for n in range(3)}
        in_specs = in_specs + [pl.BlockSpec(memory_space=pl.ANY)] * 3
        operands = operands + tuple(before)
    return kernel_call(
        functools.partial(attention_back_body, shards),
        (
            shape((tokens, width), bf16),
            shape((tokens, 2 * HEAD), f32),
            shape((shards - 1, tokens, 2 * HEAD), bf16),
        ),
        in_specs,
        (
            pl.BlockSpec((rows, width), lambda i, n: (m, 0)),
            pl.BlockSpec((rows, 2 * HEAD), lambda i, n: (m, 0)),
            pl.BlockSpec((shards - 1, rows, 2 * HEAD), lambda i, n: (0, m, 0)),
        ),
        operands,
        index=index,
        grid=(1,),
        scratch=(
            VMEM((keys, rows), f32),
            VMEM((keys, 2 * HEAD), bf16),
            VMEM((width, rows), f32),
            VMEM((keys, 2 * HEAD), f32),
        ),
        aliases=aliases,
        name="attention_back",
    )


def parts_body(steps, transposed, widths, *refs):
    count = len(widths)
    lefts, (own, other), outs = refs[:count], refs[count : count + 2], refs[count + 2 :]
    rows = outs[0].shape[0]
    step = pl.program_id(0)

    def run(weight):
        start = 0
        total = None
        for left, wide in zip(lefts, widths):
            if transposed:
                term = dot_nt(left[...], weight[:, start : start + wide])
            else:
                term = dot(left[...], weight[start : start + wide, :])
            total = term if total is None else total + term
            start += wide
        for m in range(CHIPS):
            outs[m][...] = total[m * rows : (m + 1) * rows, :].astype(outs[m].dtype)

    @pl.when(step < steps)
    def _():
        run(own)

    @pl.when(step >= steps)
    def _():
        run(other)


def parts_call(lefts, own, other, transposed, name):
    tokens = lefts[0].shape[0]
    rows = tokens // CHIPS
    widths = tuple(left.shape[1] for left in lefts)
    depth = sum(widths)
    half = own.shape[0] if transposed else own.shape[1]
    tile = 256
    steps = half // tile
    last = steps - 1
    if transposed:
        weight_specs = [
            pl.BlockSpec((tile, depth), lambda j: (jnp.minimum(j, last), 0)),
            pl.BlockSpec((tile, depth), lambda j: (jnp.maximum(j - steps, 0), 0)),
        ]
    else:
        weight_specs = [
            pl.BlockSpec((depth, tile), lambda j: (0, jnp.minimum(j, last))),
            pl.BlockSpec((depth, tile), lambda j: (0, jnp.maximum(j - steps, 0))),
        ]
    return kernel_call(
        functools.partial(parts_body, steps, transposed, widths),
        tuple(shape((rows, 2 * half), f32 if m == 0 else bf16) for m in range(CHIPS)),
        [pl.BlockSpec((tokens, wide), lambda j: (0, 0)) for wide in widths] + weight_specs,
        tuple(pl.BlockSpec((rows, tile), lambda j: (0, j)) for _ in range(CHIPS)),
        (*lefts, own, other),
        grid=(2 * steps,),
        name=name,
    )


def gate_body(*refs):
    twos = refs[:CHIPS]
    gate_own, up_own, gate_other, up_other, act, for_gate, for_up, two_all = refs[CHIPS:]
    rows, width = twos[0].shape
    half = width // 2

    @pl.when(pl.program_id(0) == 0)
    def _():
        for m in range(CHIPS):
            two_all[m * rows : (m + 1) * rows, :] = twos[m][...]

    own = jnp.concatenate([gate_own[...], up_own[...]], axis=1)
    other = jnp.concatenate([gate_other[...], up_other[...]], axis=1)
    both = dot(two_all[:, :half], own) + dot(two_all[:, half:], other)
    wide = gate_own.shape[1]
    gate, up = both[:, :wide], both[:, wide:]
    sig = 1.0 / (1.0 + jnp.exp(-gate))
    silu = gate * sig
    act[...] = (silu * up).astype(bf16)
    for_gate[...] = (up * sig * (1.0 + gate * (1.0 - sig))).astype(bf16)
    for_up[...] = silu.astype(bf16)


def gate_call(twos, own, other):
    rows, width = twos[0].shape
    tokens = CHIPS * rows
    half = width // 2
    ff = own.shape[1] // 2
    tile = LANES
    steps = ff // tile
    weight = [
        pl.BlockSpec((half, tile), lambda j: (0, j)),
        pl.BlockSpec((half, tile), lambda j: (0, j + steps)),
    ]
    column = pl.BlockSpec((tokens, tile), lambda j: (0, j))
    return kernel_call(
        gate_body,
        tuple(shape((tokens, ff), bf16) for _ in range(3)) + (shape((tokens, width), bf16),),
        [pl.BlockSpec((rows, width), lambda j: (0, 0))] * CHIPS + weight + weight,
        (column, column, column, pl.BlockSpec((tokens, width), lambda j: (0, 0))),
        (*twos, own, own, other, other),
        grid=(steps,),
        name="gate",
    )


def hidden_back_body(g, own, other, for_gate, for_up, grads):
    half = g.shape[1] // 2
    ff = own.shape[0]
    hidden = dot_nt(g[:, :half], own[...]) + dot_nt(g[:, half:], other[...])
    grads[:, :ff] = (hidden * for_gate[...].astype(f32)).astype(bf16)
    grads[:, ff:] = (hidden * for_up[...].astype(f32)).astype(bf16)


def hidden_back_call(g, own, other, for_gate, for_up):
    tokens, width = g.shape
    ff, half = own.shape
    block = tokens // 2
    row = lambda i: (i, 0)
    fixed = lambda i: (0, 0)
    return kernel_call(
        hidden_back_body,
        shape((tokens, 2 * ff), bf16),
        [
            pl.BlockSpec((block, width), row),
            pl.BlockSpec((ff, half), fixed),
            pl.BlockSpec((ff, half), fixed),
            pl.BlockSpec((block, ff), row),
            pl.BlockSpec((block, ff), row),
        ],
        pl.BlockSpec((block, 2 * ff), row),
        (g, own, other, for_gate, for_up),
        grid=(2,),
        name="hidden_back",
    )


def weight_grad_body(splits, added, left, *refs):
    count = sum(splits)
    rights = refs[:count]
    outs = refs[-len(splits) :]
    extra = refs[count : count + len(splits)] if added else ()
    first = 0
    for n, (split, out) in enumerate(zip(splits, outs)):
        start = 0
        for right in rights[first : first + split]:
            wide = right.shape[1]
            term = dot_tn(left[...], right[...])
            if added:
                term = term + extra[n][:, start : start + wide].astype(f32)
            out[:, start : start + wide] = term.astype(bf16)
            start += wide
        first += split


def weight_grad(left, left_side, groups, added, name, moved=0):
    tokens = left.shape[0]
    rows = left.shape[1] // (1 if left_side is None else 2)
    tile = 256 if rows % 256 == 0 else LANES
    steps = rows // tile
    first = 0 if left_side is None else left_side * steps
    blocks = [block for group in groups for block in group]
    widths = [sum(block[1] for block in group) for group in groups]
    in_specs = [pl.BlockSpec((tokens, tile), lambda i: (0, first + i))]
    in_specs += [
        pl.BlockSpec((tokens, wide), functools.partial(lambda spot, i: (0, spot), spot))
        for _, wide, spot in blocks
    ]
    operands = (left, *(block[0] for block in blocks))
    tiles = [pl.BlockSpec((tile, width), lambda i: (i, 0)) for width in widths]
    if added is not None:
        in_specs += tiles
        operands = operands + tuple(added)
    return kernel_call(
        functools.partial(weight_grad_body, tuple(len(group) for group in groups), added is not None),
        tuple(shape((rows, width), bf16) for width in widths),
        in_specs,
        tuple(tiles),
        operands,
        grid=(steps,),
        name=name,
        moved=moved,
    )


def rows_result_body(local, index, *refs):
    pieces, out = refs[:PIECES], refs[PIECES]
    half = local // 2
    shards = out.shape[1] // local
    for m in range(CHIPS):
        for core in range(2):

            @pl.when((pl.program_id(0) == m) & (index[1] == core))
            def _():
                for side in range(2):
                    piece = pieces[2 * m + side]
                    for s in range(shards):
                        spot = s * local + (core ^ side) * half
                        out[:, spot : spot + half] = piece[:, s * half : (s + 1) * half].astype(f32)


def rows_result(index, pieces, local, name):
    cut, half_width = pieces[0].shape
    return kernel_call(
        functools.partial(rows_result_body, local),
        shape((CHIPS * cut, 2 * half_width), f32),
        [pl.BlockSpec((cut, half_width), lambda i, n: (0, 0))] * PIECES,
        pl.BlockSpec((cut, 2 * half_width), lambda i, n: (n[0] ^ i, 0)),
        tuple(pieces),
        index=index,
        grid=(CHIPS,),
        name=name,
    )


def out_result_body(local, base, index, *refs):
    pieces, out = refs[:PIECES], refs[PIECES]
    half = local // 2
    cut = local // CHIPS
    shards = out.shape[1] // local
    for m in range(CHIPS):
        for core in range(2):

            @pl.when((pl.program_id(0) == m) & (index[1] == core))
            def _():
                for side in range(2):
                    piece = pieces[2 * m + side]
                    for s in range(shards):
                        spot = s * local + (core ^ side) * half
                        row, column = (0, s * half) if s * half < 512 else (cut, s * half - 512)
                        column += base
                        out[:, spot : spot + half] = piece[row : row + cut, column : column + half].astype(f32)


def out_result(index, pieces, local, width, base):
    cut = local // CHIPS
    return kernel_call(
        functools.partial(out_result_body, local, base),
        shape((local, width), f32),
        [pl.BlockSpec(pieces[0].shape, lambda i, n: (0, 0))] * PIECES,
        pl.BlockSpec((cut, width), lambda i, n: (n[0] ^ i, 0)),
        tuple(pieces),
        index=index,
        grid=(CHIPS,),
        name="out_result",
    )


def lane_sum(value):
    total = value[:, :LANES]
    for n in range(1, value.shape[1] // LANES):
        total = total + value[:, n * LANES : (n + 1) * LANES]
    return total


def feedforward_result_body(ff_local, cut, index, *refs):
    pieces = refs[:CHIPS]
    gate_weight, up_weight, gain = refs[CHIPS : CHIPS + 3]
    gate_out, up_out, gain_out = refs[-3:]
    shards = gate_weight.shape[1] // ff_local
    width = shards * cut
    for chip in range(CHIPS):

        @pl.when(index[0] == chip)
        def _():
            @pl.loop(0, gate_out.shape[0] // 16)
            def _(n):
                rows = pl.ds(pl.multiple_of(n * 16, 16), 16)
                scale = gain[rows, :1]
                total = jnp.zeros((16, LANES), f32)
                for base, weight, out in ((0, gate_weight, gate_out), (width, up_weight, up_out)):
                    parts = []
                    for s in range(shards):
                        for owner in range(CHIPS):
                            start = base + s * cut
                            parts.append(pieces[owner ^ chip][rows, start : start + cut].astype(f32))
                    wide = jnp.concatenate(parts, axis=1)
                    total = total + lane_sum(wide * weight[rows, :].astype(f32))
                    out[rows, :] = wide * scale
                gain_out[rows, :] = total


def feedforward_result(index, side, pieces, gate_weight, up_weight, gain, ff_local, before):
    local, ff = gate_weight.shape
    half = local // 2
    rows = 64
    steps = half // rows
    row = lambda i, n: ((n[1] ^ side) * steps + i, 0)
    in_specs = [pl.BlockSpec((rows, pieces[0].shape[1]), lambda i, n: (i, 0))] * CHIPS
    in_specs += [pl.BlockSpec((rows, ff), row)] * 2 + [pl.BlockSpec((rows, LANES), row)]
    operands = (*pieces, gate_weight, up_weight, gain)
    aliases = {}
    if before is not None:
        aliases = {1 + len(operands) + n: n for n in range(3)}
        in_specs = in_specs + [pl.BlockSpec(memory_space=pl.ANY)] * 3
        operands = operands + tuple(before)
    return kernel_call(
        functools.partial(feedforward_result_body, ff_local, ff_local // CHIPS),
        (shape((local, ff), f32), shape((local, ff), f32), shape((local, LANES), f32)),
        in_specs,
        (pl.BlockSpec((rows, ff), row), pl.BlockSpec((rows, ff), row), pl.BlockSpec((rows, LANES), row)),
        operands,
        index=index,
        grid=(steps,),
        aliases=aliases,
        name="feedforward_result",
    )


def qkv_result_body(local, group_shards, index, *refs):
    pieces = refs[:PIECES]
    weights, gain = refs[PIECES : PIECES + 3], refs[PIECES + 3]
    outs, gain_out = refs[PIECES + 4 : PIECES + 7], refs[PIECES + 7]
    q_width = GROUP * HEAD
    cut = local // CHIPS
    scale = gain[:, :1]
    for chip in range(CHIPS):
        for side in range(2):

            @pl.when((index[0] == chip) & (pl.program_id(0) == side))
            def _():
                parts, k_parts, v_parts = [], [], []
                for owner in range(CHIPS):
                    piece = pieces[2 * (owner ^ chip) + side]
                    for s in range(group_shards):
                        for j in range(CHIPS):
                            start = ((j ^ owner) * group_shards + s) * cut
                            parts.append(piece[:, start : start + cut].astype(f32))
                    k_parts.append(piece[:, q_width : q_width + HEAD].astype(f32))
                    v_parts.append(piece[:, q_width + HEAD : q_width + 2 * HEAD].astype(f32))
                total = jnp.zeros((gain.shape[0], LANES), f32)
                for part, weight, out in zip((parts, k_parts, v_parts), weights, outs):
                    wide = jnp.concatenate(part, axis=1)
                    total = total + lane_sum(wide * weight[...].astype(f32))
                    out[...] = wide * scale
                gain_out[...] = total


def qkv_result(index, pieces, query, key, value, gain):
    local, width = query.shape
    half = local // 2
    group_shards = width // local // CHIPS
    row = lambda i, n: (n[1] ^ i, 0)
    kv_width = key.shape[1]
    return kernel_call(
        functools.partial(qkv_result_body, local, group_shards),
        (
            shape((local, width), f32),
            shape((local, kv_width), f32),
            shape((local, kv_width), f32),
            shape((local, LANES), f32),
        ),
        [pl.BlockSpec(pieces[0].shape, lambda i, n: (0, 0))] * PIECES
        + [
            pl.BlockSpec((half, width), row),
            pl.BlockSpec((half, kv_width), row),
            pl.BlockSpec((half, kv_width), row),
            pl.BlockSpec((half, LANES), row),
        ],
        (
            pl.BlockSpec((half, width), row),
            pl.BlockSpec((half, kv_width), row),
            pl.BlockSpec((half, kv_width), row),
            pl.BlockSpec((half, LANES), row),
        ),
        (*pieces, query, key, value, gain),
        index=index,
        grid=(2,),
        name="qkv_result",
    )


def per_device(
    hidden_in,
    attention_gain,
    query_weight,
    key_weight,
    value_weight,
    output_weight,
    feedforward_gain,
    gate_weight,
    up_weight,
    down_weight,
    out_grad,
):
    rows, width = hidden_in.shape
    shards = lax.axis_size("shard")
    replicas = lax.axis_size("replica")
    place = lax.axis_index("replica")
    depth = lax.axis_index("shard")
    core = place & 1
    chip = (place >> 1) & (CHIPS - 1)
    local = width // shards
    half = local // 2
    ff_local = down_weight.shape[0]
    group_shards = shards // CHIPS
    q_width = GROUP * HEAD
    qkv_width = q_width + 2 * HEAD
    index = jnp.stack([chip, core, depth]).astype(jnp.int32)

    gain_one = jnp.broadcast_to(attention_gain.astype(f32)[:, None], (local, LANES))
    gain_two = jnp.broadcast_to(feedforward_gain.astype(f32)[:, None], (local, LANES))

    x = own_first(index, (hidden_in,), local)[0]
    xs = plane_gather(x)

    at_block = attention_block(index, query_weight, key_weight, value_weight, output_weight, after(gain_one, x))
    at_own = lax.all_gather(at_block, "shard", axis=0, tiled=True)
    gu_block = feedforward_block(index, gate_weight, up_weight, after(gain_two, at_block), ff_local)
    gu_own = lax.all_gather(gu_block, "shard", axis=0, tiled=True)
    down_own = lax.all_gather(down_block(index, down_weight, local), "shard", axis=0, tiled=True)
    at_own = after(at_own, gu_block, *xs[1:])
    g = own_first(index, (out_grad,), local)[0]

    qkv_own = at_own[:, :qkv_width]
    qkv_other = swap(qkv_own, 1)
    inverse = rope_base ** (-jnp.arange(0, HEAD, 2, dtype=f32) / HEAD)
    places = (depth * rows + jnp.arange(rows, dtype=jnp.int32)).astype(f32)
    angles = inverse[:, None] * places[None, :]
    angles = jnp.concatenate([angles, angles], axis=0)
    cosine, sine = jnp.cos(angles), jnp.sin(angles)

    xhat, queries, kv = qkv_call(xs, qkv_own, qkv_other, cosine, sine)
    kvs = [kv] + [shift(kv, d) for d in range(1, shards)]
    g_all = jnp.concatenate(plane_gather(after(g, *xs[1:])), axis=0)
    turned, attended, stats = attention_call(index, after(queries, g_all), kvs)

    at_late = after(at_own, *kvs[1:])

    def out_for(mask):
        start = (chip ^ mask) * group_shards * half
        return lax.dynamic_slice(at_late, (start, qkv_width), (group_shards * half, 512))

    out_pieces = [out_for(0)] + [swap(out_for(m), 2 * m) for m in range(1, CHIPS)]
    out_rows = []
    for piece in out_pieces:
        split = piece.reshape(group_shards, 2, half // 2, 512)
        out_rows.append(
            jnp.concatenate([split[:, 0], split[:, 1]], axis=-1).reshape(-1, width // 2)
        )
    wo_own = jnp.concatenate(out_rows, axis=0)
    wo_other = swap(wo_own, 1)

    mid_parts = plane_send(parts_call((attended,), wo_own, wo_other, False, "attention_out"))
    middle, two = middle_call(mid_parts, x)
    twos = plane_gather(two)

    gu_own = after(gu_own, *twos[1:])
    gu_other = swap(gu_own, 1)
    act, for_gate, for_up, two_all = gate_call(twos, gu_own, gu_other)

    def over_groups(kept):
        if replicas > PIECES:
            groups = [
                [e * PIECES + i for e in range(replicas // PIECES)] for i in range(PIECES)
            ]
            kept = lax.psum(kept, "replica", axis_index_groups=groups)
        return kept

    def reduced(term):
        kept = lax.psum_scatter(term, "shard", scatter_dimension=0, tiled=True)
        return over_groups(kept)

    def plane_pieces(kept):
        mine = plane_gather(kept)
        return mine, [swap(part, 1) for part in mine]

    def mixed(mine, theirs):
        return [part for pair in zip(mine, theirs) for part in pair]

    quarter = width // 4

    def quarters(side):
        return [[(g_all, quarter, 2 * side + n)] for n in range(2)]

    down_sent = [swap(term, 1) for term in weight_grad(act, None, quarters(1), None, "down_grad_other")]
    down_terms = weight_grad(act, None, quarters(0), down_sent, "down_grad")
    down_kept = [reduced(term) for term in down_terms]
    down_own = after(down_own, *down_terms)
    down_other = swap(down_own, 1)

    grads = hidden_back_call(after(g_all, *down_terms), down_own, down_other, for_gate, for_up)
    e_terms = parts_call((grads,), gu_own, gu_other, True, "feedforward_back")
    e_parts = plane_send(after(e_terms, down_kept[0]))
    both = [[(grads, grads.shape[1], 0)]]
    gu_sent = swap(
        weight_grad(after(two_all, e_terms[0], down_kept[0]), 1, both, None, "gate_grad_other")[0], 1
    )
    gu_term = weight_grad(after(two_all, *e_parts[1:]), 0, both, (gu_sent,), "gate_grad")[0]
    gu_kept = reduced(gu_term)

    middle_late = after(middle, gu_term, *down_kept)
    grad_middle, branch = grad_middle_call(e_parts, middle_late, g)
    branches = plane_gather(branch)

    def back_block(m, block, before):
        return attention_back_call(
            index, m, block, wo_own, wo_other, queries, turned, stats, cosine, sine, kvs, before
        )

    before = back_block(0, branch, None)
    act_late = after(act, before[1])
    out_terms = parts_call((act_late,), down_own, down_other, False, "feedforward_out")
    for m in range(1, CHIPS):
        before = back_block(m, after(branches[m], out_terms[0]), before)
    out_parts = plane_send(after(out_terms, *branches[1:]))
    output = output_call(index, out_parts, middle, local)
    grad_q, grad_first, grad_rest = before

    branch_all = jnp.concatenate([after(block, grad_first) for block in branches], axis=0)
    half_wide = width // 2
    wo_sent = weight_grad(attended, None, [[(branch_all, half_wide, 1)]], None, "out_grad_other")
    wo_sent = (swap(wo_sent[0], 1),)
    wo_term = weight_grad(attended, None, [[(branch_all, half_wide, 0)]], wo_sent, "out_grad")[0]
    wo_cut = q_width // CHIPS
    wo_chips = [wo_term[:wo_cut]] + [
        swap(wo_term[m * wo_cut : (m + 1) * wo_cut], 2 * m) for m in range(1, CHIPS)
    ]
    wo_stack = jnp.stack(wo_chips)
    wo_block = jnp.concatenate(
        [lax.dynamic_index_in_dim(wo_stack, chip ^ i, 0, keepdims=False) for i in range(CHIPS)],
        axis=0,
    )

    kv_rest = [shift(grad_rest[d - 1], -d) for d in range(1, shards)]
    grad_kv = grad_kv_call(grad_first, kv_rest, cosine, sine)
    pairs = [[(grad_q, q_width, 0), (grad_kv, 2 * HEAD, 0)]]
    qkv_sent = (swap(weight_grad(xhat, 1, pairs, None, "qkv_grad_other")[0], 1),)
    qkv_term = weight_grad(xhat, 0, pairs, qkv_sent, "qkv_grad")[0]
    wo_wide = wo_block.reshape(shards, half // 2, 2, 512).transpose(0, 2, 1, 3).reshape(-1, 512)
    at_kept = reduced(after(jnp.concatenate([qkv_term, wo_wide], axis=1), gu_kept))

    down_kept = after(jnp.concatenate(down_kept, axis=1), *branches)
    down_out = rows_result(index, mixed(*plane_pieces(down_kept)), local, "down_result")
    e_one = plane_send(parts_call((grad_q, after(grad_kv, qkv_term, output, down_out)), qkv_own, qkv_other, True, "qkv_back"))
    grad_input = grad_input_call(index, e_one, x, grad_middle, local)

    gu_mine, gu_theirs = plane_pieces(gu_kept)
    gu_out = feedforward_result(index, 0, gu_mine, gate_weight, up_weight, gain_two, ff_local, None)
    gu_out = feedforward_result(index, 1, gu_theirs, gate_weight, up_weight, gain_two, ff_local, gu_out)
    at_pieces = mixed(*plane_pieces(at_kept))
    wo_out = out_result(index, at_pieces, local, width, qkv_width)
    q_out, k_out, v_out, gain_one_sums = qkv_result(
        index, at_pieces, query_weight, key_weight, value_weight, gain_one
    )
    return (
        output,
        grad_input,
        jnp.sum(gain_one_sums, axis=1),
        q_out,
        k_out,
        v_out,
        wo_out,
        jnp.sum(gu_out[2], axis=1),
        gu_out[0],
        gu_out[1],
        down_out,
    )


def solution(mesh):
    return jax.shard_map(
        per_device,
        mesh=mesh,
        in_specs=(
            P(("replica", "shard"), None),
            P("shard"),
            P("shard", None),
            P("shard", None),
            P("shard", None),
            P("shard", None),
            P("shard"),
            P("shard", None),
            P("shard", None),
            P("shard", None),
            P(("replica", "shard"), None),
        ),
        out_specs=(
            P(("replica", "shard"), None),
            P(("replica", "shard"), None),
            P("shard"),
            P("shard", None),
            P("shard", None),
            P("shard", None),
            P("shard", None),
            P("shard"),
            P("shard", None),
            P("shard", None),
            P("shard", None),
        ),
        check_vma=False,
    )
```

```python
import functools

import jax
import jax.numpy as jnp
from jax import lax
from jax.experimental import pallas as pl
from jax.experimental.pallas import tpu as pltpu
from jax.sharding import PartitionSpec as P

HEADS = 32
KV_HEADS = 4
HEAD = 64
GROUP = HEADS // KV_HEADS
CHIPS = 4
PIECES = 2 * CHIPS
PAIR = 2
LANES = 128

norm_eps = 1e-05
rope_base = 10000.0
masked_score = -1e30

f32 = jnp.float32
bf16 = jnp.bfloat16
VMEM = pltpu.VMEM
NT = (((1,), (1,)), ((), ()))
TN = (((0,), (0,)), ((), ()))


def dot(left, right):
    return jnp.dot(left, right, preferred_element_type=f32)


def dot_nt(left, right):
    return lax.dot_general(left, right, NT, preferred_element_type=f32)


def dot_tn(left, right):
    return lax.dot_general(left, right, TN, preferred_element_type=f32)


def shape(dims, kind):
    return jax.ShapeDtypeStruct(dims, kind)


def whole():
    return pl.BlockSpec(memory_space=VMEM)


def kernel_call(body, out_shape, in_specs, out_specs, operands, *, index=None, grid=(), scratch=(),
                moved=0, aliases=None, name=None):
    params = pltpu.CompilerParams(
        vmem_limit_bytes=52 * 2**20, dimension_semantics=("arbitrary",) * len(grid)
    )
    cost = pl.CostEstimate(flops=0, bytes_accessed=int(moved), transcendentals=0)
    common = dict(
        out_shape=out_shape,
        compiler_params=params,
        cost_estimate=cost,
        input_output_aliases=aliases or {},
        name=name,
    )
    if index is None:
        spec = pl.GridSpec(grid=grid, in_specs=in_specs, out_specs=out_specs, scratch_shapes=scratch)
        return pl.pallas_call(body, grid_spec=spec, **common)(*operands)
    spec = pltpu.PrefetchScalarGridSpec(
        num_scalar_prefetch=1, grid=grid, in_specs=in_specs, out_specs=out_specs,
        scratch_shapes=scratch,
    )
    return pl.pallas_call(body, grid_spec=spec, **common)(index, *operands)


def swap(value, mask):
    size = lax.axis_size("replica")
    return lax.ppermute(value, "replica", [(i, i ^ mask) for i in range(size)])


def shift(value, step):
    size = lax.axis_size("shard")
    pairs = [(i, i + step) for i in range(size) if 0 <= i + step < size]
    return lax.ppermute(value, "shard", pairs)


def plane_gather(value):
    return [value] + [swap(value, 2 * m) for m in range(1, CHIPS)]


def plane_send(parts):
    return [parts[0]] + [swap(parts[m], 2 * m) for m in range(1, len(parts))]


def group_of(chip):
    return 2 * (chip & 1) + (chip >> 1)


def after(value, *others):
    return lax.optimization_barrier((value, *others))[0]


def attention_block_body(local, group_shards, index, q, k, v, o, gain, out, wo_out):
    scale = gain[:, :1]
    q_width = GROUP * HEAD
    cut = local // CHIPS
    for chip in range(CHIPS):

        group = group_of(chip)

        @pl.when(index[0] == chip)
        def _(group=group):
            parts = []
            for m in range(CHIPS):
                for s in range(group_shards):
                    start = group * q_width + s * local + (m ^ chip) * cut
                    parts.append(q[:, start : start + cut])
            parts.append(k[:, group * HEAD : (group + 1) * HEAD])
            parts.append(v[:, group * HEAD : (group + 1) * HEAD])
            wide = jnp.concatenate([part.astype(f32) for part in parts], axis=1)
            out[...] = (wide * scale).astype(bf16)

    half = local // 2
    shards = o.shape[1] // local
    for core in range(2):

        @pl.when(index[1] == core)
        def _():
            for s in range(shards):
                piece = o[:, s * local + core * half : s * local + (core + 1) * half]
                wo_out[:, s * half : (s + 1) * half] = piece


def attention_block(index, query, key, value, output, gain):
    local, width = query.shape
    half = local // 2
    shards = width // local
    return kernel_call(
        functools.partial(attention_block_body, local, shards // CHIPS),
        (
            shape((half, GROUP * HEAD + 2 * HEAD), bf16),
            shape((local // CHIPS, width // 2), bf16),
        ),
        [
            pl.BlockSpec((half, width), lambda i, n: (n[1], 0)),
            pl.BlockSpec((half, key.shape[1]), lambda i, n: (n[1], 0)),
            pl.BlockSpec((half, key.shape[1]), lambda i, n: (n[1], 0)),
            pl.BlockSpec((local // CHIPS, width), lambda i, n: (n[0], 0)),
            pl.BlockSpec((half, LANES), lambda i, n: (n[1], 0)),
        ],
        (
            pl.BlockSpec((half, GROUP * HEAD + 2 * HEAD), lambda i, n: (0, 0)),
            pl.BlockSpec((local // CHIPS, width // 2), lambda i, n: (0, 0)),
        ),
        (query, key, value, output, gain),
        index=index,
        grid=(1,),
        name="attention_block",
    )


def feedforward_block_body(ff_local, cut, index, gate, up, gain, out):
    scale = gain[:, :1]
    shards = gate.shape[1] // ff_local
    width = shards * cut
    for chip in range(CHIPS):

        @pl.when(index[0] == chip)
        def _():
            for n, source in enumerate((gate, up)):
                parts = [
                    source[:, s * ff_local + chip * cut : s * ff_local + (chip + 1) * cut].astype(f32)
                    for s in range(shards)
                ]
                wide = jnp.concatenate(parts, axis=1)
                out[:, n * width : (n + 1) * width] = (wide * scale).astype(bf16)


def feedforward_block(index, gate, up, gain, ff_local):
    local, ff = gate.shape
    half = local // 2
    rows = 64
    steps = half // rows
    cut = ff_local // CHIPS
    width = 2 * (ff // CHIPS)
    return kernel_call(
        functools.partial(feedforward_block_body, ff_local, cut),
        shape((half, width), bf16),
        [
            pl.BlockSpec((rows, ff), lambda i, n: (n[1] * steps + i, 0)),
            pl.BlockSpec((rows, ff), lambda i, n: (n[1] * steps + i, 0)),
            pl.BlockSpec((rows, LANES), lambda i, n: (n[1] * steps + i, 0)),
        ],
        pl.BlockSpec((rows, width), lambda i, n: (i, 0)),
        (gate, up, gain),
        index=index,
        grid=(steps,),
        name="feedforward_block",
    )


def own_first_body(local, index, *refs):
    count = len(refs) // 2
    half = local // 2
    for core in range(2):

        @pl.when(index[1] == core)
        def _():
            for source, out in zip(refs[:count], refs[count:]):
                shards = source.shape[1] // local
                sides = out.shape[1] // (shards * half)
                for side in range(sides):
                    for s in range(shards):
                        start = s * local + (core ^ side) * half
                        spot = (side * shards + s) * half
                        out[:, spot : spot + half] = source[:, start : start + half]


def own_first(index, sources, local, halves=2):
    return kernel_call(
        functools.partial(own_first_body, local),
        tuple(shape((v.shape[0], v.shape[1] * halves // 2), bf16) for v in sources),
        [pl.BlockSpec(v.shape, lambda i, n: (0, 0)) for v in sources],
        tuple(
            pl.BlockSpec((v.shape[0], v.shape[1] * halves // 2), lambda i, n: (0, 0)) for v in sources
        ),
        tuple(sources),
        index=index,
        grid=(1,),
        name="own_first",
    )


def down_block_body(local, index, source, out):
    own_first_body(local, index, source, out)


def down_block(index, down, local):
    ff_local, width = down.shape
    cut = ff_local // CHIPS
    return kernel_call(
        functools.partial(down_block_body, local),
        shape((cut, width // 2), bf16),
        [pl.BlockSpec((cut, width), lambda i, n: (n[0], 0))],
        pl.BlockSpec((cut, width // 2), lambda i, n: (0, 0)),
        (down,),
        index=index,
        grid=(1,),
        name="down_block",
    )


def part_sum(parts):
    total = parts[0][...]
    for part in parts[1:]:
        total = total + part[...].astype(f32)
    return total


def mean_of(values):
    return jnp.mean(values, axis=1, keepdims=True)


def middle_body(*refs):
    parts, (x, middle, two) = refs[:PAIR], refs[PAIR:]
    total = x[...].astype(f32) + part_sum(parts)
    middle[...] = total
    two[...] = (total * lax.rsqrt(mean_of(total * total) + norm_eps)).astype(bf16)


def middle_call(parts, x):
    return kernel_call(
        middle_body,
        (shape(x.shape, f32), shape(x.shape, bf16)),
        [whole()] * (PAIR + 1),
        (whole(), whole()),
        (*parts, x),
        name="middle",
    )


def norm_back(e, values):
    inverse = lax.rsqrt(mean_of(values * values) + norm_eps)
    return inverse * e - values * (inverse * inverse * inverse) * mean_of(e * values)


def grad_middle_body(*refs):
    parts, (middle, g, grad, low) = refs[:CHIPS], refs[CHIPS:]
    total = g[...].astype(f32) + norm_back(part_sum(parts), middle[...])
    grad[...] = total
    low[...] = total.astype(bf16)


def grad_middle_call(parts, middle, g):
    return kernel_call(
        grad_middle_body,
        (shape(g.shape, f32), shape(g.shape, bf16)),
        [whole()] * (CHIPS + 2),
        (whole(), whole()),
        (*parts, middle, g),
        name="grad_middle",
    )


def store_in_order(local, index, value, out):
    half = local // 2
    shards = out.shape[1] // local
    for core in range(2):

        @pl.when(index[1] == core)
        def _():
            for side in range(2):
                for s in range(shards):
                    spot = s * local + (core ^ side) * half
                    start = (side * shards + s) * half
                    out[:, spot : spot + half] = value[:, start : start + half].astype(bf16)


def output_body(local, index, *refs):
    parts, (middle, out) = refs[:CHIPS], refs[CHIPS:]
    store_in_order(local, index, middle[...] + part_sum(parts), out)


def output_call(index, parts, middle, local):
    spec = pl.BlockSpec(middle.shape, lambda i, n: (0, 0))
    return kernel_call(
        functools.partial(output_body, local),
        shape(middle.shape, bf16),
        [spec] * (CHIPS + 1),
        spec,
        (*parts, middle),
        index=index,
        grid=(1,),
        name="output",
    )


def grad_input_body(local, index, *refs):
    parts, (x, grad, out) = refs[:PAIR], refs[PAIR:]
    total = grad[...] + norm_back(part_sum(parts), x[...].astype(f32))
    store_in_order(local, index, total, out)


def grad_input_call(index, parts, x, grad, local):
    spec = pl.BlockSpec(x.shape, lambda i, n: (0, 0))
    return kernel_call(
        functools.partial(grad_input_body, local),
        shape(x.shape, bf16),
        [spec] * (PAIR + 2),
        spec,
        (*parts, x, grad),
        index=index,
        grid=(1,),
        name="grad_input",
    )


def grad_kv_body(shards, *refs):
    first, rest, (cosine, sine, out) = refs[0], refs[1:shards], refs[shards:]
    total = first[...]
    for term in rest:
        total = total + term[...].astype(f32)
    rows = cosine.shape[1]
    cos, sin = cosine[...], sine[...]
    for m in range(PAIR):
        turned = total[m * rows : (m + 1) * rows, :].T
        k = turned[:HEAD]
        k = k * cos - half_rotated(k) * sin
        both = jnp.concatenate([k, turned[HEAD:]], axis=0)
        out[m * rows : (m + 1) * rows, :] = both.T.astype(bf16)


def grad_kv_call(first, rest, cosine, sine):
    return kernel_call(
        functools.partial(grad_kv_body, len(rest) + 1),
        shape(first.shape, bf16),
        [whole()] * (len(rest) + 3),
        whole(),
        (first, *rest, cosine, sine),
        name="grad_kv",
    )


def half_rotated(values):
    middle = values.shape[0] // 2
    return jnp.concatenate([-values[middle:], values[:middle]], axis=0)


def qkv_body(make, *refs):
    if make:
        xs, (own, other, cosine, sine, queries, kv, xhat) = refs[:PAIR], refs[PAIR:]
        rows, width = xs[0].shape
        for m in range(PAIR):
            x = xs[m][...].astype(f32)
            inverse = lax.rsqrt(mean_of(x * x) + norm_eps)
            xhat[m * rows : (m + 1) * rows, :] = (x * inverse).astype(bf16)
    else:
        xhat, own, other, cosine, sine, queries, kv = refs
        rows, width = cosine.shape[1], xhat.shape[1]
    cos, sin = cosine[...], sine[...]
    total = dot(xhat[:, : width // 2], own[...]) + dot(xhat[:, width // 2 :], other[...])
    for m in range(PAIR):
        turned = total[m * rows : (m + 1) * rows].T
        for h in range(GROUP + 1):
            u = turned[h * HEAD : (h + 1) * HEAD]
            u = u * cos + half_rotated(u) * sin
            if h < GROUP:
                queries[m, :, h * rows : (h + 1) * rows] = (u * HEAD ** (-0.5)).astype(bf16)
            else:
                both = jnp.concatenate([u, turned[(h + 1) * HEAD :]], axis=0)
                kv[m * rows : (m + 1) * rows, :] = both.T.astype(bf16)


def qkv_call(xs, own, other, cosine, sine):
    make = isinstance(xs, list)
    rows = cosine.shape[1]
    tokens = PAIR * rows
    outs = (shape((PAIR, HEAD, GROUP * rows), bf16), shape((tokens, 2 * HEAD), bf16))
    if make:
        outs = outs + (shape((tokens, xs[0].shape[1]), bf16),)
    operands = (*(xs if make else (xs,)), own, other, cosine, sine)
    return kernel_call(
        functools.partial(qkv_body, make),
        outs,
        [whole()] * len(operands),
        tuple(whole() for _ in outs),
        operands,
        name="qkv",
    )


def out_rows_body(index, *refs):
    pieces, out = refs[:CHIPS], refs[CHIPS]
    cut = pieces[0].shape[0] // PAIR
    for row in range(2):

        @pl.when(index[0] >> 1 == row)
        def _():
            for n in range(PAIR):
                for m in range(CHIPS):
                    spot = (n * CHIPS + m) * cut
                    start = (n ^ row) * cut
                    out[spot : spot + cut, :] = pieces[m ^ (2 * n)][start : start + cut, :]


def out_rows_call(index, pieces):
    rows, width = pieces[0].shape
    return kernel_call(
        out_rows_body,
        shape((CHIPS * rows, width), bf16),
        [pl.BlockSpec((rows, width), lambda i, n: (0, 0))] * CHIPS,
        pl.BlockSpec((CHIPS * rows, width), lambda i, n: (0, 0)),
        tuple(pieces),
        index=index,
        grid=(1,),
        name="out_rows",
    )


LANE_HEADS = 4


def own_block_bias(rows):
    key = lax.broadcasted_iota(jnp.int32, (rows, rows), 0)
    mine = lax.broadcasted_iota(jnp.int32, (rows, rows), 1)
    return jnp.where(key <= mine, 0.0, masked_score)


def set_bias(bias):
    rows = bias.shape[0]
    value = own_block_bias(rows)
    for h in range(LANE_HEADS):
        bias[:, h * rows : (h + 1) * rows] = value


def far_bias(depth, d):
    return jnp.where(d <= depth, 0.0, masked_score) if d else 0.0


def attention_body(shards, index, queries, *refs):
    kvs = refs[:shards]
    turned_out, out, stats, bias, terms, out_turned = refs[shards:]
    rows = bias.shape[0]
    wide = LANE_HEADS * rows

    @pl.when(pl.program_id(0) == 0)
    def _():
        set_bias(bias)

    ks = [kv[:, :HEAD] for kv in kvs]
    v_turned = jnp.concatenate([kv[...] for kv in kvs], axis=0).astype(f32).T[HEAD:].astype(bf16)
    for n in range(GROUP // LANE_HEADS):
        span = slice(n * wide, (n + 1) * wide)
        q = queries[0, :, span]
        scores, top = [], None
        for d in range(shards):
            score = dot(ks[d], q)
            if d == 0:
                score = score + bias[...]
            scores.append(score)
            highest = jnp.max(score, axis=0, keepdims=True) + far_bias(index[2], d)
            top = highest if top is None else jnp.maximum(top, highest)
        total = None
        for d in range(shards):
            term = jnp.exp(scores[d] - (top - far_bias(index[2], d)))
            part = jnp.sum(term, axis=0, keepdims=True)
            total = part if total is None else total + part
            terms[d * rows : (d + 1) * rows, :] = term.astype(bf16)
        out_turned[:, span] = dot(v_turned, terms[...]) / total
        stats[0, :, span] = top + jnp.log(total)
    turned_out[0] = out_turned[...].astype(bf16)
    straight = out_turned[...].T
    for h in range(GROUP):
        out[:, h * HEAD : (h + 1) * HEAD] = straight[h * rows : (h + 1) * rows].astype(bf16)


def attention_call(index, queries, kvs):
    chips, _, wide = queries.shape
    rows = wide // GROUP
    shards = len(kvs)
    keys = shards * rows
    block = pl.BlockSpec((1, HEAD, wide), lambda i, n: (i, 0, 0))
    return kernel_call(
        functools.partial(attention_body, shards),
        (
            shape((chips, HEAD, wide), bf16),
            shape((chips * rows, GROUP * HEAD), bf16),
            shape((chips, 1, wide), f32),
        ),
        [block] + [pl.BlockSpec((rows, 2 * HEAD), lambda i, n: (i, 0))] * shards,
        (
            block,
            pl.BlockSpec((rows, GROUP * HEAD), lambda i, n: (i, 0)),
            pl.BlockSpec((1, 1, wide), lambda i, n: (i, 0, 0)),
        ),
        (queries, *kvs),
        index=index,
        grid=(chips,),
        scratch=(
            VMEM((rows, LANE_HEADS * rows), f32),
            VMEM((keys, LANE_HEADS * rows), bf16),
            VMEM((HEAD, wide), f32),
        ),
        name="attention",
    )


def attention_back_body(shards, index, branch, wo_own, wo_other, cosine, sine, *refs):
    per_group = 3 + shards
    inputs = [refs[n * per_group : (n + 1) * per_group] for n in range(PAIR)]
    outs = [refs[-10 + 3 * n : -7 + 3 * n] for n in range(PAIR)]
    bias, probs_low, grads_low, grad_lanes = refs[-4:]
    rows = bias.shape[0]
    wide = LANE_HEADS * rows
    width = branch.shape[1]
    set_bias(bias)
    cos, sin = cosine[...], sine[...]
    for (queries, turned_out, stats, *kvs), (grad_q, grad_first, grad_rest), n in zip(inputs, outs, range(PAIR)):
        heads = slice(n * GROUP * HEAD, (n + 1) * GROUP * HEAD)
        grad_out = dot_nt(wo_own[heads, :], branch[:, : width // 2])
        grad_out = grad_out + dot_nt(wo_other[heads, :], branch[:, width // 2 :])
        for h in range(GROUP):
            grad_lanes[:, h * rows : (h + 1) * rows] = grad_out[h * HEAD : (h + 1) * HEAD].astype(bf16)
        ks = [kv[:, :HEAD] for kv in kvs]
        vs = [kv[:, HEAD:] for kv in kvs]
        k_turned = jnp.concatenate([kv[...] for kv in kvs], axis=0).astype(f32).T[:HEAD].astype(bf16)
        k_total, v_total, parts = None, None, []
        for c in range(GROUP // LANE_HEADS):
            span = slice(c * wide, (c + 1) * wide)
            q, mine = queries[0, :, span], grad_lanes[:, span]
            delta = jnp.sum(
                mine.astype(f32) * turned_out[0, :, span].astype(f32), axis=0, keepdims=True
            )
            for d in range(shards):
                score = dot(ks[d], q)
                if d == 0:
                    score = score + bias[...]
                probs = jnp.exp(score - (stats[0, :, span] - far_bias(index[2], d)))
                grad_scores = probs * (dot(vs[d], mine) - delta)
                probs_low[d * rows : (d + 1) * rows, :] = probs.astype(bf16)
                grads_low[d * rows : (d + 1) * rows, :] = grad_scores.astype(bf16)
            u = dot(k_turned, grads_low[...]) * HEAD ** (-0.5)
            parts.append(u * cos - half_rotated(u) * sin)
            k_term = dot_nt(grads_low[...], q)
            v_term = dot_nt(probs_low[...], mine)
            k_total = k_term if k_total is None else k_total + k_term
            v_total = v_term if v_total is None else v_total + v_term
        straight = jnp.concatenate(parts, axis=1).T
        for h in range(GROUP):
            grad_q[:, h * HEAD : (h + 1) * HEAD] = straight[h * rows : (h + 1) * rows].astype(bf16)
        both = jnp.concatenate([k_total, v_total], axis=1)
        grad_first[...] = both[:rows, :]
        for d in range(1, shards):
            grad_rest[d - 1] = both[d * rows : (d + 1) * rows, :].astype(bf16)


def attention_back_call(index, m, branch, wo_own, wo_other, cosine, sine, groups, before):
    chips, _, wide = groups[0][0].shape
    rows = wide // GROUP
    shards = len(groups[0][3])
    keys = shards * rows
    tokens = chips * rows
    block = pl.BlockSpec((1, HEAD, wide), lambda i, n: (m, 0, 0))
    in_specs = [whole()] * 5
    operands = [branch, wo_own, wo_other, jnp.tile(cosine, (1, LANE_HEADS)), jnp.tile(sine, (1, LANE_HEADS))]
    for queries, turned, stats, kvs in groups:
        in_specs += [block, block, pl.BlockSpec((1, 1, wide), lambda i, n: (m, 0, 0))]
        in_specs += [pl.BlockSpec((rows, 2 * HEAD), lambda i, n: (m, 0))] * shards
        operands += [queries, turned, stats, *kvs]
    aliases = {}
    if before is not None:
        aliases = {1 + len(operands) + n: n for n in range(3 * PAIR)}
        in_specs += [pl.BlockSpec(memory_space=pl.ANY)] * (3 * PAIR)
        operands += list(before)
    outs = (
        shape((tokens, GROUP * HEAD), bf16),
        shape((tokens, 2 * HEAD), f32),
        shape((shards - 1, tokens, 2 * HEAD), bf16),
    )
    out_specs = (
        pl.BlockSpec((rows, GROUP * HEAD), lambda i, n: (m, 0)),
        pl.BlockSpec((rows, 2 * HEAD), lambda i, n: (m, 0)),
        pl.BlockSpec((shards - 1, rows, 2 * HEAD), lambda i, n: (0, m, 0)),
    )
    return kernel_call(
        functools.partial(attention_back_body, shards),
        outs * PAIR,
        in_specs,
        out_specs * PAIR,
        tuple(operands),
        index=index,
        grid=(1,),
        scratch=(
            VMEM((rows, LANE_HEADS * rows), f32),
            VMEM((keys, LANE_HEADS * rows), bf16),
            VMEM((keys, LANE_HEADS * rows), bf16),
            VMEM((HEAD, wide), bf16),
        ),
        aliases=aliases,
        name="attention_back",
    )


def parts_body(steps, transposed, count, *refs):
    lefts, owns, others = refs[:count], refs[count : 2 * count], refs[2 * count : 3 * count]
    outs = refs[3 * count :]
    rows = outs[0].shape[0]
    step = pl.program_id(0)

    def run(weights):
        total = None
        for left, weight in zip(lefts, weights):
            term = (dot_nt if transposed else dot)(left[...], weight[...])
            total = term if total is None else total + term
        for m, out in enumerate(outs):
            out[...] = total[m * rows : (m + 1) * rows, :].astype(out.dtype)

    @pl.when(step < steps)
    def _():
        run(owns)

    @pl.when(step >= steps)
    def _():
        run(others)


def parts_call(terms, rows, transposed, name):
    tokens = terms[0][0].shape[0]
    half = terms[0][1].shape[0] if transposed else terms[0][1].shape[1]
    tile = 256
    steps = half // tile
    last = steps - 1
    specs = [pl.BlockSpec((tokens, term[0].shape[1]), lambda j: (0, 0)) for term in terms]
    for side in range(2):
        for left, _, _, spot in terms:
            depth = left.shape[1]

            def place(side, spot, j):
                step = jnp.maximum(j - steps, 0) if side else jnp.minimum(j, last)
                return (step, spot) if transposed else (spot, step)

            block = (tile, depth) if transposed else (depth, tile)
            specs.append(pl.BlockSpec(block, functools.partial(place, side, spot)))
    count = tokens // rows
    return kernel_call(
        functools.partial(parts_body, steps, transposed, len(terms)),
        tuple(shape((rows, 2 * half), f32 if m == 0 else bf16) for m in range(count)),
        specs,
        tuple(pl.BlockSpec((rows, tile), lambda j: (0, j)) for _ in range(count)),
        (*(term[0] for term in terms), *(term[1] for term in terms), *(term[2] for term in terms)),
        grid=(2 * steps,),
        name=name,
    )


def gate_body(*refs):
    twos = refs[:CHIPS]
    gate_own, up_own, gate_other, up_other, act, for_gate, for_up, two_all = refs[CHIPS:]
    rows, width = twos[0].shape
    half = width // 2

    @pl.when(pl.program_id(0) == 0)
    def _():
        for m in range(CHIPS):
            two_all[m * rows : (m + 1) * rows, :] = twos[m][...]

    own = jnp.concatenate([gate_own[...], up_own[...]], axis=1)
    other = jnp.concatenate([gate_other[...], up_other[...]], axis=1)
    both = dot(two_all[:, :half], own) + dot(two_all[:, half:], other)
    wide = gate_own.shape[1]
    gate, up = both[:, :wide], both[:, wide:]
    sig = 1.0 / (1.0 + jnp.exp(-gate))
    silu = gate * sig
    act[...] = (silu * up).astype(bf16)
    for_gate[...] = (up * sig * (1.0 + gate * (1.0 - sig))).astype(bf16)
    for_up[...] = silu.astype(bf16)


def gate_call(twos, own, other):
    rows, width = twos[0].shape
    tokens = CHIPS * rows
    half = width // 2
    ff = own.shape[1] // 2
    tile = LANES
    steps = ff // tile
    weight = [
        pl.BlockSpec((half, tile), lambda j: (0, j)),
        pl.BlockSpec((half, tile), lambda j: (0, j + steps)),
    ]
    column = pl.BlockSpec((tokens, tile), lambda j: (0, j))
    return kernel_call(
        gate_body,
        tuple(shape((tokens, ff), bf16) for _ in range(3)) + (shape((tokens, width), bf16),),
        [pl.BlockSpec((rows, width), lambda j: (0, 0))] * CHIPS + weight + weight,
        (column, column, column, pl.BlockSpec((tokens, width), lambda j: (0, 0))),
        (*twos, own, own, other, other),
        grid=(steps,),
        name="gate",
    )


def hidden_back_body(g, own, other, for_gate, for_up, grads):
    half = g.shape[1] // 2
    ff = own.shape[0]
    hidden = dot_nt(g[:, :half], own[...]) + dot_nt(g[:, half:], other[...])
    grads[:, :ff] = (hidden * for_gate[...].astype(f32)).astype(bf16)
    grads[:, ff:] = (hidden * for_up[...].astype(f32)).astype(bf16)


def hidden_back_call(g, own, other, for_gate, for_up):
    tokens, width = g.shape
    ff, half = own.shape
    block = tokens // 2
    row = lambda i: (i, 0)
    fixed = lambda i: (0, 0)
    return kernel_call(
        hidden_back_body,
        shape((tokens, 2 * ff), bf16),
        [
            pl.BlockSpec((block, width), row),
            pl.BlockSpec((ff, half), fixed),
            pl.BlockSpec((ff, half), fixed),
            pl.BlockSpec((block, ff), row),
            pl.BlockSpec((block, ff), row),
        ],
        pl.BlockSpec((block, 2 * ff), row),
        (g, own, other, for_gate, for_up),
        grid=(2,),
        name="hidden_back",
    )


def weight_grad_body(per, outputs, adds, left, right, *refs):
    added = [refs[n * outputs : (n + 1) * outputs] for n in range(adds)]
    outs, turned = refs[adds * outputs : -1], refs[-1]
    step = pl.program_id(0)

    @pl.when(step == 0)
    def _():
        turned[...] = left[...].T

    for n in range(outputs):

        @pl.when(step // per == n)
        def _(n=n):
            total = dot(turned[...], right[...])
            for terms in added:
                total = total + terms[n][...].astype(f32)
            outs[n][...] = total.astype(bf16)


def weight_grad(left, left_side, right, place, width, outputs, added, name):
    tokens = left.shape[0]
    rows = left.shape[1] // (1 if left_side is None else 2)
    tile = 256 if width % 256 == 0 else width
    per = width // tile
    first = place * width // tile
    side = left_side or 0

    def spot(n, j):
        return (0, jnp.clip(j - n * per, 0, per - 1))

    tiles = [pl.BlockSpec((rows, tile), functools.partial(spot, n)) for n in range(outputs)]
    return kernel_call(
        functools.partial(weight_grad_body, per, outputs, len(added)),
        tuple(shape((rows, width), bf16) for _ in range(outputs)),
        [
            pl.BlockSpec((tokens, rows), lambda j: (0, side)),
            pl.BlockSpec((tokens, tile), lambda j: (0, first + j)),
        ]
        + tiles * len(added),
        tuple(tiles),
        (left, right, *(term for terms in added for term in terms)),
        grid=(per * outputs,),
        scratch=(VMEM((rows, tokens), bf16),),
        name=name,
    )


def rows_result_body(local, index, *refs):
    pieces, out = refs[:PIECES], refs[PIECES]
    half = local // 2
    shards = out.shape[1] // local
    for m in range(CHIPS):
        for core in range(2):

            @pl.when((pl.program_id(0) == m) & (index[1] == core))
            def _():
                for side in range(2):
                    piece = pieces[2 * m + side]
                    for s in range(shards):
                        spot = s * local + (core ^ side) * half
                        out[:, spot : spot + half] = piece[:, s * half : (s + 1) * half].astype(f32)


def rows_result(index, pieces, local, name):
    cut, half_width = pieces[0].shape
    return kernel_call(
        functools.partial(rows_result_body, local),
        shape((CHIPS * cut, 2 * half_width), f32),
        [pl.BlockSpec((cut, half_width), lambda i, n: (0, 0))] * PIECES,
        pl.BlockSpec((cut, 2 * half_width), lambda i, n: (n[0] ^ i, 0)),
        tuple(pieces),
        index=index,
        grid=(CHIPS,),
        name=name,
    )


def out_result_body(local, base, index, *refs):
    pieces, out = refs[:PIECES], refs[PIECES]
    half = local // 2
    cut = local // CHIPS
    shards = out.shape[1] // local
    for m in range(CHIPS):
        for core in range(2):

            @pl.when((pl.program_id(0) == m) & (index[1] == core))
            def _():
                for side in range(2):
                    piece = pieces[2 * m + side]
                    for s in range(shards):
                        spot = s * local + (core ^ side) * half
                        row, column = (0, s * half) if s * half < 512 else (cut, s * half - 512)
                        column += base
                        out[:, spot : spot + half] = piece[row : row + cut, column : column + half].astype(f32)


def out_result(index, pieces, local, width, base):
    cut = local // CHIPS
    return kernel_call(
        functools.partial(out_result_body, local, base),
        shape((local, width), f32),
        [pl.BlockSpec(pieces[0].shape, lambda i, n: (0, 0))] * PIECES,
        pl.BlockSpec((cut, width), lambda i, n: (n[0] ^ i, 0)),
        tuple(pieces),
        index=index,
        grid=(CHIPS,),
        name="out_result",
    )


def lane_sum(value):
    total = value[:, :LANES]
    for n in range(1, value.shape[1] // LANES):
        total = total + value[:, n * LANES : (n + 1) * LANES]
    return total


def feedforward_result_body(ff_local, cut, index, *refs):
    pieces = refs[:CHIPS]
    gate_weight, up_weight, gain = refs[CHIPS : CHIPS + 3]
    gate_out, up_out, gain_out = refs[-3:]
    shards = gate_weight.shape[1] // ff_local
    width = shards * cut
    for chip in range(CHIPS):

        @pl.when(index[0] == chip)
        def _():
            @pl.loop(0, gate_out.shape[0] // 16)
            def _(n):
                rows = pl.ds(pl.multiple_of(n * 16, 16), 16)
                scale = gain[rows, :1]
                total = jnp.zeros((16, LANES), f32)
                for base, weight, out in ((0, gate_weight, gate_out), (width, up_weight, up_out)):
                    parts = []
                    for s in range(shards):
                        for owner in range(CHIPS):
                            start = base + s * cut
                            parts.append(pieces[owner ^ chip][rows, start : start + cut].astype(f32))
                    wide = jnp.concatenate(parts, axis=1)
                    total = total + lane_sum(wide * weight[rows, :].astype(f32))
                    out[rows, :] = wide * scale
                gain_out[rows, :] = total


def feedforward_result(index, side, pieces, gate_weight, up_weight, gain, ff_local, before):
    local, ff = gate_weight.shape
    half = local // 2
    rows = 64
    steps = half // rows
    row = lambda i, n: ((n[1] ^ side) * steps + i, 0)
    in_specs = [pl.BlockSpec((rows, pieces[0].shape[1]), lambda i, n: (i, 0))] * CHIPS
    in_specs += [pl.BlockSpec((rows, ff), row)] * 2 + [pl.BlockSpec((rows, LANES), row)]
    operands = (*pieces, gate_weight, up_weight, gain)
    aliases = {}
    if before is not None:
        aliases = {1 + len(operands) + n: n for n in range(3)}
        in_specs = in_specs + [pl.BlockSpec(memory_space=pl.ANY)] * 3
        operands = operands + tuple(before)
    return kernel_call(
        functools.partial(feedforward_result_body, ff_local, ff_local // CHIPS),
        (shape((local, ff), f32), shape((local, ff), f32), shape((local, LANES), f32)),
        in_specs,
        (pl.BlockSpec((rows, ff), row), pl.BlockSpec((rows, ff), row), pl.BlockSpec((rows, LANES), row)),
        operands,
        index=index,
        grid=(steps,),
        aliases=aliases,
        name="feedforward_result",
    )


def qkv_result_body(local, group_shards, index, *refs):
    pieces = refs[:PIECES]
    weights, gain = refs[PIECES : PIECES + 3], refs[PIECES + 3]
    outs, gain_out = refs[PIECES + 4 : PIECES + 7], refs[PIECES + 7]
    q_width = GROUP * HEAD
    cut = local // CHIPS
    scale = gain[:, :1]
    for chip in range(CHIPS):
        for side in range(2):

            @pl.when((index[0] == chip) & (pl.program_id(0) == side))
            def _():
                parts, k_parts, v_parts = [], [], []
                for group in range(CHIPS):
                    owner = (group >> 1) + 2 * (group & 1)
                    piece = pieces[2 * (owner ^ chip) + side]
                    for s in range(group_shards):
                        for j in range(CHIPS):
                            start = ((j ^ owner) * group_shards + s) * cut
                            parts.append(piece[:, start : start + cut].astype(f32))
                    k_parts.append(piece[:, q_width : q_width + HEAD].astype(f32))
                    v_parts.append(piece[:, q_width + HEAD : q_width + 2 * HEAD].astype(f32))
                total = jnp.zeros((gain.shape[0], LANES), f32)
                for part, weight, out in zip((parts, k_parts, v_parts), weights, outs):
                    wide = jnp.concatenate(part, axis=1)
                    total = total + lane_sum(wide * weight[...].astype(f32))
                    out[...] = wide * scale
                gain_out[...] = total


def qkv_result(index, pieces, query, key, value, gain):
    local, width = query.shape
    half = local // 2
    group_shards = width // local // CHIPS
    row = lambda i, n: (n[1] ^ i, 0)
    kv_width = key.shape[1]
    return kernel_call(
        functools.partial(qkv_result_body, local, group_shards),
        (
            shape((local, width), f32),
            shape((local, kv_width), f32),
            shape((local, kv_width), f32),
            shape((local, LANES), f32),
        ),
        [pl.BlockSpec(pieces[0].shape, lambda i, n: (0, 0))] * PIECES
        + [
            pl.BlockSpec((half, width), row),
            pl.BlockSpec((half, kv_width), row),
            pl.BlockSpec((half, kv_width), row),
            pl.BlockSpec((half, LANES), row),
        ],
        (
            pl.BlockSpec((half, width), row),
            pl.BlockSpec((half, kv_width), row),
            pl.BlockSpec((half, kv_width), row),
            pl.BlockSpec((half, LANES), row),
        ),
        (*pieces, query, key, value, gain),
        index=index,
        grid=(2,),
        name="qkv_result",
    )


def per_device(
    hidden_in,
    attention_gain,
    query_weight,
    key_weight,
    value_weight,
    output_weight,
    feedforward_gain,
    gate_weight,
    up_weight,
    down_weight,
    out_grad,
):
    rows, width = hidden_in.shape
    shards = lax.axis_size("shard")
    replicas = lax.axis_size("replica")
    place = lax.axis_index("replica")
    depth = lax.axis_index("shard")
    core = place & 1
    chip = (place >> 1) & (CHIPS - 1)
    local = width // shards
    half = local // 2
    ff_local = down_weight.shape[0]
    group_shards = shards // CHIPS
    q_width = GROUP * HEAD
    qkv_width = q_width + 2 * HEAD
    index = jnp.stack([chip, core, depth]).astype(jnp.int32)

    gain_one = jnp.broadcast_to(attention_gain.astype(f32)[:, None], (local, LANES))
    gain_two = jnp.broadcast_to(feedforward_gain.astype(f32)[:, None], (local, LANES))

    x = own_first(index, (hidden_in,), local)[0]
    xs = [x, swap(x, 2)]

    at_block, out_block = attention_block(
        index, query_weight, key_weight, value_weight, output_weight, after(gain_one, x)
    )
    at_own = lax.all_gather(at_block, "shard", axis=0, tiled=True)
    out_all = lax.all_gather(out_block, "shard", axis=0, tiled=True)
    gu_block = feedforward_block(index, gate_weight, up_weight, after(gain_two, at_block), ff_local)
    gu_own = lax.all_gather(gu_block, "shard", axis=0, tiled=True)
    down_own = lax.all_gather(down_block(index, down_weight, local), "shard", axis=0, tiled=True)
    g = own_first(index, (after(out_grad, x),), local)[0]
    g_blocks = [g, swap(g, 2), swap(g, 4)]
    at_own = after(at_own, gu_block, xs[1], *g_blocks[1:])

    qkv_own = [at_own]
    qkv_own.append(swap(qkv_own[0], 4))
    qkv_other = [swap(qkv_own[0], 1)]
    inverse = rope_base ** (-jnp.arange(0, HEAD, 2, dtype=f32) / HEAD)
    places = (depth * rows + jnp.arange(rows, dtype=jnp.int32)).astype(f32)
    angles = inverse[:, None] * places[None, :]
    angles = jnp.concatenate([angles, angles], axis=0)
    cosine, sine = jnp.cos(angles), jnp.sin(angles)

    def shifted(kv):
        return [kv] + [shift(kv, d) for d in range(1, shards)]

    queries, kv, xhat = qkv_call(xs, qkv_own[0], qkv_other[0], cosine, sine)
    kvs = shifted(kv)
    qkv_own[1] = after(qkv_own[1], *kvs[1:])
    qkv_other.append(swap(qkv_own[1], 1))
    queries_two, kv_two = qkv_call(xhat, qkv_own[1], qkv_other[1], cosine, sine)
    kvs_two = shifted(kv_two)
    groups = [(queries, *attention_call(index, queries, kvs), kvs)]
    groups.append((queries_two, *attention_call(index, queries_two, kvs_two), kvs_two))
    attended = [group[2] for group in groups]
    groups = [(group[0], group[1], group[3], group[4]) for group in groups]

    out_all = after(out_all, qkv_own[1])
    x_place = chip & 1
    low_group = (chip >> 1) == 0
    pair_rows = PAIR * group_shards * half // 2

    def out_for(mask):
        return lax.dynamic_slice_in_dim(out_all, ((chip ^ mask) & 1) * pair_rows, pair_rows, 0)

    out_pieces = [out_for(0)] + [swap(out_for(m), 2 * m) for m in range(1, CHIPS)]
    wo_own = out_rows_call(index, [after(piece, *kvs_two[1:]) for piece in out_pieces])
    wo_other = swap(wo_own, 1)

    mid_terms = [(attended[n], wo_own, wo_other, n) for n in range(PAIR)]
    middle, two = middle_call(plane_send(parts_call(mid_terms, rows, False, "attention_out")), x)
    twos = plane_gather(two)

    gu_own = after(gu_own, *twos[1:])
    gu_other = swap(gu_own, 1)
    act, for_gate, for_up, two_all = gate_call(twos, gu_own, gu_other)
    g_blocks.append(after(swap(after(g, *twos[1:]), 6), act))
    g_all = jnp.concatenate(g_blocks, axis=0)

    def over_groups(kept):
        if replicas > PIECES:
            groups = [
                [e * PIECES + i for e in range(replicas // PIECES)] for i in range(PIECES)
            ]
            kept = lax.psum(kept, "replica", axis_index_groups=groups)
        return kept

    def reduced(term):
        kept = lax.psum_scatter(term, "shard", scatter_dimension=0, tiled=True)
        return over_groups(kept)

    def plane_pieces(kept):
        mine = plane_gather(kept)
        return mine, [swap(part, 1) for part in mine]

    def mixed(mine, theirs):
        return [part for pair in zip(mine, theirs) for part in pair]

    quarter = width // 4
    down_sent = [
        swap(term, 1) for term in weight_grad(act, None, g_all, 2, quarter, 2, (), "down_grad_other")
    ]
    down_terms = weight_grad(act, None, g_all, 0, quarter, 2, (down_sent,), "down_grad")
    down_kept = [reduced(term) for term in down_terms]
    down_own = after(down_own, *down_terms)
    down_other = swap(down_own, 1)

    grads = hidden_back_call(after(g_all, *down_terms), down_own, down_other, for_gate, for_up)
    e_terms = parts_call([(grads, gu_own, gu_other, 0)], rows, True, "feedforward_back")
    e_parts = plane_send(after(e_terms, down_kept[0]))
    grads_wide = grads.shape[1]
    gu_sent = weight_grad(
        after(two_all, e_terms[0], down_kept[0]), 1, grads, 0, grads_wide, 1, (), "gate_grad_other"
    )
    gu_sent = [swap(gu_sent[0], 1)]
    gu_term = weight_grad(
        after(two_all, *e_parts[1:]), 0, grads, 0, grads_wide, 1, (gu_sent,), "gate_grad"
    )[0]
    gu_kept = reduced(gu_term)

    middle_late = after(middle, gu_term, *down_kept)
    grad_middle, branch = grad_middle_call(e_parts, middle_late, g)
    branches = [branch, swap(branch, 2)]

    def back_block(m, block, before):
        return attention_back_call(index, m, block, wo_own, wo_other, cosine, sine, groups, before)

    before = back_block(0, branch, None)
    act_late = after(act, before[1])
    out_terms = parts_call([(act_late, down_own, down_other, 0)], rows, False, "feedforward_out")
    before = back_block(1, after(branches[1], out_terms[0]), before)
    out_parts = plane_send(after(out_terms, branches[1]))
    output = output_call(index, out_parts, middle, local)

    grad_qkv = []
    for grad_q, grad_first, grad_rest in (before[:3], before[3:]):
        rest = [shift(grad_rest[d - 1], -d) for d in range(1, shards)]
        grad_kv = grad_kv_call(grad_first, rest, cosine, sine)
        grad_qkv.append(jnp.concatenate([grad_q, grad_kv], axis=1))

    half_wide = width // 2
    branch_all = jnp.concatenate([after(block, before[1]) for block in branches], axis=0)
    both_attended = jnp.concatenate(attended, axis=1)
    wo_sent = weight_grad(both_attended, None, branch_all, 1, half_wide, 1, (), "out_grad_other")
    wo_sent = [swap(wo_sent[0], 1)]
    wo_term = weight_grad(both_attended, None, branch_all, 0, half_wide, 1, (wo_sent,), "out_grad")[0]
    wo_term = wo_term.reshape(PAIR, CHIPS, -1, half_wide)

    def wo_for(m):
        one, two = wo_term[0, m], wo_term[1, m ^ 2]
        return jnp.stack([jnp.where(low_group, one, two), jnp.where(low_group, two, one)])

    wo_chips = [wo_for(0)] + [swap(wo_for(m), 2 * m) for m in range(1, CHIPS)]
    wo_mine = wo_chips[0].astype(f32) + wo_chips[2].astype(f32)
    wo_theirs = wo_chips[1].astype(f32) + wo_chips[3].astype(f32)
    left_place = x_place == 0
    wo_block = jnp.stack(
        [jnp.where(left_place, wo_mine, wo_theirs), jnp.where(left_place, wo_theirs, wo_mine)]
    ).astype(bf16)
    wo_wide = wo_block.reshape(shards, half // 2, 2, 512).transpose(0, 2, 1, 3).reshape(-1, 512)

    def qkv_grad(n, side, added, name):
        return weight_grad(xhat, side, grad_qkv[n], 0, qkv_width, 1, added, name)

    qkv_sent = [[swap(qkv_grad(n, 1, (), "qkv_grad_other")[0], 1)] for n in (1, 0)]
    qkv_second = [swap(qkv_grad(1, 0, (qkv_sent[0],), "qkv_grad")[0], 4)]
    qkv_term = qkv_grad(0, 0, (qkv_sent[1], qkv_second), "qkv_grad")[0]
    at_kept = reduced(after(jnp.concatenate([qkv_term, wo_wide], axis=1), gu_kept))

    down_kept = after(jnp.concatenate(down_kept, axis=1), *branches)
    down_out = rows_result(index, mixed(*plane_pieces(down_kept)), local, "down_result")
    back_terms = [(grad_qkv[n], qkv_own[n], qkv_other[n], 0) for n in range(PAIR)]
    e_one = plane_send(parts_call(back_terms, rows, True, "qkv_back"))
    grad_input = grad_input_call(index, e_one, x, grad_middle, local)

    gu_mine, gu_theirs = plane_pieces(gu_kept)
    gu_out = feedforward_result(index, 0, gu_mine, gate_weight, up_weight, gain_two, ff_local, None)
    gu_out = feedforward_result(index, 1, gu_theirs, gate_weight, up_weight, gain_two, ff_local, gu_out)
    at_pieces = mixed(*plane_pieces(at_kept))
    wo_out = out_result(index, at_pieces, local, width, qkv_width)
    q_out, k_out, v_out, gain_one_sums = qkv_result(
        index, at_pieces, query_weight, key_weight, value_weight, gain_one
    )
    return (
        output,
        grad_input,
        jnp.sum(gain_one_sums, axis=1),
        q_out,
        k_out,
        v_out,
        wo_out,
        jnp.sum(gu_out[2], axis=1),
        gu_out[0],
        gu_out[1],
        down_out,
    )


def solution(mesh):
    return jax.shard_map(
        per_device,
        mesh=mesh,
        in_specs=(
            P(("replica", "shard"), None),
            P("shard"),
            P("shard", None),
            P("shard", None),
            P("shard", None),
            P("shard", None),
            P("shard"),
            P("shard", None),
            P("shard", None),
            P("shard", None),
            P(("replica", "shard"), None),
        ),
        out_specs=(
            P(("replica", "shard"), None),
            P(("replica", "shard"), None),
            P("shard"),
            P("shard", None),
            P("shard", None),
            P("shard", None),
            P("shard", None),
            P("shard"),
            P("shard", None),
            P("shard", None),
            P("shard", None),
        ),
        check_vma=False,
    )
```

```python
import functools

import jax
import jax.numpy as jnp
from jax import lax
from jax.experimental import pallas as pl
from jax.experimental.pallas import tpu as pltpu
from jax.sharding import PartitionSpec as P

HEADS = 32
KV_HEADS = 4
HEAD = 64
GROUP = HEADS // KV_HEADS
CHIPS = 4
PIECES = 2 * CHIPS
PAIR = 2
LANES = 128

norm_eps = 1e-05
rope_base = 10000.0
masked_score = -1e30

f32 = jnp.float32
bf16 = jnp.bfloat16
VMEM = pltpu.VMEM
NT = (((1,), (1,)), ((), ()))
TN = (((0,), (0,)), ((), ()))


def dot(left, right):
    return jnp.dot(left, right, preferred_element_type=f32)


def dot_nt(left, right):
    return lax.dot_general(left, right, NT, preferred_element_type=f32)


def dot_tn(left, right):
    return lax.dot_general(left, right, TN, preferred_element_type=f32)


def shape(dims, kind):
    return jax.ShapeDtypeStruct(dims, kind)


def whole():
    return pl.BlockSpec(memory_space=VMEM)


def kernel_call(body, out_shape, in_specs, out_specs, operands, *, index=None, grid=(), scratch=(),
                moved=0, aliases=None, name=None):
    params = pltpu.CompilerParams(
        vmem_limit_bytes=52 * 2**20, dimension_semantics=("arbitrary",) * len(grid)
    )
    cost = pl.CostEstimate(flops=0, bytes_accessed=int(moved), transcendentals=0)
    common = dict(
        out_shape=out_shape,
        compiler_params=params,
        cost_estimate=cost,
        input_output_aliases=aliases or {},
        name=name,
    )
    if index is None:
        spec = pl.GridSpec(grid=grid, in_specs=in_specs, out_specs=out_specs, scratch_shapes=scratch)
        return pl.pallas_call(body, grid_spec=spec, **common)(*operands)
    spec = pltpu.PrefetchScalarGridSpec(
        num_scalar_prefetch=1, grid=grid, in_specs=in_specs, out_specs=out_specs,
        scratch_shapes=scratch,
    )
    return pl.pallas_call(body, grid_spec=spec, **common)(index, *operands)


def swap(value, mask):
    size = lax.axis_size("replica")
    return lax.ppermute(value, "replica", [(i, i ^ mask) for i in range(size)])


def shift(value, step):
    size = lax.axis_size("shard")
    pairs = [(i, i + step) for i in range(size) if 0 <= i + step < size]
    return lax.ppermute(value, "shard", pairs)


def plane_gather(value):
    return [value] + [swap(value, 2 * m) for m in range(1, CHIPS)]


def plane_gather_forward(value):
    middle = value.shape[0] // 2
    across, along = swap(value, 2), swap(value, 4)
    return [value, across, along, swap(across[:middle], 4), swap(along[middle:], 2)]


def plane_send(parts):
    return [parts[0]] + [swap(parts[m], 2 * m) for m in range(1, len(parts))]


def group_of(chip):
    return 2 * (chip & 1) + (chip >> 1)


def after(value, *others):
    return lax.optimization_barrier((value, *others))[0]


def attention_block_body(local, group_shards, index, q, k, v, o, gain, out, wo_out):
    scale = gain[:, :1]
    q_width = GROUP * HEAD
    cut = local // CHIPS
    for chip in range(CHIPS):

        group = group_of(chip)

        @pl.when(index[0] == chip)
        def _(group=group):
            parts = []
            for m in range(CHIPS):
                for s in range(group_shards):
                    start = group * q_width + s * local + (m ^ chip) * cut
                    parts.append(q[:, start : start + cut])
            parts.append(k[:, group * HEAD : (group + 1) * HEAD])
            parts.append(v[:, group * HEAD : (group + 1) * HEAD])
            wide = jnp.concatenate([part.astype(f32) for part in parts], axis=1)
            out[...] = (wide * scale).astype(bf16)

    half = local // 2
    shards = o.shape[1] // local
    for core in range(2):

        @pl.when(index[1] == core)
        def _():
            for s in range(shards):
                piece = o[:, s * local + core * half : s * local + (core + 1) * half]
                wo_out[:, s * half : (s + 1) * half] = piece


def attention_block(index, query, key, value, output, gain):
    local, width = query.shape
    half = local // 2
    shards = width // local
    return kernel_call(
        functools.partial(attention_block_body, local, shards // CHIPS),
        (
            shape((half, GROUP * HEAD + 2 * HEAD), bf16),
            shape((local // CHIPS, width // 2), bf16),
        ),
        [
            pl.BlockSpec((half, width), lambda i, n: (n[1], 0)),
            pl.BlockSpec((half, key.shape[1]), lambda i, n: (n[1], 0)),
            pl.BlockSpec((half, key.shape[1]), lambda i, n: (n[1], 0)),
            pl.BlockSpec((local // CHIPS, width), lambda i, n: (n[0], 0)),
            pl.BlockSpec((half, LANES), lambda i, n: (n[1], 0)),
        ],
        (
            pl.BlockSpec((half, GROUP * HEAD + 2 * HEAD), lambda i, n: (0, 0)),
            pl.BlockSpec((local // CHIPS, width // 2), lambda i, n: (0, 0)),
        ),
        (query, key, value, output, gain),
        index=index,
        grid=(1,),
        name="attention_block",
    )


def feedforward_block_body(ff_local, cut, index, gate, up, gain, out):
    scale = gain[:, :1]
    shards = gate.shape[1] // ff_local
    width = shards * cut
    for chip in range(CHIPS):

        @pl.when(index[0] == chip)
        def _():
            for n, source in enumerate((gate, up)):
                parts = [
                    source[:, s * ff_local + chip * cut : s * ff_local + (chip + 1) * cut].astype(f32)
                    for s in range(shards)
                ]
                wide = jnp.concatenate(parts, axis=1)
                out[:, n * width : (n + 1) * width] = (wide * scale).astype(bf16)


def feedforward_block(index, gate, up, gain, ff_local):
    local, ff = gate.shape
    half = local // 2
    rows = 64
    steps = half // rows
    cut = ff_local // CHIPS
    width = 2 * (ff // CHIPS)
    return kernel_call(
        functools.partial(feedforward_block_body, ff_local, cut),
        shape((half, width), bf16),
        [
            pl.BlockSpec((rows, ff), lambda i, n: (n[1] * steps + i, 0)),
            pl.BlockSpec((rows, ff), lambda i, n: (n[1] * steps + i, 0)),
            pl.BlockSpec((rows, LANES), lambda i, n: (n[1] * steps + i, 0)),
        ],
        pl.BlockSpec((rows, width), lambda i, n: (i, 0)),
        (gate, up, gain),
        index=index,
        grid=(steps,),
        name="feedforward_block",
    )


def own_first_body(local, index, *refs):
    count = len(refs) // 2
    half = local // 2
    for core in range(2):

        @pl.when(index[1] == core)
        def _():
            for source, out in zip(refs[:count], refs[count:]):
                shards = source.shape[1] // local
                sides = out.shape[1] // (shards * half)
                for side in range(sides):
                    for s in range(shards):
                        start = s * local + (core ^ side) * half
                        spot = (side * shards + s) * half
                        out[:, spot : spot + half] = source[:, start : start + half]


def own_first(index, sources, local, halves=2):
    return kernel_call(
        functools.partial(own_first_body, local),
        tuple(shape((v.shape[0], v.shape[1] * halves // 2), bf16) for v in sources),
        [pl.BlockSpec(v.shape, lambda i, n: (0, 0)) for v in sources],
        tuple(
            pl.BlockSpec((v.shape[0], v.shape[1] * halves // 2), lambda i, n: (0, 0)) for v in sources
        ),
        tuple(sources),
        index=index,
        grid=(1,),
        name="own_first",
    )


def down_block_body(local, index, source, out):
    own_first_body(local, index, source, out)


def down_block(index, down, local):
    ff_local, width = down.shape
    cut = ff_local // CHIPS
    return kernel_call(
        functools.partial(down_block_body, local),
        shape((cut, width // 2), bf16),
        [pl.BlockSpec((cut, width), lambda i, n: (n[0], 0))],
        pl.BlockSpec((cut, width // 2), lambda i, n: (0, 0)),
        (down,),
        index=index,
        grid=(1,),
        name="down_block",
    )


def part_sum(parts):
    total = parts[0][...]
    for part in parts[1:]:
        total = total + part[...].astype(f32)
    return total


def mean_of(values):
    return jnp.mean(values, axis=1, keepdims=True)


def middle_body(*refs):
    parts, (x, middle, two) = refs[:PAIR], refs[PAIR:]
    total = x[...].astype(f32) + part_sum(parts)
    middle[...] = total
    two[...] = (total * lax.rsqrt(mean_of(total * total) + norm_eps)).astype(bf16)


def middle_call(parts, x):
    return kernel_call(
        middle_body,
        (shape(x.shape, f32), shape(x.shape, bf16)),
        [whole()] * (PAIR + 1),
        (whole(), whole()),
        (*parts, x),
        name="middle",
    )


def norm_back(e, values):
    inverse = lax.rsqrt(mean_of(values * values) + norm_eps)
    return inverse * e - values * (inverse * inverse * inverse) * mean_of(e * values)


def grad_middle_body(*refs):
    parts, (middle, g, grad, low) = refs[:CHIPS], refs[CHIPS:]
    total = g[...].astype(f32) + norm_back(part_sum(parts), middle[...])
    grad[...] = total
    low[...] = total.astype(bf16)


def grad_middle_call(parts, middle, g):
    return kernel_call(
        grad_middle_body,
        (shape(g.shape, f32), shape(g.shape, bf16)),
        [whole()] * (CHIPS + 2),
        (whole(), whole()),
        (*parts, middle, g),
        name="grad_middle",
    )


def store_in_order(local, index, value, out):
    half = local // 2
    shards = out.shape[1] // local
    for core in range(2):

        @pl.when(index[1] == core)
        def _():
            for side in range(2):
                for s in range(shards):
                    spot = s * local + (core ^ side) * half
                    start = (side * shards + s) * half
                    out[:, spot : spot + half] = value[:, start : start + half].astype(bf16)


def output_body(local, index, *refs):
    parts, (middle, out) = refs[:CHIPS], refs[CHIPS:]
    store_in_order(local, index, middle[...] + part_sum(parts), out)


def output_call(index, parts, middle, local):
    spec = pl.BlockSpec(middle.shape, lambda i, n: (0, 0))
    return kernel_call(
        functools.partial(output_body, local),
        shape(middle.shape, bf16),
        [spec] * (CHIPS + 1),
        spec,
        (*parts, middle),
        index=index,
        grid=(1,),
        name="output",
    )


def grad_input_body(local, index, *refs):
    parts, (x, grad, out) = refs[:PAIR], refs[PAIR:]
    total = grad[...] + norm_back(part_sum(parts), x[...].astype(f32))
    store_in_order(local, index, total, out)


def grad_input_call(index, parts, x, grad, local):
    spec = pl.BlockSpec(x.shape, lambda i, n: (0, 0))
    return kernel_call(
        functools.partial(grad_input_body, local),
        shape(x.shape, bf16),
        [spec] * (PAIR + 2),
        spec,
        (*parts, x, grad),
        index=index,
        grid=(1,),
        name="grad_input",
    )


def grad_qkv_body(shards, grad_q, first, *refs):
    rest, (cosine, sine), outs = refs[: shards - 1], refs[shards - 1 : shards + 1], refs[shards + 1 :]
    total = first[...]
    for term in rest:
        total = total + term[...].astype(f32)
    rows = cosine.shape[1]
    width = GROUP * HEAD
    cos, sin = cosine[...], sine[...]
    for n, out in enumerate(outs):
        out[:, :width] = grad_q[:, n * width : (n + 1) * width]
        for m in range(PAIR):
            span = slice(m * rows, (m + 1) * rows)
            turned = total[span, n * 2 * HEAD : (n + 1) * 2 * HEAD].T
            k = turned[:HEAD]
            k = k * cos - half_rotated(k) * sin
            both = jnp.concatenate([k, turned[HEAD:]], axis=0)
            out[span, width:] = both.T.astype(bf16)


def grad_qkv_call(grad_q, first, rest, cosine, sine):
    tokens = grad_q.shape[0]
    return kernel_call(
        functools.partial(grad_qkv_body, len(rest) + 1),
        (shape((tokens, GROUP * HEAD + 2 * HEAD), bf16),) * PAIR,
        [whole()] * (len(rest) + 4),
        (whole(),) * PAIR,
        (grad_q, first, *rest, cosine, sine),
        name="grad_qkv",
    )


def out_sends_body(index, term, *outs):
    cut = outs[0].shape[0] // PAIR
    for row in range(2):

        @pl.when(index[0] >> 1 == row)
        def _():
            for n in range(PAIR):
                for m in range(CHIPS):
                    spot = (n * CHIPS + m) * cut
                    start = (n ^ row) * cut
                    outs[m ^ (2 * n)][start : start + cut, :] = term[spot : spot + cut, :]


def out_sends(index, term):
    rows, width = term.shape
    rows //= CHIPS
    return kernel_call(
        out_sends_body,
        (shape((rows, width), bf16),) * CHIPS,
        [pl.BlockSpec(term.shape, lambda i, n: (0, 0))],
        (pl.BlockSpec((rows, width), lambda i, n: (0, 0)),) * CHIPS,
        (term,),
        index=index,
        grid=(1,),
        name="out_sends",
    )


def out_block_body(shards, index, *refs):
    parts, out = refs[:CHIPS], refs[CHIPS]
    group_shards = shards // CHIPS
    cut = parts[0].shape[0] // (PAIR * group_shards)
    sums = [parts[m][...].astype(f32) + parts[m + 2][...].astype(f32) for m in range(2)]
    for side in range(2):

        @pl.when(index[0] & 1 == side)
        def _():
            for m in range(2):
                for n in range(PAIR * group_shards):
                    shard = (m ^ side) * PAIR * group_shards + n
                    rows = sums[m][n * cut : (n + 1) * cut].astype(bf16)
                    out[2 * shard * cut : (2 * shard + 1) * cut, :] = rows[:, :512]
                    out[(2 * shard + 1) * cut : (2 * shard + 2) * cut, :] = rows[:, 512:]


def out_block_call(index, parts, shards):
    rows, width = parts[0].shape
    return kernel_call(
        functools.partial(out_block_body, shards),
        shape((2 * PAIR * rows, width // 2), bf16),
        [pl.BlockSpec((rows, width), lambda i, n: (0, 0))] * CHIPS,
        pl.BlockSpec((2 * PAIR * rows, width // 2), lambda i, n: (0, 0)),
        tuple(parts),
        index=index,
        grid=(1,),
        name="out_block",
    )


def half_rotated(values):
    middle = values.shape[0] // 2
    return jnp.concatenate([-values[middle:], values[:middle]], axis=0)


def qkv_body(make, *refs):
    if make:
        xs, (own, other, cosine, sine, queries, kv, xhat) = refs[:PAIR], refs[PAIR:]
        rows, width = xs[0].shape
        for m in range(PAIR):
            x = xs[m][...].astype(f32)
            inverse = lax.rsqrt(mean_of(x * x) + norm_eps)
            xhat[m * rows : (m + 1) * rows, :] = (x * inverse).astype(bf16)
    else:
        xhat, own, other, cosine, sine, queries, kv = refs
        rows, width = cosine.shape[1], xhat.shape[1]
    cos, sin = cosine[...], sine[...]
    total = dot(xhat[:, : width // 2], own[...]) + dot(xhat[:, width // 2 :], other[...])
    for m in range(PAIR):
        turned = total[m * rows : (m + 1) * rows].T
        for h in range(GROUP + 1):
            u = turned[h * HEAD : (h + 1) * HEAD]
            u = u * cos + half_rotated(u) * sin
            if h < GROUP:
                queries[m, :, h * rows : (h + 1) * rows] = (u * HEAD ** (-0.5)).astype(bf16)
            else:
                both = jnp.concatenate([u, turned[(h + 1) * HEAD :]], axis=0)
                kv[m * rows : (m + 1) * rows, :] = both.T.astype(bf16)


def qkv_call(xs, own, other, cosine, sine):
    make = isinstance(xs, list)
    rows = cosine.shape[1]
    tokens = PAIR * rows
    outs = (shape((PAIR, HEAD, GROUP * rows), bf16), shape((tokens, 2 * HEAD), bf16))
    if make:
        outs = outs + (shape((tokens, xs[0].shape[1]), bf16),)
    operands = (*(xs if make else (xs,)), own, other, cosine, sine)
    return kernel_call(
        functools.partial(qkv_body, make),
        outs,
        [whole()] * len(operands),
        tuple(whole() for _ in outs),
        operands,
        name="qkv",
    )


def out_rows_body(index, *refs):
    pieces, out = refs[:CHIPS], refs[CHIPS]
    cut = pieces[0].shape[0] // PAIR
    for row in range(2):

        @pl.when(index[0] >> 1 == row)
        def _():
            for n in range(PAIR):
                for m in range(CHIPS):
                    spot = (n * CHIPS + m) * cut
                    start = (n ^ row) * cut
                    out[spot : spot + cut, :] = pieces[m ^ (2 * n)][start : start + cut, :]


def out_rows_call(index, pieces):
    rows, width = pieces[0].shape
    return kernel_call(
        out_rows_body,
        shape((CHIPS * rows, width), bf16),
        [pl.BlockSpec((rows, width), lambda i, n: (0, 0))] * CHIPS,
        pl.BlockSpec((CHIPS * rows, width), lambda i, n: (0, 0)),
        tuple(pieces),
        index=index,
        grid=(1,),
        name="out_rows",
    )


LANE_HEADS = 4


def own_block_bias(rows):
    key = lax.broadcasted_iota(jnp.int32, (rows, rows), 0)
    mine = lax.broadcasted_iota(jnp.int32, (rows, rows), 1)
    return jnp.where(key <= mine, 0.0, masked_score)


def set_bias(bias):
    rows = bias.shape[0]
    value = own_block_bias(rows)
    for h in range(LANE_HEADS):
        bias[:, h * rows : (h + 1) * rows] = value


def far_bias(depth, d):
    return jnp.where(d <= depth, 0.0, masked_score) if d else 0.0


def attention_body(shards, index, queries, *refs):
    kvs = refs[:shards]
    turned_out, out, stats, bias, terms, out_turned = refs[shards:]
    rows = bias.shape[0]
    wide = LANE_HEADS * rows

    @pl.when(pl.program_id(0) == 0)
    def _():
        set_bias(bias)

    ks = [kv[:, :HEAD] for kv in kvs]
    v_turned = jnp.concatenate([kv[...] for kv in kvs], axis=0).astype(f32).T[HEAD:].astype(bf16)
    for n in range(GROUP // LANE_HEADS):
        span = slice(n * wide, (n + 1) * wide)
        q = queries[0, :, span]
        scores, top = [], None
        for d in range(shards):
            score = dot(ks[d], q)
            if d == 0:
                score = score + bias[...]
            scores.append(score)
            highest = jnp.max(score, axis=0, keepdims=True) + far_bias(index[2], d)
            top = highest if top is None else jnp.maximum(top, highest)
        total = None
        for d in range(shards):
            term = jnp.exp(scores[d] - (top - far_bias(index[2], d)))
            part = jnp.sum(term, axis=0, keepdims=True)
            total = part if total is None else total + part
            terms[d * rows : (d + 1) * rows, :] = term.astype(bf16)
        out_turned[:, span] = dot(v_turned, terms[...]) / total
        stats[0, :, span] = top + jnp.log(total)
    turned_out[0] = out_turned[...].astype(bf16)
    straight = out_turned[...].T
    for h in range(GROUP):
        out[:, h * HEAD : (h + 1) * HEAD] = straight[h * rows : (h + 1) * rows].astype(bf16)


def attention_call(index, queries, kvs):
    chips, _, wide = queries.shape
    rows = wide // GROUP
    shards = len(kvs)
    keys = shards * rows
    block = pl.BlockSpec((1, HEAD, wide), lambda i, n: (i, 0, 0))
    return kernel_call(
        functools.partial(attention_body, shards),
        (
            shape((chips, HEAD, wide), bf16),
            shape((chips * rows, GROUP * HEAD), bf16),
            shape((chips, 1, wide), f32),
        ),
        [block] + [pl.BlockSpec((rows, 2 * HEAD), lambda i, n: (i, 0))] * shards,
        (
            block,
            pl.BlockSpec((rows, GROUP * HEAD), lambda i, n: (i, 0)),
            pl.BlockSpec((1, 1, wide), lambda i, n: (i, 0, 0)),
        ),
        (queries, *kvs),
        index=index,
        grid=(chips,),
        scratch=(
            VMEM((rows, LANE_HEADS * rows), f32),
            VMEM((keys, LANE_HEADS * rows), bf16),
            VMEM((HEAD, wide), f32),
        ),
        name="attention",
    )


def attention_back_body(shards, index, branch, wo_own, wo_other, cosine, sine, *refs):
    per_group = 3 + shards
    inputs = [refs[n * per_group : (n + 1) * per_group] for n in range(PAIR)]
    grad_q, grad_first, grad_rest = refs[-7:-4]
    bias, probs_low, grads_low, grad_lanes = refs[-4:]
    rows = bias.shape[0]
    wide = LANE_HEADS * rows
    width = branch.shape[1]
    set_bias(bias)
    cos, sin = cosine[...], sine[...]
    for n, (queries, turned_out, stats, *kvs) in enumerate(inputs):
        heads = slice(n * GROUP * HEAD, (n + 1) * GROUP * HEAD)
        grad_out = dot_nt(wo_own[heads, :], branch[:, : width // 2])
        grad_out = grad_out + dot_nt(wo_other[heads, :], branch[:, width // 2 :])
        for h in range(GROUP):
            grad_lanes[:, h * rows : (h + 1) * rows] = grad_out[h * HEAD : (h + 1) * HEAD].astype(bf16)
        ks = [kv[:, :HEAD] for kv in kvs]
        vs = [kv[:, HEAD:] for kv in kvs]
        k_turned = jnp.concatenate([kv[...] for kv in kvs], axis=0).astype(f32).T[:HEAD].astype(bf16)
        k_total, v_total, parts = None, None, []
        for c in range(GROUP // LANE_HEADS):
            span = slice(c * wide, (c + 1) * wide)
            q, mine = queries[0, :, span], grad_lanes[:, span]
            delta = jnp.sum(
                mine.astype(f32) * turned_out[0, :, span].astype(f32), axis=0, keepdims=True
            )
            for d in range(shards):
                score = dot(ks[d], q)
                if d == 0:
                    score = score + bias[...]
                probs = jnp.exp(score - (stats[0, :, span] - far_bias(index[2], d)))
                grad_scores = probs * (dot(vs[d], mine) - delta)
                probs_low[d * rows : (d + 1) * rows, :] = probs.astype(bf16)
                grads_low[d * rows : (d + 1) * rows, :] = grad_scores.astype(bf16)
            u = dot(k_turned, grads_low[...]) * HEAD ** (-0.5)
            parts.append(u * cos - half_rotated(u) * sin)
            k_term = dot_nt(grads_low[...], q)
            v_term = dot_nt(probs_low[...], mine)
            k_total = k_term if k_total is None else k_total + k_term
            v_total = v_term if v_total is None else v_total + v_term
        straight = jnp.concatenate(parts, axis=1).T
        for h in range(GROUP):
            spot = (n * GROUP + h) * HEAD
            grad_q[:, spot : spot + HEAD] = straight[h * rows : (h + 1) * rows].astype(bf16)
        both = jnp.concatenate([k_total, v_total], axis=1)
        spot = slice(n * 2 * HEAD, (n + 1) * 2 * HEAD)
        grad_first[:, spot] = both[:rows, :]
        for d in range(1, shards):
            grad_rest[d - 1, :, spot] = both[d * rows : (d + 1) * rows, :].astype(bf16)


def attention_back_call(index, m, branch, wo_own, wo_other, cosine, sine, groups, before):
    chips, _, wide = groups[0][0].shape
    rows = wide // GROUP
    shards = len(groups[0][3])
    keys = shards * rows
    tokens = chips * rows
    block = pl.BlockSpec((1, HEAD, wide), lambda i, n: (m, 0, 0))
    in_specs = [whole()] * 5
    operands = [branch, wo_own, wo_other, jnp.tile(cosine, (1, LANE_HEADS)), jnp.tile(sine, (1, LANE_HEADS))]
    for queries, turned, stats, kvs in groups:
        in_specs += [block, block, pl.BlockSpec((1, 1, wide), lambda i, n: (m, 0, 0))]
        in_specs += [pl.BlockSpec((rows, 2 * HEAD), lambda i, n: (m, 0))] * shards
        operands += [queries, turned, stats, *kvs]
    aliases = {}
    if before is not None:
        aliases = {1 + len(operands) + n: n for n in range(3)}
        in_specs += [pl.BlockSpec(memory_space=pl.ANY)] * 3
        operands += list(before)
    outs = (
        shape((tokens, PAIR * GROUP * HEAD), bf16),
        shape((tokens, PAIR * 2 * HEAD), f32),
        shape((shards - 1, tokens, PAIR * 2 * HEAD), bf16),
    )
    out_specs = (
        pl.BlockSpec((rows, PAIR * GROUP * HEAD), lambda i, n: (m, 0)),
        pl.BlockSpec((rows, PAIR * 2 * HEAD), lambda i, n: (m, 0)),
        pl.BlockSpec((shards - 1, rows, PAIR * 2 * HEAD), lambda i, n: (0, m, 0)),
    )
    return kernel_call(
        functools.partial(attention_back_body, shards),
        outs,
        in_specs,
        out_specs,
        tuple(operands),
        index=index,
        grid=(1,),
        scratch=(
            VMEM((rows, LANE_HEADS * rows), f32),
            VMEM((keys, LANE_HEADS * rows), bf16),
            VMEM((keys, LANE_HEADS * rows), bf16),
            VMEM((HEAD, wide), bf16),
        ),
        aliases=aliases,
        name="attention_back",
    )


def parts_body(steps, transposed, count, *refs):
    lefts, owns, others = refs[:count], refs[count : 2 * count], refs[2 * count : 3 * count]
    outs = refs[3 * count :]
    rows = outs[0].shape[0]
    step = pl.program_id(0)

    def run(weights):
        total = None
        for left, weight in zip(lefts, weights):
            term = (dot_nt if transposed else dot)(left[...], weight[...])
            total = term if total is None else total + term
        for m, out in enumerate(outs):
            out[...] = total[m * rows : (m + 1) * rows, :].astype(out.dtype)

    @pl.when(step < steps)
    def _():
        run(owns)

    @pl.when(step >= steps)
    def _():
        run(others)


def parts_call(terms, rows, transposed, name):
    tokens = terms[0][0].shape[0]
    half = terms[0][1].shape[0] if transposed else terms[0][1].shape[1]
    tile = 256
    steps = half // tile
    last = steps - 1
    specs = [pl.BlockSpec((tokens, term[0].shape[1]), lambda j: (0, 0)) for term in terms]
    for side in range(2):
        for left, _, _, spot in terms:
            depth = left.shape[1]

            def place(side, spot, j):
                step = jnp.maximum(j - steps, 0) if side else jnp.minimum(j, last)
                return (step, spot) if transposed else (spot, step)

            block = (tile, depth) if transposed else (depth, tile)
            specs.append(pl.BlockSpec(block, functools.partial(place, side, spot)))
    count = tokens // rows
    return kernel_call(
        functools.partial(parts_body, steps, transposed, len(terms)),
        tuple(shape((rows, 2 * half), f32 if m == 0 else bf16) for m in range(count)),
        specs,
        tuple(pl.BlockSpec((rows, tile), lambda j: (0, j)) for _ in range(count)),
        (*(term[0] for term in terms), *(term[1] for term in terms), *(term[2] for term in terms)),
        grid=(2 * steps,),
        name=name,
    )


def gate_body(count, *refs):
    twos = refs[:count]
    gate_own, up_own, gate_other, up_other, act, for_gate, for_up, two_all = refs[count:]
    half = two_all.shape[1] // 2

    @pl.when(pl.program_id(0) == 0)
    def _():
        start = 0
        for two in twos:
            two_all[start : start + two.shape[0], :] = two[...]
            start += two.shape[0]

    own = jnp.concatenate([gate_own[...], up_own[...]], axis=1)
    other = jnp.concatenate([gate_other[...], up_other[...]], axis=1)
    both = dot(two_all[:, :half], own) + dot(two_all[:, half:], other)
    wide = gate_own.shape[1]
    gate, up = both[:, :wide], both[:, wide:]
    sig = 1.0 / (1.0 + jnp.exp(-gate))
    silu = gate * sig
    act[...] = (silu * up).astype(bf16)
    for_gate[...] = (up * sig * (1.0 + gate * (1.0 - sig))).astype(bf16)
    for_up[...] = silu.astype(bf16)


def gate_call(twos, own, other):
    rows, width = twos[0].shape
    tokens = CHIPS * rows
    half = width // 2
    ff = own.shape[1] // 2
    tile = LANES
    steps = ff // tile
    weight = [
        pl.BlockSpec((half, tile), lambda j: (0, j)),
        pl.BlockSpec((half, tile), lambda j: (0, j + steps)),
    ]
    column = pl.BlockSpec((tokens, tile), lambda j: (0, j))
    return kernel_call(
        functools.partial(gate_body, len(twos)),
        tuple(shape((tokens, ff), bf16) for _ in range(3)) + (shape((tokens, width), bf16),),
        [pl.BlockSpec(two.shape, lambda j: (0, 0)) for two in twos] + weight + weight,
        (column, column, column, pl.BlockSpec((tokens, width), lambda j: (0, 0))),
        (*twos, own, own, other, other),
        grid=(steps,),
        name="gate",
    )


def hidden_back_body(g, own, other, for_gate, for_up, grads):
    half = g.shape[1] // 2
    ff = own.shape[0]
    hidden = dot_nt(g[:, :half], own[...]) + dot_nt(g[:, half:], other[...])
    grads[:, :ff] = (hidden * for_gate[...].astype(f32)).astype(bf16)
    grads[:, ff:] = (hidden * for_up[...].astype(f32)).astype(bf16)


def hidden_back_call(g, own, other, for_gate, for_up):
    tokens, width = g.shape
    ff, half = own.shape
    block = tokens // 2
    row = lambda i: (i, 0)
    fixed = lambda i: (0, 0)
    return kernel_call(
        hidden_back_body,
        shape((tokens, 2 * ff), bf16),
        [
            pl.BlockSpec((block, width), row),
            pl.BlockSpec((ff, half), fixed),
            pl.BlockSpec((ff, half), fixed),
            pl.BlockSpec((block, ff), row),
            pl.BlockSpec((block, ff), row),
        ],
        pl.BlockSpec((block, 2 * ff), row),
        (g, own, other, for_gate, for_up),
        grid=(2,),
        name="hidden_back",
    )


def weight_grad_body(per, outputs, adds, left, right, *refs):
    added = [refs[n * outputs : (n + 1) * outputs] for n in range(adds)]
    outs, turned = refs[adds * outputs : -1], refs[-1]
    step = pl.program_id(0)

    @pl.when(step == 0)
    def _():
        turned[...] = left[...].T

    for n in range(outputs):

        @pl.when(step // per == n)
        def _(n=n):
            total = dot(turned[...], right[...])
            for terms in added:
                total = total + terms[n][...].astype(f32)
            outs[n][...] = total.astype(bf16)


def weight_grad(left, left_side, right, place, width, outputs, added, name):
    tokens = left.shape[0]
    rows = left.shape[1] // (1 if left_side is None else 2)
    tile = 256 if width % 256 == 0 else width
    per = width // tile
    first = place * width // tile
    side = left_side or 0

    def spot(n, j):
        return (0, jnp.clip(j - n * per, 0, per - 1))

    tiles = [pl.BlockSpec((rows, tile), functools.partial(spot, n)) for n in range(outputs)]
    return kernel_call(
        functools.partial(weight_grad_body, per, outputs, len(added)),
        tuple(shape((rows, width), bf16) for _ in range(outputs)),
        [
            pl.BlockSpec((tokens, rows), lambda j: (0, side)),
            pl.BlockSpec((tokens, tile), lambda j: (0, first + j)),
        ]
        + tiles * len(added),
        tuple(tiles),
        (left, right, *(term for terms in added for term in terms)),
        grid=(per * outputs,),
        scratch=(VMEM((rows, tokens), bf16),),
        name=name,
    )


def rows_result_body(local, index, *refs):
    pieces, out = refs[:PIECES], refs[PIECES]
    half = local // 2
    shards = out.shape[1] // local
    for m in range(CHIPS):
        for core in range(2):

            @pl.when((pl.program_id(0) == m) & (index[1] == core))
            def _():
                for side in range(2):
                    piece = pieces[2 * m + side]
                    for s in range(shards):
                        spot = s * local + (core ^ side) * half
                        out[:, spot : spot + half] = piece[:, s * half : (s + 1) * half].astype(f32)


def rows_result(index, pieces, local, name):
    cut, half_width = pieces[0].shape
    return kernel_call(
        functools.partial(rows_result_body, local),
        shape((CHIPS * cut, 2 * half_width), f32),
        [pl.BlockSpec((cut, half_width), lambda i, n: (0, 0))] * PIECES,
        pl.BlockSpec((cut, 2 * half_width), lambda i, n: (n[0] ^ i, 0)),
        tuple(pieces),
        index=index,
        grid=(CHIPS,),
        name=name,
    )


def out_result_body(local, base, index, *refs):
    pieces, out = refs[:PIECES], refs[PIECES]
    half = local // 2
    cut = local // CHIPS
    shards = out.shape[1] // local
    for m in range(CHIPS):
        for core in range(2):

            @pl.when((pl.program_id(0) == m) & (index[1] == core))
            def _():
                for side in range(2):
                    piece = pieces[2 * m + side]
                    for s in range(shards):
                        spot = s * local + (core ^ side) * half
                        row, column = (0, s * half) if s * half < 512 else (cut, s * half - 512)
                        column += base
                        out[:, spot : spot + half] = piece[row : row + cut, column : column + half].astype(f32)


def out_result(index, pieces, local, width, base):
    cut = local // CHIPS
    return kernel_call(
        functools.partial(out_result_body, local, base),
        shape((local, width), f32),
        [pl.BlockSpec(pieces[0].shape, lambda i, n: (0, 0))] * PIECES,
        pl.BlockSpec((cut, width), lambda i, n: (n[0] ^ i, 0)),
        tuple(pieces),
        index=index,
        grid=(CHIPS,),
        name="out_result",
    )


def lane_sum(value):
    total = value[:, :LANES]
    for n in range(1, value.shape[1] // LANES):
        total = total + value[:, n * LANES : (n + 1) * LANES]
    return total


def feedforward_result_body(ff_local, cut, index, *refs):
    pieces = refs[:CHIPS]
    gate_weight, up_weight, gain = refs[CHIPS : CHIPS + 3]
    gate_out, up_out, gain_out = refs[-3:]
    shards = gate_weight.shape[1] // ff_local
    width = shards * cut
    for chip in range(CHIPS):

        @pl.when(index[0] == chip)
        def _():
            @pl.loop(0, gate_out.shape[0] // 16)
            def _(n):
                rows = pl.ds(pl.multiple_of(n * 16, 16), 16)
                scale = gain[rows, :1]
                total = jnp.zeros((16, LANES), f32)
                for base, weight, out in ((0, gate_weight, gate_out), (width, up_weight, up_out)):
                    parts = []
                    for s in range(shards):
                        for owner in range(CHIPS):
                            start = base + s * cut
                            parts.append(pieces[owner ^ chip][rows, start : start + cut].astype(f32))
                    wide = jnp.concatenate(parts, axis=1)
                    total = total + lane_sum(wide * weight[rows, :].astype(f32))
                    out[rows, :] = wide * scale
                gain_out[rows, :] = total


def feedforward_result(index, side, pieces, gate_weight, up_weight, gain, ff_local, before):
    local, ff = gate_weight.shape
    half = local // 2
    rows = 64
    steps = half // rows
    row = lambda i, n: ((n[1] ^ side) * steps + i, 0)
    in_specs = [pl.BlockSpec((rows, pieces[0].shape[1]), lambda i, n: (i, 0))] * CHIPS
    in_specs += [pl.BlockSpec((rows, ff), row)] * 2 + [pl.BlockSpec((rows, LANES), row)]
    operands = (*pieces, gate_weight, up_weight, gain)
    aliases = {}
    if before is not None:
        aliases = {1 + len(operands) + n: n for n in range(3)}
        in_specs = in_specs + [pl.BlockSpec(memory_space=pl.ANY)] * 3
        operands = operands + tuple(before)
    return kernel_call(
        functools.partial(feedforward_result_body, ff_local, ff_local // CHIPS),
        (shape((local, ff), f32), shape((local, ff), f32), shape((local, LANES), f32)),
        in_specs,
        (pl.BlockSpec((rows, ff), row), pl.BlockSpec((rows, ff), row), pl.BlockSpec((rows, LANES), row)),
        operands,
        index=index,
        grid=(steps,),
        aliases=aliases,
        name="feedforward_result",
    )


def qkv_result_body(local, group_shards, index, *refs):
    pieces = refs[:PIECES]
    weights, gain = refs[PIECES : PIECES + 3], refs[PIECES + 3]
    outs, gain_out = refs[PIECES + 4 : PIECES + 7], refs[PIECES + 7]
    q_width = GROUP * HEAD
    cut = local // CHIPS
    scale = gain[:, :1]
    for chip in range(CHIPS):
        for side in range(2):

            @pl.when((index[0] == chip) & (pl.program_id(0) == side))
            def _():
                parts, k_parts, v_parts = [], [], []
                for group in range(CHIPS):
                    owner = (group >> 1) + 2 * (group & 1)
                    piece = pieces[2 * (owner ^ chip) + side]
                    for s in range(group_shards):
                        for j in range(CHIPS):
                            start = ((j ^ owner) * group_shards + s) * cut
                            parts.append(piece[:, start : start + cut].astype(f32))
                    k_parts.append(piece[:, q_width : q_width + HEAD].astype(f32))
                    v_parts.append(piece[:, q_width + HEAD : q_width + 2 * HEAD].astype(f32))
                total = jnp.zeros((gain.shape[0], LANES), f32)
                for part, weight, out in zip((parts, k_parts, v_parts), weights, outs):
                    wide = jnp.concatenate(part, axis=1)
                    total = total + lane_sum(wide * weight[...].astype(f32))
                    out[...] = wide * scale
                gain_out[...] = total


def qkv_result(index, pieces, query, key, value, gain):
    local, width = query.shape
    half = local // 2
    group_shards = width // local // CHIPS
    row = lambda i, n: (n[1] ^ i, 0)
    kv_width = key.shape[1]
    return kernel_call(
        functools.partial(qkv_result_body, local, group_shards),
        (
            shape((local, width), f32),
            shape((local, kv_width), f32),
            shape((local, kv_width), f32),
            shape((local, LANES), f32),
        ),
        [pl.BlockSpec(pieces[0].shape, lambda i, n: (0, 0))] * PIECES
        + [
            pl.BlockSpec((half, width), row),
            pl.BlockSpec((half, kv_width), row),
            pl.BlockSpec((half, kv_width), row),
            pl.BlockSpec((half, LANES), row),
        ],
        (
            pl.BlockSpec((half, width), row),
            pl.BlockSpec((half, kv_width), row),
            pl.BlockSpec((half, kv_width), row),
            pl.BlockSpec((half, LANES), row),
        ),
        (*pieces, query, key, value, gain),
        index=index,
        grid=(2,),
        name="qkv_result",
    )


def per_device(
    hidden_in,
    attention_gain,
    query_weight,
    key_weight,
    value_weight,
    output_weight,
    feedforward_gain,
    gate_weight,
    up_weight,
    down_weight,
    out_grad,
):
    rows, width = hidden_in.shape
    shards = lax.axis_size("shard")
    replicas = lax.axis_size("replica")
    place = lax.axis_index("replica")
    depth = lax.axis_index("shard")
    core = place & 1
    chip = (place >> 1) & (CHIPS - 1)
    local = width // shards
    half = local // 2
    ff_local = down_weight.shape[0]
    group_shards = shards // CHIPS
    q_width = GROUP * HEAD
    qkv_width = q_width + 2 * HEAD
    index = jnp.stack([chip, core, depth]).astype(jnp.int32)

    gain_one = jnp.broadcast_to(attention_gain.astype(f32)[:, None], (local, LANES))
    gain_two = jnp.broadcast_to(feedforward_gain.astype(f32)[:, None], (local, LANES))

    x = own_first(index, (hidden_in,), local)[0]
    xs = [x, swap(x, 2)]

    at_block, out_block = attention_block(
        index, query_weight, key_weight, value_weight, output_weight, after(gain_one, x)
    )
    at_own = lax.all_gather(at_block, "shard", axis=0, tiled=True)
    out_all = lax.all_gather(out_block, "shard", axis=0, tiled=True)
    gu_block = feedforward_block(index, gate_weight, up_weight, after(gain_two, at_block), ff_local)
    gu_own = lax.all_gather(gu_block, "shard", axis=0, tiled=True)
    down_own = lax.all_gather(down_block(index, down_weight, local), "shard", axis=0, tiled=True)
    g = own_first(index, (after(out_grad, x),), local)[0]
    g_blocks = [g, swap(g, 2), swap(g, 4)]
    at_own = after(at_own, gu_block, xs[1], *g_blocks[1:])

    qkv_own = [at_own]
    qkv_own.append(swap(qkv_own[0], 4))
    qkv_other = [swap(qkv_own[0], 1)]
    inverse = rope_base ** (-jnp.arange(0, HEAD, 2, dtype=f32) / HEAD)
    places = (depth * rows + jnp.arange(rows, dtype=jnp.int32)).astype(f32)
    angles = inverse[:, None] * places[None, :]
    angles = jnp.concatenate([angles, angles], axis=0)
    cosine, sine = jnp.cos(angles), jnp.sin(angles)

    def shifted(kv):
        return [kv] + [shift(kv, d) for d in range(1, shards)]

    queries, kv, xhat = qkv_call(xs, qkv_own[0], qkv_other[0], cosine, sine)
    kvs = shifted(kv)
    qkv_own[1] = after(qkv_own[1], *kvs[1:])
    qkv_other.append(swap(qkv_own[1], 1))
    queries_two, kv_two = qkv_call(xhat, qkv_own[1], qkv_other[1], cosine, sine)
    kvs_two = shifted(kv_two)
    groups = [(queries, *attention_call(index, queries, kvs), kvs)]
    groups.append((queries_two, *attention_call(index, queries_two, kvs_two), kvs_two))
    attended = [group[2] for group in groups]
    groups = [(group[0], group[1], group[3], group[4]) for group in groups]

    out_all = after(out_all, qkv_own[1])
    x_place = chip & 1
    low_group = (chip >> 1) == 0
    pair_rows = PAIR * group_shards * half // 2

    def out_for(mask):
        return lax.dynamic_slice_in_dim(out_all, ((chip ^ mask) & 1) * pair_rows, pair_rows, 0)

    out_pieces = [out_for(0)] + [swap(out_for(m), 2 * m) for m in range(1, CHIPS)]
    wo_own = out_rows_call(index, [after(piece, *kvs_two[1:]) for piece in out_pieces])
    wo_other = swap(wo_own, 1)

    mid_terms = [(attended[n], wo_own, wo_other, n) for n in range(PAIR)]
    g_blocks.append(swap(after(g, *out_pieces[1:]), 6))
    mid_out = parts_call(mid_terms, rows, False, "attention_out")
    g_all = jnp.concatenate([after(block, mid_out[0]) for block in g_blocks], axis=0)
    middle, two = middle_call(plane_send(mid_out), after(x, g_all))
    twos = plane_gather_forward(two)

    gu_own = after(gu_own, *twos[1:])
    gu_other = swap(gu_own, 1)
    act, for_gate, for_up, two_all = gate_call(twos, gu_own, gu_other)

    def over_groups(kept):
        if replicas > PIECES:
            groups = [
                [e * PIECES + i for e in range(replicas // PIECES)] for i in range(PIECES)
            ]
            kept = lax.psum(kept, "replica", axis_index_groups=groups)
        return kept

    def reduced(term):
        kept = lax.psum_scatter(term, "shard", scatter_dimension=0, tiled=True)
        return over_groups(kept)

    def plane_pieces(kept):
        mine = plane_gather(kept)
        return mine, [swap(part, 1) for part in mine]

    def mixed(mine, theirs):
        return [part for pair in zip(mine, theirs) for part in pair]

    quarter = width // 4
    down_sent = [
        swap(term, 1) for term in weight_grad(act, None, g_all, 2, quarter, 2, (), "down_grad_other")
    ]
    down_terms = weight_grad(act, None, g_all, 0, quarter, 2, (down_sent,), "down_grad")
    down_kept = [reduced(term) for term in down_terms]
    down_own = after(down_own, *down_terms)
    down_other = swap(down_own, 1)

    grads = hidden_back_call(after(g_all, *down_terms), down_own, down_other, for_gate, for_up)
    grads_wide = grads.shape[1]
    gu_sent = weight_grad(two_all, 1, grads, 0, grads_wide, 1, (), "gate_grad_other")
    grads_late = after(grads, *gu_sent, down_kept[0])
    gu_sent = [swap(gu_sent[0], 1)]
    e_terms = parts_call([(grads_late, gu_own, gu_other, 0)], rows, True, "feedforward_back")
    e_parts = plane_send(e_terms)
    gu_term = weight_grad(
        after(two_all, *e_parts[1:]), 0, grads, 0, grads_wide, 1, (gu_sent,), "gate_grad"
    )[0]
    gu_kept = reduced(gu_term)

    middle_late = after(middle, gu_term, *down_kept)
    grad_middle, branch = grad_middle_call(e_parts, middle_late, g)
    branches = [branch, swap(branch, 2)]
    down_mine = plane_gather(after(jnp.concatenate(down_kept, axis=1), *e_parts[1:]))

    def back_block(m, block, before):
        return attention_back_call(index, m, block, wo_own, wo_other, cosine, sine, groups, before)

    before = back_block(0, after(branch, *down_mine[1:]), None)
    act_late = after(act, before[1])
    out_terms = parts_call([(act_late, down_own, down_other, 0)], rows, False, "feedforward_out")
    before = back_block(1, after(branches[1], out_terms[0]), before)
    out_parts = plane_send(out_terms)
    output = output_call(index, out_parts, middle, local)
    grad_q, grad_first, grad_rest = before
    rest = [shift(grad_rest[d - 1], -d) for d in range(1, shards)]

    half_wide = width // 2
    branch_all = jnp.concatenate([after(block, grad_first) for block in branches], axis=0)
    both_attended = jnp.concatenate(attended, axis=1)
    wo_sent = weight_grad(both_attended, None, branch_all, 1, half_wide, 1, (), "out_grad_other")
    wo_sent = [swap(wo_sent[0], 1)]
    wo_term = weight_grad(both_attended, None, branch_all, 0, half_wide, 1, (wo_sent,), "out_grad")[0]
    wo_terms = out_sends(index, wo_term)
    wo_wide = out_block_call(index, plane_send(wo_terms), shards)
    down_theirs = [swap(part, 1) for part in down_mine]
    down_out = rows_result(index, mixed(down_mine, down_theirs), local, "down_result")

    grad_first = after(grad_first, wo_terms[0], *out_parts[1:3])
    grad_qkv = grad_qkv_call(grad_q, grad_first, rest, cosine, sine)

    def qkv_grad(n, side, added, name):
        return weight_grad(xhat, side, grad_qkv[n], 0, qkv_width, 1, added, name)

    qkv_sent = [[swap(qkv_grad(n, 1, (), "qkv_grad_other")[0], 1)] for n in (1, 0)]
    qkv_second = [swap(qkv_grad(1, 0, (qkv_sent[0],), "qkv_grad")[0], 4)]
    qkv_sent[1] = after(qkv_sent[1], output, down_out)
    qkv_term = qkv_grad(0, 0, (qkv_sent[1], qkv_second), "qkv_grad")[0]
    at_kept = reduced(after(jnp.concatenate([qkv_term, wo_wide], axis=1), gu_kept))

    back_terms = [(grad_qkv[n], qkv_own[n], qkv_other[n], 0) for n in range(PAIR)]
    e_one = plane_send(parts_call(back_terms, rows, True, "qkv_back"))
    grad_input = grad_input_call(index, e_one, x, grad_middle, local)

    gu_mine = plane_gather_forward(gu_kept)
    gu_mine = gu_mine[:3] + [jnp.concatenate(gu_mine[3:], axis=0)]
    gu_theirs = [swap(part, 1) for part in gu_mine]
    gu_out = feedforward_result(index, 0, gu_mine, gate_weight, up_weight, gain_two, ff_local, None)
    gu_out = feedforward_result(index, 1, gu_theirs, gate_weight, up_weight, gain_two, ff_local, gu_out)
    at_pieces = mixed(*plane_pieces(at_kept))
    wo_out = out_result(index, at_pieces, local, width, qkv_width)
    q_out, k_out, v_out, gain_one_sums = qkv_result(
        index, at_pieces, query_weight, key_weight, value_weight, gain_one
    )
    return (
        output,
        grad_input,
        jnp.sum(gain_one_sums, axis=1),
        q_out,
        k_out,
        v_out,
        wo_out,
        jnp.sum(gu_out[2], axis=1),
        gu_out[0],
        gu_out[1],
        down_out,
    )


def solution(mesh):
    return jax.shard_map(
        per_device,
        mesh=mesh,
        in_specs=(
            P(("replica", "shard"), None),
            P("shard"),
            P("shard", None),
            P("shard", None),
            P("shard", None),
            P("shard", None),
            P("shard"),
            P("shard", None),
            P("shard", None),
            P("shard", None),
            P(("replica", "shard"), None),
        ),
        out_specs=(
            P(("replica", "shard"), None),
            P(("replica", "shard"), None),
            P("shard"),
            P("shard", None),
            P("shard", None),
            P("shard", None),
            P("shard", None),
            P("shard"),
            P("shard", None),
            P("shard", None),
            P("shard", None),
        ),
        check_vma=False,
    )
```

```python
import functools

import jax
import jax.numpy as jnp
from jax import lax
from jax.experimental import pallas as pl
from jax.experimental.pallas import tpu as pltpu
from jax.sharding import PartitionSpec as P

HEADS = 32
KV_HEADS = 4
HEAD = 64
GROUP = HEADS // KV_HEADS
CHIPS = 4
PIECES = 2 * CHIPS
PAIR = 2
LANES = 128

norm_eps = 1e-05
rope_base = 10000.0
masked_score = -1e30

f32 = jnp.float32
bf16 = jnp.bfloat16
VMEM = pltpu.VMEM
NT = (((1,), (1,)), ((), ()))
TN = (((0,), (0,)), ((), ()))


def dot(left, right):
    return jnp.dot(left, right, preferred_element_type=f32)


def dot_nt(left, right):
    return lax.dot_general(left, right, NT, preferred_element_type=f32)


def dot_tn(left, right):
    return lax.dot_general(left, right, TN, preferred_element_type=f32)


def shape(dims, kind):
    return jax.ShapeDtypeStruct(dims, kind)


def whole():
    return pl.BlockSpec(memory_space=VMEM)


def kernel_call(body, out_shape, in_specs, out_specs, operands, *, index=None, grid=(), scratch=(),
                moved=0, aliases=None, name=None):
    params = pltpu.CompilerParams(
        vmem_limit_bytes=52 * 2**20, dimension_semantics=("arbitrary",) * len(grid)
    )
    cost = pl.CostEstimate(flops=0, bytes_accessed=int(moved), transcendentals=0)
    common = dict(
        out_shape=out_shape,
        compiler_params=params,
        cost_estimate=cost,
        input_output_aliases=aliases or {},
        name=name,
    )
    if index is None:
        spec = pl.GridSpec(grid=grid, in_specs=in_specs, out_specs=out_specs, scratch_shapes=scratch)
        return pl.pallas_call(body, grid_spec=spec, **common)(*operands)
    spec = pltpu.PrefetchScalarGridSpec(
        num_scalar_prefetch=1, grid=grid, in_specs=in_specs, out_specs=out_specs,
        scratch_shapes=scratch,
    )
    return pl.pallas_call(body, grid_spec=spec, **common)(index, *operands)


def swap(value, mask):
    size = lax.axis_size("replica")
    return lax.ppermute(value, "replica", [(i, i ^ mask) for i in range(size)])


def shift(value, step):
    size = lax.axis_size("shard")
    pairs = [(i, i + step) for i in range(size) if 0 <= i + step < size]
    return lax.ppermute(value, "shard", pairs)


def plane_gather(value):
    return [value] + [swap(value, 2 * m) for m in range(1, CHIPS)]


def plane_gather_forward(value):
    middle = value.shape[0] // 2
    across, along = swap(value, 2), swap(value, 4)
    return [value, across, along, swap(across[:middle], 4), swap(along[middle:], 2)]


def plane_send(parts):
    return [parts[0]] + [swap(parts[m], 2 * m) for m in range(1, len(parts))]


def group_of(chip):
    return 2 * (chip & 1) + (chip >> 1)


def after(value, *others):
    return lax.optimization_barrier((value, *others))[0]


def attention_block_body(local, group_shards, index, q, k, v, o, gain, out, wo_out):
    scale = gain[:, :1]
    q_width = GROUP * HEAD
    cut = local // CHIPS
    for chip in range(CHIPS):

        group = group_of(chip)

        @pl.when(index[0] == chip)
        def _(group=group):
            parts = []
            for m in range(CHIPS):
                for s in range(group_shards):
                    start = group * q_width + s * local + (m ^ chip) * cut
                    parts.append(q[:, start : start + cut])
            parts.append(k[:, group * HEAD : (group + 1) * HEAD])
            parts.append(v[:, group * HEAD : (group + 1) * HEAD])
            wide = jnp.concatenate([part.astype(f32) for part in parts], axis=1)
            out[...] = (wide * scale).astype(bf16)

    half = local // 2
    shards = o.shape[1] // local
    for core in range(2):

        @pl.when(index[1] == core)
        def _():
            for s in range(shards):
                piece = o[:, s * local + core * half : s * local + (core + 1) * half]
                wo_out[:, s * half : (s + 1) * half] = piece


def attention_block(index, query, key, value, output, gain):
    local, width = query.shape
    half = local // 2
    shards = width // local
    return kernel_call(
        functools.partial(attention_block_body, local, shards // CHIPS),
        (
            shape((half, GROUP * HEAD + 2 * HEAD), bf16),
            shape((local // CHIPS, width // 2), bf16),
        ),
        [
            pl.BlockSpec((half, width), lambda i, n: (n[1], 0)),
            pl.BlockSpec((half, key.shape[1]), lambda i, n: (n[1], 0)),
            pl.BlockSpec((half, key.shape[1]), lambda i, n: (n[1], 0)),
            pl.BlockSpec((local // CHIPS, width), lambda i, n: (n[0], 0)),
            pl.BlockSpec((half, LANES), lambda i, n: (n[1], 0)),
        ],
        (
            pl.BlockSpec((half, GROUP * HEAD + 2 * HEAD), lambda i, n: (0, 0)),
            pl.BlockSpec((local // CHIPS, width // 2), lambda i, n: (0, 0)),
        ),
        (query, key, value, output, gain),
        index=index,
        grid=(1,),
        name="attention_block",
    )


def feedforward_block_body(ff_local, cut, index, gate, up, gain, out):
    scale = gain[:, :1]
    shards = gate.shape[1] // ff_local
    width = shards * cut
    for chip in range(CHIPS):

        @pl.when(index[0] == chip)
        def _():
            for n, source in enumerate((gate, up)):
                parts = [
                    source[:, s * ff_local + chip * cut : s * ff_local + (chip + 1) * cut].astype(f32)
                    for s in range(shards)
                ]
                wide = jnp.concatenate(parts, axis=1)
                out[:, n * width : (n + 1) * width] = (wide * scale).astype(bf16)


def feedforward_block(index, gate, up, gain, ff_local):
    local, ff = gate.shape
    half = local // 2
    rows = 64
    steps = half // rows
    cut = ff_local // CHIPS
    width = 2 * (ff // CHIPS)
    return kernel_call(
        functools.partial(feedforward_block_body, ff_local, cut),
        shape((half, width), bf16),
        [
            pl.BlockSpec((rows, ff), lambda i, n: (n[1] * steps + i, 0)),
            pl.BlockSpec((rows, ff), lambda i, n: (n[1] * steps + i, 0)),
            pl.BlockSpec((rows, LANES), lambda i, n: (n[1] * steps + i, 0)),
        ],
        pl.BlockSpec((rows, width), lambda i, n: (i, 0)),
        (gate, up, gain),
        index=index,
        grid=(steps,),
        name="feedforward_block",
    )


def own_first_body(local, index, *refs):
    count = len(refs) // 2
    half = local // 2
    for core in range(2):

        @pl.when(index[1] == core)
        def _():
            for source, out in zip(refs[:count], refs[count:]):
                shards = source.shape[1] // local
                sides = out.shape[1] // (shards * half)
                for side in range(sides):
                    for s in range(shards):
                        start = s * local + (core ^ side) * half
                        spot = (side * shards + s) * half
                        out[:, spot : spot + half] = source[:, start : start + half]


def own_first(index, sources, local, halves=2):
    return kernel_call(
        functools.partial(own_first_body, local),
        tuple(shape((v.shape[0], v.shape[1] * halves // 2), bf16) for v in sources),
        [pl.BlockSpec(v.shape, lambda i, n: (0, 0)) for v in sources],
        tuple(
            pl.BlockSpec((v.shape[0], v.shape[1] * halves // 2), lambda i, n: (0, 0)) for v in sources
        ),
        tuple(sources),
        index=index,
        grid=(1,),
        name="own_first",
    )


def down_block_body(local, index, source, out):
    own_first_body(local, index, source, out)


def down_block(index, down, local):
    ff_local, width = down.shape
    cut = ff_local // CHIPS
    return kernel_call(
        functools.partial(down_block_body, local),
        shape((cut, width // 2), bf16),
        [pl.BlockSpec((cut, width), lambda i, n: (n[0], 0))],
        pl.BlockSpec((cut, width // 2), lambda i, n: (0, 0)),
        (down,),
        index=index,
        grid=(1,),
        name="down_block",
    )


def part_sum(parts):
    total = parts[0][...]
    for part in parts[1:]:
        total = total + part[...].astype(f32)
    return total


def mean_of(values):
    return jnp.mean(values, axis=1, keepdims=True)


def middle_body(*refs):
    parts, (x, middle, two) = refs[:PAIR], refs[PAIR:]
    total = x[...].astype(f32) + part_sum(parts)
    middle[...] = total
    two[...] = (total * lax.rsqrt(mean_of(total * total) + norm_eps)).astype(bf16)


def middle_call(parts, x):
    return kernel_call(
        middle_body,
        (shape(x.shape, f32), shape(x.shape, bf16)),
        [whole()] * (PAIR + 1),
        (whole(), whole()),
        (*parts, x),
        name="middle",
    )


def norm_back(e, values):
    inverse = lax.rsqrt(mean_of(values * values) + norm_eps)
    return inverse * e - values * (inverse * inverse * inverse) * mean_of(e * values)


def grad_middle_body(*refs):
    parts, (middle, g, grad, low) = refs[:CHIPS], refs[CHIPS:]
    total = g[...].astype(f32) + norm_back(part_sum(parts), middle[...])
    grad[...] = total
    low[...] = total.astype(bf16)


def grad_middle_call(parts, middle, g):
    return kernel_call(
        grad_middle_body,
        (shape(g.shape, f32), shape(g.shape, bf16)),
        [whole()] * (CHIPS + 2),
        (whole(), whole()),
        (*parts, middle, g),
        name="grad_middle",
    )


def store_in_order(local, index, value, out):
    half = local // 2
    shards = out.shape[1] // local
    for core in range(2):

        @pl.when(index[1] == core)
        def _():
            for side in range(2):
                for s in range(shards):
                    spot = s * local + (core ^ side) * half
                    start = (side * shards + s) * half
                    out[:, spot : spot + half] = value[:, start : start + half].astype(bf16)


def output_body(local, index, *refs):
    parts, (middle, out) = refs[:CHIPS], refs[CHIPS:]
    store_in_order(local, index, middle[...] + part_sum(parts), out)


def output_call(index, parts, middle, local):
    spec = pl.BlockSpec(middle.shape, lambda i, n: (0, 0))
    return kernel_call(
        functools.partial(output_body, local),
        shape(middle.shape, bf16),
        [spec] * (CHIPS + 1),
        spec,
        (*parts, middle),
        index=index,
        grid=(1,),
        name="output",
    )


def grad_input_body(local, index, *refs):
    parts, (x, grad, out) = refs[:PAIR], refs[PAIR:]
    total = grad[...] + norm_back(part_sum(parts), x[...].astype(f32))
    store_in_order(local, index, total, out)


def grad_input_call(index, parts, x, grad, local):
    spec = pl.BlockSpec(x.shape, lambda i, n: (0, 0))
    return kernel_call(
        functools.partial(grad_input_body, local),
        shape(x.shape, bf16),
        [spec] * (PAIR + 2),
        spec,
        (*parts, x, grad),
        index=index,
        grid=(1,),
        name="grad_input",
    )


def grad_qkv_body(shards, grad_q, first, *refs):
    rest, (cosine, sine), outs = refs[: shards - 1], refs[shards - 1 : shards + 1], refs[shards + 1 :]
    total = first[...]
    for term in rest:
        total = total + term[...].astype(f32)
    rows = cosine.shape[1]
    width = GROUP * HEAD
    cos, sin = cosine[...], sine[...]
    for n, out in enumerate(outs):
        out[:, :width] = grad_q[:, n * width : (n + 1) * width]
        for m in range(PAIR):
            span = slice(m * rows, (m + 1) * rows)
            turned = total[span, n * 2 * HEAD : (n + 1) * 2 * HEAD].T
            k = turned[:HEAD]
            k = k * cos - half_rotated(k) * sin
            both = jnp.concatenate([k, turned[HEAD:]], axis=0)
            out[span, width:] = both.T.astype(bf16)


def grad_qkv_call(grad_q, first, rest, cosine, sine):
    tokens = grad_q.shape[0]
    return kernel_call(
        functools.partial(grad_qkv_body, len(rest) + 1),
        (shape((tokens, GROUP * HEAD + 2 * HEAD), bf16),) * PAIR,
        [whole()] * (len(rest) + 4),
        (whole(),) * PAIR,
        (grad_q, first, *rest, cosine, sine),
        name="grad_qkv",
    )


def out_sends_body(index, term, *outs):
    cut = outs[0].shape[0] // PAIR
    for row in range(2):

        @pl.when(index[0] >> 1 == row)
        def _():
            for n in range(PAIR):
                for m in range(CHIPS):
                    spot = (n * CHIPS + m) * cut
                    start = (n ^ row) * cut
                    outs[m ^ (2 * n)][start : start + cut, :] = term[spot : spot + cut, :]


def out_sends(index, term):
    rows, width = term.shape
    rows //= CHIPS
    return kernel_call(
        out_sends_body,
        (shape((rows, width), bf16),) * CHIPS,
        [pl.BlockSpec(term.shape, lambda i, n: (0, 0))],
        (pl.BlockSpec((rows, width), lambda i, n: (0, 0)),) * CHIPS,
        (term,),
        index=index,
        grid=(1,),
        name="out_sends",
    )


def out_block_body(shards, index, *refs):
    parts, out = refs[:CHIPS], refs[CHIPS]
    group_shards = shards // CHIPS
    cut = parts[0].shape[0] // (PAIR * group_shards)
    sums = [parts[m][...].astype(f32) + parts[m + 2][...].astype(f32) for m in range(2)]
    for side in range(2):

        @pl.when(index[0] & 1 == side)
        def _():
            for m in range(2):
                for n in range(PAIR * group_shards):
                    shard = (m ^ side) * PAIR * group_shards + n
                    rows = sums[m][n * cut : (n + 1) * cut].astype(bf16)
                    out[2 * shard * cut : (2 * shard + 1) * cut, :] = rows[:, :512]
                    out[(2 * shard + 1) * cut : (2 * shard + 2) * cut, :] = rows[:, 512:]


def out_block_call(index, parts, shards):
    rows, width = parts[0].shape
    return kernel_call(
        functools.partial(out_block_body, shards),
        shape((2 * PAIR * rows, width // 2), bf16),
        [pl.BlockSpec((rows, width), lambda i, n: (0, 0))] * CHIPS,
        pl.BlockSpec((2 * PAIR * rows, width // 2), lambda i, n: (0, 0)),
        tuple(parts),
        index=index,
        grid=(1,),
        name="out_block",
    )


def half_rotated(values):
    middle = values.shape[0] // 2
    return jnp.concatenate([-values[middle:], values[:middle]], axis=0)


def qkv_body(make, *refs):
    if make:
        xs, (own, other, cosine, sine, queries, kv, xhat) = refs[:PAIR], refs[PAIR:]
        rows, width = xs[0].shape
        for m in range(PAIR):
            x = xs[m][...].astype(f32)
            inverse = lax.rsqrt(mean_of(x * x) + norm_eps)
            xhat[m * rows : (m + 1) * rows, :] = (x * inverse).astype(bf16)
    else:
        xhat, own, other, cosine, sine, queries, kv = refs
        rows, width = cosine.shape[1], xhat.shape[1]
    cos, sin = cosine[...], sine[...]
    total = dot(xhat[:, : width // 2], own[...]) + dot(xhat[:, width // 2 :], other[...])
    for m in range(PAIR):
        turned = total[m * rows : (m + 1) * rows].T
        for h in range(GROUP + 1):
            u = turned[h * HEAD : (h + 1) * HEAD]
            u = u * cos + half_rotated(u) * sin
            if h < GROUP:
                queries[m, :, h * rows : (h + 1) * rows] = (u * HEAD ** (-0.5)).astype(bf16)
            else:
                both = jnp.concatenate([u, turned[(h + 1) * HEAD :]], axis=0)
                kv[m * rows : (m + 1) * rows, :] = both.T.astype(bf16)


def qkv_call(xs, own, other, cosine, sine):
    make = isinstance(xs, list)
    rows = cosine.shape[1]
    tokens = PAIR * rows
    outs = (shape((PAIR, HEAD, GROUP * rows), bf16), shape((tokens, 2 * HEAD), bf16))
    if make:
        outs = outs + (shape((tokens, xs[0].shape[1]), bf16),)
    operands = (*(xs if make else (xs,)), own, other, cosine, sine)
    return kernel_call(
        functools.partial(qkv_body, make),
        outs,
        [whole()] * len(operands),
        tuple(whole() for _ in outs),
        operands,
        name="qkv",
    )


def out_rows_body(index, *refs):
    pieces, out = refs[:CHIPS], refs[CHIPS]
    cut = pieces[0].shape[0] // PAIR
    for row in range(2):

        @pl.when(index[0] >> 1 == row)
        def _():
            for n in range(PAIR):
                for m in range(CHIPS):
                    spot = (n * CHIPS + m) * cut
                    start = (n ^ row) * cut
                    out[spot : spot + cut, :] = pieces[m ^ (2 * n)][start : start + cut, :]


def out_rows_call(index, pieces):
    rows, width = pieces[0].shape
    return kernel_call(
        out_rows_body,
        shape((CHIPS * rows, width), bf16),
        [pl.BlockSpec((rows, width), lambda i, n: (0, 0))] * CHIPS,
        pl.BlockSpec((CHIPS * rows, width), lambda i, n: (0, 0)),
        tuple(pieces),
        index=index,
        grid=(1,),
        name="out_rows",
    )


LANE_HEADS = 4


def own_block_bias(rows):
    key = lax.broadcasted_iota(jnp.int32, (rows, rows), 0)
    mine = lax.broadcasted_iota(jnp.int32, (rows, rows), 1)
    return jnp.where(key <= mine, 0.0, masked_score)


def set_bias(bias):
    rows = bias.shape[0]
    value = own_block_bias(rows)
    for h in range(LANE_HEADS):
        bias[:, h * rows : (h + 1) * rows] = value


def far_bias(depth, d):
    return jnp.where(d <= depth, 0.0, masked_score) if d else 0.0


def attention_body(shards, index, queries, *refs):
    kvs = refs[:shards]
    turned_out, out, stats, bias, terms, out_turned = refs[shards:]
    rows = bias.shape[0]
    wide = LANE_HEADS * rows

    @pl.when(pl.program_id(0) == 0)
    def _():
        set_bias(bias)

    ks = [kv[:, :HEAD] for kv in kvs]
    v_turned = jnp.concatenate([kv[...] for kv in kvs], axis=0).astype(f32).T[HEAD:].astype(bf16)
    for n in range(GROUP // LANE_HEADS):
        span = slice(n * wide, (n + 1) * wide)
        q = queries[0, :, span]
        scores, top = [], None
        for d in range(shards):
            score = dot(ks[d], q)
            if d == 0:
                score = score + bias[...]
            scores.append(score)
            highest = jnp.max(score, axis=0, keepdims=True) + far_bias(index[2], d)
            top = highest if top is None else jnp.maximum(top, highest)
        total = None
        for d in range(shards):
            term = jnp.exp(scores[d] - (top - far_bias(index[2], d)))
            part = jnp.sum(term, axis=0, keepdims=True)
            total = part if total is None else total + part
            terms[d * rows : (d + 1) * rows, :] = term.astype(bf16)
        out_turned[:, span] = dot(v_turned, terms[...]) / total
        stats[0, :, span] = top + jnp.log(total)
    turned_out[0] = out_turned[...].astype(bf16)
    straight = out_turned[...].T
    for h in range(GROUP):
        out[:, h * HEAD : (h + 1) * HEAD] = straight[h * rows : (h + 1) * rows].astype(bf16)


def attention_call(index, queries, kvs):
    chips, _, wide = queries.shape
    rows = wide // GROUP
    shards = len(kvs)
    keys = shards * rows
    block = pl.BlockSpec((1, HEAD, wide), lambda i, n: (i, 0, 0))
    return kernel_call(
        functools.partial(attention_body, shards),
        (
            shape((chips, HEAD, wide), bf16),
            shape((chips * rows, GROUP * HEAD), bf16),
            shape((chips, 1, wide), f32),
        ),
        [block] + [pl.BlockSpec((rows, 2 * HEAD), lambda i, n: (i, 0))] * shards,
        (
            block,
            pl.BlockSpec((rows, GROUP * HEAD), lambda i, n: (i, 0)),
            pl.BlockSpec((1, 1, wide), lambda i, n: (i, 0, 0)),
        ),
        (queries, *kvs),
        index=index,
        grid=(chips,),
        scratch=(
            VMEM((rows, LANE_HEADS * rows), f32),
            VMEM((keys, LANE_HEADS * rows), bf16),
            VMEM((HEAD, wide), f32),
        ),
        name="attention",
    )


def attention_back_body(shards, index, branch, wo_own, wo_other, cosine, sine, *refs):
    per_group = 3 + shards
    inputs = [refs[n * per_group : (n + 1) * per_group] for n in range(PAIR)]
    grad_q, grad_first, grad_rest = refs[-7:-4]
    bias, probs_low, grads_low, grad_lanes = refs[-4:]
    rows = bias.shape[0]
    wide = LANE_HEADS * rows
    width = branch.shape[1]
    set_bias(bias)
    cos, sin = cosine[...], sine[...]
    for n, (queries, turned_out, stats, *kvs) in enumerate(inputs):
        heads = slice(n * GROUP * HEAD, (n + 1) * GROUP * HEAD)
        grad_out = dot_nt(wo_own[heads, :], branch[:, : width // 2])
        grad_out = grad_out + dot_nt(wo_other[heads, :], branch[:, width // 2 :])
        for h in range(GROUP):
            grad_lanes[:, h * rows : (h + 1) * rows] = grad_out[h * HEAD : (h + 1) * HEAD].astype(bf16)
        ks = [kv[:, :HEAD] for kv in kvs]
        vs = [kv[:, HEAD:] for kv in kvs]
        k_turned = jnp.concatenate([kv[...] for kv in kvs], axis=0).astype(f32).T[:HEAD].astype(bf16)
        k_total, v_total, parts = None, None, []
        for c in range(GROUP // LANE_HEADS):
            span = slice(c * wide, (c + 1) * wide)
            q, mine = queries[0, :, span], grad_lanes[:, span]
            delta = jnp.sum(
                mine.astype(f32) * turned_out[0, :, span].astype(f32), axis=0, keepdims=True
            )
            for d in range(shards):
                score = dot(ks[d], q)
                if d == 0:
                    score = score + bias[...]
                probs = jnp.exp(score - (stats[0, :, span] - far_bias(index[2], d)))
                grad_scores = probs * (dot(vs[d], mine) - delta)
                probs_low[d * rows : (d + 1) * rows, :] = probs.astype(bf16)
                grads_low[d * rows : (d + 1) * rows, :] = grad_scores.astype(bf16)
            u = dot(k_turned, grads_low[...]) * HEAD ** (-0.5)
            parts.append(u * cos - half_rotated(u) * sin)
            k_term = dot_nt(grads_low[...], q)
            v_term = dot_nt(probs_low[...], mine)
            k_total = k_term if k_total is None else k_total + k_term
            v_total = v_term if v_total is None else v_total + v_term
        straight = jnp.concatenate(parts, axis=1).T
        for h in range(GROUP):
            spot = (n * GROUP + h) * HEAD
            grad_q[:, spot : spot + HEAD] = straight[h * rows : (h + 1) * rows].astype(bf16)
        both = jnp.concatenate([k_total, v_total], axis=1)
        spot = slice(n * 2 * HEAD, (n + 1) * 2 * HEAD)
        grad_first[:, spot] = both[:rows, :]
        for d in range(1, shards):
            grad_rest[d - 1, :, spot] = both[d * rows : (d + 1) * rows, :].astype(bf16)


def attention_back_call(index, m, branch, wo_own, wo_other, cosine, sine, groups, before):
    chips, _, wide = groups[0][0].shape
    rows = wide // GROUP
    shards = len(groups[0][3])
    keys = shards * rows
    tokens = chips * rows
    block = pl.BlockSpec((1, HEAD, wide), lambda i, n: (m, 0, 0))
    in_specs = [whole()] * 5
    operands = [branch, wo_own, wo_other, jnp.tile(cosine, (1, LANE_HEADS)), jnp.tile(sine, (1, LANE_HEADS))]
    for queries, turned, stats, kvs in groups:
        in_specs += [block, block, pl.BlockSpec((1, 1, wide), lambda i, n: (m, 0, 0))]
        in_specs += [pl.BlockSpec((rows, 2 * HEAD), lambda i, n: (m, 0))] * shards
        operands += [queries, turned, stats, *kvs]
    aliases = {}
    if before is not None:
        aliases = {1 + len(operands) + n: n for n in range(3)}
        in_specs += [pl.BlockSpec(memory_space=pl.ANY)] * 3
        operands += list(before)
    outs = (
        shape((tokens, PAIR * GROUP * HEAD), bf16),
        shape((tokens, PAIR * 2 * HEAD), f32),
        shape((shards - 1, tokens, PAIR * 2 * HEAD), bf16),
    )
    out_specs = (
        pl.BlockSpec((rows, PAIR * GROUP * HEAD), lambda i, n: (m, 0)),
        pl.BlockSpec((rows, PAIR * 2 * HEAD), lambda i, n: (m, 0)),
        pl.BlockSpec((shards - 1, rows, PAIR * 2 * HEAD), lambda i, n: (0, m, 0)),
    )
    return kernel_call(
        functools.partial(attention_back_body, shards),
        outs,
        in_specs,
        out_specs,
        tuple(operands),
        index=index,
        grid=(1,),
        scratch=(
            VMEM((rows, LANE_HEADS * rows), f32),
            VMEM((keys, LANE_HEADS * rows), bf16),
            VMEM((keys, LANE_HEADS * rows), bf16),
            VMEM((HEAD, wide), bf16),
        ),
        aliases=aliases,
        name="attention_back",
    )


def parts_body(steps, transposed, count, *refs):
    lefts, owns, others = refs[:count], refs[count : 2 * count], refs[2 * count : 3 * count]
    outs = refs[3 * count :]
    rows = outs[0].shape[0]
    step = pl.program_id(0)

    def run(weights):
        total = None
        for left, weight in zip(lefts, weights):
            term = (dot_nt if transposed else dot)(left[...], weight[...])
            total = term if total is None else total + term
        for m, out in enumerate(outs):
            out[...] = total[m * rows : (m + 1) * rows, :].astype(out.dtype)

    @pl.when(step < steps)
    def _():
        run(owns)

    @pl.when(step >= steps)
    def _():
        run(others)


def parts_call(terms, rows, transposed, name):
    tokens = terms[0][0].shape[0]
    half = terms[0][1].shape[0] if transposed else terms[0][1].shape[1]
    tile = 256
    steps = half // tile
    last = steps - 1
    specs = [pl.BlockSpec((tokens, term[0].shape[1]), lambda j: (0, 0)) for term in terms]
    for side in range(2):
        for left, _, _, spot in terms:
            depth = left.shape[1]

            def place(side, spot, j):
                step = jnp.maximum(j - steps, 0) if side else jnp.minimum(j, last)
                return (step, spot) if transposed else (spot, step)

            block = (tile, depth) if transposed else (depth, tile)
            specs.append(pl.BlockSpec(block, functools.partial(place, side, spot)))
    count = tokens // rows
    return kernel_call(
        functools.partial(parts_body, steps, transposed, len(terms)),
        tuple(shape((rows, 2 * half), f32 if m == 0 else bf16) for m in range(count)),
        specs,
        tuple(pl.BlockSpec((rows, tile), lambda j: (0, j)) for _ in range(count)),
        (*(term[0] for term in terms), *(term[1] for term in terms), *(term[2] for term in terms)),
        grid=(2 * steps,),
        name=name,
    )


def gate_body(count, *refs):
    twos = refs[:count]
    gate_own, up_own, gate_other, up_other, act, for_gate, for_up, two_all = refs[count:]
    half = two_all.shape[1] // 2

    @pl.when(pl.program_id(0) == 0)
    def _():
        start = 0
        for two in twos:
            two_all[start : start + two.shape[0], :] = two[...]
            start += two.shape[0]

    own = jnp.concatenate([gate_own[...], up_own[...]], axis=1)
    other = jnp.concatenate([gate_other[...], up_other[...]], axis=1)
    both = dot(two_all[:, :half], own) + dot(two_all[:, half:], other)
    wide = gate_own.shape[1]
    gate, up = both[:, :wide], both[:, wide:]
    sig = 1.0 / (1.0 + jnp.exp(-gate))
    silu = gate * sig
    act[...] = (silu * up).astype(bf16)
    for_gate[...] = (up * sig * (1.0 + gate * (1.0 - sig))).astype(bf16)
    for_up[...] = silu.astype(bf16)


def gate_call(twos, own, other):
    rows, width = twos[0].shape
    tokens = CHIPS * rows
    half = width // 2
    ff = own.shape[1] // 2
    tile = LANES
    steps = ff // tile
    weight = [
        pl.BlockSpec((half, tile), lambda j: (0, j)),
        pl.BlockSpec((half, tile), lambda j: (0, j + steps)),
    ]
    column = pl.BlockSpec((tokens, tile), lambda j: (0, j))
    return kernel_call(
        functools.partial(gate_body, len(twos)),
        tuple(shape((tokens, ff), bf16) for _ in range(3)) + (shape((tokens, width), bf16),),
        [pl.BlockSpec(two.shape, lambda j: (0, 0)) for two in twos] + weight + weight,
        (column, column, column, pl.BlockSpec((tokens, width), lambda j: (0, 0))),
        (*twos, own, own, other, other),
        grid=(steps,),
        name="gate",
    )


def hidden_back_body(g, own, other, for_gate, for_up, grads):
    half = g.shape[1] // 2
    ff = own.shape[0]
    hidden = dot_nt(g[:, :half], own[...]) + dot_nt(g[:, half:], other[...])
    grads[:, :ff] = (hidden * for_gate[...].astype(f32)).astype(bf16)
    grads[:, ff:] = (hidden * for_up[...].astype(f32)).astype(bf16)


def hidden_back_call(g, own, other, for_gate, for_up):
    tokens, width = g.shape
    ff, half = own.shape
    block = tokens // 2
    row = lambda i: (i, 0)
    fixed = lambda i: (0, 0)
    return kernel_call(
        hidden_back_body,
        shape((tokens, 2 * ff), bf16),
        [
            pl.BlockSpec((block, width), row),
            pl.BlockSpec((ff, half), fixed),
            pl.BlockSpec((ff, half), fixed),
            pl.BlockSpec((block, ff), row),
            pl.BlockSpec((block, ff), row),
        ],
        pl.BlockSpec((block, 2 * ff), row),
        (g, own, other, for_gate, for_up),
        grid=(2,),
        name="hidden_back",
    )


def weight_grad_body(per, outputs, adds, left, right, *refs):
    added = [refs[n * outputs : (n + 1) * outputs] for n in range(adds)]
    outs, turned = refs[adds * outputs : -1], refs[-1]
    step = pl.program_id(0)

    @pl.when(step == 0)
    def _():
        turned[...] = left[...].T

    for n in range(outputs):

        @pl.when(step // per == n)
        def _(n=n):
            total = dot(turned[...], right[...])
            for terms in added:
                total = total + terms[n][...].astype(f32)
            outs[n][...] = total.astype(bf16)


def weight_grad(left, left_side, right, place, width, outputs, added, name):
    tokens = left.shape[0]
    rows = left.shape[1] // (1 if left_side is None else 2)
    tile = 256 if width % 256 == 0 else width
    per = width // tile
    first = place * width // tile
    side = left_side or 0

    def spot(n, j):
        return (0, jnp.clip(j - n * per, 0, per - 1))

    tiles = [pl.BlockSpec((rows, tile), functools.partial(spot, n)) for n in range(outputs)]
    return kernel_call(
        functools.partial(weight_grad_body, per, outputs, len(added)),
        tuple(shape((rows, width), bf16) for _ in range(outputs)),
        [
            pl.BlockSpec((tokens, rows), lambda j: (0, side)),
            pl.BlockSpec((tokens, tile), lambda j: (0, first + j)),
        ]
        + tiles * len(added),
        tuple(tiles),
        (left, right, *(term for terms in added for term in terms)),
        grid=(per * outputs,),
        scratch=(VMEM((rows, tokens), bf16),),
        name=name,
    )


def rows_result_body(local, index, *refs):
    pieces, out = refs[:PIECES], refs[PIECES]
    half = local // 2
    shards = out.shape[1] // local
    for m in range(CHIPS):
        for core in range(2):

            @pl.when((pl.program_id(0) == m) & (index[1] == core))
            def _():
                for side in range(2):
                    piece = pieces[2 * m + side]
                    for s in range(shards):
                        spot = s * local + (core ^ side) * half
                        out[:, spot : spot + half] = piece[:, s * half : (s + 1) * half].astype(f32)


def rows_result(index, pieces, local, name):
    cut, half_width = pieces[0].shape
    return kernel_call(
        functools.partial(rows_result_body, local),
        shape((CHIPS * cut, 2 * half_width), f32),
        [pl.BlockSpec((cut, half_width), lambda i, n: (0, 0))] * PIECES,
        pl.BlockSpec((cut, 2 * half_width), lambda i, n: (n[0] ^ i, 0)),
        tuple(pieces),
        index=index,
        grid=(CHIPS,),
        name=name,
    )


def out_result_body(local, base, index, *refs):
    pieces, out = refs[:PIECES], refs[PIECES]
    half = local // 2
    cut = local // CHIPS
    shards = out.shape[1] // local
    for m in range(CHIPS):
        for core in range(2):

            @pl.when((pl.program_id(0) == m) & (index[1] == core))
            def _():
                for side in range(2):
                    piece = pieces[2 * m + side]
                    for s in range(shards):
                        spot = s * local + (core ^ side) * half
                        row, column = (0, s * half) if s * half < 512 else (cut, s * half - 512)
                        column += base
                        out[:, spot : spot + half] = piece[row : row + cut, column : column + half].astype(f32)


def out_result(index, pieces, local, width, base):
    cut = local // CHIPS
    return kernel_call(
        functools.partial(out_result_body, local, base),
        shape((local, width), f32),
        [pl.BlockSpec(pieces[0].shape, lambda i, n: (0, 0))] * PIECES,
        pl.BlockSpec((cut, width), lambda i, n: (n[0] ^ i, 0)),
        tuple(pieces),
        index=index,
        grid=(CHIPS,),
        name="out_result",
    )


def lane_sum(value):
    total = value[:, :LANES]
    for n in range(1, value.shape[1] // LANES):
        total = total + value[:, n * LANES : (n + 1) * LANES]
    return total


def feedforward_result_body(ff_local, cut, index, *refs):
    pieces = refs[:CHIPS]
    gate_weight, up_weight, gain = refs[CHIPS : CHIPS + 3]
    gate_out, up_out, gain_out = refs[-3:]
    shards = gate_weight.shape[1] // ff_local
    width = shards * cut
    for chip in range(CHIPS):

        @pl.when(index[0] == chip)
        def _():
            @pl.loop(0, gate_out.shape[0] // 16)
            def _(n):
                rows = pl.ds(pl.multiple_of(n * 16, 16), 16)
                scale = gain[rows, :1]
                total = jnp.zeros((16, LANES), f32)
                for base, weight, out in ((0, gate_weight, gate_out), (width, up_weight, up_out)):
                    parts = []
                    for s in range(shards):
                        for owner in range(CHIPS):
                            start = base + s * cut
                            parts.append(pieces[owner ^ chip][rows, start : start + cut].astype(f32))
                    wide = jnp.concatenate(parts, axis=1)
                    total = total + lane_sum(wide * weight[rows, :].astype(f32))
                    out[rows, :] = wide * scale
                gain_out[rows, :] = total


def feedforward_result(index, side, pieces, gate_weight, up_weight, gain, ff_local, before):
    local, ff = gate_weight.shape
    half = local // 2
    rows = 64
    steps = half // rows
    row = lambda i, n: ((n[1] ^ side) * steps + i, 0)
    in_specs = [pl.BlockSpec((rows, pieces[0].shape[1]), lambda i, n: (i, 0))] * CHIPS
    in_specs += [pl.BlockSpec((rows, ff), row)] * 2 + [pl.BlockSpec((rows, LANES), row)]
    operands = (*pieces, gate_weight, up_weight, gain)
    aliases = {}
    if before is not None:
        aliases = {1 + len(operands) + n: n for n in range(3)}
        in_specs = in_specs + [pl.BlockSpec(memory_space=pl.ANY)] * 3
        operands = operands + tuple(before)
    return kernel_call(
        functools.partial(feedforward_result_body, ff_local, ff_local // CHIPS),
        (shape((local, ff), f32), shape((local, ff), f32), shape((local, LANES), f32)),
        in_specs,
        (pl.BlockSpec((rows, ff), row), pl.BlockSpec((rows, ff), row), pl.BlockSpec((rows, LANES), row)),
        operands,
        index=index,
        grid=(steps,),
        aliases=aliases,
        name="feedforward_result",
    )


def qkv_result_body(local, group_shards, index, *refs):
    pieces = refs[:PIECES]
    weights, gain = refs[PIECES : PIECES + 3], refs[PIECES + 3]
    outs, gain_out = refs[PIECES + 4 : PIECES + 7], refs[PIECES + 7]
    q_width = GROUP * HEAD
    cut = local // CHIPS
    scale = gain[:, :1]
    for chip in range(CHIPS):
        for side in range(2):

            @pl.when((index[0] == chip) & (pl.program_id(0) == side))
            def _():
                parts, k_parts, v_parts = [], [], []
                for group in range(CHIPS):
                    owner = (group >> 1) + 2 * (group & 1)
                    piece = pieces[2 * (owner ^ chip) + side]
                    for s in range(group_shards):
                        for j in range(CHIPS):
                            start = ((j ^ owner) * group_shards + s) * cut
                            parts.append(piece[:, start : start + cut].astype(f32))
                    k_parts.append(piece[:, q_width : q_width + HEAD].astype(f32))
                    v_parts.append(piece[:, q_width + HEAD : q_width + 2 * HEAD].astype(f32))
                total = jnp.zeros((gain.shape[0], LANES), f32)
                for part, weight, out in zip((parts, k_parts, v_parts), weights, outs):
                    wide = jnp.concatenate(part, axis=1)
                    total = total + lane_sum(wide * weight[...].astype(f32))
                    out[...] = wide * scale
                gain_out[...] = total


def qkv_result(index, pieces, query, key, value, gain):
    local, width = query.shape
    half = local // 2
    group_shards = width // local // CHIPS
    row = lambda i, n: (n[1] ^ i, 0)
    kv_width = key.shape[1]
    return kernel_call(
        functools.partial(qkv_result_body, local, group_shards),
        (
            shape((local, width), f32),
            shape((local, kv_width), f32),
            shape((local, kv_width), f32),
            shape((local, LANES), f32),
        ),
        [pl.BlockSpec(pieces[0].shape, lambda i, n: (0, 0))] * PIECES
        + [
            pl.BlockSpec((half, width), row),
            pl.BlockSpec((half, kv_width), row),
            pl.BlockSpec((half, kv_width), row),
            pl.BlockSpec((half, LANES), row),
        ],
        (
            pl.BlockSpec((half, width), row),
            pl.BlockSpec((half, kv_width), row),
            pl.BlockSpec((half, kv_width), row),
            pl.BlockSpec((half, LANES), row),
        ),
        (*pieces, query, key, value, gain),
        index=index,
        grid=(2,),
        name="qkv_result",
    )


def per_device(
    hidden_in,
    attention_gain,
    query_weight,
    key_weight,
    value_weight,
    output_weight,
    feedforward_gain,
    gate_weight,
    up_weight,
    down_weight,
    out_grad,
):
    rows, width = hidden_in.shape
    shards = lax.axis_size("shard")
    replicas = lax.axis_size("replica")
    place = lax.axis_index("replica")
    depth = lax.axis_index("shard")
    core = place & 1
    chip = (place >> 1) & (CHIPS - 1)
    local = width // shards
    half = local // 2
    ff_local = down_weight.shape[0]
    group_shards = shards // CHIPS
    q_width = GROUP * HEAD
    qkv_width = q_width + 2 * HEAD
    index = jnp.stack([chip, core, depth]).astype(jnp.int32)

    gain_one = jnp.broadcast_to(attention_gain.astype(f32)[:, None], (local, LANES))
    gain_two = jnp.broadcast_to(feedforward_gain.astype(f32)[:, None], (local, LANES))


    at_block, out_block = attention_block(
        index, query_weight, key_weight, value_weight, output_weight, gain_one
    )
    x = own_first(index, (after(hidden_in, at_block),), local)[0]
    xs = [x, swap(x, 2)]
    at_own = lax.all_gather(at_block, "shard", axis=0, tiled=True)
    out_all = lax.all_gather(out_block, "shard", axis=0, tiled=True)
    gu_block = feedforward_block(index, gate_weight, up_weight, after(gain_two, at_block), ff_local)
    gu_own = lax.all_gather(gu_block, "shard", axis=0, tiled=True)
    down_own = lax.all_gather(down_block(index, down_weight, local), "shard", axis=0, tiled=True)
    g = own_first(index, (after(out_grad, x),), local)[0]
    g_blocks = [g, swap(g, 2), swap(g, 4)]
    at_own = after(at_own, gu_block, xs[1], *g_blocks[1:])

    qkv_own = [at_own]
    qkv_own.append(swap(qkv_own[0], 4))
    qkv_other = [swap(qkv_own[0], 1)]
    inverse = rope_base ** (-jnp.arange(0, HEAD, 2, dtype=f32) / HEAD)
    places = (depth * rows + jnp.arange(rows, dtype=jnp.int32)).astype(f32)
    angles = inverse[:, None] * places[None, :]
    angles = jnp.concatenate([angles, angles], axis=0)
    cosine, sine = jnp.cos(angles), jnp.sin(angles)

    def shifted(kv):
        return [kv] + [shift(kv, d) for d in range(1, shards)]

    queries, kv, xhat = qkv_call(xs, qkv_own[0], qkv_other[0], cosine, sine)
    kvs = shifted(kv)
    qkv_own[1] = after(qkv_own[1], *kvs[1:])
    qkv_other.append(swap(qkv_own[1], 1))
    queries_two, kv_two = qkv_call(xhat, qkv_own[1], qkv_other[1], cosine, sine)
    kvs_two = shifted(kv_two)
    groups = [(queries, *attention_call(index, queries, kvs), kvs)]
    groups.append((queries_two, *attention_call(index, queries_two, kvs_two), kvs_two))
    attended = [group[2] for group in groups]
    groups = [(group[0], group[1], group[3], group[4]) for group in groups]

    out_all = after(out_all, qkv_own[1])
    x_place = chip & 1
    low_group = (chip >> 1) == 0
    pair_rows = PAIR * group_shards * half // 2

    def out_for(mask):
        return lax.dynamic_slice_in_dim(out_all, ((chip ^ mask) & 1) * pair_rows, pair_rows, 0)

    out_pieces = [out_for(0)] + [swap(out_for(m), 2 * m) for m in range(1, CHIPS)]
    wo_own = out_rows_call(index, [after(piece, *kvs_two[1:]) for piece in out_pieces])
    wo_other = swap(wo_own, 1)

    mid_terms = [(attended[n], wo_own, wo_other, n) for n in range(PAIR)]
    g_blocks.append(swap(after(g, *out_pieces[1:]), 6))
    mid_out = parts_call(mid_terms, rows, False, "attention_out")
    g_all = jnp.concatenate([after(block, mid_out[0]) for block in g_blocks], axis=0)
    middle, two = middle_call(plane_send(mid_out), after(x, g_all))
    twos = plane_gather_forward(two)

    gu_own = after(gu_own, *twos[1:])
    gu_other = swap(gu_own, 1)
    act, for_gate, for_up, two_all = gate_call(twos, gu_own, gu_other)

    def over_groups(kept):
        if replicas > PIECES:
            groups = [
                [e * PIECES + i for e in range(replicas // PIECES)] for i in range(PIECES)
            ]
            kept = lax.psum(kept, "replica", axis_index_groups=groups)
        return kept

    def reduced(term):
        kept = lax.psum_scatter(term, "shard", scatter_dimension=0, tiled=True)
        return over_groups(kept)

    def plane_pieces(kept):
        mine = plane_gather(kept)
        return mine, [swap(part, 1) for part in mine]

    def mixed(mine, theirs):
        return [part for pair in zip(mine, theirs) for part in pair]

    down_sent = weight_grad(act, None, g_all, 1, width // 2, 1, (), "down_grad_other")
    down_sent = [swap(down_sent[0], 1)]
    down_sent[0] = after(down_sent[0], down_own)
    down_term = weight_grad(act, None, g_all, 0, width // 2, 1, (down_sent,), "down_grad")[0]
    down_kept = reduced(down_term)
    down_other = swap(down_own, 1)

    grads = hidden_back_call(after(g_all, down_term), down_own, down_other, for_gate, for_up)
    grads_wide = grads.shape[1]
    gu_sent = weight_grad(two_all, 1, grads, 0, grads_wide, 1, (), "gate_grad_other")
    grads_late = after(grads, *gu_sent)
    gu_sent = [swap(gu_sent[0], 1)]
    e_terms = parts_call([(grads_late, gu_own, gu_other, 0)], rows, True, "feedforward_back")
    e_parts = plane_send(e_terms)
    act_late = after(act, e_parts[1])
    out_terms = parts_call([(act_late, down_own, down_other, 0)], rows, False, "feedforward_out")

    middle_late = after(middle, out_terms[0], down_kept)
    grad_middle, branch = grad_middle_call(e_parts, middle_late, g)
    branches = [branch, swap(branch, 2)]
    gu_term = weight_grad(after(two_all, branch), 0, grads, 0, grads_wide, 1, (gu_sent,), "gate_grad")[0]
    gu_kept = reduced(gu_term)
    out_parts = plane_send(after(out_terms, branches[1]))

    def back_block(m, block, before):
        return attention_back_call(index, m, block, wo_own, wo_other, cosine, sine, groups, before)

    before = back_block(0, branch, None)
    before = back_block(1, after(branches[1], before[1]), before)
    output = output_call(index, out_parts, middle, local)
    grad_q, grad_first, grad_rest = before
    rest = [shift(grad_rest[d - 1], -d) for d in range(1, shards)]

    half_wide = width // 2
    branch_all = jnp.concatenate([after(block, grad_first) for block in branches], axis=0)
    both_attended = jnp.concatenate(attended, axis=1)
    wo_sent = weight_grad(both_attended, None, branch_all, 1, half_wide, 1, (), "out_grad_other")
    wo_sent = [swap(wo_sent[0], 1)]
    wo_term = weight_grad(both_attended, None, branch_all, 0, half_wide, 1, (wo_sent,), "out_grad")[0]
    wo_terms = out_sends(index, wo_term)
    wo_parts = plane_send(wo_terms)
    wo_wide = out_block_call(index, wo_parts, shards)
    grad_first = after(grad_first, wo_terms[0], *out_parts[1:3])
    grad_qkv = grad_qkv_call(grad_q, grad_first, rest, cosine, sine)

    def qkv_grad(n, side, added, name):
        return weight_grad(xhat, side, grad_qkv[n], 0, qkv_width, 1, added, name)

    qkv_sent = [swap(qkv_grad(n, 1, (), "qkv_grad_other")[0], 1) for n in (1, 0)]
    qkv_sent[0] = after(qkv_sent[0], *wo_parts[1:], out_parts[3])
    qkv_second = [swap(qkv_grad(1, 0, ([qkv_sent[0]],), "qkv_grad")[0], 4)]
    back_terms = [(grad_qkv[n], qkv_own[n], qkv_other[n], 0) for n in range(PAIR)]
    back_parts = parts_call(back_terms, rows, True, "qkv_back")
    e_one = plane_send(back_parts)
    qkv_sent[1] = after(qkv_sent[1], output, back_parts[0])
    qkv_term = qkv_grad(0, 0, ([qkv_sent[1]], qkv_second), "qkv_grad")[0]
    at_kept = reduced(after(jnp.concatenate([qkv_term, wo_wide], axis=1), gu_kept))

    down_mine = plane_gather(after(down_kept, qkv_term))
    down_theirs = [swap(part, 1) for part in down_mine]
    down_out = rows_result(index, mixed(down_mine, down_theirs), local, "down_result")
    grad_input = grad_input_call(index, e_one, x, grad_middle, local)

    gu_mine = plane_gather_forward(gu_kept)
    gu_mine = gu_mine[:3] + [jnp.concatenate(gu_mine[3:], axis=0)]
    gu_theirs = [swap(part, 1) for part in gu_mine]
    gu_out = feedforward_result(index, 0, gu_mine, gate_weight, up_weight, gain_two, ff_local, None)
    gu_out = feedforward_result(index, 1, gu_theirs, gate_weight, up_weight, gain_two, ff_local, gu_out)
    at_mine = [at_kept] + [after(piece, gu_out[0]) for piece in plane_gather(at_kept)[1:]]
    at_pieces = mixed(at_mine, [swap(piece, 1) for piece in at_mine])
    wo_out = out_result(index, at_pieces, local, width, qkv_width)
    q_out, k_out, v_out, gain_one_sums = qkv_result(
        index, at_pieces, query_weight, key_weight, value_weight, gain_one
    )
    return (
        output,
        grad_input,
        jnp.sum(gain_one_sums, axis=1),
        q_out,
        k_out,
        v_out,
        wo_out,
        jnp.sum(gu_out[2], axis=1),
        gu_out[0],
        gu_out[1],
        down_out,
    )


def solution(mesh):
    return jax.shard_map(
        per_device,
        mesh=mesh,
        in_specs=(
            P(("replica", "shard"), None),
            P("shard"),
            P("shard", None),
            P("shard", None),
            P("shard", None),
            P("shard", None),
            P("shard"),
            P("shard", None),
            P("shard", None),
            P("shard", None),
            P(("replica", "shard"), None),
        ),
        out_specs=(
            P(("replica", "shard"), None),
            P(("replica", "shard"), None),
            P("shard"),
            P("shard", None),
            P("shard", None),
            P("shard", None),
            P("shard", None),
            P("shard"),
            P("shard", None),
            P("shard", None),
            P("shard", None),
        ),
        check_vma=False,
    )
```

```python
import functools

import jax
import jax.numpy as jnp
from jax import lax
from jax.experimental import pallas as pl
from jax.experimental.pallas import tpu as pltpu
from jax.sharding import PartitionSpec as P

HEADS = 32
KV_HEADS = 4
HEAD = 64
GROUP = HEADS // KV_HEADS
CHIPS = 4
PIECES = 2 * CHIPS
PAIR = 2
LANES = 128

norm_eps = 1e-05
rope_base = 10000.0
masked_score = -1e30

f32 = jnp.float32
bf16 = jnp.bfloat16
VMEM = pltpu.VMEM
NT = (((1,), (1,)), ((), ()))
TN = (((0,), (0,)), ((), ()))


def dot(left, right):
    return jnp.dot(left, right, preferred_element_type=f32)


def dot_nt(left, right):
    return lax.dot_general(left, right, NT, preferred_element_type=f32)


def dot_tn(left, right):
    return lax.dot_general(left, right, TN, preferred_element_type=f32)


def shape(dims, kind):
    return jax.ShapeDtypeStruct(dims, kind)


def whole():
    return pl.BlockSpec(memory_space=VMEM)


def kernel_call(body, out_shape, in_specs, out_specs, operands, *, index=None, grid=(), scratch=(),
                moved=0, aliases=None, name=None):
    params = pltpu.CompilerParams(
        vmem_limit_bytes=52 * 2**20, dimension_semantics=("arbitrary",) * len(grid)
    )
    cost = pl.CostEstimate(flops=0, bytes_accessed=int(moved), transcendentals=0)
    common = dict(
        out_shape=out_shape,
        compiler_params=params,
        cost_estimate=cost,
        input_output_aliases=aliases or {},
        name=name,
    )
    if index is None:
        spec = pl.GridSpec(grid=grid, in_specs=in_specs, out_specs=out_specs, scratch_shapes=scratch)
        return pl.pallas_call(body, grid_spec=spec, **common)(*operands)
    spec = pltpu.PrefetchScalarGridSpec(
        num_scalar_prefetch=1, grid=grid, in_specs=in_specs, out_specs=out_specs,
        scratch_shapes=scratch,
    )
    return pl.pallas_call(body, grid_spec=spec, **common)(index, *operands)


def swap(value, mask):
    size = lax.axis_size("replica")
    return lax.ppermute(value, "replica", [(i, i ^ mask) for i in range(size)])


def shift(value, step):
    size = lax.axis_size("shard")
    pairs = [(i, i + step) for i in range(size) if 0 <= i + step < size]
    return lax.ppermute(value, "shard", pairs)


def plane_gather(value):
    return [value] + [swap(value, 2 * m) for m in range(1, CHIPS)]


def plane_gather_forward(value):
    middle = value.shape[0] // 2
    across, along = swap(value, 2), swap(value, 4)
    return [value, across, along, swap(across[:middle], 4), swap(along[middle:], 2)]


def plane_send(parts):
    return [parts[0]] + [swap(parts[m], 2 * m) for m in range(1, len(parts))]


def group_of(chip):
    return 2 * (chip & 1) + (chip >> 1)


def after(value, *others):
    return lax.optimization_barrier((value, *others))[0]


def attention_block_body(local, group_shards, index, q, k, v, o, gain, out, wo_out):
    scale = gain[:, :1]
    q_width = GROUP * HEAD
    cut = local // CHIPS
    for chip in range(CHIPS):

        group = group_of(chip)

        @pl.when(index[0] == chip)
        def _(group=group):
            parts = []
            for m in range(CHIPS):
                for s in range(group_shards):
                    start = group * q_width + s * local + (m ^ chip) * cut
                    parts.append(q[:, start : start + cut])
            parts.append(k[:, group * HEAD : (group + 1) * HEAD])
            parts.append(v[:, group * HEAD : (group + 1) * HEAD])
            wide = jnp.concatenate([part.astype(f32) for part in parts], axis=1)
            out[...] = (wide * scale).astype(bf16)

    half = local // 2
    shards = o.shape[1] // local
    for core in range(2):

        @pl.when(index[1] == core)
        def _():
            for s in range(shards):
                piece = o[:, s * local + core * half : s * local + (core + 1) * half]
                wo_out[:, s * half : (s + 1) * half] = piece


def attention_block(index, query, key, value, output, gain):
    local, width = query.shape
    half = local // 2
    shards = width // local
    return kernel_call(
        functools.partial(attention_block_body, local, shards // CHIPS),
        (
            shape((half, GROUP * HEAD + 2 * HEAD), bf16),
            shape((local // CHIPS, width // 2), bf16),
        ),
        [
            pl.BlockSpec((half, width), lambda i, n: (n[1], 0)),
            pl.BlockSpec((half, key.shape[1]), lambda i, n: (n[1], 0)),
            pl.BlockSpec((half, key.shape[1]), lambda i, n: (n[1], 0)),
            pl.BlockSpec((local // CHIPS, width), lambda i, n: (n[0], 0)),
            pl.BlockSpec((half, LANES), lambda i, n: (n[1], 0)),
        ],
        (
            pl.BlockSpec((half, GROUP * HEAD + 2 * HEAD), lambda i, n: (0, 0)),
            pl.BlockSpec((local // CHIPS, width // 2), lambda i, n: (0, 0)),
        ),
        (query, key, value, output, gain),
        index=index,
        grid=(1,),
        name="attention_block",
    )


def feedforward_block_body(ff_local, cut, index, gate, up, gain, out):
    scale = gain[:, :1]
    shards = gate.shape[1] // ff_local
    width = shards * cut
    for chip in range(CHIPS):

        @pl.when(index[0] == chip)
        def _():
            for n, source in enumerate((gate, up)):
                parts = [
                    source[:, s * ff_local + chip * cut : s * ff_local + (chip + 1) * cut].astype(f32)
                    for s in range(shards)
                ]
                wide = jnp.concatenate(parts, axis=1)
                out[:, n * width : (n + 1) * width] = (wide * scale).astype(bf16)


def feedforward_block(index, gate, up, gain, ff_local):
    local, ff = gate.shape
    half = local // 2
    rows = 64
    steps = half // rows
    cut = ff_local // CHIPS
    width = 2 * (ff // CHIPS)
    return kernel_call(
        functools.partial(feedforward_block_body, ff_local, cut),
        shape((half, width), bf16),
        [
            pl.BlockSpec((rows, ff), lambda i, n: (n[1] * steps + i, 0)),
            pl.BlockSpec((rows, ff), lambda i, n: (n[1] * steps + i, 0)),
            pl.BlockSpec((rows, LANES), lambda i, n: (n[1] * steps + i, 0)),
        ],
        pl.BlockSpec((rows, width), lambda i, n: (i, 0)),
        (gate, up, gain),
        index=index,
        grid=(steps,),
        name="feedforward_block",
    )


def own_first_body(local, index, *refs):
    count = len(refs) // 2
    half = local // 2
    for core in range(2):

        @pl.when(index[1] == core)
        def _():
            for source, out in zip(refs[:count], refs[count:]):
                shards = source.shape[1] // local
                sides = out.shape[1] // (shards * half)
                for side in range(sides):
                    for s in range(shards):
                        start = s * local + (core ^ side) * half
                        spot = (side * shards + s) * half
                        out[:, spot : spot + half] = source[:, start : start + half]


def own_first(index, sources, local, halves=2):
    return kernel_call(
        functools.partial(own_first_body, local),
        tuple(shape((v.shape[0], v.shape[1] * halves // 2), bf16) for v in sources),
        [pl.BlockSpec(v.shape, lambda i, n: (0, 0)) for v in sources],
        tuple(
            pl.BlockSpec((v.shape[0], v.shape[1] * halves // 2), lambda i, n: (0, 0)) for v in sources
        ),
        tuple(sources),
        index=index,
        grid=(1,),
        name="own_first",
    )


def down_block_body(local, index, source, out):
    own_first_body(local, index, source, out)


def down_block(index, down, local):
    ff_local, width = down.shape
    cut = ff_local // CHIPS
    return kernel_call(
        functools.partial(down_block_body, local),
        shape((cut, width // 2), bf16),
        [pl.BlockSpec((cut, width), lambda i, n: (n[0], 0))],
        pl.BlockSpec((cut, width // 2), lambda i, n: (0, 0)),
        (down,),
        index=index,
        grid=(1,),
        name="down_block",
    )


def part_sum(parts):
    total = parts[0][...]
    for part in parts[1:]:
        total = total + part[...].astype(f32)
    return total


def mean_of(values):
    return jnp.mean(values, axis=1, keepdims=True)


def middle_body(*refs):
    parts, (x, middle, two) = refs[:PAIR], refs[PAIR:]
    total = x[...].astype(f32) + part_sum(parts)
    middle[...] = total
    two[...] = (total * lax.rsqrt(mean_of(total * total) + norm_eps)).astype(bf16)


def middle_call(parts, x):
    return kernel_call(
        middle_body,
        (shape(x.shape, f32), shape(x.shape, bf16)),
        [whole()] * (PAIR + 1),
        (whole(), whole()),
        (*parts, x),
        name="middle",
    )


def norm_back(e, values):
    inverse = lax.rsqrt(mean_of(values * values) + norm_eps)
    return inverse * e - values * (inverse * inverse * inverse) * mean_of(e * values)


def grad_middle_body(*refs):
    parts, (middle, g, grad, low) = refs[:CHIPS], refs[CHIPS:]
    total = g[...].astype(f32) + norm_back(part_sum(parts), middle[...])
    grad[...] = total
    low[...] = total.astype(bf16)


def grad_middle_call(parts, middle, g):
    return kernel_call(
        grad_middle_body,
        (shape(g.shape, f32), shape(g.shape, bf16)),
        [whole()] * (CHIPS + 2),
        (whole(), whole()),
        (*parts, middle, g),
        name="grad_middle",
    )


def store_in_order(local, index, value, out):
    half = local // 2
    shards = out.shape[1] // local
    for core in range(2):

        @pl.when(index[1] == core)
        def _():
            for side in range(2):
                for s in range(shards):
                    spot = s * local + (core ^ side) * half
                    start = (side * shards + s) * half
                    out[:, spot : spot + half] = value[:, start : start + half].astype(bf16)


def output_body(local, index, *refs):
    parts, (middle, out) = refs[:CHIPS], refs[CHIPS:]
    store_in_order(local, index, middle[...] + part_sum(parts), out)


def output_call(index, parts, middle, local):
    spec = pl.BlockSpec(middle.shape, lambda i, n: (0, 0))
    return kernel_call(
        functools.partial(output_body, local),
        shape(middle.shape, bf16),
        [spec] * (CHIPS + 1),
        spec,
        (*parts, middle),
        index=index,
        grid=(1,),
        name="output",
    )


def grad_input_body(local, index, *refs):
    parts, (x, grad, out) = refs[:PAIR], refs[PAIR:]
    total = grad[...] + norm_back(part_sum(parts), x[...].astype(f32))
    store_in_order(local, index, total, out)


def grad_input_call(index, parts, x, grad, local):
    spec = pl.BlockSpec(x.shape, lambda i, n: (0, 0))
    return kernel_call(
        functools.partial(grad_input_body, local),
        shape(x.shape, bf16),
        [spec] * (PAIR + 2),
        spec,
        (*parts, x, grad),
        index=index,
        grid=(1,),
        name="grad_input",
    )


def grad_qkv_body(shards, grad_q, first, *refs):
    rest, (cosine, sine), outs = refs[: shards - 1], refs[shards - 1 : shards + 1], refs[shards + 1 :]
    total = first[...]
    for term in rest:
        total = total + term[...].astype(f32)
    rows = cosine.shape[1]
    width = GROUP * HEAD
    cos, sin = cosine[...], sine[...]
    for n, out in enumerate(outs):
        out[:, :width] = grad_q[:, n * width : (n + 1) * width]
        for m in range(PAIR):
            span = slice(m * rows, (m + 1) * rows)
            turned = total[span, n * 2 * HEAD : (n + 1) * 2 * HEAD].T
            k = turned[:HEAD]
            k = k * cos - half_rotated(k) * sin
            both = jnp.concatenate([k, turned[HEAD:]], axis=0)
            out[span, width:] = both.T.astype(bf16)


def grad_qkv_call(grad_q, first, rest, cosine, sine):
    tokens = grad_q.shape[0]
    return kernel_call(
        functools.partial(grad_qkv_body, len(rest) + 1),
        (shape((tokens, GROUP * HEAD + 2 * HEAD), bf16),) * PAIR,
        [whole()] * (len(rest) + 4),
        (whole(),) * PAIR,
        (grad_q, first, *rest, cosine, sine),
        name="grad_qkv",
    )


def out_sends_body(index, term, *outs):
    cut = outs[0].shape[0] // PAIR
    for row in range(2):

        @pl.when(index[0] >> 1 == row)
        def _():
            for n in range(PAIR):
                for m in range(CHIPS):
                    spot = (n * CHIPS + m) * cut
                    start = (n ^ row) * cut
                    outs[m ^ (2 * n)][start : start + cut, :] = term[spot : spot + cut, :]


def out_sends(index, term):
    rows, width = term.shape
    rows //= CHIPS
    return kernel_call(
        out_sends_body,
        (shape((rows, width), bf16),) * CHIPS,
        [pl.BlockSpec(term.shape, lambda i, n: (0, 0))],
        (pl.BlockSpec((rows, width), lambda i, n: (0, 0)),) * CHIPS,
        (term,),
        index=index,
        grid=(1,),
        name="out_sends",
    )


def out_block_body(shards, index, *refs):
    parts, out = refs[:CHIPS], refs[CHIPS]
    group_shards = shards // CHIPS
    cut = parts[0].shape[0] // (PAIR * group_shards)
    sums = [parts[m][...].astype(f32) + parts[m + 2][...].astype(f32) for m in range(2)]
    for side in range(2):

        @pl.when(index[0] & 1 == side)
        def _():
            for m in range(2):
                for n in range(PAIR * group_shards):
                    shard = (m ^ side) * PAIR * group_shards + n
                    rows = sums[m][n * cut : (n + 1) * cut].astype(bf16)
                    out[2 * shard * cut : (2 * shard + 1) * cut, :] = rows[:, :512]
                    out[(2 * shard + 1) * cut : (2 * shard + 2) * cut, :] = rows[:, 512:]


def out_block_call(index, parts, shards):
    rows, width = parts[0].shape
    return kernel_call(
        functools.partial(out_block_body, shards),
        shape((2 * PAIR * rows, width // 2), bf16),
        [pl.BlockSpec((rows, width), lambda i, n: (0, 0))] * CHIPS,
        pl.BlockSpec((2 * PAIR * rows, width // 2), lambda i, n: (0, 0)),
        tuple(parts),
        index=index,
        grid=(1,),
        name="out_block",
    )


def half_rotated(values):
    middle = values.shape[0] // 2
    return jnp.concatenate([-values[middle:], values[:middle]], axis=0)


def qkv_body(make, *refs):
    if make:
        xs, (own, other, cosine, sine, queries, kv, xhat) = refs[:PAIR], refs[PAIR:]
        rows, width = xs[0].shape
        for m in range(PAIR):
            x = xs[m][...].astype(f32)
            inverse = lax.rsqrt(mean_of(x * x) + norm_eps)
            xhat[m * rows : (m + 1) * rows, :] = (x * inverse).astype(bf16)
    else:
        xhat, own, other, cosine, sine, queries, kv = refs
        rows, width = cosine.shape[1], xhat.shape[1]
    cos, sin = cosine[...], sine[...]
    total = dot(xhat[:, : width // 2], own[...]) + dot(xhat[:, width // 2 :], other[...])
    for m in range(PAIR):
        turned = total[m * rows : (m + 1) * rows].T
        for h in range(GROUP + 1):
            u = turned[h * HEAD : (h + 1) * HEAD]
            u = u * cos + half_rotated(u) * sin
            if h < GROUP:
                queries[m, :, h * rows : (h + 1) * rows] = (u * HEAD ** (-0.5)).astype(bf16)
            else:
                both = jnp.concatenate([u, turned[(h + 1) * HEAD :]], axis=0)
                kv[m * rows : (m + 1) * rows, :] = both.T.astype(bf16)


def qkv_call(xs, own, other, cosine, sine):
    make = isinstance(xs, list)
    rows = cosine.shape[1]
    tokens = PAIR * rows
    outs = (shape((PAIR, HEAD, GROUP * rows), bf16), shape((tokens, 2 * HEAD), bf16))
    if make:
        outs = outs + (shape((tokens, xs[0].shape[1]), bf16),)
    operands = (*(xs if make else (xs,)), own, other, cosine, sine)
    return kernel_call(
        functools.partial(qkv_body, make),
        outs,
        [whole()] * len(operands),
        tuple(whole() for _ in outs),
        operands,
        name="qkv",
    )


def out_rows_body(index, *refs):
    pieces, out = refs[:CHIPS], refs[CHIPS]
    cut = pieces[0].shape[0] // PAIR
    for row in range(2):

        @pl.when(index[0] >> 1 == row)
        def _():
            for n in range(PAIR):
                for m in range(CHIPS):
                    spot = (n * CHIPS + m) * cut
                    start = (n ^ row) * cut
                    out[spot : spot + cut, :] = pieces[m ^ (2 * n)][start : start + cut, :]


def out_rows_call(index, pieces):
    rows, width = pieces[0].shape
    return kernel_call(
        out_rows_body,
        shape((CHIPS * rows, width), bf16),
        [pl.BlockSpec((rows, width), lambda i, n: (0, 0))] * CHIPS,
        pl.BlockSpec((CHIPS * rows, width), lambda i, n: (0, 0)),
        tuple(pieces),
        index=index,
        grid=(1,),
        name="out_rows",
    )


LANE_HEADS = 4


def own_block_bias(rows):
    key = lax.broadcasted_iota(jnp.int32, (rows, rows), 0)
    mine = lax.broadcasted_iota(jnp.int32, (rows, rows), 1)
    return jnp.where(key <= mine, 0.0, masked_score)


def set_bias(bias):
    rows = bias.shape[0]
    value = own_block_bias(rows)
    for h in range(LANE_HEADS):
        bias[:, h * rows : (h + 1) * rows] = value


def far_bias(depth, d):
    return jnp.where(d <= depth, 0.0, masked_score) if d else 0.0


def attention_body(shards, index, queries, *refs):
    kvs = refs[:shards]
    turned_out, out, stats, bias, terms, out_turned = refs[shards:]
    rows = bias.shape[0]
    wide = LANE_HEADS * rows

    @pl.when(pl.program_id(0) == 0)
    def _():
        set_bias(bias)

    ks = [kv[:, :HEAD] for kv in kvs]
    v_turned = jnp.concatenate([kv[...] for kv in kvs], axis=0).astype(f32).T[HEAD:].astype(bf16)
    for n in range(GROUP // LANE_HEADS):
        span = slice(n * wide, (n + 1) * wide)
        q = queries[0, :, span]
        scores, top = [], None
        for d in range(shards):
            score = dot(ks[d], q)
            if d == 0:
                score = score + bias[...]
            scores.append(score)
            highest = jnp.max(score, axis=0, keepdims=True) + far_bias(index[2], d)
            top = highest if top is None else jnp.maximum(top, highest)
        total = None
        for d in range(shards):
            term = jnp.exp(scores[d] - (top - far_bias(index[2], d)))
            part = jnp.sum(term, axis=0, keepdims=True)
            total = part if total is None else total + part
            terms[d * rows : (d + 1) * rows, :] = term.astype(bf16)
        out_turned[:, span] = dot(v_turned, terms[...]) / total
        stats[0, :, span] = top + jnp.log(total)
    turned_out[0] = out_turned[...].astype(bf16)
    straight = out_turned[...].T
    for h in range(GROUP):
        out[:, h * HEAD : (h + 1) * HEAD] = straight[h * rows : (h + 1) * rows].astype(bf16)


def attention_call(index, queries, kvs):
    chips, _, wide = queries.shape
    rows = wide // GROUP
    shards = len(kvs)
    keys = shards * rows
    block = pl.BlockSpec((1, HEAD, wide), lambda i, n: (i, 0, 0))
    return kernel_call(
        functools.partial(attention_body, shards),
        (
            shape((chips, HEAD, wide), bf16),
            shape((chips * rows, GROUP * HEAD), bf16),
            shape((chips, 1, wide), f32),
        ),
        [block] + [pl.BlockSpec((rows, 2 * HEAD), lambda i, n: (i, 0))] * shards,
        (
            block,
            pl.BlockSpec((rows, GROUP * HEAD), lambda i, n: (i, 0)),
            pl.BlockSpec((1, 1, wide), lambda i, n: (i, 0, 0)),
        ),
        (queries, *kvs),
        index=index,
        grid=(chips,),
        scratch=(
            VMEM((rows, LANE_HEADS * rows), f32),
            VMEM((keys, LANE_HEADS * rows), bf16),
            VMEM((HEAD, wide), f32),
        ),
        name="attention",
    )


def attention_back_body(shards, index, branch, wo_own, wo_other, cosine, sine, *refs):
    per_group = 3 + shards
    inputs = [refs[n * per_group : (n + 1) * per_group] for n in range(PAIR)]
    grad_q, grad_first, grad_rest = refs[-7:-4]
    bias, probs_low, grads_low, grad_lanes = refs[-4:]
    rows = bias.shape[0]
    wide = LANE_HEADS * rows
    width = branch.shape[1]
    set_bias(bias)
    cos, sin = cosine[...], sine[...]
    for n, (queries, turned_out, stats, *kvs) in enumerate(inputs):
        heads = slice(n * GROUP * HEAD, (n + 1) * GROUP * HEAD)
        grad_out = dot_nt(wo_own[heads, :], branch[:, : width // 2])
        grad_out = grad_out + dot_nt(wo_other[heads, :], branch[:, width // 2 :])
        for h in range(GROUP):
            grad_lanes[:, h * rows : (h + 1) * rows] = grad_out[h * HEAD : (h + 1) * HEAD].astype(bf16)
        ks = [kv[:, :HEAD] for kv in kvs]
        vs = [kv[:, HEAD:] for kv in kvs]
        k_turned = jnp.concatenate([kv[...] for kv in kvs], axis=0).astype(f32).T[:HEAD].astype(bf16)
        k_total, v_total, parts = None, None, []
        for c in range(GROUP // LANE_HEADS):
            span = slice(c * wide, (c + 1) * wide)
            q, mine = queries[0, :, span], grad_lanes[:, span]
            delta = jnp.sum(
                mine.astype(f32) * turned_out[0, :, span].astype(f32), axis=0, keepdims=True
            )
            for d in range(shards):
                score = dot(ks[d], q)
                if d == 0:
                    score = score + bias[...]
                probs = jnp.exp(score - (stats[0, :, span] - far_bias(index[2], d)))
                grad_scores = probs * (dot(vs[d], mine) - delta)
                probs_low[d * rows : (d + 1) * rows, :] = probs.astype(bf16)
                grads_low[d * rows : (d + 1) * rows, :] = grad_scores.astype(bf16)
            u = dot(k_turned, grads_low[...]) * HEAD ** (-0.5)
            parts.append(u * cos - half_rotated(u) * sin)
            k_term = dot_nt(grads_low[...], q)
            v_term = dot_nt(probs_low[...], mine)
            k_total = k_term if k_total is None else k_total + k_term
            v_total = v_term if v_total is None else v_total + v_term
        straight = jnp.concatenate(parts, axis=1).T
        for h in range(GROUP):
            spot = (n * GROUP + h) * HEAD
            grad_q[:, spot : spot + HEAD] = straight[h * rows : (h + 1) * rows].astype(bf16)
        both = jnp.concatenate([k_total, v_total], axis=1)
        spot = slice(n * 2 * HEAD, (n + 1) * 2 * HEAD)
        grad_first[:, spot] = both[:rows, :]
        for d in range(1, shards):
            grad_rest[d - 1, :, spot] = both[d * rows : (d + 1) * rows, :].astype(bf16)


def attention_back_call(index, m, branch, wo_own, wo_other, cosine, sine, groups, before):
    chips, _, wide = groups[0][0].shape
    rows = wide // GROUP
    shards = len(groups[0][3])
    keys = shards * rows
    tokens = chips * rows
    block = pl.BlockSpec((1, HEAD, wide), lambda i, n: (m, 0, 0))
    in_specs = [whole()] * 5
    operands = [branch, wo_own, wo_other, jnp.tile(cosine, (1, LANE_HEADS)), jnp.tile(sine, (1, LANE_HEADS))]
    for queries, turned, stats, kvs in groups:
        in_specs += [block, block, pl.BlockSpec((1, 1, wide), lambda i, n: (m, 0, 0))]
        in_specs += [pl.BlockSpec((rows, 2 * HEAD), lambda i, n: (m, 0))] * shards
        operands += [queries, turned, stats, *kvs]
    aliases = {}
    if before is not None:
        aliases = {1 + len(operands) + n: n for n in range(3)}
        in_specs += [pl.BlockSpec(memory_space=pl.ANY)] * 3
        operands += list(before)
    outs = (
        shape((tokens, PAIR * GROUP * HEAD), bf16),
        shape((tokens, PAIR * 2 * HEAD), f32),
        shape((shards - 1, tokens, PAIR * 2 * HEAD), bf16),
    )
    out_specs = (
        pl.BlockSpec((rows, PAIR * GROUP * HEAD), lambda i, n: (m, 0)),
        pl.BlockSpec((rows, PAIR * 2 * HEAD), lambda i, n: (m, 0)),
        pl.BlockSpec((shards - 1, rows, PAIR * 2 * HEAD), lambda i, n: (0, m, 0)),
    )
    return kernel_call(
        functools.partial(attention_back_body, shards),
        outs,
        in_specs,
        out_specs,
        tuple(operands),
        index=index,
        grid=(1,),
        scratch=(
            VMEM((rows, LANE_HEADS * rows), f32),
            VMEM((keys, LANE_HEADS * rows), bf16),
            VMEM((keys, LANE_HEADS * rows), bf16),
            VMEM((HEAD, wide), bf16),
        ),
        aliases=aliases,
        name="attention_back",
    )


def parts_body(steps, transposed, count, *refs):
    lefts, owns, others = refs[:count], refs[count : 2 * count], refs[2 * count : 3 * count]
    outs = refs[3 * count :]
    rows = outs[0].shape[0]
    step = pl.program_id(0)

    def run(weights):
        total = None
        for left, weight in zip(lefts, weights):
            term = (dot_nt if transposed else dot)(left[...], weight[...])
            total = term if total is None else total + term
        for m, out in enumerate(outs):
            out[...] = total[m * rows : (m + 1) * rows, :].astype(out.dtype)

    @pl.when(step < steps)
    def _():
        run(owns)

    @pl.when(step >= steps)
    def _():
        run(others)


def parts_call(terms, rows, transposed, name):
    tokens = terms[0][0].shape[0]
    half = terms[0][1].shape[0] if transposed else terms[0][1].shape[1]
    tile = 256
    steps = half // tile
    last = steps - 1
    specs = [pl.BlockSpec((tokens, term[0].shape[1]), lambda j: (0, 0)) for term in terms]
    for side in range(2):
        for left, _, _, spot in terms:
            depth = left.shape[1]

            def place(side, spot, j):
                step = jnp.maximum(j - steps, 0) if side else jnp.minimum(j, last)
                return (step, spot) if transposed else (spot, step)

            block = (tile, depth) if transposed else (depth, tile)
            specs.append(pl.BlockSpec(block, functools.partial(place, side, spot)))
    count = tokens // rows
    return kernel_call(
        functools.partial(parts_body, steps, transposed, len(terms)),
        tuple(shape((rows, 2 * half), f32 if m == 0 else bf16) for m in range(count)),
        specs,
        tuple(pl.BlockSpec((rows, tile), lambda j: (0, j)) for _ in range(count)),
        (*(term[0] for term in terms), *(term[1] for term in terms), *(term[2] for term in terms)),
        grid=(2 * steps,),
        name=name,
    )


def gate_body(count, *refs):
    twos = refs[:count]
    gate_own, up_own, gate_other, up_other, act, for_gate, for_up, two_all = refs[count:]
    half = two_all.shape[1] // 2

    @pl.when(pl.program_id(0) == 0)
    def _():
        start = 0
        for two in twos:
            two_all[start : start + two.shape[0], :] = two[...]
            start += two.shape[0]

    own = jnp.concatenate([gate_own[...], up_own[...]], axis=1)
    other = jnp.concatenate([gate_other[...], up_other[...]], axis=1)
    both = dot(two_all[:, :half], own) + dot(two_all[:, half:], other)
    wide = gate_own.shape[1]
    gate, up = both[:, :wide], both[:, wide:]
    sig = 1.0 / (1.0 + jnp.exp(-gate))
    silu = gate * sig
    act[...] = (silu * up).astype(bf16)
    for_gate[...] = (up * sig * (1.0 + gate * (1.0 - sig))).astype(bf16)
    for_up[...] = silu.astype(bf16)


def gate_call(twos, own, other):
    rows, width = twos[0].shape
    tokens = CHIPS * rows
    half = width // 2
    ff = own.shape[1] // 2
    tile = LANES
    steps = ff // tile
    weight = [
        pl.BlockSpec((half, tile), lambda j: (0, j)),
        pl.BlockSpec((half, tile), lambda j: (0, j + steps)),
    ]
    column = pl.BlockSpec((tokens, tile), lambda j: (0, j))
    return kernel_call(
        functools.partial(gate_body, len(twos)),
        tuple(shape((tokens, ff), bf16) for _ in range(3)) + (shape((tokens, width), bf16),),
        [pl.BlockSpec(two.shape, lambda j: (0, 0)) for two in twos] + weight + weight,
        (column, column, column, pl.BlockSpec((tokens, width), lambda j: (0, 0))),
        (*twos, own, own, other, other),
        grid=(steps,),
        name="gate",
    )


def hidden_back_body(g, own, other, for_gate, for_up, grads):
    half = g.shape[1] // 2
    ff = own.shape[0]
    hidden = dot_nt(g[:, :half], own[...]) + dot_nt(g[:, half:], other[...])
    grads[:, :ff] = (hidden * for_gate[...].astype(f32)).astype(bf16)
    grads[:, ff:] = (hidden * for_up[...].astype(f32)).astype(bf16)


def hidden_back_call(g, own, other, for_gate, for_up):
    tokens, width = g.shape
    ff, half = own.shape
    block = tokens // 2
    row = lambda i: (i, 0)
    fixed = lambda i: (0, 0)
    return kernel_call(
        hidden_back_body,
        shape((tokens, 2 * ff), bf16),
        [
            pl.BlockSpec((block, width), row),
            pl.BlockSpec((ff, half), fixed),
            pl.BlockSpec((ff, half), fixed),
            pl.BlockSpec((block, ff), row),
            pl.BlockSpec((block, ff), row),
        ],
        pl.BlockSpec((block, 2 * ff), row),
        (g, own, other, for_gate, for_up),
        grid=(2,),
        name="hidden_back",
    )


def weight_grad_body(per, outputs, adds, left, right, *refs):
    added = [refs[n * outputs : (n + 1) * outputs] for n in range(adds)]
    outs, turned = refs[adds * outputs : -1], refs[-1]
    step = pl.program_id(0)

    @pl.when(step == 0)
    def _():
        turned[...] = left[...].T

    for n in range(outputs):

        @pl.when(step // per == n)
        def _(n=n):
            total = dot(turned[...], right[...])
            for terms in added:
                total = total + terms[n][...].astype(f32)
            outs[n][...] = total.astype(bf16)


def weight_grad(left, left_side, right, place, width, outputs, added, name):
    tokens = left.shape[0]
    rows = left.shape[1] // (1 if left_side is None else 2)
    tile = 256 if width % 256 == 0 else width
    per = width // tile
    first = place * width // tile
    side = left_side or 0

    def spot(n, j):
        return (0, jnp.clip(j - n * per, 0, per - 1))

    tiles = [pl.BlockSpec((rows, tile), functools.partial(spot, n)) for n in range(outputs)]
    return kernel_call(
        functools.partial(weight_grad_body, per, outputs, len(added)),
        tuple(shape((rows, width), bf16) for _ in range(outputs)),
        [
            pl.BlockSpec((tokens, rows), lambda j: (0, side)),
            pl.BlockSpec((tokens, tile), lambda j: (0, first + j)),
        ]
        + tiles * len(added),
        tuple(tiles),
        (left, right, *(term for terms in added for term in terms)),
        grid=(per * outputs,),
        scratch=(VMEM((rows, tokens), bf16),),
        name=name,
    )


def rows_result_body(local, index, *refs):
    pieces, out = refs[:PIECES], refs[PIECES]
    half = local // 2
    shards = out.shape[1] // local
    for m in range(CHIPS):
        for core in range(2):

            @pl.when((pl.program_id(0) == m) & (index[1] == core))
            def _():
                for side in range(2):
                    piece = pieces[2 * m + side]
                    for s in range(shards):
                        spot = s * local + (core ^ side) * half
                        out[:, spot : spot + half] = piece[:, s * half : (s + 1) * half].astype(f32)


def rows_result(index, pieces, local, name):
    cut, half_width = pieces[0].shape
    return kernel_call(
        functools.partial(rows_result_body, local),
        shape((CHIPS * cut, 2 * half_width), f32),
        [pl.BlockSpec((cut, half_width), lambda i, n: (0, 0))] * PIECES,
        pl.BlockSpec((cut, 2 * half_width), lambda i, n: (n[0] ^ i, 0)),
        tuple(pieces),
        index=index,
        grid=(CHIPS,),
        name=name,
    )


def out_result_body(local, base, index, *refs):
    pieces, out = refs[:PIECES], refs[PIECES]
    half = local // 2
    cut = local // CHIPS
    shards = out.shape[1] // local
    for m in range(CHIPS):
        for core in range(2):

            @pl.when((pl.program_id(0) == m) & (index[1] == core))
            def _():
                for side in range(2):
                    piece = pieces[2 * m + side]
                    for s in range(shards):
                        spot = s * local + (core ^ side) * half
                        row, column = (0, s * half) if s * half < 512 else (cut, s * half - 512)
                        column += base
                        out[:, spot : spot + half] = piece[row : row + cut, column : column + half].astype(f32)


def out_result(index, pieces, local, width, base):
    cut = local // CHIPS
    return kernel_call(
        functools.partial(out_result_body, local, base),
        shape((local, width), f32),
        [pl.BlockSpec(pieces[0].shape, lambda i, n: (0, 0))] * PIECES,
        pl.BlockSpec((cut, width), lambda i, n: (n[0] ^ i, 0)),
        tuple(pieces),
        index=index,
        grid=(CHIPS,),
        name="out_result",
    )


def lane_sum(value):
    total = value[:, :LANES]
    for n in range(1, value.shape[1] // LANES):
        total = total + value[:, n * LANES : (n + 1) * LANES]
    return total


def feedforward_result_body(ff_local, cut, index, *refs):
    pieces = refs[:CHIPS]
    gate_weight, up_weight, gain = refs[CHIPS : CHIPS + 3]
    gate_out, up_out, gain_out = refs[-3:]
    shards = gate_weight.shape[1] // ff_local
    width = shards * cut
    for chip in range(CHIPS):

        @pl.when(index[0] == chip)
        def _():
            @pl.loop(0, gate_out.shape[0] // 16)
            def _(n):
                rows = pl.ds(pl.multiple_of(n * 16, 16), 16)
                scale = gain[rows, :1]
                total = jnp.zeros((16, LANES), f32)
                for base, weight, out in ((0, gate_weight, gate_out), (width, up_weight, up_out)):
                    parts = []
                    for s in range(shards):
                        for owner in range(CHIPS):
                            start = base + s * cut
                            parts.append(pieces[owner ^ chip][rows, start : start + cut].astype(f32))
                    wide = jnp.concatenate(parts, axis=1)
                    total = total + lane_sum(wide * weight[rows, :].astype(f32))
                    out[rows, :] = wide * scale
                gain_out[rows, :] = total


def feedforward_result(index, side, pieces, gate_weight, up_weight, gain, ff_local, before):
    local, ff = gate_weight.shape
    half = local // 2
    rows = 64
    steps = half // rows
    row = lambda i, n: ((n[1] ^ side) * steps + i, 0)
    in_specs = [pl.BlockSpec((rows, pieces[0].shape[1]), lambda i, n: (i, 0))] * CHIPS
    in_specs += [pl.BlockSpec((rows, ff), row)] * 2 + [pl.BlockSpec((rows, LANES), row)]
    operands = (*pieces, gate_weight, up_weight, gain)
    aliases = {}
    if before is not None:
        aliases = {1 + len(operands) + n: n for n in range(3)}
        in_specs = in_specs + [pl.BlockSpec(memory_space=pl.ANY)] * 3
        operands = operands + tuple(before)
    return kernel_call(
        functools.partial(feedforward_result_body, ff_local, ff_local // CHIPS),
        (shape((local, ff), f32), shape((local, ff), f32), shape((local, LANES), f32)),
        in_specs,
        (pl.BlockSpec((rows, ff), row), pl.BlockSpec((rows, ff), row), pl.BlockSpec((rows, LANES), row)),
        operands,
        index=index,
        grid=(steps,),
        aliases=aliases,
        name="feedforward_result",
    )


def qkv_result_body(local, group_shards, index, *refs):
    pieces = refs[:PIECES]
    weights, gain = refs[PIECES : PIECES + 3], refs[PIECES + 3]
    outs, gain_out = refs[PIECES + 4 : PIECES + 7], refs[PIECES + 7]
    q_width = GROUP * HEAD
    cut = local // CHIPS
    scale = gain[:, :1]
    for chip in range(CHIPS):
        for side in range(2):

            @pl.when((index[0] == chip) & (pl.program_id(0) == side))
            def _():
                parts, k_parts, v_parts = [], [], []
                for group in range(CHIPS):
                    owner = (group >> 1) + 2 * (group & 1)
                    piece = pieces[2 * (owner ^ chip) + side]
                    for s in range(group_shards):
                        for j in range(CHIPS):
                            start = ((j ^ owner) * group_shards + s) * cut
                            parts.append(piece[:, start : start + cut].astype(f32))
                    k_parts.append(piece[:, q_width : q_width + HEAD].astype(f32))
                    v_parts.append(piece[:, q_width + HEAD : q_width + 2 * HEAD].astype(f32))
                total = jnp.zeros((gain.shape[0], LANES), f32)
                for part, weight, out in zip((parts, k_parts, v_parts), weights, outs):
                    wide = jnp.concatenate(part, axis=1)
                    total = total + lane_sum(wide * weight[...].astype(f32))
                    out[...] = wide * scale
                gain_out[...] = total


def qkv_result(index, pieces, query, key, value, gain):
    local, width = query.shape
    half = local // 2
    group_shards = width // local // CHIPS
    row = lambda i, n: (n[1] ^ i, 0)
    kv_width = key.shape[1]
    return kernel_call(
        functools.partial(qkv_result_body, local, group_shards),
        (
            shape((local, width), f32),
            shape((local, kv_width), f32),
            shape((local, kv_width), f32),
            shape((local, LANES), f32),
        ),
        [pl.BlockSpec(pieces[0].shape, lambda i, n: (0, 0))] * PIECES
        + [
            pl.BlockSpec((half, width), row),
            pl.BlockSpec((half, kv_width), row),
            pl.BlockSpec((half, kv_width), row),
            pl.BlockSpec((half, LANES), row),
        ],
        (
            pl.BlockSpec((half, width), row),
            pl.BlockSpec((half, kv_width), row),
            pl.BlockSpec((half, kv_width), row),
            pl.BlockSpec((half, LANES), row),
        ),
        (*pieces, query, key, value, gain),
        index=index,
        grid=(2,),
        name="qkv_result",
    )


def per_device(
    hidden_in,
    attention_gain,
    query_weight,
    key_weight,
    value_weight,
    output_weight,
    feedforward_gain,
    gate_weight,
    up_weight,
    down_weight,
    out_grad,
):
    rows, width = hidden_in.shape
    shards = lax.axis_size("shard")
    replicas = lax.axis_size("replica")
    place = lax.axis_index("replica")
    depth = lax.axis_index("shard")
    core = place & 1
    chip = (place >> 1) & (CHIPS - 1)
    local = width // shards
    half = local // 2
    ff_local = down_weight.shape[0]
    group_shards = shards // CHIPS
    q_width = GROUP * HEAD
    qkv_width = q_width + 2 * HEAD
    index = jnp.stack([chip, core, depth]).astype(jnp.int32)

    gain_one = jnp.broadcast_to(attention_gain.astype(f32)[:, None], (local, LANES))
    gain_two = jnp.broadcast_to(feedforward_gain.astype(f32)[:, None], (local, LANES))


    at_block, out_block = attention_block(
        index, query_weight, key_weight, value_weight, output_weight, gain_one
    )
    x = own_first(index, (after(hidden_in, at_block),), local)[0]
    xs = [x, swap(x, 2)]
    at_own = lax.all_gather(at_block, "shard", axis=0, tiled=True)
    out_all = lax.all_gather(out_block, "shard", axis=0, tiled=True)
    gu_block = feedforward_block(index, gate_weight, up_weight, after(gain_two, at_block), ff_local)
    gu_own = lax.all_gather(gu_block, "shard", axis=0, tiled=True)
    down_own = lax.all_gather(down_block(index, down_weight, local), "shard", axis=0, tiled=True)
    g = own_first(index, (after(out_grad, x),), local)[0]
    g_blocks = [g, swap(g, 2), swap(g, 4)]
    at_own = after(at_own, gu_block, xs[1], *g_blocks[1:])

    qkv_own = [at_own]
    qkv_own.append(swap(qkv_own[0], 4))
    qkv_other = [swap(qkv_own[0], 1)]
    inverse = rope_base ** (-jnp.arange(0, HEAD, 2, dtype=f32) / HEAD)
    places = (depth * rows + jnp.arange(rows, dtype=jnp.int32)).astype(f32)
    angles = inverse[:, None] * places[None, :]
    angles = jnp.concatenate([angles, angles], axis=0)
    cosine, sine = jnp.cos(angles), jnp.sin(angles)

    def shifted(kv):
        return [kv] + [shift(kv, d) for d in range(1, shards)]

    queries, kv, xhat = qkv_call(xs, qkv_own[0], qkv_other[0], cosine, sine)
    kvs = shifted(kv)
    qkv_own[1] = after(qkv_own[1], *kvs[1:])
    qkv_other.append(swap(qkv_own[1], 1))
    queries_two, kv_two = qkv_call(xhat, qkv_own[1], qkv_other[1], cosine, sine)
    kvs_two = shifted(kv_two)
    groups = [(queries, *attention_call(index, queries, kvs), kvs)]
    groups.append((queries_two, *attention_call(index, queries_two, kvs_two), kvs_two))
    attended = [group[2] for group in groups]
    groups = [(group[0], group[1], group[3], group[4]) for group in groups]

    out_all = after(out_all, qkv_own[1])
    x_place = chip & 1
    low_group = (chip >> 1) == 0
    pair_rows = PAIR * group_shards * half // 2

    def out_for(mask):
        return lax.dynamic_slice_in_dim(out_all, ((chip ^ mask) & 1) * pair_rows, pair_rows, 0)

    out_pieces = [out_for(0)] + [swap(out_for(m), 2 * m) for m in range(1, CHIPS)]
    wo_own = out_rows_call(index, [after(piece, *kvs_two[1:]) for piece in out_pieces])
    wo_other = swap(wo_own, 1)

    mid_terms = [(attended[n], wo_own, wo_other, n) for n in range(PAIR)]
    g_blocks.append(swap(after(g, *out_pieces[1:]), 6))
    mid_out = parts_call(mid_terms, rows, False, "attention_out")
    g_all = jnp.concatenate([after(block, mid_out[0]) for block in g_blocks], axis=0)
    middle, two = middle_call(plane_send(mid_out), after(x, g_all))
    twos = plane_gather_forward(two)

    gu_own = after(gu_own, *twos[1:])
    gu_other = swap(gu_own, 1)
    act, for_gate, for_up, two_all = gate_call(twos, gu_own, gu_other)

    def over_groups(kept):
        if replicas > PIECES:
            groups = [
                [e * PIECES + i for e in range(replicas // PIECES)] for i in range(PIECES)
            ]
            kept = lax.psum(kept, "replica", axis_index_groups=groups)
        return kept

    def reduced(term):
        kept = lax.psum_scatter(term, "shard", scatter_dimension=0, tiled=True)
        return over_groups(kept)

    def plane_pieces(kept):
        mine = plane_gather(kept)
        return mine, [swap(part, 1) for part in mine]

    def mixed(mine, theirs):
        return [part for pair in zip(mine, theirs) for part in pair]

    down_sent = weight_grad(act, None, g_all, 1, width // 2, 1, (), "down_grad_other")
    down_sent = [swap(down_sent[0], 1)]
    down_sent[0] = after(down_sent[0], down_own)
    down_term = weight_grad(act, None, g_all, 0, width // 2, 1, (down_sent,), "down_grad")[0]
    down_kept = reduced(down_term)
    down_other = swap(down_own, 1)

    grads = hidden_back_call(after(g_all, down_term), down_own, down_other, for_gate, for_up)
    grads_wide = grads.shape[1]
    gu_sent = weight_grad(two_all, 1, grads, 0, grads_wide, 1, (), "gate_grad_other")
    grads_late = after(grads, *gu_sent)
    gu_sent = [swap(gu_sent[0], 1)]
    e_terms = parts_call([(grads_late, gu_own, gu_other, 0)], rows, True, "feedforward_back")
    e_parts = plane_send(e_terms)
    gu_term = weight_grad(
        after(two_all, e_terms[0]), 0, grads, 0, grads_wide, 1, (gu_sent,), "gate_grad"
    )[0]
    gu_kept = reduced(gu_term)
    act_late = after(act, e_terms[0])
    out_terms = parts_call([(act_late, down_own, down_other, 0)], rows, False, "feedforward_out")

    middle_late = after(middle, out_terms[0], down_kept, gu_term)
    grad_middle, branch = grad_middle_call(e_parts, middle_late, g)
    branches = [branch, swap(branch, 2)]

    def back_block(m, block, before):
        return attention_back_call(index, m, block, wo_own, wo_other, cosine, sine, groups, before)

    before = back_block(0, branch, None)
    out_parts = plane_send(after(out_terms, branches[1], before[1]))
    before = back_block(1, after(branches[1], before[1]), before)
    output = output_call(index, out_parts, middle, local)
    grad_q, grad_first, grad_rest = before
    grad_rest = after(grad_rest, *out_parts[1:3])
    rest = [shift(grad_rest[d - 1], -d) for d in range(1, shards)]

    half_wide = width // 2
    branch_all = jnp.concatenate([after(block, grad_first) for block in branches], axis=0)
    both_attended = jnp.concatenate(attended, axis=1)
    wo_sent = weight_grad(both_attended, None, branch_all, 1, half_wide, 1, (), "out_grad_other")
    wo_sent = [swap(wo_sent[0], 1)]
    wo_term = weight_grad(both_attended, None, branch_all, 0, half_wide, 1, (wo_sent,), "out_grad")[0]
    wo_terms = out_sends(index, wo_term)
    wo_parts = plane_send(wo_terms)
    wo_wide = out_block_call(index, wo_parts, shards)
    grad_first = after(grad_first, wo_terms[0], *out_parts[1:])
    grad_qkv = grad_qkv_call(grad_q, grad_first, rest, cosine, sine)

    def qkv_grad(n, side, added, name):
        return weight_grad(xhat, side, grad_qkv[n], 0, qkv_width, 1, added, name)

    qkv_sent = [swap(qkv_grad(n, 1, (), "qkv_grad_other")[0], 1) for n in (1, 0)]
    back_terms = [(grad_qkv[n], qkv_own[n], qkv_other[n], 0) for n in range(PAIR)]
    qkv_second = qkv_grad(1, 0, ([qkv_sent[0]],), "qkv_grad")[0]
    qkv_term = qkv_grad(0, 0, ([qkv_sent[1]],), "qkv_grad")[0]
    at_term = jnp.concatenate([qkv_term, qkv_second, wo_wide], axis=1)
    at_kept = reduced(after(at_term, gu_kept))
    back_terms[0] = (after(grad_qkv[0], qkv_term, qkv_second), *back_terms[0][1:])
    back_parts = parts_call(back_terms, rows, True, "qkv_back")
    e_one = plane_send(back_parts)
    gu_mine = plane_gather_forward(gu_kept)
    gu_mine = gu_mine[:3] + [jnp.concatenate(gu_mine[3:], axis=0)]
    gu_theirs = [swap(part, 1) for part in gu_mine]
    gu_out = feedforward_result(index, 0, gu_mine, gate_weight, up_weight, gain_two, ff_local, None)
    gu_out = feedforward_result(index, 1, gu_theirs, gate_weight, up_weight, gain_two, ff_local, gu_out)

    down_mine = plane_gather(after(down_kept, *gu_mine[1:]))
    down_theirs = [swap(part, 1) for part in down_mine]
    down_out = rows_result(index, mixed(down_mine, down_theirs), local, "down_result")
    grad_input = grad_input_call(index, e_one, x, grad_middle, local)

    at_kept = after(at_kept, gu_out[0])
    second = swap(at_kept[:, qkv_width : 2 * qkv_width], 4)
    first = at_kept[:, :qkv_width].astype(f32) + second.astype(f32)
    at_kept = jnp.concatenate([first.astype(bf16), at_kept[:, 2 * qkv_width :]], axis=1)
    at_pieces = mixed(*plane_pieces(at_kept))
    wo_out = out_result(index, at_pieces, local, width, qkv_width)
    q_out, k_out, v_out, gain_one_sums = qkv_result(
        index, at_pieces, query_weight, key_weight, value_weight, gain_one
    )
    return (
        output,
        grad_input,
        jnp.sum(gain_one_sums, axis=1),
        q_out,
        k_out,
        v_out,
        wo_out,
        jnp.sum(gu_out[2], axis=1),
        gu_out[0],
        gu_out[1],
        down_out,
    )


def solution(mesh):
    return jax.shard_map(
        per_device,
        mesh=mesh,
        in_specs=(
            P(("replica", "shard"), None),
            P("shard"),
            P("shard", None),
            P("shard", None),
            P("shard", None),
            P("shard", None),
            P("shard"),
            P("shard", None),
            P("shard", None),
            P("shard", None),
            P(("replica", "shard"), None),
        ),
        out_specs=(
            P(("replica", "shard"), None),
            P(("replica", "shard"), None),
            P("shard"),
            P("shard", None),
            P("shard", None),
            P("shard", None),
            P("shard", None),
            P("shard"),
            P("shard", None),
            P("shard", None),
            P("shard", None),
        ),
        check_vma=False,
    )
```

```python
import functools

import jax
import jax.numpy as jnp
from jax import lax
from jax.experimental import pallas as pl
from jax.experimental.pallas import tpu as pltpu
from jax.sharding import PartitionSpec as P

HEADS = 32
KV_HEADS = 4
HEAD = 64
GROUP = HEADS // KV_HEADS
CHIPS = 4
PIECES = 2 * CHIPS
PAIR = 2
LANES = 128

norm_eps = 1e-05
rope_base = 10000.0
masked_score = -1e30

f32 = jnp.float32
bf16 = jnp.bfloat16
VMEM = pltpu.VMEM
NT = (((1,), (1,)), ((), ()))
TN = (((0,), (0,)), ((), ()))


def dot(left, right):
    return jnp.dot(left, right, preferred_element_type=f32)


def dot_nt(left, right):
    return lax.dot_general(left, right, NT, preferred_element_type=f32)


def dot_tn(left, right):
    return lax.dot_general(left, right, TN, preferred_element_type=f32)


def shape(dims, kind):
    return jax.ShapeDtypeStruct(dims, kind)


def whole():
    return pl.BlockSpec(memory_space=VMEM)


TIMES = {
    "attention_back": 13.0,
    "feedforward_out": 11.0,
    "grad_middle": 5.0,
    "out_grad_other": 5.0,
    "out_grad": 5.0,
    "out_sends": 3.0,
    "out_block": 3.0,
    "grad_qkv": 2.5,
    "qkv_grad_other": 2.2,
    "qkv_grad": 2.6,
    "qkv_back": 8.0,
    "output": 4.3,
    "grad_input": 4.2,
    "down_result": 8.0,
    "feedforward_result": 10.4,
    "qkv_result": 6.0,
    "out_result": 5.0,
}


def kernel_call(body, out_shape, in_specs, out_specs, operands, *, index=None, grid=(), scratch=(),
                aliases=None, name=None):
    params = pltpu.CompilerParams(
        vmem_limit_bytes=52 * 2**20, dimension_semantics=("arbitrary",) * len(grid)
    )
    moved = int(TIMES.get(name, 0.0) * 3.69e6)
    cost = pl.CostEstimate(flops=0, bytes_accessed=moved, transcendentals=0)
    common = dict(
        out_shape=out_shape,
        compiler_params=params,
        cost_estimate=cost,
        input_output_aliases=aliases or {},
        name=name,
    )
    if index is None:
        spec = pl.GridSpec(grid=grid, in_specs=in_specs, out_specs=out_specs, scratch_shapes=scratch)
        return pl.pallas_call(body, grid_spec=spec, **common)(*operands)
    spec = pltpu.PrefetchScalarGridSpec(
        num_scalar_prefetch=1, grid=grid, in_specs=in_specs, out_specs=out_specs,
        scratch_shapes=scratch,
    )
    return pl.pallas_call(body, grid_spec=spec, **common)(index, *operands)


def swap(value, mask):
    size = lax.axis_size("replica")
    return lax.ppermute(value, "replica", [(i, i ^ mask) for i in range(size)])


def shift(value, step):
    size = lax.axis_size("shard")
    pairs = [(i, i + step) for i in range(size) if 0 <= i + step < size]
    return lax.ppermute(value, "shard", pairs)


def plane_gather(value):
    return [value] + [swap(value, 2 * m) for m in range(1, CHIPS)]


def plane_gather_forward(value):
    middle = value.shape[0] // 2
    across, along = swap(value, 2), swap(value, 4)
    return [value, across, along, swap(across[:middle], 4), swap(along[middle:], 2)]


def plane_send(parts):
    return [parts[0]] + [swap(parts[m], 2 * m) for m in range(1, len(parts))]


def group_of(chip):
    return 2 * (chip & 1) + (chip >> 1)


def after(value, *others):
    return lax.optimization_barrier((value, *others))[0]


def attention_block_body(local, group_shards, index, q, k, v, o, gain, out, wo_out):
    scale = gain[:, :1]
    q_width = GROUP * HEAD
    cut = local // CHIPS
    for chip in range(CHIPS):

        group = group_of(chip)

        @pl.when(index[0] == chip)
        def _(group=group):
            parts = []
            for m in range(CHIPS):
                for s in range(group_shards):
                    start = group * q_width + s * local + (m ^ chip) * cut
                    parts.append(q[:, start : start + cut])
            parts.append(k[:, group * HEAD : (group + 1) * HEAD])
            parts.append(v[:, group * HEAD : (group + 1) * HEAD])
            wide = jnp.concatenate([part.astype(f32) for part in parts], axis=1)
            out[...] = (wide * scale).astype(bf16)

    half = local // 2
    shards = o.shape[1] // local
    for core in range(2):

        @pl.when(index[1] == core)
        def _():
            for s in range(shards):
                piece = o[:, s * local + core * half : s * local + (core + 1) * half]
                wo_out[:, s * half : (s + 1) * half] = piece


def attention_block(index, query, key, value, output, gain):
    local, width = query.shape
    half = local // 2
    shards = width // local
    return kernel_call(
        functools.partial(attention_block_body, local, shards // CHIPS),
        (
            shape((half, GROUP * HEAD + 2 * HEAD), bf16),
            shape((local // CHIPS, width // 2), bf16),
        ),
        [
            pl.BlockSpec((half, width), lambda i, n: (n[1], 0)),
            pl.BlockSpec((half, key.shape[1]), lambda i, n: (n[1], 0)),
            pl.BlockSpec((half, key.shape[1]), lambda i, n: (n[1], 0)),
            pl.BlockSpec((local // CHIPS, width), lambda i, n: (n[0], 0)),
            pl.BlockSpec((half, LANES), lambda i, n: (n[1], 0)),
        ],
        (
            pl.BlockSpec((half, GROUP * HEAD + 2 * HEAD), lambda i, n: (0, 0)),
            pl.BlockSpec((local // CHIPS, width // 2), lambda i, n: (0, 0)),
        ),
        (query, key, value, output, gain),
        index=index,
        grid=(1,),
        name="attention_block",
    )


def feedforward_block_body(ff_local, cut, index, gate, up, gain, out):
    scale = gain[:, :1]
    shards = gate.shape[1] // ff_local
    width = shards * cut
    for chip in range(CHIPS):

        @pl.when(index[0] == chip)
        def _():
            for n, source in enumerate((gate, up)):
                parts = [
                    source[:, s * ff_local + chip * cut : s * ff_local + (chip + 1) * cut].astype(f32)
                    for s in range(shards)
                ]
                wide = jnp.concatenate(parts, axis=1)
                out[:, n * width : (n + 1) * width] = (wide * scale).astype(bf16)


def feedforward_block(index, gate, up, gain, ff_local):
    local, ff = gate.shape
    half = local // 2
    rows = 64
    steps = half // rows
    cut = ff_local // CHIPS
    width = 2 * (ff // CHIPS)
    return kernel_call(
        functools.partial(feedforward_block_body, ff_local, cut),
        shape((half, width), bf16),
        [
            pl.BlockSpec((rows, ff), lambda i, n: (n[1] * steps + i, 0)),
            pl.BlockSpec((rows, ff), lambda i, n: (n[1] * steps + i, 0)),
            pl.BlockSpec((rows, LANES), lambda i, n: (n[1] * steps + i, 0)),
        ],
        pl.BlockSpec((rows, width), lambda i, n: (i, 0)),
        (gate, up, gain),
        index=index,
        grid=(steps,),
        name="feedforward_block",
    )


def own_first_body(local, index, *refs):
    count = len(refs) // 2
    half = local // 2
    for core in range(2):

        @pl.when(index[1] == core)
        def _():
            for source, out in zip(refs[:count], refs[count:]):
                shards = source.shape[1] // local
                sides = out.shape[1] // (shards * half)
                for side in range(sides):
                    for s in range(shards):
                        start = s * local + (core ^ side) * half
                        spot = (side * shards + s) * half
                        out[:, spot : spot + half] = source[:, start : start + half]


def own_first(index, sources, local, halves=2):
    return kernel_call(
        functools.partial(own_first_body, local),
        tuple(shape((v.shape[0], v.shape[1] * halves // 2), bf16) for v in sources),
        [pl.BlockSpec(v.shape, lambda i, n: (0, 0)) for v in sources],
        tuple(
            pl.BlockSpec((v.shape[0], v.shape[1] * halves // 2), lambda i, n: (0, 0)) for v in sources
        ),
        tuple(sources),
        index=index,
        grid=(1,),
        name="own_first",
    )


def down_block_body(local, index, source, out):
    own_first_body(local, index, source, out)


def down_block(index, down, local):
    ff_local, width = down.shape
    cut = ff_local // CHIPS
    return kernel_call(
        functools.partial(down_block_body, local),
        shape((cut, width // 2), bf16),
        [pl.BlockSpec((cut, width), lambda i, n: (n[0], 0))],
        pl.BlockSpec((cut, width // 2), lambda i, n: (0, 0)),
        (down,),
        index=index,
        grid=(1,),
        name="down_block",
    )


def part_sum(parts):
    total = parts[0][...]
    for part in parts[1:]:
        total = total + part[...].astype(f32)
    return total


def mean_of(values):
    return jnp.mean(values, axis=1, keepdims=True)


def middle_body(*refs):
    parts, (x, middle, two) = refs[:PAIR], refs[PAIR:]
    total = x[...].astype(f32) + part_sum(parts)
    middle[...] = total
    two[...] = (total * lax.rsqrt(mean_of(total * total) + norm_eps)).astype(bf16)


def middle_call(parts, x):
    return kernel_call(
        middle_body,
        (shape(x.shape, f32), shape(x.shape, bf16)),
        [whole()] * (PAIR + 1),
        (whole(), whole()),
        (*parts, x),
        name="middle",
    )


def norm_back(e, values):
    inverse = lax.rsqrt(mean_of(values * values) + norm_eps)
    return inverse * e - values * (inverse * inverse * inverse) * mean_of(e * values)


def grad_middle_body(*refs):
    parts, (middle, g, grad, low) = refs[:CHIPS], refs[CHIPS:]
    total = g[...].astype(f32) + norm_back(part_sum(parts), middle[...])
    grad[...] = total
    low[...] = total.astype(bf16)


def grad_middle_call(parts, middle, g):
    return kernel_call(
        grad_middle_body,
        (shape(g.shape, f32), shape(g.shape, bf16)),
        [whole()] * (CHIPS + 2),
        (whole(), whole()),
        (*parts, middle, g),
        name="grad_middle",
    )


def store_in_order(local, index, value, out):
    half = local // 2
    shards = out.shape[1] // local
    for core in range(2):

        @pl.when(index[1] == core)
        def _():
            for side in range(2):
                for s in range(shards):
                    spot = s * local + (core ^ side) * half
                    start = (side * shards + s) * half
                    out[:, spot : spot + half] = value[:, start : start + half].astype(bf16)


def output_body(local, index, *refs):
    parts, (middle, out) = refs[:CHIPS], refs[CHIPS:]
    store_in_order(local, index, middle[...] + part_sum(parts), out)


def output_call(index, parts, middle, local):
    spec = pl.BlockSpec(middle.shape, lambda i, n: (0, 0))
    return kernel_call(
        functools.partial(output_body, local),
        shape(middle.shape, bf16),
        [spec] * (CHIPS + 1),
        spec,
        (*parts, middle),
        index=index,
        grid=(1,),
        name="output",
    )


def grad_input_body(local, index, *refs):
    parts, (x, grad, out) = refs[:PAIR], refs[PAIR:]
    total = grad[...] + norm_back(part_sum(parts), x[...].astype(f32))
    store_in_order(local, index, total, out)


def grad_input_call(index, parts, x, grad, local):
    spec = pl.BlockSpec(x.shape, lambda i, n: (0, 0))
    return kernel_call(
        functools.partial(grad_input_body, local),
        shape(x.shape, bf16),
        [spec] * (PAIR + 2),
        spec,
        (*parts, x, grad),
        index=index,
        grid=(1,),
        name="grad_input",
    )


def grad_qkv_body(shards, grad_q, first, *refs):
    rest, (cosine, sine), outs = refs[: shards - 1], refs[shards - 1 : shards + 1], refs[shards + 1 :]
    total = first[...]
    for term in rest:
        total = total + term[...].astype(f32)
    rows = cosine.shape[1]
    width = GROUP * HEAD
    cos, sin = cosine[...], sine[...]
    for n, out in enumerate(outs):
        out[:, :width] = grad_q[:, n * width : (n + 1) * width]
        for m in range(PAIR):
            span = slice(m * rows, (m + 1) * rows)
            turned = total[span, n * 2 * HEAD : (n + 1) * 2 * HEAD].T
            k = turned[:HEAD]
            k = k * cos - half_rotated(k) * sin
            both = jnp.concatenate([k, turned[HEAD:]], axis=0)
            out[span, width:] = both.T.astype(bf16)


def grad_qkv_call(grad_q, first, rest, cosine, sine):
    tokens = grad_q.shape[0]
    return kernel_call(
        functools.partial(grad_qkv_body, len(rest) + 1),
        (shape((tokens, GROUP * HEAD + 2 * HEAD), bf16),) * PAIR,
        [whole()] * (len(rest) + 4),
        (whole(),) * PAIR,
        (grad_q, first, *rest, cosine, sine),
        name="grad_qkv",
    )


def out_sends_body(index, term, *outs):
    cut = outs[0].shape[0] // PAIR
    for row in range(2):

        @pl.when(index[0] >> 1 == row)
        def _():
            for n in range(PAIR):
                for m in range(CHIPS):
                    spot = (n * CHIPS + m) * cut
                    start = (n ^ row) * cut
                    outs[m ^ (2 * n)][start : start + cut, :] = term[spot : spot + cut, :]


def out_sends(index, term):
    rows, width = term.shape
    rows //= CHIPS
    return kernel_call(
        out_sends_body,
        (shape((rows, width), bf16),) * CHIPS,
        [pl.BlockSpec(term.shape, lambda i, n: (0, 0))],
        (pl.BlockSpec((rows, width), lambda i, n: (0, 0)),) * CHIPS,
        (term,),
        index=index,
        grid=(1,),
        name="out_sends",
    )


def out_block_body(shards, index, *refs):
    parts, out = refs[:CHIPS], refs[CHIPS]
    group_shards = shards // CHIPS
    cut = parts[0].shape[0] // (PAIR * group_shards)
    sums = [parts[m][...].astype(f32) + parts[m + 2][...].astype(f32) for m in range(2)]
    for side in range(2):

        @pl.when(index[0] & 1 == side)
        def _():
            for m in range(2):
                for n in range(PAIR * group_shards):
                    shard = (m ^ side) * PAIR * group_shards + n
                    rows = sums[m][n * cut : (n + 1) * cut].astype(bf16)
                    out[2 * shard * cut : (2 * shard + 1) * cut, :] = rows[:, :512]
                    out[(2 * shard + 1) * cut : (2 * shard + 2) * cut, :] = rows[:, 512:]


def out_block_call(index, parts, shards):
    rows, width = parts[0].shape
    return kernel_call(
        functools.partial(out_block_body, shards),
        shape((2 * PAIR * rows, width // 2), bf16),
        [pl.BlockSpec((rows, width), lambda i, n: (0, 0))] * CHIPS,
        pl.BlockSpec((2 * PAIR * rows, width // 2), lambda i, n: (0, 0)),
        tuple(parts),
        index=index,
        grid=(1,),
        name="out_block",
    )


def half_rotated(values):
    middle = values.shape[0] // 2
    return jnp.concatenate([-values[middle:], values[:middle]], axis=0)


def qkv_body(make, *refs):
    if make:
        xs, (own, other, cosine, sine, queries, kv, xhat) = refs[:PAIR], refs[PAIR:]
        rows, width = xs[0].shape
        for m in range(PAIR):
            x = xs[m][...].astype(f32)
            inverse = lax.rsqrt(mean_of(x * x) + norm_eps)
            xhat[m * rows : (m + 1) * rows, :] = (x * inverse).astype(bf16)
    else:
        xhat, own, other, cosine, sine, queries, kv = refs
        rows, width = cosine.shape[1], xhat.shape[1]
    cos, sin = cosine[...], sine[...]
    total = dot(xhat[:, : width // 2], own[...]) + dot(xhat[:, width // 2 :], other[...])
    for m in range(PAIR):
        turned = total[m * rows : (m + 1) * rows].T
        for h in range(GROUP + 1):
            u = turned[h * HEAD : (h + 1) * HEAD]
            u = u * cos + half_rotated(u) * sin
            if h < GROUP:
                queries[m, :, h * rows : (h + 1) * rows] = (u * HEAD ** (-0.5)).astype(bf16)
            else:
                both = jnp.concatenate([u, turned[(h + 1) * HEAD :]], axis=0)
                kv[m * rows : (m + 1) * rows, :] = both.T.astype(bf16)


def qkv_call(xs, own, other, cosine, sine):
    make = isinstance(xs, list)
    rows = cosine.shape[1]
    tokens = PAIR * rows
    outs = (shape((PAIR, HEAD, GROUP * rows), bf16), shape((tokens, 2 * HEAD), bf16))
    if make:
        outs = outs + (shape((tokens, xs[0].shape[1]), bf16),)
    operands = (*(xs if make else (xs,)), own, other, cosine, sine)
    return kernel_call(
        functools.partial(qkv_body, make),
        outs,
        [whole()] * len(operands),
        tuple(whole() for _ in outs),
        operands,
        name="qkv",
    )


def out_rows_body(index, *refs):
    pieces, out = refs[:CHIPS], refs[CHIPS]
    cut = pieces[0].shape[0] // PAIR
    for row in range(2):

        @pl.when(index[0] >> 1 == row)
        def _():
            for n in range(PAIR):
                for m in range(CHIPS):
                    spot = (n * CHIPS + m) * cut
                    start = (n ^ row) * cut
                    out[spot : spot + cut, :] = pieces[m ^ (2 * n)][start : start + cut, :]


def out_rows_call(index, pieces):
    rows, width = pieces[0].shape
    return kernel_call(
        out_rows_body,
        shape((CHIPS * rows, width), bf16),
        [pl.BlockSpec((rows, width), lambda i, n: (0, 0))] * CHIPS,
        pl.BlockSpec((CHIPS * rows, width), lambda i, n: (0, 0)),
        tuple(pieces),
        index=index,
        grid=(1,),
        name="out_rows",
    )


LANE_HEADS = 4


def own_block_bias(rows):
    key = lax.broadcasted_iota(jnp.int32, (rows, rows), 0)
    mine = lax.broadcasted_iota(jnp.int32, (rows, rows), 1)
    return jnp.where(key <= mine, 0.0, masked_score)


def set_bias(bias):
    rows = bias.shape[0]
    value = own_block_bias(rows)
    for h in range(LANE_HEADS):
        bias[:, h * rows : (h + 1) * rows] = value


def far_bias(depth, d):
    return jnp.where(d <= depth, 0.0, masked_score) if d else 0.0


def attention_body(shards, index, queries, *refs):
    kvs = refs[:shards]
    turned_out, out, stats, bias, terms, out_turned = refs[shards:]
    rows = bias.shape[0]
    wide = LANE_HEADS * rows

    @pl.when(pl.program_id(0) == 0)
    def _():
        set_bias(bias)

    ks = [kv[:, :HEAD] for kv in kvs]
    v_turned = jnp.concatenate([kv[...] for kv in kvs], axis=0).astype(f32).T[HEAD:].astype(bf16)
    for n in range(GROUP // LANE_HEADS):
        span = slice(n * wide, (n + 1) * wide)
        q = queries[0, :, span]
        scores, top = [], None
        for d in range(shards):
            score = dot(ks[d], q)
            if d == 0:
                score = score + bias[...]
            scores.append(score)
            highest = jnp.max(score, axis=0, keepdims=True) + far_bias(index[2], d)
            top = highest if top is None else jnp.maximum(top, highest)
        total = None
        for d in range(shards):
            term = jnp.exp(scores[d] - (top - far_bias(index[2], d)))
            part = jnp.sum(term, axis=0, keepdims=True)
            total = part if total is None else total + part
            terms[d * rows : (d + 1) * rows, :] = term.astype(bf16)
        out_turned[:, span] = dot(v_turned, terms[...]) / total
        stats[0, :, span] = top + jnp.log(total)
    turned_out[0] = out_turned[...].astype(bf16)
    straight = out_turned[...].T
    for h in range(GROUP):
        out[:, h * HEAD : (h + 1) * HEAD] = straight[h * rows : (h + 1) * rows].astype(bf16)


def attention_call(index, queries, kvs):
    chips, _, wide = queries.shape
    rows = wide // GROUP
    shards = len(kvs)
    keys = shards * rows
    block = pl.BlockSpec((1, HEAD, wide), lambda i, n: (i, 0, 0))
    return kernel_call(
        functools.partial(attention_body, shards),
        (
            shape((chips, HEAD, wide), bf16),
            shape((chips * rows, GROUP * HEAD), bf16),
            shape((chips, 1, wide), f32),
        ),
        [block] + [pl.BlockSpec((rows, 2 * HEAD), lambda i, n: (i, 0))] * shards,
        (
            block,
            pl.BlockSpec((rows, GROUP * HEAD), lambda i, n: (i, 0)),
            pl.BlockSpec((1, 1, wide), lambda i, n: (i, 0, 0)),
        ),
        (queries, *kvs),
        index=index,
        grid=(chips,),
        scratch=(
            VMEM((rows, LANE_HEADS * rows), f32),
            VMEM((keys, LANE_HEADS * rows), bf16),
            VMEM((HEAD, wide), f32),
        ),
        name="attention",
    )


def attention_back_body(shards, index, branch, wo_own, wo_other, cosine, sine, *refs):
    per_group = 3 + shards
    inputs = [refs[n * per_group : (n + 1) * per_group] for n in range(PAIR)]
    grad_q, grad_first, grad_rest = refs[-7:-4]
    bias, probs_low, grads_low, grad_lanes = refs[-4:]
    rows = bias.shape[0]
    wide = LANE_HEADS * rows
    width = branch.shape[1]
    set_bias(bias)
    cos, sin = cosine[...], sine[...]
    for n, (queries, turned_out, stats, *kvs) in enumerate(inputs):
        heads = slice(n * GROUP * HEAD, (n + 1) * GROUP * HEAD)
        grad_out = dot_nt(wo_own[heads, :], branch[:, : width // 2])
        grad_out = grad_out + dot_nt(wo_other[heads, :], branch[:, width // 2 :])
        for h in range(GROUP):
            grad_lanes[:, h * rows : (h + 1) * rows] = grad_out[h * HEAD : (h + 1) * HEAD].astype(bf16)
        ks = [kv[:, :HEAD] for kv in kvs]
        vs = [kv[:, HEAD:] for kv in kvs]
        k_turned = jnp.concatenate([kv[...] for kv in kvs], axis=0).astype(f32).T[:HEAD].astype(bf16)
        k_total, v_total, parts = None, None, []
        for c in range(GROUP // LANE_HEADS):
            span = slice(c * wide, (c + 1) * wide)
            q, mine = queries[0, :, span], grad_lanes[:, span]
            delta = jnp.sum(
                mine.astype(f32) * turned_out[0, :, span].astype(f32), axis=0, keepdims=True
            )
            for d in range(shards):
                score = dot(ks[d], q)
                if d == 0:
                    score = score + bias[...]
                probs = jnp.exp(score - (stats[0, :, span] - far_bias(index[2], d)))
                grad_scores = probs * (dot(vs[d], mine) - delta)
                probs_low[d * rows : (d + 1) * rows, :] = probs.astype(bf16)
                grads_low[d * rows : (d + 1) * rows, :] = grad_scores.astype(bf16)
            u = dot(k_turned, grads_low[...]) * HEAD ** (-0.5)
            parts.append(u * cos - half_rotated(u) * sin)
            k_term = dot_nt(grads_low[...], q)
            v_term = dot_nt(probs_low[...], mine)
            k_total = k_term if k_total is None else k_total + k_term
            v_total = v_term if v_total is None else v_total + v_term
        straight = jnp.concatenate(parts, axis=1).T
        for h in range(GROUP):
            spot = (n * GROUP + h) * HEAD
            grad_q[:, spot : spot + HEAD] = straight[h * rows : (h + 1) * rows].astype(bf16)
        both = jnp.concatenate([k_total, v_total], axis=1)
        spot = slice(n * 2 * HEAD, (n + 1) * 2 * HEAD)
        grad_first[:, spot] = both[:rows, :]
        for d in range(1, shards):
            grad_rest[d - 1, :, spot] = both[d * rows : (d + 1) * rows, :].astype(bf16)


def attention_back_call(index, m, branch, wo_own, wo_other, cosine, sine, groups, before):
    chips, _, wide = groups[0][0].shape
    rows = wide // GROUP
    shards = len(groups[0][3])
    keys = shards * rows
    tokens = chips * rows
    block = pl.BlockSpec((1, HEAD, wide), lambda i, n: (m, 0, 0))
    in_specs = [whole()] * 5
    operands = [branch, wo_own, wo_other, jnp.tile(cosine, (1, LANE_HEADS)), jnp.tile(sine, (1, LANE_HEADS))]
    for queries, turned, stats, kvs in groups:
        in_specs += [block, block, pl.BlockSpec((1, 1, wide), lambda i, n: (m, 0, 0))]
        in_specs += [pl.BlockSpec((rows, 2 * HEAD), lambda i, n: (m, 0))] * shards
        operands += [queries, turned, stats, *kvs]
    aliases = {}
    if before is not None:
        aliases = {1 + len(operands) + n: n for n in range(3)}
        in_specs += [pl.BlockSpec(memory_space=pl.ANY)] * 3
        operands += list(before)
    outs = (
        shape((tokens, PAIR * GROUP * HEAD), bf16),
        shape((tokens, PAIR * 2 * HEAD), f32),
        shape((shards - 1, tokens, PAIR * 2 * HEAD), bf16),
    )
    out_specs = (
        pl.BlockSpec((rows, PAIR * GROUP * HEAD), lambda i, n: (m, 0)),
        pl.BlockSpec((rows, PAIR * 2 * HEAD), lambda i, n: (m, 0)),
        pl.BlockSpec((shards - 1, rows, PAIR * 2 * HEAD), lambda i, n: (0, m, 0)),
    )
    return kernel_call(
        functools.partial(attention_back_body, shards),
        outs,
        in_specs,
        out_specs,
        tuple(operands),
        index=index,
        grid=(1,),
        scratch=(
            VMEM((rows, LANE_HEADS * rows), f32),
            VMEM((keys, LANE_HEADS * rows), bf16),
            VMEM((keys, LANE_HEADS * rows), bf16),
            VMEM((HEAD, wide), bf16),
        ),
        aliases=aliases,
        name="attention_back",
    )


def parts_body(steps, transposed, count, *refs):
    lefts, owns, others = refs[:count], refs[count : 2 * count], refs[2 * count : 3 * count]
    outs = refs[3 * count :]
    rows = outs[0].shape[0]
    step = pl.program_id(0)

    def run(weights):
        total = None
        for left, weight in zip(lefts, weights):
            term = (dot_nt if transposed else dot)(left[...], weight[...])
            total = term if total is None else total + term
        for m, out in enumerate(outs):
            out[...] = total[m * rows : (m + 1) * rows, :].astype(out.dtype)

    @pl.when(step < steps)
    def _():
        run(owns)

    @pl.when(step >= steps)
    def _():
        run(others)


def parts_call(terms, rows, transposed, name):
    tokens = terms[0][0].shape[0]
    half = terms[0][1].shape[0] if transposed else terms[0][1].shape[1]
    tile = 256
    steps = half // tile
    last = steps - 1
    specs = [pl.BlockSpec((tokens, term[0].shape[1]), lambda j: (0, 0)) for term in terms]
    for side in range(2):
        for left, _, _, spot in terms:
            depth = left.shape[1]

            def place(side, spot, j):
                step = jnp.maximum(j - steps, 0) if side else jnp.minimum(j, last)
                return (step, spot) if transposed else (spot, step)

            block = (tile, depth) if transposed else (depth, tile)
            specs.append(pl.BlockSpec(block, functools.partial(place, side, spot)))
    count = tokens // rows
    return kernel_call(
        functools.partial(parts_body, steps, transposed, len(terms)),
        tuple(shape((rows, 2 * half), f32 if m == 0 else bf16) for m in range(count)),
        specs,
        tuple(pl.BlockSpec((rows, tile), lambda j: (0, j)) for _ in range(count)),
        (*(term[0] for term in terms), *(term[1] for term in terms), *(term[2] for term in terms)),
        grid=(2 * steps,),
        name=name,
    )


def gate_body(count, *refs):
    twos = refs[:count]
    gate_own, up_own, gate_other, up_other, act, for_gate, for_up, two_all = refs[count:]
    half = two_all.shape[1] // 2

    @pl.when(pl.program_id(0) == 0)
    def _():
        start = 0
        for two in twos:
            two_all[start : start + two.shape[0], :] = two[...]
            start += two.shape[0]

    own = jnp.concatenate([gate_own[...], up_own[...]], axis=1)
    other = jnp.concatenate([gate_other[...], up_other[...]], axis=1)
    both = dot(two_all[:, :half], own) + dot(two_all[:, half:], other)
    wide = gate_own.shape[1]
    gate, up = both[:, :wide], both[:, wide:]
    sig = 1.0 / (1.0 + jnp.exp(-gate))
    silu = gate * sig
    act[...] = (silu * up).astype(bf16)
    for_gate[...] = (up * sig * (1.0 + gate * (1.0 - sig))).astype(bf16)
    for_up[...] = silu.astype(bf16)


def gate_call(twos, own, other):
    rows, width = twos[0].shape
    tokens = CHIPS * rows
    half = width // 2
    ff = own.shape[1] // 2
    tile = LANES
    steps = ff // tile
    weight = [
        pl.BlockSpec((half, tile), lambda j: (0, j)),
        pl.BlockSpec((half, tile), lambda j: (0, j + steps)),
    ]
    column = pl.BlockSpec((tokens, tile), lambda j: (0, j))
    return kernel_call(
        functools.partial(gate_body, len(twos)),
        tuple(shape((tokens, ff), bf16) for _ in range(3)) + (shape((tokens, width), bf16),),
        [pl.BlockSpec(two.shape, lambda j: (0, 0)) for two in twos] + weight + weight,
        (column, column, column, pl.BlockSpec((tokens, width), lambda j: (0, 0))),
        (*twos, own, own, other, other),
        grid=(steps,),
        name="gate",
    )


def hidden_back_body(g, own, other, for_gate, for_up, grads):
    half = g.shape[1] // 2
    ff = own.shape[0]
    hidden = dot_nt(g[:, :half], own[...]) + dot_nt(g[:, half:], other[...])
    grads[:, :ff] = (hidden * for_gate[...].astype(f32)).astype(bf16)
    grads[:, ff:] = (hidden * for_up[...].astype(f32)).astype(bf16)


def hidden_back_call(g, own, other, for_gate, for_up):
    tokens, width = g.shape
    ff, half = own.shape
    block = tokens // 2
    row = lambda i: (i, 0)
    fixed = lambda i: (0, 0)
    return kernel_call(
        hidden_back_body,
        shape((tokens, 2 * ff), bf16),
        [
            pl.BlockSpec((block, width), row),
            pl.BlockSpec((ff, half), fixed),
            pl.BlockSpec((ff, half), fixed),
            pl.BlockSpec((block, ff), row),
            pl.BlockSpec((block, ff), row),
        ],
        pl.BlockSpec((block, 2 * ff), row),
        (g, own, other, for_gate, for_up),
        grid=(2,),
        name="hidden_back",
    )


def weight_grad_body(per, outputs, adds, left, right, *refs):
    added = [refs[n * outputs : (n + 1) * outputs] for n in range(adds)]
    outs, turned = refs[adds * outputs : -1], refs[-1]
    step = pl.program_id(0)

    @pl.when(step == 0)
    def _():
        turned[...] = left[...].T

    for n in range(outputs):

        @pl.when(step // per == n)
        def _(n=n):
            total = dot(turned[...], right[...])
            for terms in added:
                total = total + terms[n][...].astype(f32)
            outs[n][...] = total.astype(bf16)


def weight_grad(left, left_side, right, place, width, outputs, added, name):
    tokens = left.shape[0]
    rows = left.shape[1] // (1 if left_side is None else 2)
    tile = 256 if width % 256 == 0 else width
    per = width // tile
    first = place * width // tile
    side = left_side or 0

    def spot(n, j):
        return (0, jnp.clip(j - n * per, 0, per - 1))

    tiles = [pl.BlockSpec((rows, tile), functools.partial(spot, n)) for n in range(outputs)]
    return kernel_call(
        functools.partial(weight_grad_body, per, outputs, len(added)),
        tuple(shape((rows, width), bf16) for _ in range(outputs)),
        [
            pl.BlockSpec((tokens, rows), lambda j: (0, side)),
            pl.BlockSpec((tokens, tile), lambda j: (0, first + j)),
        ]
        + tiles * len(added),
        tuple(tiles),
        (left, right, *(term for terms in added for term in terms)),
        grid=(per * outputs,),
        scratch=(VMEM((rows, tokens), bf16),),
        name=name,
    )


def rows_result_body(local, index, *refs):
    pieces, out = refs[:PIECES], refs[PIECES]
    half = local // 2
    shards = out.shape[1] // local
    for m in range(CHIPS):
        for core in range(2):

            @pl.when((pl.program_id(0) == m) & (index[1] == core))
            def _():
                for side in range(2):
                    piece = pieces[2 * m + side]
                    for s in range(shards):
                        spot = s * local + (core ^ side) * half
                        out[:, spot : spot + half] = piece[:, s * half : (s + 1) * half].astype(f32)


def rows_result(index, pieces, local, name):
    cut, half_width = pieces[0].shape
    return kernel_call(
        functools.partial(rows_result_body, local),
        shape((CHIPS * cut, 2 * half_width), f32),
        [pl.BlockSpec((cut, half_width), lambda i, n: (0, 0))] * PIECES,
        pl.BlockSpec((cut, 2 * half_width), lambda i, n: (n[0] ^ i, 0)),
        tuple(pieces),
        index=index,
        grid=(CHIPS,),
        name=name,
    )


def out_result_body(local, base, index, *refs):
    pieces, out = refs[:PIECES], refs[PIECES]
    half = local // 2
    cut = local // CHIPS
    shards = out.shape[1] // local
    for m in range(CHIPS):
        for core in range(2):

            @pl.when((pl.program_id(0) == m) & (index[1] == core))
            def _():
                for side in range(2):
                    piece = pieces[2 * m + side]
                    for s in range(shards):
                        spot = s * local + (core ^ side) * half
                        row, column = (0, s * half) if s * half < 512 else (cut, s * half - 512)
                        column += base
                        out[:, spot : spot + half] = piece[row : row + cut, column : column + half].astype(f32)


def out_result(index, pieces, local, width, base):
    cut = local // CHIPS
    return kernel_call(
        functools.partial(out_result_body, local, base),
        shape((local, width), f32),
        [pl.BlockSpec(pieces[0].shape, lambda i, n: (0, 0))] * PIECES,
        pl.BlockSpec((cut, width), lambda i, n: (n[0] ^ i, 0)),
        tuple(pieces),
        index=index,
        grid=(CHIPS,),
        name="out_result",
    )


def lane_sum(value):
    total = value[:, :LANES]
    for n in range(1, value.shape[1] // LANES):
        total = total + value[:, n * LANES : (n + 1) * LANES]
    return total


def feedforward_result_body(ff_local, cut, index, *refs):
    pieces = refs[:CHIPS]
    gate_weight, up_weight, gain = refs[CHIPS : CHIPS + 3]
    gate_out, up_out, gain_out = refs[-3:]
    shards = gate_weight.shape[1] // ff_local
    width = shards * cut
    for chip in range(CHIPS):

        @pl.when(index[0] == chip)
        def _():
            @pl.loop(0, gate_out.shape[0] // 16)
            def _(n):
                rows = pl.ds(pl.multiple_of(n * 16, 16), 16)
                scale = gain[rows, :1]
                total = jnp.zeros((16, LANES), f32)
                for base, weight, out in ((0, gate_weight, gate_out), (width, up_weight, up_out)):
                    parts = []
                    for s in range(shards):
                        for owner in range(CHIPS):
                            start = base + s * cut
                            parts.append(pieces[owner ^ chip][rows, start : start + cut].astype(f32))
                    wide = jnp.concatenate(parts, axis=1)
                    total = total + lane_sum(wide * weight[rows, :].astype(f32))
                    out[rows, :] = wide * scale
                gain_out[rows, :] = total


def feedforward_result(index, side, pieces, gate_weight, up_weight, gain, ff_local, before):
    local, ff = gate_weight.shape
    half = local // 2
    rows = 64
    steps = half // rows
    row = lambda i, n: ((n[1] ^ side) * steps + i, 0)
    in_specs = [pl.BlockSpec((rows, pieces[0].shape[1]), lambda i, n: (i, 0))] * CHIPS
    in_specs += [pl.BlockSpec((rows, ff), row)] * 2 + [pl.BlockSpec((rows, LANES), row)]
    operands = (*pieces, gate_weight, up_weight, gain)
    aliases = {}
    if before is not None:
        aliases = {1 + len(operands) + n: n for n in range(3)}
        in_specs = in_specs + [pl.BlockSpec(memory_space=pl.ANY)] * 3
        operands = operands + tuple(before)
    return kernel_call(
        functools.partial(feedforward_result_body, ff_local, ff_local // CHIPS),
        (shape((local, ff), f32), shape((local, ff), f32), shape((local, LANES), f32)),
        in_specs,
        (pl.BlockSpec((rows, ff), row), pl.BlockSpec((rows, ff), row), pl.BlockSpec((rows, LANES), row)),
        operands,
        index=index,
        grid=(steps,),
        aliases=aliases,
        name="feedforward_result",
    )


def qkv_result_body(local, group_shards, index, *refs):
    pieces = refs[:PIECES]
    weights, gain = refs[PIECES : PIECES + 3], refs[PIECES + 3]
    outs, gain_out = refs[PIECES + 4 : PIECES + 7], refs[PIECES + 7]
    q_width = GROUP * HEAD
    cut = local // CHIPS
    scale = gain[:, :1]
    for chip in range(CHIPS):
        for side in range(2):

            @pl.when((index[0] == chip) & (pl.program_id(0) == side))
            def _():
                parts, k_parts, v_parts = [], [], []
                for group in range(CHIPS):
                    owner = (group >> 1) + 2 * (group & 1)
                    piece = pieces[2 * (owner ^ chip) + side]
                    for s in range(group_shards):
                        for j in range(CHIPS):
                            start = ((j ^ owner) * group_shards + s) * cut
                            parts.append(piece[:, start : start + cut].astype(f32))
                    k_parts.append(piece[:, q_width : q_width + HEAD].astype(f32))
                    v_parts.append(piece[:, q_width + HEAD : q_width + 2 * HEAD].astype(f32))
                total = jnp.zeros((gain.shape[0], LANES), f32)
                for part, weight, out in zip((parts, k_parts, v_parts), weights, outs):
                    wide = jnp.concatenate(part, axis=1)
                    total = total + lane_sum(wide * weight[...].astype(f32))
                    out[...] = wide * scale
                gain_out[...] = total


def qkv_result(index, pieces, query, key, value, gain):
    local, width = query.shape
    half = local // 2
    group_shards = width // local // CHIPS
    row = lambda i, n: (n[1] ^ i, 0)
    kv_width = key.shape[1]
    return kernel_call(
        functools.partial(qkv_result_body, local, group_shards),
        (
            shape((local, width), f32),
            shape((local, kv_width), f32),
            shape((local, kv_width), f32),
            shape((local, LANES), f32),
        ),
        [pl.BlockSpec(pieces[0].shape, lambda i, n: (0, 0))] * PIECES
        + [
            pl.BlockSpec((half, width), row),
            pl.BlockSpec((half, kv_width), row),
            pl.BlockSpec((half, kv_width), row),
            pl.BlockSpec((half, LANES), row),
        ],
        (
            pl.BlockSpec((half, width), row),
            pl.BlockSpec((half, kv_width), row),
            pl.BlockSpec((half, kv_width), row),
            pl.BlockSpec((half, LANES), row),
        ),
        (*pieces, query, key, value, gain),
        index=index,
        grid=(2,),
        name="qkv_result",
    )


def per_device(
    hidden_in,
    attention_gain,
    query_weight,
    key_weight,
    value_weight,
    output_weight,
    feedforward_gain,
    gate_weight,
    up_weight,
    down_weight,
    out_grad,
):
    rows, width = hidden_in.shape
    shards = lax.axis_size("shard")
    replicas = lax.axis_size("replica")
    place = lax.axis_index("replica")
    depth = lax.axis_index("shard")
    core = place & 1
    chip = (place >> 1) & (CHIPS - 1)
    local = width // shards
    half = local // 2
    ff_local = down_weight.shape[0]
    group_shards = shards // CHIPS
    q_width = GROUP * HEAD
    qkv_width = q_width + 2 * HEAD
    index = jnp.stack([chip, core, depth]).astype(jnp.int32)

    gain_one = jnp.broadcast_to(attention_gain.astype(f32)[:, None], (local, LANES))
    gain_two = jnp.broadcast_to(feedforward_gain.astype(f32)[:, None], (local, LANES))


    at_block, out_block = attention_block(
        index, query_weight, key_weight, value_weight, output_weight, gain_one
    )
    x = own_first(index, (after(hidden_in, at_block),), local)[0]
    xs = [x, swap(x, 2)]
    at_own = lax.all_gather(at_block, "shard", axis=0, tiled=True)
    out_all = lax.all_gather(out_block, "shard", axis=0, tiled=True)
    gu_block = feedforward_block(index, gate_weight, up_weight, after(gain_two, at_block), ff_local)
    gu_own = lax.all_gather(gu_block, "shard", axis=0, tiled=True)
    down_own = lax.all_gather(down_block(index, down_weight, local), "shard", axis=0, tiled=True)
    g = own_first(index, (after(out_grad, x),), local)[0]
    g_blocks = [g, swap(g, 2), swap(g, 4)]
    at_own = after(at_own, gu_block, xs[1], *g_blocks[1:])

    qkv_own = [at_own]
    qkv_own.append(swap(qkv_own[0], 4))
    qkv_other = [swap(qkv_own[0], 1)]
    inverse = rope_base ** (-jnp.arange(0, HEAD, 2, dtype=f32) / HEAD)
    places = (depth * rows + jnp.arange(rows, dtype=jnp.int32)).astype(f32)
    angles = inverse[:, None] * places[None, :]
    angles = jnp.concatenate([angles, angles], axis=0)
    cosine, sine = jnp.cos(angles), jnp.sin(angles)

    def shifted(kv):
        return [kv] + [shift(kv, d) for d in range(1, shards)]

    queries, kv, xhat = qkv_call(xs, qkv_own[0], qkv_other[0], cosine, sine)
    kvs = shifted(kv)
    qkv_own[1] = after(qkv_own[1], *kvs[1:])
    qkv_other.append(swap(qkv_own[1], 1))
    queries_two, kv_two = qkv_call(xhat, qkv_own[1], qkv_other[1], cosine, sine)
    kvs_two = shifted(kv_two)
    groups = [(queries, *attention_call(index, queries, kvs), kvs)]
    groups.append((queries_two, *attention_call(index, queries_two, kvs_two), kvs_two))
    attended = [group[2] for group in groups]
    groups = [(group[0], group[1], group[3], group[4]) for group in groups]

    out_all = after(out_all, qkv_own[1])
    x_place = chip & 1
    low_group = (chip >> 1) == 0
    pair_rows = PAIR * group_shards * half // 2

    def out_for(mask):
        return lax.dynamic_slice_in_dim(out_all, ((chip ^ mask) & 1) * pair_rows, pair_rows, 0)

    out_pieces = [out_for(0)] + [swap(out_for(m), 2 * m) for m in range(1, CHIPS)]
    wo_own = out_rows_call(index, [after(piece, *kvs_two[1:]) for piece in out_pieces])
    wo_other = swap(wo_own, 1)

    mid_terms = [(attended[n], wo_own, wo_other, n) for n in range(PAIR)]
    g_blocks.append(swap(after(g, *out_pieces[1:]), 6))
    mid_out = parts_call(mid_terms, rows, False, "attention_out")
    g_all = jnp.concatenate([after(block, mid_out[0]) for block in g_blocks], axis=0)
    middle, two = middle_call(plane_send(mid_out), after(x, g_all))
    twos = plane_gather_forward(two)

    gu_own = after(gu_own, *twos[1:])
    gu_other = swap(gu_own, 1)
    act, for_gate, for_up, two_all = gate_call(twos, gu_own, gu_other)

    def over_groups(kept):
        if replicas > PIECES:
            groups = [
                [e * PIECES + i for e in range(replicas // PIECES)] for i in range(PIECES)
            ]
            kept = lax.psum(kept, "replica", axis_index_groups=groups)
        return kept

    def reduced(term):
        kept = lax.psum_scatter(term, "shard", scatter_dimension=0, tiled=True)
        return over_groups(kept)

    def plane_pieces(kept):
        mine = plane_gather(kept)
        return mine, [swap(part, 1) for part in mine]

    def mixed(mine, theirs):
        return [part for pair in zip(mine, theirs) for part in pair]

    down_sent = weight_grad(act, None, g_all, 1, width // 2, 1, (), "down_grad_other")
    down_sent = [swap(down_sent[0], 1)]
    down_sent[0] = after(down_sent[0], down_own)
    down_term = weight_grad(act, None, g_all, 0, width // 2, 1, (down_sent,), "down_grad")[0]
    down_kept = reduced(down_term)
    down_other = swap(down_own, 1)

    grads = hidden_back_call(after(g_all, down_term), down_own, down_other, for_gate, for_up)
    grads_wide = grads.shape[1]
    e_terms = parts_call([(grads, gu_own, gu_other, 0)], rows, True, "feedforward_back")
    e_parts = plane_send(e_terms)
    two_late = after(two_all, e_parts[1])
    gu_sent = weight_grad(two_late, 1, grads, 0, grads_wide, 1, (), "gate_grad_other")
    gu_sent = [swap(gu_sent[0], 1)]
    gu_term = weight_grad(
        two_late, 0, grads, 0, grads_wide, 1, (gu_sent,), "gate_grad"
    )[0]
    gu_kept = reduced(gu_term)
    middle_late = after(middle, down_kept)
    grad_middle, branch = grad_middle_call(e_parts, middle_late, g)
    branches = [branch, swap(branch, 2)]

    def back_block(m, block, before):
        return attention_back_call(index, m, block, wo_own, wo_other, cosine, sine, groups, before)

    before = back_block(0, branch, None)
    act_late = after(act, before[1])
    out_terms = parts_call([(act_late, down_own, down_other, 0)], rows, False, "feedforward_out")
    out_parts = plane_send(out_terms)
    before = back_block(1, after(branches[1], before[1]), before)
    output = output_call(index, out_parts, middle, local)
    grad_q, grad_first, grad_rest = before
    rest = [shift(grad_rest[d - 1], -d) for d in range(1, shards)]

    half_wide = width // 2
    branch_all = jnp.concatenate([after(block, grad_first) for block in branches], axis=0)
    both_attended = jnp.concatenate(attended, axis=1)
    wo_sent = weight_grad(both_attended, None, branch_all, 1, half_wide, 1, (), "out_grad_other")
    wo_sent = [swap(wo_sent[0], 1)]
    wo_term = weight_grad(both_attended, None, branch_all, 0, half_wide, 1, (wo_sent,), "out_grad")[0]
    wo_terms = out_sends(index, wo_term)
    wo_parts = plane_send(wo_terms)
    wo_wide = out_block_call(index, wo_parts, shards)
    grad_first = after(grad_first, wo_terms[0], out_terms[0])
    grad_qkv = grad_qkv_call(grad_q, grad_first, rest, cosine, sine)

    def qkv_grad(n, side, added, name):
        return weight_grad(xhat, side, grad_qkv[n], 0, qkv_width, 1, added, name)

    qkv_sent = [swap(qkv_grad(n, 1, (), "qkv_grad_other")[0], 1) for n in (1, 0)]
    back_terms = [(grad_qkv[n], qkv_own[n], qkv_other[n], 0) for n in range(PAIR)]
    qkv_second = qkv_grad(1, 0, ([qkv_sent[0]],), "qkv_grad")[0]
    qkv_term = qkv_grad(0, 0, ([qkv_sent[1]],), "qkv_grad")[0]
    at_term = jnp.concatenate([qkv_term, qkv_second, wo_wide], axis=1)
    at_kept = reduced(after(at_term, gu_kept))
    back_terms[0] = (after(grad_qkv[0], qkv_term, qkv_second), *back_terms[0][1:])
    back_parts = parts_call(back_terms, rows, True, "qkv_back")
    e_one = plane_send(back_parts)
    gu_mine = plane_gather_forward(gu_kept)
    gu_mine = gu_mine[:3] + [jnp.concatenate(gu_mine[3:], axis=0)]
    gu_theirs = [swap(part, 1) for part in gu_mine]
    gu_mine[0] = after(gu_mine[0], back_parts[0], output)
    gu_out = feedforward_result(index, 0, gu_mine, gate_weight, up_weight, gain_two, ff_local, None)
    gu_out = feedforward_result(index, 1, gu_theirs, gate_weight, up_weight, gain_two, ff_local, gu_out)

    down_mine = plane_gather(after(down_kept, *gu_mine[1:]))
    down_theirs = [swap(part, 1) for part in down_mine]
    down_out = rows_result(index, mixed(down_mine, down_theirs), local, "down_result")
    grad_input = grad_input_call(index, e_one, x, grad_middle, local)

    at_kept = after(at_kept, gu_out[0], grad_input)
    second = swap(at_kept[:, qkv_width : 2 * qkv_width], 4)
    first = at_kept[:, :qkv_width].astype(f32) + second.astype(f32)
    at_kept = jnp.concatenate([first.astype(bf16), at_kept[:, 2 * qkv_width :]], axis=1)
    at_pieces = mixed(*plane_pieces(at_kept))
    wo_out = out_result(index, at_pieces, local, width, qkv_width)
    q_out, k_out, v_out, gain_one_sums = qkv_result(
        index, at_pieces, query_weight, key_weight, value_weight, gain_one
    )
    return (
        output,
        grad_input,
        jnp.sum(gain_one_sums, axis=1),
        q_out,
        k_out,
        v_out,
        wo_out,
        jnp.sum(gu_out[2], axis=1),
        gu_out[0],
        gu_out[1],
        down_out,
    )


def solution(mesh):
    return jax.shard_map(
        per_device,
        mesh=mesh,
        in_specs=(
            P(("replica", "shard"), None),
            P("shard"),
            P("shard", None),
            P("shard", None),
            P("shard", None),
            P("shard", None),
            P("shard"),
            P("shard", None),
            P("shard", None),
            P("shard", None),
            P(("replica", "shard"), None),
        ),
        out_specs=(
            P(("replica", "shard"), None),
            P(("replica", "shard"), None),
            P("shard"),
            P("shard", None),
            P("shard", None),
            P("shard", None),
            P("shard", None),
            P("shard"),
            P("shard", None),
            P("shard", None),
            P("shard", None),
        ),
        check_vma=False,
    )
```

```python
import functools

import jax
import jax.numpy as jnp
from jax import lax
from jax.experimental import pallas as pl
from jax.experimental.pallas import tpu as pltpu
from jax.sharding import PartitionSpec as P

HEADS = 32
KV_HEADS = 4
HEAD = 64
GROUP = HEADS // KV_HEADS
CHIPS = 4
PIECES = 2 * CHIPS
PAIR = 2
LANES = 128

norm_eps = 1e-05
rope_base = 10000.0
masked_score = -1e30

f32 = jnp.float32
bf16 = jnp.bfloat16
VMEM = pltpu.VMEM
NT = (((1,), (1,)), ((), ()))
TN = (((0,), (0,)), ((), ()))


def dot(left, right):
    return jnp.dot(left, right, preferred_element_type=f32)


def dot_nt(left, right):
    return lax.dot_general(left, right, NT, preferred_element_type=f32)


def dot_tn(left, right):
    return lax.dot_general(left, right, TN, preferred_element_type=f32)


def shape(dims, kind):
    return jax.ShapeDtypeStruct(dims, kind)


def whole():
    return pl.BlockSpec(memory_space=VMEM)


TIMES = {"attention_back": 13.0}


def kernel_call(body, out_shape, in_specs, out_specs, operands, *, index=None, grid=(), scratch=(),
                aliases=None, name=None):
    params = pltpu.CompilerParams(
        vmem_limit_bytes=52 * 2**20, dimension_semantics=("arbitrary",) * len(grid)
    )
    moved = int(TIMES.get(name, 0.0) * 3.69e6)
    cost = pl.CostEstimate(flops=0, bytes_accessed=moved, transcendentals=0)
    common = dict(
        out_shape=out_shape,
        compiler_params=params,
        cost_estimate=cost,
        input_output_aliases=aliases or {},
        name=name,
    )
    if index is None:
        spec = pl.GridSpec(grid=grid, in_specs=in_specs, out_specs=out_specs, scratch_shapes=scratch)
        return pl.pallas_call(body, grid_spec=spec, **common)(*operands)
    spec = pltpu.PrefetchScalarGridSpec(
        num_scalar_prefetch=1, grid=grid, in_specs=in_specs, out_specs=out_specs,
        scratch_shapes=scratch,
    )
    return pl.pallas_call(body, grid_spec=spec, **common)(index, *operands)


def swap(value, mask):
    size = lax.axis_size("replica")
    return lax.ppermute(value, "replica", [(i, i ^ mask) for i in range(size)])


def shift(value, step):
    size = lax.axis_size("shard")
    pairs = [(i, i + step) for i in range(size) if 0 <= i + step < size]
    return lax.ppermute(value, "shard", pairs)


def plane_gather(value):
    return [value] + [swap(value, 2 * m) for m in range(1, CHIPS)]


def plane_gather_forward(value, *before):
    middle = value.shape[0] // 2
    across, along = swap(value, 2), swap(value, 4)
    if before:
        across, along = after(across, *before), after(along, *before)
    return [value, across, along, swap(across[:middle], 4), swap(along[middle:], 2)]


def plane_send(parts):
    return [parts[0]] + [swap(parts[m], 2 * m) for m in range(1, len(parts))]


def group_of(chip):
    return 2 * (chip & 1) + (chip >> 1)


def after(value, *others):
    return lax.optimization_barrier((value, *others))[0]


def attention_block_body(local, group_shards, index, q, k, v, o, gain, out, wo_out):
    scale = gain[:, :1]
    q_width = GROUP * HEAD
    cut = local // CHIPS
    for chip in range(CHIPS):

        group = group_of(chip)

        @pl.when(index[0] == chip)
        def _(group=group):
            parts = []
            for m in range(CHIPS):
                for s in range(group_shards):
                    start = group * q_width + s * local + (m ^ chip) * cut
                    parts.append(q[:, start : start + cut])
            parts.append(k[:, group * HEAD : (group + 1) * HEAD])
            parts.append(v[:, group * HEAD : (group + 1) * HEAD])
            wide = jnp.concatenate([part.astype(f32) for part in parts], axis=1)
            out[...] = (wide * scale).astype(bf16)

    half = local // 2
    shards = o.shape[1] // local
    for core in range(2):

        @pl.when(index[1] == core)
        def _():
            for s in range(shards):
                piece = o[:, s * local + core * half : s * local + (core + 1) * half]
                wo_out[:, s * half : (s + 1) * half] = piece


def attention_block(index, query, key, value, output, gain):
    local, width = query.shape
    half = local // 2
    shards = width // local
    return kernel_call(
        functools.partial(attention_block_body, local, shards // CHIPS),
        (
            shape((half, GROUP * HEAD + 2 * HEAD), bf16),
            shape((local // CHIPS, width // 2), bf16),
        ),
        [
            pl.BlockSpec((half, width), lambda i, n: (n[1], 0)),
            pl.BlockSpec((half, key.shape[1]), lambda i, n: (n[1], 0)),
            pl.BlockSpec((half, key.shape[1]), lambda i, n: (n[1], 0)),
            pl.BlockSpec((local // CHIPS, width), lambda i, n: (n[0], 0)),
            pl.BlockSpec((half, LANES), lambda i, n: (n[1], 0)),
        ],
        (
            pl.BlockSpec((half, GROUP * HEAD + 2 * HEAD), lambda i, n: (0, 0)),
            pl.BlockSpec((local // CHIPS, width // 2), lambda i, n: (0, 0)),
        ),
        (query, key, value, output, gain),
        index=index,
        grid=(1,),
        name="attention_block",
    )


def feedforward_block_body(ff_local, cut, index, gate, up, gain, out):
    scale = gain[:, :1]
    shards = gate.shape[1] // ff_local
    width = shards * cut
    for chip in range(CHIPS):

        @pl.when(index[0] == chip)
        def _():
            for n, source in enumerate((gate, up)):
                parts = [
                    source[:, s * ff_local + chip * cut : s * ff_local + (chip + 1) * cut].astype(f32)
                    for s in range(shards)
                ]
                wide = jnp.concatenate(parts, axis=1)
                out[:, n * width : (n + 1) * width] = (wide * scale).astype(bf16)


def feedforward_block(index, gate, up, gain, ff_local):
    local, ff = gate.shape
    half = local // 2
    rows = 64
    steps = half // rows
    cut = ff_local // CHIPS
    width = 2 * (ff // CHIPS)
    return kernel_call(
        functools.partial(feedforward_block_body, ff_local, cut),
        shape((half, width), bf16),
        [
            pl.BlockSpec((rows, ff), lambda i, n: (n[1] * steps + i, 0)),
            pl.BlockSpec((rows, ff), lambda i, n: (n[1] * steps + i, 0)),
            pl.BlockSpec((rows, LANES), lambda i, n: (n[1] * steps + i, 0)),
        ],
        pl.BlockSpec((rows, width), lambda i, n: (i, 0)),
        (gate, up, gain),
        index=index,
        grid=(steps,),
        name="feedforward_block",
    )


def own_first_body(local, index, *refs):
    count = len(refs) // 2
    half = local // 2
    for core in range(2):

        @pl.when(index[1] == core)
        def _():
            for source, out in zip(refs[:count], refs[count:]):
                shards = source.shape[1] // local
                sides = out.shape[1] // (shards * half)
                for side in range(sides):
                    for s in range(shards):
                        start = s * local + (core ^ side) * half
                        spot = (side * shards + s) * half
                        out[:, spot : spot + half] = source[:, start : start + half]


def own_first(index, sources, local, halves=2):
    return kernel_call(
        functools.partial(own_first_body, local),
        tuple(shape((v.shape[0], v.shape[1] * halves // 2), bf16) for v in sources),
        [pl.BlockSpec(v.shape, lambda i, n: (0, 0)) for v in sources],
        tuple(
            pl.BlockSpec((v.shape[0], v.shape[1] * halves // 2), lambda i, n: (0, 0)) for v in sources
        ),
        tuple(sources),
        index=index,
        grid=(1,),
        name="own_first",
    )


def down_block_body(local, index, source, out):
    own_first_body(local, index, source, out)


def down_block(index, down, local):
    ff_local, width = down.shape
    cut = ff_local // CHIPS
    return kernel_call(
        functools.partial(down_block_body, local),
        shape((cut, width // 2), bf16),
        [pl.BlockSpec((cut, width), lambda i, n: (n[0], 0))],
        pl.BlockSpec((cut, width // 2), lambda i, n: (0, 0)),
        (down,),
        index=index,
        grid=(1,),
        name="down_block",
    )


def part_sum(parts):
    total = parts[0][...]
    for part in parts[1:]:
        total = total + part[...].astype(f32)
    return total


def mean_of(values):
    return jnp.mean(values, axis=1, keepdims=True)


def middle_body(*refs):
    parts, (x, middle, two) = refs[:PAIR], refs[PAIR:]
    total = x[...].astype(f32) + part_sum(parts)
    middle[...] = total
    two[...] = (total * lax.rsqrt(mean_of(total * total) + norm_eps)).astype(bf16)


def middle_call(parts, x):
    return kernel_call(
        middle_body,
        (shape(x.shape, f32), shape(x.shape, bf16)),
        [whole()] * (PAIR + 1),
        (whole(), whole()),
        (*parts, x),
        name="middle",
    )


def norm_back(e, values):
    inverse = lax.rsqrt(mean_of(values * values) + norm_eps)
    return inverse * e - values * (inverse * inverse * inverse) * mean_of(e * values)


def grad_middle_body(*refs):
    parts, (middle, g, grad, low) = refs[:CHIPS], refs[CHIPS:]
    total = g[...].astype(f32) + norm_back(part_sum(parts), middle[...])
    grad[...] = total
    low[...] = total.astype(bf16)


def grad_middle_call(parts, middle, g):
    return kernel_call(
        grad_middle_body,
        (shape(g.shape, f32), shape(g.shape, bf16)),
        [whole()] * (CHIPS + 2),
        (whole(), whole()),
        (*parts, middle, g),
        name="grad_middle",
    )


def store_in_order(local, index, value, out):
    half = local // 2
    shards = out.shape[1] // local
    for core in range(2):

        @pl.when(index[1] == core)
        def _():
            for side in range(2):
                for s in range(shards):
                    spot = s * local + (core ^ side) * half
                    start = (side * shards + s) * half
                    out[:, spot : spot + half] = value[:, start : start + half].astype(bf16)


def output_body(local, index, *refs):
    parts, (middle, out) = refs[:CHIPS], refs[CHIPS:]
    store_in_order(local, index, middle[...] + part_sum(parts), out)


def output_call(index, parts, middle, local):
    spec = pl.BlockSpec(middle.shape, lambda i, n: (0, 0))
    return kernel_call(
        functools.partial(output_body, local),
        shape(middle.shape, bf16),
        [spec] * (CHIPS + 1),
        spec,
        (*parts, middle),
        index=index,
        grid=(1,),
        name="output",
    )


def grad_input_body(local, index, *refs):
    parts, (x, grad, out) = refs[:PAIR], refs[PAIR:]
    total = grad[...] + norm_back(part_sum(parts), x[...].astype(f32))
    store_in_order(local, index, total, out)


def grad_input_call(index, parts, x, grad, local):
    spec = pl.BlockSpec(x.shape, lambda i, n: (0, 0))
    return kernel_call(
        functools.partial(grad_input_body, local),
        shape(x.shape, bf16),
        [spec] * (PAIR + 2),
        spec,
        (*parts, x, grad),
        index=index,
        grid=(1,),
        name="grad_input",
    )


def grad_qkv_body(shards, grad_q, first, *refs):
    rest, (cosine, sine), outs = refs[: shards - 1], refs[shards - 1 : shards + 1], refs[shards + 1 :]
    total = first[...]
    for term in rest:
        total = total + term[...].astype(f32)
    rows = cosine.shape[1]
    width = GROUP * HEAD
    cos, sin = cosine[...], sine[...]
    for n, out in enumerate(outs):
        out[:, :width] = grad_q[:, n * width : (n + 1) * width]
        for m in range(PAIR):
            span = slice(m * rows, (m + 1) * rows)
            turned = total[span, n * 2 * HEAD : (n + 1) * 2 * HEAD].T
            k = turned[:HEAD]
            k = k * cos - half_rotated(k) * sin
            both = jnp.concatenate([k, turned[HEAD:]], axis=0)
            out[span, width:] = both.T.astype(bf16)


def grad_qkv_call(grad_q, first, rest, cosine, sine):
    tokens = grad_q.shape[0]
    return kernel_call(
        functools.partial(grad_qkv_body, len(rest) + 1),
        (shape((tokens, GROUP * HEAD + 2 * HEAD), bf16),) * PAIR,
        [whole()] * (len(rest) + 4),
        (whole(),) * PAIR,
        (grad_q, first, *rest, cosine, sine),
        name="grad_qkv",
    )


def out_sends_body(index, term, *outs):
    cut = outs[0].shape[0] // PAIR
    for row in range(2):

        @pl.when(index[0] >> 1 == row)
        def _():
            for n in range(PAIR):
                for m in range(CHIPS):
                    spot = (n * CHIPS + m) * cut
                    start = (n ^ row) * cut
                    outs[m ^ (2 * n)][start : start + cut, :] = term[spot : spot + cut, :]


def out_sends(index, term):
    rows, width = term.shape
    rows //= CHIPS
    return kernel_call(
        out_sends_body,
        (shape((rows, width), bf16),) * CHIPS,
        [pl.BlockSpec(term.shape, lambda i, n: (0, 0))],
        (pl.BlockSpec((rows, width), lambda i, n: (0, 0)),) * CHIPS,
        (term,),
        index=index,
        grid=(1,),
        name="out_sends",
    )


def out_block_body(shards, index, *refs):
    parts, out = refs[:CHIPS], refs[CHIPS]
    group_shards = shards // CHIPS
    cut = parts[0].shape[0] // (PAIR * group_shards)
    sums = [parts[m][...].astype(f32) + parts[m + 2][...].astype(f32) for m in range(2)]
    for side in range(2):

        @pl.when(index[0] & 1 == side)
        def _():
            for m in range(2):
                for n in range(PAIR * group_shards):
                    shard = (m ^ side) * PAIR * group_shards + n
                    rows = sums[m][n * cut : (n + 1) * cut].astype(bf16)
                    out[2 * shard * cut : (2 * shard + 1) * cut, :] = rows[:, :512]
                    out[(2 * shard + 1) * cut : (2 * shard + 2) * cut, :] = rows[:, 512:]


def out_block_call(index, parts, shards):
    rows, width = parts[0].shape
    return kernel_call(
        functools.partial(out_block_body, shards),
        shape((2 * PAIR * rows, width // 2), bf16),
        [pl.BlockSpec((rows, width), lambda i, n: (0, 0))] * CHIPS,
        pl.BlockSpec((2 * PAIR * rows, width // 2), lambda i, n: (0, 0)),
        tuple(parts),
        index=index,
        grid=(1,),
        name="out_block",
    )


def half_rotated(values):
    middle = values.shape[0] // 2
    return jnp.concatenate([-values[middle:], values[:middle]], axis=0)


def qkv_body(make, *refs):
    if make:
        xs, (own, other, cosine, sine, queries, kv, xhat) = refs[:PAIR], refs[PAIR:]
        rows, width = xs[0].shape
        for m in range(PAIR):
            x = xs[m][...].astype(f32)
            inverse = lax.rsqrt(mean_of(x * x) + norm_eps)
            xhat[m * rows : (m + 1) * rows, :] = (x * inverse).astype(bf16)
    else:
        xhat, own, other, cosine, sine, queries, kv = refs
        rows, width = cosine.shape[1], xhat.shape[1]
    cos, sin = cosine[...], sine[...]
    total = dot(xhat[:, : width // 2], own[...]) + dot(xhat[:, width // 2 :], other[...])
    for m in range(PAIR):
        turned = total[m * rows : (m + 1) * rows].T
        for h in range(GROUP + 1):
            u = turned[h * HEAD : (h + 1) * HEAD]
            u = u * cos + half_rotated(u) * sin
            if h < GROUP:
                queries[m, :, h * rows : (h + 1) * rows] = (u * HEAD ** (-0.5)).astype(bf16)
            else:
                both = jnp.concatenate([u, turned[(h + 1) * HEAD :]], axis=0)
                kv[m * rows : (m + 1) * rows, :] = both.T.astype(bf16)


def qkv_call(xs, own, other, cosine, sine):
    make = isinstance(xs, list)
    rows = cosine.shape[1]
    tokens = PAIR * rows
    outs = (shape((PAIR, HEAD, GROUP * rows), bf16), shape((tokens, 2 * HEAD), bf16))
    if make:
        outs = outs + (shape((tokens, xs[0].shape[1]), bf16),)
    operands = (*(xs if make else (xs,)), own, other, cosine, sine)
    return kernel_call(
        functools.partial(qkv_body, make),
        outs,
        [whole()] * len(operands),
        tuple(whole() for _ in outs),
        operands,
        name="qkv",
    )


def out_rows_body(index, *refs):
    pieces, out = refs[:CHIPS], refs[CHIPS]
    cut = pieces[0].shape[0] // PAIR
    for row in range(2):

        @pl.when(index[0] >> 1 == row)
        def _():
            for n in range(PAIR):
                for m in range(CHIPS):
                    spot = (n * CHIPS + m) * cut
                    start = (n ^ row) * cut
                    out[spot : spot + cut, :] = pieces[m ^ (2 * n)][start : start + cut, :]


def out_rows_call(index, pieces):
    rows, width = pieces[0].shape
    return kernel_call(
        out_rows_body,
        shape((CHIPS * rows, width), bf16),
        [pl.BlockSpec((rows, width), lambda i, n: (0, 0))] * CHIPS,
        pl.BlockSpec((CHIPS * rows, width), lambda i, n: (0, 0)),
        tuple(pieces),
        index=index,
        grid=(1,),
        name="out_rows",
    )


LANE_HEADS = 4


def own_block_bias(rows):
    key = lax.broadcasted_iota(jnp.int32, (rows, rows), 0)
    mine = lax.broadcasted_iota(jnp.int32, (rows, rows), 1)
    return jnp.where(key <= mine, 0.0, masked_score)


def set_bias(bias):
    rows = bias.shape[0]
    value = own_block_bias(rows)
    for h in range(LANE_HEADS):
        bias[:, h * rows : (h + 1) * rows] = value


def far_bias(depth, d):
    return jnp.where(d <= depth, 0.0, masked_score) if d else 0.0


def attention_body(shards, index, queries, *refs):
    kvs = refs[:shards]
    turned_out, out, stats, bias, terms, out_turned = refs[shards:]
    rows = bias.shape[0]
    wide = LANE_HEADS * rows

    @pl.when(pl.program_id(0) == 0)
    def _():
        set_bias(bias)

    ks = [kv[:, :HEAD] for kv in kvs]
    v_turned = jnp.concatenate([kv[...] for kv in kvs], axis=0).astype(f32).T[HEAD:].astype(bf16)
    for n in range(GROUP // LANE_HEADS):
        span = slice(n * wide, (n + 1) * wide)
        q = queries[0, :, span]
        scores, top = [], None
        for d in range(shards):
            score = dot(ks[d], q)
            if d == 0:
                score = score + bias[...]
            scores.append(score)
            highest = jnp.max(score, axis=0, keepdims=True) + far_bias(index[2], d)
            top = highest if top is None else jnp.maximum(top, highest)
        total = None
        for d in range(shards):
            term = jnp.exp(scores[d] - (top - far_bias(index[2], d)))
            part = jnp.sum(term, axis=0, keepdims=True)
            total = part if total is None else total + part
            terms[d * rows : (d + 1) * rows, :] = term.astype(bf16)
        out_turned[:, span] = dot(v_turned, terms[...]) / total
        stats[0, :, span] = top + jnp.log(total)
    turned_out[0] = out_turned[...].astype(bf16)
    straight = out_turned[...].T
    for h in range(GROUP):
        out[:, h * HEAD : (h + 1) * HEAD] = straight[h * rows : (h + 1) * rows].astype(bf16)


def attention_call(index, queries, kvs):
    chips, _, wide = queries.shape
    rows = wide // GROUP
    shards = len(kvs)
    keys = shards * rows
    block = pl.BlockSpec((1, HEAD, wide), lambda i, n: (i, 0, 0))
    return kernel_call(
        functools.partial(attention_body, shards),
        (
            shape((chips, HEAD, wide), bf16),
            shape((chips * rows, GROUP * HEAD), bf16),
            shape((chips, 1, wide), f32),
        ),
        [block] + [pl.BlockSpec((rows, 2 * HEAD), lambda i, n: (i, 0))] * shards,
        (
            block,
            pl.BlockSpec((rows, GROUP * HEAD), lambda i, n: (i, 0)),
            pl.BlockSpec((1, 1, wide), lambda i, n: (i, 0, 0)),
        ),
        (queries, *kvs),
        index=index,
        grid=(chips,),
        scratch=(
            VMEM((rows, LANE_HEADS * rows), f32),
            VMEM((keys, LANE_HEADS * rows), bf16),
            VMEM((HEAD, wide), f32),
        ),
        name="attention",
    )


def attention_back_body(shards, index, branch, wo_own, wo_other, cosine, sine, *refs):
    per_group = 3 + shards
    inputs = [refs[n * per_group : (n + 1) * per_group] for n in range(PAIR)]
    grad_q, grad_first, grad_rest = refs[-7:-4]
    bias, probs_low, grads_low, grad_lanes = refs[-4:]
    rows = bias.shape[0]
    wide = LANE_HEADS * rows
    width = branch.shape[1]
    set_bias(bias)
    cos, sin = cosine[...], sine[...]
    for n, (queries, turned_out, stats, *kvs) in enumerate(inputs):
        heads = slice(n * GROUP * HEAD, (n + 1) * GROUP * HEAD)
        grad_out = dot_nt(wo_own[heads, :], branch[:, : width // 2])
        grad_out = grad_out + dot_nt(wo_other[heads, :], branch[:, width // 2 :])
        for h in range(GROUP):
            grad_lanes[:, h * rows : (h + 1) * rows] = grad_out[h * HEAD : (h + 1) * HEAD].astype(bf16)
        ks = [kv[:, :HEAD] for kv in kvs]
        vs = [kv[:, HEAD:] for kv in kvs]
        k_turned = jnp.concatenate([kv[...] for kv in kvs], axis=0).astype(f32).T[:HEAD].astype(bf16)
        k_total, v_total, parts = None, None, []
        for c in range(GROUP // LANE_HEADS):
            span = slice(c * wide, (c + 1) * wide)
            q, mine = queries[0, :, span], grad_lanes[:, span]
            delta = jnp.sum(
                mine.astype(f32) * turned_out[0, :, span].astype(f32), axis=0, keepdims=True
            )
            for d in range(shards):
                score = dot(ks[d], q)
                if d == 0:
                    score = score + bias[...]
                probs = jnp.exp(score - (stats[0, :, span] - far_bias(index[2], d)))
                grad_scores = probs * (dot(vs[d], mine) - delta)
                probs_low[d * rows : (d + 1) * rows, :] = probs.astype(bf16)
                grads_low[d * rows : (d + 1) * rows, :] = grad_scores.astype(bf16)
            u = dot(k_turned, grads_low[...]) * HEAD ** (-0.5)
            parts.append(u * cos - half_rotated(u) * sin)
            k_term = dot_nt(grads_low[...], q)
            v_term = dot_nt(probs_low[...], mine)
            k_total = k_term if k_total is None else k_total + k_term
            v_total = v_term if v_total is None else v_total + v_term
        straight = jnp.concatenate(parts, axis=1).T
        for h in range(GROUP):
            spot = (n * GROUP + h) * HEAD
            grad_q[:, spot : spot + HEAD] = straight[h * rows : (h + 1) * rows].astype(bf16)
        both = jnp.concatenate([k_total, v_total], axis=1)
        spot = slice(n * 2 * HEAD, (n + 1) * 2 * HEAD)
        grad_first[:, spot] = both[:rows, :]
        for d in range(1, shards):
            grad_rest[d - 1, :, spot] = both[d * rows : (d + 1) * rows, :].astype(bf16)


def attention_back_call(index, m, branch, wo_own, wo_other, cosine, sine, groups, before):
    chips, _, wide = groups[0][0].shape
    rows = wide // GROUP
    shards = len(groups[0][3])
    keys = shards * rows
    tokens = chips * rows
    block = pl.BlockSpec((1, HEAD, wide), lambda i, n: (m, 0, 0))
    in_specs = [whole()] * 5
    operands = [branch, wo_own, wo_other, jnp.tile(cosine, (1, LANE_HEADS)), jnp.tile(sine, (1, LANE_HEADS))]
    for queries, turned, stats, kvs in groups:
        in_specs += [block, block, pl.BlockSpec((1, 1, wide), lambda i, n: (m, 0, 0))]
        in_specs += [pl.BlockSpec((rows, 2 * HEAD), lambda i, n: (m, 0))] * shards
        operands += [queries, turned, stats, *kvs]
    aliases = {}
    if before is not None:
        aliases = {1 + len(operands) + n: n for n in range(3)}
        in_specs += [pl.BlockSpec(memory_space=pl.ANY)] * 3
        operands += list(before)
    outs = (
        shape((tokens, PAIR * GROUP * HEAD), bf16),
        shape((tokens, PAIR * 2 * HEAD), f32),
        shape((shards - 1, tokens, PAIR * 2 * HEAD), bf16),
    )
    out_specs = (
        pl.BlockSpec((rows, PAIR * GROUP * HEAD), lambda i, n: (m, 0)),
        pl.BlockSpec((rows, PAIR * 2 * HEAD), lambda i, n: (m, 0)),
        pl.BlockSpec((shards - 1, rows, PAIR * 2 * HEAD), lambda i, n: (0, m, 0)),
    )
    return kernel_call(
        functools.partial(attention_back_body, shards),
        outs,
        in_specs,
        out_specs,
        tuple(operands),
        index=index,
        grid=(1,),
        scratch=(
            VMEM((rows, LANE_HEADS * rows), f32),
            VMEM((keys, LANE_HEADS * rows), bf16),
            VMEM((keys, LANE_HEADS * rows), bf16),
            VMEM((HEAD, wide), bf16),
        ),
        aliases=aliases,
        name="attention_back",
    )


def parts_body(steps, transposed, count, *refs):
    lefts, owns, others = refs[:count], refs[count : 2 * count], refs[2 * count : 3 * count]
    outs = refs[3 * count :]
    rows = outs[0].shape[0]
    step = pl.program_id(0)

    def run(weights):
        total = None
        for left, weight in zip(lefts, weights):
            term = (dot_nt if transposed else dot)(left[...], weight[...])
            total = term if total is None else total + term
        for m, out in enumerate(outs):
            out[...] = total[m * rows : (m + 1) * rows, :].astype(out.dtype)

    @pl.when(step < steps)
    def _():
        run(owns)

    @pl.when(step >= steps)
    def _():
        run(others)


def parts_call(terms, rows, transposed, name):
    tokens = terms[0][0].shape[0]
    half = terms[0][1].shape[0] if transposed else terms[0][1].shape[1]
    tile = 256
    steps = half // tile
    last = steps - 1
    specs = [pl.BlockSpec((tokens, term[0].shape[1]), lambda j: (0, 0)) for term in terms]
    for side in range(2):
        for left, _, _, spot in terms:
            depth = left.shape[1]

            def place(side, spot, j):
                step = jnp.maximum(j - steps, 0) if side else jnp.minimum(j, last)
                return (step, spot) if transposed else (spot, step)

            block = (tile, depth) if transposed else (depth, tile)
            specs.append(pl.BlockSpec(block, functools.partial(place, side, spot)))
    count = tokens // rows
    return kernel_call(
        functools.partial(parts_body, steps, transposed, len(terms)),
        tuple(shape((rows, 2 * half), f32 if m == 0 else bf16) for m in range(count)),
        specs,
        tuple(pl.BlockSpec((rows, tile), lambda j: (0, j)) for _ in range(count)),
        (*(term[0] for term in terms), *(term[1] for term in terms), *(term[2] for term in terms)),
        grid=(2 * steps,),
        name=name,
    )


def gate_body(count, *refs):
    twos = refs[:count]
    gate_own, up_own, gate_other, up_other, act, for_gate, for_up, two_all = refs[count:]
    half = two_all.shape[1] // 2

    @pl.when(pl.program_id(0) == 0)
    def _():
        start = 0
        for two in twos:
            two_all[start : start + two.shape[0], :] = two[...]
            start += two.shape[0]

    own = jnp.concatenate([gate_own[...], up_own[...]], axis=1)
    other = jnp.concatenate([gate_other[...], up_other[...]], axis=1)
    both = dot(two_all[:, :half], own) + dot(two_all[:, half:], other)
    wide = gate_own.shape[1]
    gate, up = both[:, :wide], both[:, wide:]
    sig = 1.0 / (1.0 + jnp.exp(-gate))
    silu = gate * sig
    act[...] = (silu * up).astype(bf16)
    for_gate[...] = (up * sig * (1.0 + gate * (1.0 - sig))).astype(bf16)
    for_up[...] = silu.astype(bf16)


def gate_call(twos, own, other):
    rows, width = twos[0].shape
    tokens = CHIPS * rows
    half = width // 2
    ff = own.shape[1] // 2
    tile = LANES
    steps = ff // tile
    weight = [
        pl.BlockSpec((half, tile), lambda j: (0, j)),
        pl.BlockSpec((half, tile), lambda j: (0, j + steps)),
    ]
    column = pl.BlockSpec((tokens, tile), lambda j: (0, j))
    return kernel_call(
        functools.partial(gate_body, len(twos)),
        tuple(shape((tokens, ff), bf16) for _ in range(3)) + (shape((tokens, width), bf16),),
        [pl.BlockSpec(two.shape, lambda j: (0, 0)) for two in twos] + weight + weight,
        (column, column, column, pl.BlockSpec((tokens, width), lambda j: (0, 0))),
        (*twos, own, own, other, other),
        grid=(steps,),
        name="gate",
    )


def hidden_back_body(g, own, other, for_gate, for_up, grads):
    half = g.shape[1] // 2
    ff = own.shape[0]
    hidden = dot_nt(g[:, :half], own[...]) + dot_nt(g[:, half:], other[...])
    grads[:, :ff] = (hidden * for_gate[...].astype(f32)).astype(bf16)
    grads[:, ff:] = (hidden * for_up[...].astype(f32)).astype(bf16)


def hidden_back_call(g, own, other, for_gate, for_up):
    tokens, width = g.shape
    ff, half = own.shape
    block = tokens // 2
    row = lambda i: (i, 0)
    fixed = lambda i: (0, 0)
    return kernel_call(
        hidden_back_body,
        shape((tokens, 2 * ff), bf16),
        [
            pl.BlockSpec((block, width), row),
            pl.BlockSpec((ff, half), fixed),
            pl.BlockSpec((ff, half), fixed),
            pl.BlockSpec((block, ff), row),
            pl.BlockSpec((block, ff), row),
        ],
        pl.BlockSpec((block, 2 * ff), row),
        (g, own, other, for_gate, for_up),
        grid=(2,),
        name="hidden_back",
    )


def weight_grad_body(per, outputs, adds, left, right, *refs):
    added = [refs[n * outputs : (n + 1) * outputs] for n in range(adds)]
    outs, turned = refs[adds * outputs : -1], refs[-1]
    step = pl.program_id(0)

    @pl.when(step == 0)
    def _():
        turned[...] = left[...].T

    for n in range(outputs):

        @pl.when(step // per == n)
        def _(n=n):
            total = dot(turned[...], right[...])
            for terms in added:
                total = total + terms[n][...].astype(f32)
            outs[n][...] = total.astype(bf16)


def weight_grad(left, left_side, right, place, width, outputs, added, name):
    tokens = left.shape[0]
    rows = left.shape[1] // (1 if left_side is None else 2)
    tile = 256 if width % 256 == 0 else width
    per = width // tile
    first = place * width // tile
    side = left_side or 0

    def spot(n, j):
        return (0, jnp.clip(j - n * per, 0, per - 1))

    tiles = [pl.BlockSpec((rows, tile), functools.partial(spot, n)) for n in range(outputs)]
    return kernel_call(
        functools.partial(weight_grad_body, per, outputs, len(added)),
        tuple(shape((rows, width), bf16) for _ in range(outputs)),
        [
            pl.BlockSpec((tokens, rows), lambda j: (0, side)),
            pl.BlockSpec((tokens, tile), lambda j: (0, first + j)),
        ]
        + tiles * len(added),
        tuple(tiles),
        (left, right, *(term for terms in added for term in terms)),
        grid=(per * outputs,),
        scratch=(VMEM((rows, tokens), bf16),),
        name=name,
    )


def rows_result_body(local, index, *refs):
    pieces, out = refs[:PIECES], refs[PIECES]
    half = local // 2
    shards = out.shape[1] // local
    for m in range(CHIPS):
        for core in range(2):

            @pl.when((pl.program_id(0) == m) & (index[1] == core))
            def _():
                for side in range(2):
                    piece = pieces[2 * m + side]
                    for s in range(shards):
                        spot = s * local + (core ^ side) * half
                        out[:, spot : spot + half] = piece[:, s * half : (s + 1) * half].astype(f32)


def rows_result(index, pieces, local, name):
    cut, half_width = pieces[0].shape
    return kernel_call(
        functools.partial(rows_result_body, local),
        shape((CHIPS * cut, 2 * half_width), f32),
        [pl.BlockSpec((cut, half_width), lambda i, n: (0, 0))] * PIECES,
        pl.BlockSpec((cut, 2 * half_width), lambda i, n: (n[0] ^ i, 0)),
        tuple(pieces),
        index=index,
        grid=(CHIPS,),
        name=name,
    )


def out_result_body(local, base, index, *refs):
    pieces, out = refs[:PIECES], refs[PIECES]
    half = local // 2
    cut = local // CHIPS
    shards = out.shape[1] // local
    for m in range(CHIPS):
        for core in range(2):

            @pl.when((pl.program_id(0) == m) & (index[1] == core))
            def _():
                for side in range(2):
                    piece = pieces[2 * m + side]
                    for s in range(shards):
                        spot = s * local + (core ^ side) * half
                        row, column = (0, s * half) if s * half < 512 else (cut, s * half - 512)
                        column += base
                        out[:, spot : spot + half] = piece[row : row + cut, column : column + half].astype(f32)


def out_result(index, pieces, local, width, base):
    cut = local // CHIPS
    return kernel_call(
        functools.partial(out_result_body, local, base),
        shape((local, width), f32),
        [pl.BlockSpec(pieces[0].shape, lambda i, n: (0, 0))] * PIECES,
        pl.BlockSpec((cut, width), lambda i, n: (n[0] ^ i, 0)),
        tuple(pieces),
        index=index,
        grid=(CHIPS,),
        name="out_result",
    )


def lane_sum(value):
    total = value[:, :LANES]
    for n in range(1, value.shape[1] // LANES):
        total = total + value[:, n * LANES : (n + 1) * LANES]
    return total


def feedforward_result_body(ff_local, cut, index, *refs):
    pieces = refs[:CHIPS]
    gate_weight, up_weight, gain = refs[CHIPS : CHIPS + 3]
    gate_out, up_out, gain_out = refs[-3:]
    shards = gate_weight.shape[1] // ff_local
    width = shards * cut
    for chip in range(CHIPS):

        @pl.when(index[0] == chip)
        def _():
            @pl.loop(0, gate_out.shape[0] // 16)
            def _(n):
                rows = pl.ds(pl.multiple_of(n * 16, 16), 16)
                scale = gain[rows, :1]
                total = jnp.zeros((16, LANES), f32)
                for base, weight, out in ((0, gate_weight, gate_out), (width, up_weight, up_out)):
                    parts = []
                    for s in range(shards):
                        for owner in range(CHIPS):
                            start = base + s * cut
                            parts.append(pieces[owner ^ chip][rows, start : start + cut].astype(f32))
                    wide = jnp.concatenate(parts, axis=1)
                    total = total + lane_sum(wide * weight[rows, :].astype(f32))
                    out[rows, :] = wide * scale
                gain_out[rows, :] = total


def feedforward_result(index, side, pieces, gate_weight, up_weight, gain, ff_local, before):
    local, ff = gate_weight.shape
    half = local // 2
    rows = 64
    steps = half // rows
    row = lambda i, n: ((n[1] ^ side) * steps + i, 0)
    in_specs = [pl.BlockSpec((rows, pieces[0].shape[1]), lambda i, n: (i, 0))] * CHIPS
    in_specs += [pl.BlockSpec((rows, ff), row)] * 2 + [pl.BlockSpec((rows, LANES), row)]
    operands = (*pieces, gate_weight, up_weight, gain)
    aliases = {}
    if before is not None:
        aliases = {1 + len(operands) + n: n for n in range(3)}
        in_specs = in_specs + [pl.BlockSpec(memory_space=pl.ANY)] * 3
        operands = operands + tuple(before)
    return kernel_call(
        functools.partial(feedforward_result_body, ff_local, ff_local // CHIPS),
        (shape((local, ff), f32), shape((local, ff), f32), shape((local, LANES), f32)),
        in_specs,
        (pl.BlockSpec((rows, ff), row), pl.BlockSpec((rows, ff), row), pl.BlockSpec((rows, LANES), row)),
        operands,
        index=index,
        grid=(steps,),
        aliases=aliases,
        name="feedforward_result",
    )


def qkv_result_body(local, group_shards, index, *refs):
    pieces = refs[:PIECES]
    weights, gain = refs[PIECES : PIECES + 3], refs[PIECES + 3]
    outs, gain_out = refs[PIECES + 4 : PIECES + 7], refs[PIECES + 7]
    q_width = GROUP * HEAD
    cut = local // CHIPS
    scale = gain[:, :1]
    for chip in range(CHIPS):
        for side in range(2):

            @pl.when((index[0] == chip) & (pl.program_id(0) == side))
            def _():
                parts, k_parts, v_parts = [], [], []
                for group in range(CHIPS):
                    owner = (group >> 1) + 2 * (group & 1)
                    piece = pieces[2 * (owner ^ chip) + side]
                    for s in range(group_shards):
                        for j in range(CHIPS):
                            start = ((j ^ owner) * group_shards + s) * cut
                            parts.append(piece[:, start : start + cut].astype(f32))
                    k_parts.append(piece[:, q_width : q_width + HEAD].astype(f32))
                    v_parts.append(piece[:, q_width + HEAD : q_width + 2 * HEAD].astype(f32))
                total = jnp.zeros((gain.shape[0], LANES), f32)
                for part, weight, out in zip((parts, k_parts, v_parts), weights, outs):
                    wide = jnp.concatenate(part, axis=1)
                    total = total + lane_sum(wide * weight[...].astype(f32))
                    out[...] = wide * scale
                gain_out[...] = total


def qkv_result(index, pieces, query, key, value, gain):
    local, width = query.shape
    half = local // 2
    group_shards = width // local // CHIPS
    row = lambda i, n: (n[1] ^ i, 0)
    kv_width = key.shape[1]
    return kernel_call(
        functools.partial(qkv_result_body, local, group_shards),
        (
            shape((local, width), f32),
            shape((local, kv_width), f32),
            shape((local, kv_width), f32),
            shape((local, LANES), f32),
        ),
        [pl.BlockSpec(pieces[0].shape, lambda i, n: (0, 0))] * PIECES
        + [
            pl.BlockSpec((half, width), row),
            pl.BlockSpec((half, kv_width), row),
            pl.BlockSpec((half, kv_width), row),
            pl.BlockSpec((half, LANES), row),
        ],
        (
            pl.BlockSpec((half, width), row),
            pl.BlockSpec((half, kv_width), row),
            pl.BlockSpec((half, kv_width), row),
            pl.BlockSpec((half, LANES), row),
        ),
        (*pieces, query, key, value, gain),
        index=index,
        grid=(2,),
        name="qkv_result",
    )


def per_device(
    hidden_in,
    attention_gain,
    query_weight,
    key_weight,
    value_weight,
    output_weight,
    feedforward_gain,
    gate_weight,
    up_weight,
    down_weight,
    out_grad,
):
    rows, width = hidden_in.shape
    shards = lax.axis_size("shard")
    replicas = lax.axis_size("replica")
    place = lax.axis_index("replica")
    depth = lax.axis_index("shard")
    core = place & 1
    chip = (place >> 1) & (CHIPS - 1)
    local = width // shards
    half = local // 2
    ff_local = down_weight.shape[0]
    group_shards = shards // CHIPS
    q_width = GROUP * HEAD
    qkv_width = q_width + 2 * HEAD
    index = jnp.stack([chip, core, depth]).astype(jnp.int32)

    gain_one = jnp.broadcast_to(attention_gain.astype(f32)[:, None], (local, LANES))
    gain_two = jnp.broadcast_to(feedforward_gain.astype(f32)[:, None], (local, LANES))


    at_block, out_block = attention_block(
        index, query_weight, key_weight, value_weight, output_weight, gain_one
    )
    x = own_first(index, (after(hidden_in, at_block),), local)[0]
    xs = [x, swap(x, 2)]
    at_own = lax.all_gather(at_block, "shard", axis=0, tiled=True)
    out_all = lax.all_gather(out_block, "shard", axis=0, tiled=True)
    gu_block = feedforward_block(index, gate_weight, up_weight, after(gain_two, at_block), ff_local)
    gu_own = lax.all_gather(gu_block, "shard", axis=0, tiled=True)
    down_own = lax.all_gather(down_block(index, down_weight, local), "shard", axis=0, tiled=True)
    g = own_first(index, (after(out_grad, x),), local)[0]
    g_blocks = [g, swap(g, 2), swap(g, 4)]
    at_own = after(at_own, gu_block, xs[1], *g_blocks[1:])

    qkv_own = [at_own]
    qkv_own.append(swap(qkv_own[0], 4))
    qkv_other = [swap(qkv_own[0], 1)]
    inverse = rope_base ** (-jnp.arange(0, HEAD, 2, dtype=f32) / HEAD)
    places = (depth * rows + jnp.arange(rows, dtype=jnp.int32)).astype(f32)
    angles = inverse[:, None] * places[None, :]
    angles = jnp.concatenate([angles, angles], axis=0)
    cosine, sine = jnp.cos(angles), jnp.sin(angles)

    def shifted(kv):
        return [kv] + [shift(kv, d) for d in range(1, shards)]

    queries, kv, xhat = qkv_call(xs, qkv_own[0], qkv_other[0], cosine, sine)
    kvs = shifted(kv)
    qkv_own[1] = after(qkv_own[1], *kvs[1:])
    qkv_other.append(swap(qkv_own[1], 1))
    queries_two, kv_two = qkv_call(xhat, qkv_own[1], qkv_other[1], cosine, sine)
    kvs_two = shifted(kv_two)
    groups = [(queries, *attention_call(index, queries, kvs), kvs)]
    groups.append((queries_two, *attention_call(index, queries_two, kvs_two), kvs_two))
    attended = [group[2] for group in groups]
    groups = [(group[0], group[1], group[3], group[4]) for group in groups]

    out_all = after(out_all, qkv_own[1])
    x_place = chip & 1
    low_group = (chip >> 1) == 0
    pair_rows = PAIR * group_shards * half // 2

    def out_for(mask):
        return lax.dynamic_slice_in_dim(out_all, ((chip ^ mask) & 1) * pair_rows, pair_rows, 0)

    out_pieces = [out_for(0)] + [swap(out_for(m), 2 * m) for m in range(1, CHIPS)]
    wo_own = out_rows_call(index, [after(piece, *kvs_two[1:]) for piece in out_pieces])
    wo_other = swap(wo_own, 1)

    mid_terms = [(attended[n], wo_own, wo_other, n) for n in range(PAIR)]
    g_blocks.append(swap(after(g, *out_pieces[1:]), 6))
    mid_out = parts_call(mid_terms, rows, False, "attention_out")
    g_all = jnp.concatenate([after(block, mid_out[0]) for block in g_blocks], axis=0)
    middle, two = middle_call(plane_send(mid_out), after(x, g_all))
    twos = plane_gather_forward(two)

    gu_own = after(gu_own, *twos[1:])
    gu_other = swap(gu_own, 1)
    act, for_gate, for_up, two_all = gate_call(twos, gu_own, gu_other)

    def over_groups(kept):
        if replicas > PIECES:
            groups = [
                [e * PIECES + i for e in range(replicas // PIECES)] for i in range(PIECES)
            ]
            kept = lax.psum(kept, "replica", axis_index_groups=groups)
        return kept

    def reduced(term):
        kept = lax.psum_scatter(term, "shard", scatter_dimension=0, tiled=True)
        return over_groups(kept)

    def plane_pieces(kept):
        mine = plane_gather(kept)
        return mine, [swap(part, 1) for part in mine]

    def mixed(mine, theirs):
        return [part for pair in zip(mine, theirs) for part in pair]

    down_sent = weight_grad(act, None, g_all, 1, width // 2, 1, (), "down_grad_other")
    down_sent = [swap(down_sent[0], 1)]
    down_sent[0] = after(down_sent[0], down_own)
    down_term = weight_grad(act, None, g_all, 0, width // 2, 1, (down_sent,), "down_grad")[0]
    down_kept = reduced(down_term)
    down_other = swap(down_own, 1)

    grads = hidden_back_call(after(g_all, down_term), down_own, down_other, for_gate, for_up)
    grads_wide = grads.shape[1]
    gu_sent = weight_grad(two_all, 1, grads, 0, grads_wide, 1, (), "gate_grad_other")
    gu_sent = [swap(gu_sent[0], 1)]
    gu_term = weight_grad(two_all, 0, grads, 0, grads_wide, 1, (gu_sent,), "gate_grad")[0]
    gu_kept = reduced(gu_term)
    grads_late = after(grads, gu_term)
    e_terms = parts_call([(grads_late, gu_own, gu_other, 0)], rows, True, "feedforward_back")
    e_parts = plane_send(e_terms)
    act_late = after(act, e_terms[0])
    out_terms = parts_call([(act_late, down_own, down_other, 0)], rows, False, "feedforward_out")

    middle_late = after(middle, out_terms[0], down_kept)
    grad_middle, branch = grad_middle_call(e_parts, middle_late, g)
    branches = [branch, swap(branch, 2)]

    def back_block(m, block, before):
        return attention_back_call(index, m, block, wo_own, wo_other, cosine, sine, groups, before)

    before = back_block(0, branch, None)
    out_parts = plane_send(after(out_terms, branches[1], before[1]))
    before = back_block(1, after(branches[1], before[1]), before)
    output = output_call(index, out_parts, middle, local)
    grad_q, grad_first, grad_rest = before
    grad_rest = after(grad_rest, *out_parts[1:3])
    rest = [shift(grad_rest[d - 1], -d) for d in range(1, shards)]

    half_wide = width // 2
    branch_all = jnp.concatenate([after(block, grad_first, *out_parts[1:3]) for block in branches], axis=0)
    both_attended = jnp.concatenate(attended, axis=1)
    wo_sent = weight_grad(both_attended, None, branch_all, 1, half_wide, 1, (), "out_grad_other")
    wo_sent = [after(swap(wo_sent[0], 1), rest[-1])]
    wo_term = weight_grad(both_attended, None, branch_all, 0, half_wide, 1, (wo_sent,), "out_grad")[0]
    wo_terms = out_sends(index, wo_term)
    wo_parts = plane_send(wo_terms)
    wo_wide = out_block_call(index, [after(wo_parts[0], gu_kept), *wo_parts[1:]], shards)
    grad_first = after(grad_first, out_parts[3], wo_terms[0])
    grad_qkv = grad_qkv_call(grad_q, grad_first, rest, cosine, sine)

    def qkv_grad(n, side, added, name):
        return weight_grad(xhat, side, grad_qkv[n], 0, qkv_width, 1, added, name)

    qkv_sent = [swap(qkv_grad(n, 1, (), "qkv_grad_other")[0], 1) for n in (1, 0)]
    back_terms = [(grad_qkv[n], qkv_own[n], qkv_other[n], 0) for n in range(PAIR)]
    qkv_sent[0] = after(qkv_sent[0], *wo_parts[1:3])
    qkv_second = qkv_grad(1, 0, ([qkv_sent[0]],), "qkv_grad")[0]
    qkv_term = qkv_grad(0, 0, ([qkv_sent[1]],), "qkv_grad")[0]
    at_term = jnp.concatenate([qkv_term, qkv_second, wo_wide], axis=1)
    at_kept = reduced(after(at_term, gu_kept))
    back_terms[0] = (after(grad_qkv[0], qkv_term, qkv_second), *back_terms[0][1:])
    back_parts = parts_call(back_terms, rows, True, "qkv_back")
    e_one = plane_send(back_parts)
    gu_mine = plane_gather_forward(gu_kept, back_parts[0])
    gu_mine = gu_mine[:3] + [jnp.concatenate(gu_mine[3:], axis=0)]
    gu_theirs = [swap(after(part, output), 1) for part in gu_mine]
    gu_out = feedforward_result(index, 0, gu_mine, gate_weight, up_weight, gain_two, ff_local, None)
    at_kept = after(at_kept, gu_out[0])
    gu_out = feedforward_result(index, 1, gu_theirs, gate_weight, up_weight, gain_two, ff_local, gu_out)

    down_mine = plane_gather(after(down_kept, *gu_mine[1:]))
    down_theirs = [swap(part, 1) for part in down_mine]
    down_out = rows_result(index, mixed(down_mine, down_theirs), local, "down_result")
    grad_input = grad_input_call(index, e_one, x, grad_middle, local)

    second = swap(at_kept[:, qkv_width : 2 * qkv_width], 4)
    first = at_kept[:, :qkv_width].astype(f32) + second.astype(f32)
    at_kept = jnp.concatenate([first.astype(bf16), at_kept[:, 2 * qkv_width :]], axis=1)
    at_pieces = mixed(*plane_pieces(at_kept))
    at_pieces[0] = after(at_pieces[0], gu_out[0], down_out, grad_input)
    wo_out = out_result(index, at_pieces, local, width, qkv_width)
    q_out, k_out, v_out, gain_one_sums = qkv_result(
        index, at_pieces, query_weight, key_weight, value_weight, gain_one
    )
    return (
        output,
        grad_input,
        jnp.sum(gain_one_sums, axis=1),
        q_out,
        k_out,
        v_out,
        wo_out,
        jnp.sum(gu_out[2], axis=1),
        gu_out[0],
        gu_out[1],
        down_out,
    )


def solution(mesh):
    return jax.shard_map(
        per_device,
        mesh=mesh,
        in_specs=(
            P(("replica", "shard"), None),
            P("shard"),
            P("shard", None),
            P("shard", None),
            P("shard", None),
            P("shard", None),
            P("shard"),
            P("shard", None),
            P("shard", None),
            P("shard", None),
            P(("replica", "shard"), None),
        ),
        out_specs=(
            P(("replica", "shard"), None),
            P(("replica", "shard"), None),
            P("shard"),
            P("shard", None),
            P("shard", None),
            P("shard", None),
            P("shard", None),
            P("shard"),
            P("shard", None),
            P("shard", None),
            P("shard", None),
        ),
        check_vma=False,
    )
```

```python
import functools

import jax
import jax.numpy as jnp
from jax import lax
from jax.experimental import pallas as pl
from jax.experimental.pallas import tpu as pltpu
from jax.sharding import PartitionSpec as P

HEADS = 32
KV_HEADS = 4
HEAD = 64
GROUP = HEADS // KV_HEADS
CHIPS = 4
PIECES = 2 * CHIPS
PAIR = 2
LANES = 128

norm_eps = 1e-05
rope_base = 10000.0
masked_score = -1e30

f32 = jnp.float32
bf16 = jnp.bfloat16
VMEM = pltpu.VMEM
NT = (((1,), (1,)), ((), ()))
TN = (((0,), (0,)), ((), ()))


def dot(left, right):
    return jnp.dot(left, right, preferred_element_type=f32)


def dot_nt(left, right):
    return lax.dot_general(left, right, NT, preferred_element_type=f32)


def dot_tn(left, right):
    return lax.dot_general(left, right, TN, preferred_element_type=f32)


def shape(dims, kind):
    return jax.ShapeDtypeStruct(dims, kind)


def whole():
    return pl.BlockSpec(memory_space=VMEM)


TIMES = {"attention_back": 13.0}


def kernel_call(body, out_shape, in_specs, out_specs, operands, *, index=None, grid=(), scratch=(),
                aliases=None, name=None):
    params = pltpu.CompilerParams(
        vmem_limit_bytes=52 * 2**20, dimension_semantics=("arbitrary",) * len(grid)
    )
    moved = int(TIMES.get(name, 0.0) * 3.69e6)
    cost = pl.CostEstimate(flops=0, bytes_accessed=moved, transcendentals=0)
    common = dict(
        out_shape=out_shape,
        compiler_params=params,
        cost_estimate=cost,
        input_output_aliases=aliases or {},
        name=name,
    )
    if index is None:
        spec = pl.GridSpec(grid=grid, in_specs=in_specs, out_specs=out_specs, scratch_shapes=scratch)
        return pl.pallas_call(body, grid_spec=spec, **common)(*operands)
    spec = pltpu.PrefetchScalarGridSpec(
        num_scalar_prefetch=1, grid=grid, in_specs=in_specs, out_specs=out_specs,
        scratch_shapes=scratch,
    )
    return pl.pallas_call(body, grid_spec=spec, **common)(index, *operands)


def swap(value, mask):
    size = lax.axis_size("replica")
    return lax.ppermute(value, "replica", [(i, i ^ mask) for i in range(size)])


def shift(value, step):
    size = lax.axis_size("shard")
    pairs = [(i, i + step) for i in range(size) if 0 <= i + step < size]
    return lax.ppermute(value, "shard", pairs)


def plane_gather(value):
    return [value] + [swap(value, 2 * m) for m in range(1, CHIPS)]


def plane_gather_forward(value, *before):
    middle = value.shape[0] // 2
    across, along = swap(value, 2), swap(value, 4)
    if before:
        across, along = after(across, *before), after(along, *before)
    return [value, across, along, swap(across[:middle], 4), swap(along[middle:], 2)]


def plane_send(parts):
    return [parts[0]] + [swap(parts[m], 2 * m) for m in range(1, len(parts))]


def group_of(chip):
    return 2 * (chip & 1) + (chip >> 1)


def after(value, *others):
    return lax.optimization_barrier((value, *others))[0]


def attention_block_body(local, group_shards, index, q, k, v, o, gain, out, wo_out):
    scale = gain[:, :1]
    q_width = GROUP * HEAD
    cut = local // CHIPS
    for chip in range(CHIPS):

        group = group_of(chip)

        @pl.when(index[0] == chip)
        def _(group=group):
            parts = []
            for m in range(CHIPS):
                for s in range(group_shards):
                    start = group * q_width + s * local + (m ^ chip) * cut
                    parts.append(q[:, start : start + cut])
            parts.append(k[:, group * HEAD : (group + 1) * HEAD])
            parts.append(v[:, group * HEAD : (group + 1) * HEAD])
            wide = jnp.concatenate([part.astype(f32) for part in parts], axis=1)
            out[...] = (wide * scale).astype(bf16)

    half = local // 2
    shards = o.shape[1] // local
    for core in range(2):

        @pl.when(index[1] == core)
        def _():
            for s in range(shards):
                piece = o[:, s * local + core * half : s * local + (core + 1) * half]
                wo_out[:, s * half : (s + 1) * half] = piece


def attention_block(index, query, key, value, output, gain):
    local, width = query.shape
    half = local // 2
    shards = width // local
    return kernel_call(
        functools.partial(attention_block_body, local, shards // CHIPS),
        (
            shape((half, GROUP * HEAD + 2 * HEAD), bf16),
            shape((local // CHIPS, width // 2), bf16),
        ),
        [
            pl.BlockSpec((half, width), lambda i, n: (n[1], 0)),
            pl.BlockSpec((half, key.shape[1]), lambda i, n: (n[1], 0)),
            pl.BlockSpec((half, key.shape[1]), lambda i, n: (n[1], 0)),
            pl.BlockSpec((local // CHIPS, width), lambda i, n: (n[0], 0)),
            pl.BlockSpec((half, LANES), lambda i, n: (n[1], 0)),
        ],
        (
            pl.BlockSpec((half, GROUP * HEAD + 2 * HEAD), lambda i, n: (0, 0)),
            pl.BlockSpec((local // CHIPS, width // 2), lambda i, n: (0, 0)),
        ),
        (query, key, value, output, gain),
        index=index,
        grid=(1,),
        name="attention_block",
    )


def feedforward_block_body(ff_local, cut, index, gate, up, gain, out):
    scale = gain[:, :1]
    shards = gate.shape[1] // ff_local
    width = shards * cut
    for chip in range(CHIPS):

        @pl.when(index[0] == chip)
        def _():
            for n, source in enumerate((gate, up)):
                parts = [
                    source[:, s * ff_local + chip * cut : s * ff_local + (chip + 1) * cut].astype(f32)
                    for s in range(shards)
                ]
                wide = jnp.concatenate(parts, axis=1)
                out[:, n * width : (n + 1) * width] = (wide * scale).astype(bf16)


def feedforward_block(index, gate, up, gain, ff_local):
    local, ff = gate.shape
    half = local // 2
    rows = 64
    steps = half // rows
    cut = ff_local // CHIPS
    width = 2 * (ff // CHIPS)
    return kernel_call(
        functools.partial(feedforward_block_body, ff_local, cut),
        shape((half, width), bf16),
        [
            pl.BlockSpec((rows, ff), lambda i, n: (n[1] * steps + i, 0)),
            pl.BlockSpec((rows, ff), lambda i, n: (n[1] * steps + i, 0)),
            pl.BlockSpec((rows, LANES), lambda i, n: (n[1] * steps + i, 0)),
        ],
        pl.BlockSpec((rows, width), lambda i, n: (i, 0)),
        (gate, up, gain),
        index=index,
        grid=(steps,),
        name="feedforward_block",
    )


def own_first_body(local, index, *refs):
    count = len(refs) // 2
    half = local // 2
    for core in range(2):

        @pl.when(index[1] == core)
        def _():
            for source, out in zip(refs[:count], refs[count:]):
                shards = source.shape[1] // local
                sides = out.shape[1] // (shards * half)
                for side in range(sides):
                    for s in range(shards):
                        start = s * local + (core ^ side) * half
                        spot = (side * shards + s) * half
                        out[:, spot : spot + half] = source[:, start : start + half]


def own_first(index, sources, local, halves=2):
    return kernel_call(
        functools.partial(own_first_body, local),
        tuple(shape((v.shape[0], v.shape[1] * halves // 2), bf16) for v in sources),
        [pl.BlockSpec(v.shape, lambda i, n: (0, 0)) for v in sources],
        tuple(
            pl.BlockSpec((v.shape[0], v.shape[1] * halves // 2), lambda i, n: (0, 0)) for v in sources
        ),
        tuple(sources),
        index=index,
        grid=(1,),
        name="own_first",
    )


def down_block_body(local, index, source, out):
    own_first_body(local, index, source, out)


def down_block(index, down, local):
    ff_local, width = down.shape
    cut = ff_local // CHIPS
    return kernel_call(
        functools.partial(down_block_body, local),
        shape((cut, width // 2), bf16),
        [pl.BlockSpec((cut, width), lambda i, n: (n[0], 0))],
        pl.BlockSpec((cut, width // 2), lambda i, n: (0, 0)),
        (down,),
        index=index,
        grid=(1,),
        name="down_block",
    )


def part_sum(parts):
    total = parts[0][...]
    for part in parts[1:]:
        total = total + part[...].astype(f32)
    return total


def mean_of(values):
    return jnp.mean(values, axis=1, keepdims=True)


def middle_body(*refs):
    parts, (x, middle, two) = refs[:PAIR], refs[PAIR:]
    total = x[...].astype(f32) + part_sum(parts)
    middle[...] = total
    two[...] = (total * lax.rsqrt(mean_of(total * total) + norm_eps)).astype(bf16)


def middle_call(parts, x):
    return kernel_call(
        middle_body,
        (shape(x.shape, f32), shape(x.shape, bf16)),
        [whole()] * (PAIR + 1),
        (whole(), whole()),
        (*parts, x),
        name="middle",
    )


def norm_back(e, values):
    inverse = lax.rsqrt(mean_of(values * values) + norm_eps)
    return inverse * e - values * (inverse * inverse * inverse) * mean_of(e * values)


def grad_middle_body(*refs):
    parts, (middle, g, grad, low) = refs[:CHIPS], refs[CHIPS:]
    total = g[...].astype(f32) + norm_back(part_sum(parts), middle[...])
    grad[...] = total
    low[...] = total.astype(bf16)


def grad_middle_call(parts, middle, g):
    return kernel_call(
        grad_middle_body,
        (shape(g.shape, f32), shape(g.shape, bf16)),
        [whole()] * (CHIPS + 2),
        (whole(), whole()),
        (*parts, middle, g),
        name="grad_middle",
    )


def store_in_order(local, index, value, out):
    half = local // 2
    shards = out.shape[1] // local
    for core in range(2):

        @pl.when(index[1] == core)
        def _():
            for side in range(2):
                for s in range(shards):
                    spot = s * local + (core ^ side) * half
                    start = (side * shards + s) * half
                    out[:, spot : spot + half] = value[:, start : start + half].astype(bf16)


def output_body(local, index, *refs):
    parts, (middle, out) = refs[:CHIPS], refs[CHIPS:]
    store_in_order(local, index, middle[...] + part_sum(parts), out)


def output_call(index, parts, middle, local):
    spec = pl.BlockSpec(middle.shape, lambda i, n: (0, 0))
    return kernel_call(
        functools.partial(output_body, local),
        shape(middle.shape, bf16),
        [spec] * (CHIPS + 1),
        spec,
        (*parts, middle),
        index=index,
        grid=(1,),
        name="output",
    )


def grad_input_body(local, index, *refs):
    parts, (x, grad, out) = refs[:PAIR], refs[PAIR:]
    total = grad[...] + norm_back(part_sum(parts), x[...].astype(f32))
    store_in_order(local, index, total, out)


def grad_input_call(index, parts, x, grad, local):
    spec = pl.BlockSpec(x.shape, lambda i, n: (0, 0))
    return kernel_call(
        functools.partial(grad_input_body, local),
        shape(x.shape, bf16),
        [spec] * (PAIR + 2),
        spec,
        (*parts, x, grad),
        index=index,
        grid=(1,),
        name="grad_input",
    )


def grad_qkv_body(shards, grad_q, first, *refs):
    rest, (cosine, sine), outs = refs[: shards - 1], refs[shards - 1 : shards + 1], refs[shards + 1 :]
    total = first[...]
    for term in rest:
        total = total + term[...].astype(f32)
    rows = cosine.shape[1]
    width = GROUP * HEAD
    cos, sin = cosine[...], sine[...]
    for n, out in enumerate(outs):
        out[:, :width] = grad_q[:, n * width : (n + 1) * width]
        for m in range(PAIR):
            span = slice(m * rows, (m + 1) * rows)
            turned = total[span, n * 2 * HEAD : (n + 1) * 2 * HEAD].T
            k = turned[:HEAD]
            k = k * cos - half_rotated(k) * sin
            both = jnp.concatenate([k, turned[HEAD:]], axis=0)
            out[span, width:] = both.T.astype(bf16)


def grad_qkv_call(grad_q, first, rest, cosine, sine):
    tokens = grad_q.shape[0]
    return kernel_call(
        functools.partial(grad_qkv_body, len(rest) + 1),
        (shape((tokens, GROUP * HEAD + 2 * HEAD), bf16),) * PAIR,
        [whole()] * (len(rest) + 4),
        (whole(),) * PAIR,
        (grad_q, first, *rest, cosine, sine),
        name="grad_qkv",
    )


def out_sends_body(index, term, *outs):
    cut = outs[0].shape[0] // PAIR
    for row in range(2):

        @pl.when(index[0] >> 1 == row)
        def _():
            for n in range(PAIR):
                for m in range(CHIPS):
                    spot = (n * CHIPS + m) * cut
                    start = (n ^ row) * cut
                    outs[m ^ (2 * n)][start : start + cut, :] = term[spot : spot + cut, :]


def out_sends(index, term):
    rows, width = term.shape
    rows //= CHIPS
    return kernel_call(
        out_sends_body,
        (shape((rows, width), bf16),) * CHIPS,
        [pl.BlockSpec(term.shape, lambda i, n: (0, 0))],
        (pl.BlockSpec((rows, width), lambda i, n: (0, 0)),) * CHIPS,
        (term,),
        index=index,
        grid=(1,),
        name="out_sends",
    )


def out_block_body(shards, index, *refs):
    parts, out = refs[:CHIPS], refs[CHIPS]
    group_shards = shards // CHIPS
    cut = parts[0].shape[0] // (PAIR * group_shards)
    sums = [parts[m][...].astype(f32) + parts[m + 2][...].astype(f32) for m in range(2)]
    for side in range(2):

        @pl.when(index[0] & 1 == side)
        def _():
            for m in range(2):
                for n in range(PAIR * group_shards):
                    shard = (m ^ side) * PAIR * group_shards + n
                    rows = sums[m][n * cut : (n + 1) * cut].astype(bf16)
                    out[2 * shard * cut : (2 * shard + 1) * cut, :] = rows[:, :512]
                    out[(2 * shard + 1) * cut : (2 * shard + 2) * cut, :] = rows[:, 512:]


def out_block_call(index, parts, shards):
    rows, width = parts[0].shape
    return kernel_call(
        functools.partial(out_block_body, shards),
        shape((2 * PAIR * rows, width // 2), bf16),
        [pl.BlockSpec((rows, width), lambda i, n: (0, 0))] * CHIPS,
        pl.BlockSpec((2 * PAIR * rows, width // 2), lambda i, n: (0, 0)),
        tuple(parts),
        index=index,
        grid=(1,),
        name="out_block",
    )


def half_rotated(values):
    middle = values.shape[0] // 2
    return jnp.concatenate([-values[middle:], values[:middle]], axis=0)


def qkv_body(make, *refs):
    if make:
        xs, (own, other, cosine, sine, queries, kv, xhat) = refs[:PAIR], refs[PAIR:]
        rows, width = xs[0].shape
        for m in range(PAIR):
            x = xs[m][...].astype(f32)
            inverse = lax.rsqrt(mean_of(x * x) + norm_eps)
            xhat[m * rows : (m + 1) * rows, :] = (x * inverse).astype(bf16)
    else:
        xhat, own, other, cosine, sine, queries, kv = refs
        rows, width = cosine.shape[1], xhat.shape[1]
    cos, sin = cosine[...], sine[...]
    total = dot(xhat[:, : width // 2], own[...]) + dot(xhat[:, width // 2 :], other[...])
    for m in range(PAIR):
        turned = total[m * rows : (m + 1) * rows].T
        for h in range(GROUP + 1):
            u = turned[h * HEAD : (h + 1) * HEAD]
            u = u * cos + half_rotated(u) * sin
            if h < GROUP:
                queries[m, :, h * rows : (h + 1) * rows] = (u * HEAD ** (-0.5)).astype(bf16)
            else:
                both = jnp.concatenate([u, turned[(h + 1) * HEAD :]], axis=0)
                kv[m * rows : (m + 1) * rows, :] = both.T.astype(bf16)


def qkv_call(xs, own, other, cosine, sine):
    make = isinstance(xs, list)
    rows = cosine.shape[1]
    tokens = PAIR * rows
    outs = (shape((PAIR, HEAD, GROUP * rows), bf16), shape((tokens, 2 * HEAD), bf16))
    if make:
        outs = outs + (shape((tokens, xs[0].shape[1]), bf16),)
    operands = (*(xs if make else (xs,)), own, other, cosine, sine)
    return kernel_call(
        functools.partial(qkv_body, make),
        outs,
        [whole()] * len(operands),
        tuple(whole() for _ in outs),
        operands,
        name="qkv",
    )


def out_rows_body(index, *refs):
    pieces, out = refs[:CHIPS], refs[CHIPS]
    cut = pieces[0].shape[0] // PAIR
    for row in range(2):

        @pl.when(index[0] >> 1 == row)
        def _():
            for n in range(PAIR):
                for m in range(CHIPS):
                    spot = (n * CHIPS + m) * cut
                    start = (n ^ row) * cut
                    out[spot : spot + cut, :] = pieces[m ^ (2 * n)][start : start + cut, :]


def out_rows_call(index, pieces):
    rows, width = pieces[0].shape
    return kernel_call(
        out_rows_body,
        shape((CHIPS * rows, width), bf16),
        [pl.BlockSpec((rows, width), lambda i, n: (0, 0))] * CHIPS,
        pl.BlockSpec((CHIPS * rows, width), lambda i, n: (0, 0)),
        tuple(pieces),
        index=index,
        grid=(1,),
        name="out_rows",
    )


LANE_HEADS = 4


def own_block_bias(rows):
    key = lax.broadcasted_iota(jnp.int32, (rows, rows), 0)
    mine = lax.broadcasted_iota(jnp.int32, (rows, rows), 1)
    return jnp.where(key <= mine, 0.0, masked_score)


def set_bias(bias):
    rows = bias.shape[0]
    value = own_block_bias(rows)
    for h in range(LANE_HEADS):
        bias[:, h * rows : (h + 1) * rows] = value


def far_bias(depth, d):
    return jnp.where(d <= depth, 0.0, masked_score) if d else 0.0


def attention_body(shards, index, queries, *refs):
    kvs = refs[:shards]
    turned_out, out, stats, bias, terms, out_turned = refs[shards:]
    rows = bias.shape[0]
    wide = LANE_HEADS * rows

    @pl.when(pl.program_id(0) == 0)
    def _():
        set_bias(bias)

    ks = [kv[:, :HEAD] for kv in kvs]
    v_turned = jnp.concatenate([kv[...] for kv in kvs], axis=0).astype(f32).T[HEAD:].astype(bf16)
    for n in range(GROUP // LANE_HEADS):
        span = slice(n * wide, (n + 1) * wide)
        q = queries[0, :, span]
        scores, top = [], None
        for d in range(shards):
            score = dot(ks[d], q)
            if d == 0:
                score = score + bias[...]
            scores.append(score)
            highest = jnp.max(score, axis=0, keepdims=True) + far_bias(index[2], d)
            top = highest if top is None else jnp.maximum(top, highest)
        total = None
        for d in range(shards):
            term = jnp.exp(scores[d] - (top - far_bias(index[2], d)))
            part = jnp.sum(term, axis=0, keepdims=True)
            total = part if total is None else total + part
            terms[d * rows : (d + 1) * rows, :] = term.astype(bf16)
        out_turned[:, span] = dot(v_turned, terms[...]) / total
        stats[0, :, span] = top + jnp.log(total)
    turned_out[0] = out_turned[...].astype(bf16)
    straight = out_turned[...].T
    for h in range(GROUP):
        out[:, h * HEAD : (h + 1) * HEAD] = straight[h * rows : (h + 1) * rows].astype(bf16)


def attention_call(index, queries, kvs):
    chips, _, wide = queries.shape
    rows = wide // GROUP
    shards = len(kvs)
    keys = shards * rows
    block = pl.BlockSpec((1, HEAD, wide), lambda i, n: (i, 0, 0))
    return kernel_call(
        functools.partial(attention_body, shards),
        (
            shape((chips, HEAD, wide), bf16),
            shape((chips * rows, GROUP * HEAD), bf16),
            shape((chips, 1, wide), f32),
        ),
        [block] + [pl.BlockSpec((rows, 2 * HEAD), lambda i, n: (i, 0))] * shards,
        (
            block,
            pl.BlockSpec((rows, GROUP * HEAD), lambda i, n: (i, 0)),
            pl.BlockSpec((1, 1, wide), lambda i, n: (i, 0, 0)),
        ),
        (queries, *kvs),
        index=index,
        grid=(chips,),
        scratch=(
            VMEM((rows, LANE_HEADS * rows), f32),
            VMEM((keys, LANE_HEADS * rows), bf16),
            VMEM((HEAD, wide), f32),
        ),
        name="attention",
    )


def attention_back_body(shards, index, branch, wo_own, wo_other, cosine, sine, *refs):
    per_group = 3 + shards
    inputs = [refs[n * per_group : (n + 1) * per_group] for n in range(PAIR)]
    grad_q, grad_first, grad_rest = refs[-7:-4]
    bias, probs_low, grads_low, grad_lanes = refs[-4:]
    rows = bias.shape[0]
    wide = LANE_HEADS * rows
    width = branch.shape[1]
    set_bias(bias)
    cos, sin = cosine[...], sine[...]
    for n, (queries, turned_out, stats, *kvs) in enumerate(inputs):
        heads = slice(n * GROUP * HEAD, (n + 1) * GROUP * HEAD)
        grad_out = dot_nt(wo_own[heads, :], branch[:, : width // 2])
        grad_out = grad_out + dot_nt(wo_other[heads, :], branch[:, width // 2 :])
        for h in range(GROUP):
            grad_lanes[:, h * rows : (h + 1) * rows] = grad_out[h * HEAD : (h + 1) * HEAD].astype(bf16)
        ks = [kv[:, :HEAD] for kv in kvs]
        vs = [kv[:, HEAD:] for kv in kvs]
        k_turned = jnp.concatenate([kv[...] for kv in kvs], axis=0).astype(f32).T[:HEAD].astype(bf16)
        k_total, v_total, parts = None, None, []
        for c in range(GROUP // LANE_HEADS):
            span = slice(c * wide, (c + 1) * wide)
            q, mine = queries[0, :, span], grad_lanes[:, span]
            delta = jnp.sum(
                mine.astype(f32) * turned_out[0, :, span].astype(f32), axis=0, keepdims=True
            )
            for d in range(shards):
                score = dot(ks[d], q)
                if d == 0:
                    score = score + bias[...]
                probs = jnp.exp(score - (stats[0, :, span] - far_bias(index[2], d)))
                grad_scores = probs * (dot(vs[d], mine) - delta)
                probs_low[d * rows : (d + 1) * rows, :] = probs.astype(bf16)
                grads_low[d * rows : (d + 1) * rows, :] = grad_scores.astype(bf16)
            u = dot(k_turned, grads_low[...]) * HEAD ** (-0.5)
            parts.append(u * cos - half_rotated(u) * sin)
            k_term = dot_nt(grads_low[...], q)
            v_term = dot_nt(probs_low[...], mine)
            k_total = k_term if k_total is None else k_total + k_term
            v_total = v_term if v_total is None else v_total + v_term
        straight = jnp.concatenate(parts, axis=1).T
        for h in range(GROUP):
            spot = (n * GROUP + h) * HEAD
            grad_q[:, spot : spot + HEAD] = straight[h * rows : (h + 1) * rows].astype(bf16)
        both = jnp.concatenate([k_total, v_total], axis=1)
        spot = slice(n * 2 * HEAD, (n + 1) * 2 * HEAD)
        grad_first[:, spot] = both[:rows, :]
        for d in range(1, shards):
            grad_rest[d - 1, :, spot] = both[d * rows : (d + 1) * rows, :].astype(bf16)


def attention_back_call(index, m, branch, wo_own, wo_other, cosine, sine, groups, before):
    chips, _, wide = groups[0][0].shape
    rows = wide // GROUP
    shards = len(groups[0][3])
    keys = shards * rows
    tokens = chips * rows
    block = pl.BlockSpec((1, HEAD, wide), lambda i, n: (m, 0, 0))
    in_specs = [whole()] * 5
    operands = [branch, wo_own, wo_other, jnp.tile(cosine, (1, LANE_HEADS)), jnp.tile(sine, (1, LANE_HEADS))]
    for queries, turned, stats, kvs in groups:
        in_specs += [block, block, pl.BlockSpec((1, 1, wide), lambda i, n: (m, 0, 0))]
        in_specs += [pl.BlockSpec((rows, 2 * HEAD), lambda i, n: (m, 0))] * shards
        operands += [queries, turned, stats, *kvs]
    aliases = {}
    if before is not None:
        aliases = {1 + len(operands) + n: n for n in range(3)}
        in_specs += [pl.BlockSpec(memory_space=pl.ANY)] * 3
        operands += list(before)
    outs = (
        shape((tokens, PAIR * GROUP * HEAD), bf16),
        shape((tokens, PAIR * 2 * HEAD), f32),
        shape((shards - 1, tokens, PAIR * 2 * HEAD), bf16),
    )
    out_specs = (
        pl.BlockSpec((rows, PAIR * GROUP * HEAD), lambda i, n: (m, 0)),
        pl.BlockSpec((rows, PAIR * 2 * HEAD), lambda i, n: (m, 0)),
        pl.BlockSpec((shards - 1, rows, PAIR * 2 * HEAD), lambda i, n: (0, m, 0)),
    )
    return kernel_call(
        functools.partial(attention_back_body, shards),
        outs,
        in_specs,
        out_specs,
        tuple(operands),
        index=index,
        grid=(1,),
        scratch=(
            VMEM((rows, LANE_HEADS * rows), f32),
            VMEM((keys, LANE_HEADS * rows), bf16),
            VMEM((keys, LANE_HEADS * rows), bf16),
            VMEM((HEAD, wide), bf16),
        ),
        aliases=aliases,
        name="attention_back",
    )


def parts_body(steps, transposed, count, *refs):
    lefts, owns, others = refs[:count], refs[count : 2 * count], refs[2 * count : 3 * count]
    outs = refs[3 * count :]
    rows = outs[0].shape[0]
    step = pl.program_id(0)

    def run(weights):
        total = None
        for left, weight in zip(lefts, weights):
            term = (dot_nt if transposed else dot)(left[...], weight[...])
            total = term if total is None else total + term
        for m, out in enumerate(outs):
            out[...] = total[m * rows : (m + 1) * rows, :].astype(out.dtype)

    @pl.when(step < steps)
    def _():
        run(owns)

    @pl.when(step >= steps)
    def _():
        run(others)


def parts_call(terms, rows, transposed, name):
    tokens = terms[0][0].shape[0]
    half = terms[0][1].shape[0] if transposed else terms[0][1].shape[1]
    tile = 256
    steps = half // tile
    last = steps - 1
    specs = [pl.BlockSpec((tokens, term[0].shape[1]), lambda j: (0, 0)) for term in terms]
    for side in range(2):
        for left, _, _, spot in terms:
            depth = left.shape[1]

            def place(side, spot, j):
                step = jnp.maximum(j - steps, 0) if side else jnp.minimum(j, last)
                return (step, spot) if transposed else (spot, step)

            block = (tile, depth) if transposed else (depth, tile)
            specs.append(pl.BlockSpec(block, functools.partial(place, side, spot)))
    count = tokens // rows
    return kernel_call(
        functools.partial(parts_body, steps, transposed, len(terms)),
        tuple(shape((rows, 2 * half), f32 if m == 0 else bf16) for m in range(count)),
        specs,
        tuple(pl.BlockSpec((rows, tile), lambda j: (0, j)) for _ in range(count)),
        (*(term[0] for term in terms), *(term[1] for term in terms), *(term[2] for term in terms)),
        grid=(2 * steps,),
        name=name,
    )


def gate_body(count, *refs):
    twos = refs[:count]
    gate_own, up_own, gate_other, up_other, act, for_gate, for_up, two_all = refs[count:]
    half = two_all.shape[1] // 2

    @pl.when(pl.program_id(0) == 0)
    def _():
        start = 0
        for two in twos:
            two_all[start : start + two.shape[0], :] = two[...]
            start += two.shape[0]

    own = jnp.concatenate([gate_own[...], up_own[...]], axis=1)
    other = jnp.concatenate([gate_other[...], up_other[...]], axis=1)
    both = dot(two_all[:, :half], own) + dot(two_all[:, half:], other)
    wide = gate_own.shape[1]
    gate, up = both[:, :wide], both[:, wide:]
    sig = 1.0 / (1.0 + jnp.exp(-gate))
    silu = gate * sig
    act[...] = (silu * up).astype(bf16)
    for_gate[...] = (up * sig * (1.0 + gate * (1.0 - sig))).astype(bf16)
    for_up[...] = silu.astype(bf16)


def gate_call(twos, own, other):
    rows, width = twos[0].shape
    tokens = CHIPS * rows
    half = width // 2
    ff = own.shape[1] // 2
    tile = LANES
    steps = ff // tile
    weight = [
        pl.BlockSpec((half, tile), lambda j: (0, j)),
        pl.BlockSpec((half, tile), lambda j: (0, j + steps)),
    ]
    column = pl.BlockSpec((tokens, tile), lambda j: (0, j))
    return kernel_call(
        functools.partial(gate_body, len(twos)),
        tuple(shape((tokens, ff), bf16) for _ in range(3)) + (shape((tokens, width), bf16),),
        [pl.BlockSpec(two.shape, lambda j: (0, 0)) for two in twos] + weight + weight,
        (column, column, column, pl.BlockSpec((tokens, width), lambda j: (0, 0))),
        (*twos, own, own, other, other),
        grid=(steps,),
        name="gate",
    )


def hidden_back_body(g, own, other, for_gate, for_up, grads):
    half = g.shape[1] // 2
    ff = own.shape[0]
    hidden = dot_nt(g[:, :half], own[...]) + dot_nt(g[:, half:], other[...])
    grads[:, :ff] = (hidden * for_gate[...].astype(f32)).astype(bf16)
    grads[:, ff:] = (hidden * for_up[...].astype(f32)).astype(bf16)


def hidden_back_call(g, own, other, for_gate, for_up):
    tokens, width = g.shape
    ff, half = own.shape
    block = tokens // 2
    row = lambda i: (i, 0)
    fixed = lambda i: (0, 0)
    return kernel_call(
        hidden_back_body,
        shape((tokens, 2 * ff), bf16),
        [
            pl.BlockSpec((block, width), row),
            pl.BlockSpec((ff, half), fixed),
            pl.BlockSpec((ff, half), fixed),
            pl.BlockSpec((block, ff), row),
            pl.BlockSpec((block, ff), row),
        ],
        pl.BlockSpec((block, 2 * ff), row),
        (g, own, other, for_gate, for_up),
        grid=(2,),
        name="hidden_back",
    )


def weight_grad_body(per, outputs, adds, left, right, *refs):
    added = [refs[n * outputs : (n + 1) * outputs] for n in range(adds)]
    outs, turned = refs[adds * outputs : -1], refs[-1]
    step = pl.program_id(0)

    @pl.when(step == 0)
    def _():
        turned[...] = left[...].T

    for n in range(outputs):

        @pl.when(step // per == n)
        def _(n=n):
            total = dot(turned[...], right[...])
            for terms in added:
                total = total + terms[n][...].astype(f32)
            outs[n][...] = total.astype(bf16)


def weight_grad(left, left_side, right, place, width, outputs, added, name):
    tokens = left.shape[0]
    rows = left.shape[1] // (1 if left_side is None else 2)
    tile = 256 if width % 256 == 0 else width
    per = width // tile
    first = place * width // tile
    side = left_side or 0

    def spot(n, j):
        return (0, jnp.clip(j - n * per, 0, per - 1))

    tiles = [pl.BlockSpec((rows, tile), functools.partial(spot, n)) for n in range(outputs)]
    return kernel_call(
        functools.partial(weight_grad_body, per, outputs, len(added)),
        tuple(shape((rows, width), bf16) for _ in range(outputs)),
        [
            pl.BlockSpec((tokens, rows), lambda j: (0, side)),
            pl.BlockSpec((tokens, tile), lambda j: (0, first + j)),
        ]
        + tiles * len(added),
        tuple(tiles),
        (left, right, *(term for terms in added for term in terms)),
        grid=(per * outputs,),
        scratch=(VMEM((rows, tokens), bf16),),
        name=name,
    )


def rows_result_body(local, index, *refs):
    pieces, out = refs[:PIECES], refs[PIECES]
    half = local // 2
    shards = out.shape[1] // local
    for m in range(CHIPS):
        for core in range(2):

            @pl.when((pl.program_id(0) == m) & (index[1] == core))
            def _():
                for side in range(2):
                    piece = pieces[2 * m + side]
                    for s in range(shards):
                        spot = s * local + (core ^ side) * half
                        out[:, spot : spot + half] = piece[:, s * half : (s + 1) * half].astype(f32)


def rows_result(index, pieces, local, name):
    cut, half_width = pieces[0].shape
    return kernel_call(
        functools.partial(rows_result_body, local),
        shape((CHIPS * cut, 2 * half_width), f32),
        [pl.BlockSpec((cut, half_width), lambda i, n: (0, 0))] * PIECES,
        pl.BlockSpec((cut, 2 * half_width), lambda i, n: (n[0] ^ i, 0)),
        tuple(pieces),
        index=index,
        grid=(CHIPS,),
        name=name,
    )


def out_result_body(local, base, index, *refs):
    pieces, out = refs[:PIECES], refs[PIECES]
    half = local // 2
    cut = local // CHIPS
    shards = out.shape[1] // local
    for m in range(CHIPS):
        for core in range(2):

            @pl.when((pl.program_id(0) == m) & (index[1] == core))
            def _():
                for side in range(2):
                    piece = pieces[2 * m + side]
                    for s in range(shards):
                        spot = s * local + (core ^ side) * half
                        row, column = (0, s * half) if s * half < 512 else (cut, s * half - 512)
                        column += base
                        out[:, spot : spot + half] = piece[row : row + cut, column : column + half].astype(f32)


def out_result(index, pieces, local, width, base):
    cut = local // CHIPS
    return kernel_call(
        functools.partial(out_result_body, local, base),
        shape((local, width), f32),
        [pl.BlockSpec(pieces[0].shape, lambda i, n: (0, 0))] * PIECES,
        pl.BlockSpec((cut, width), lambda i, n: (n[0] ^ i, 0)),
        tuple(pieces),
        index=index,
        grid=(CHIPS,),
        name="out_result",
    )


def lane_sum(value):
    total = value[:, :LANES]
    for n in range(1, value.shape[1] // LANES):
        total = total + value[:, n * LANES : (n + 1) * LANES]
    return total


def feedforward_result_body(ff_local, cut, index, *refs):
    pieces = refs[:CHIPS]
    gate_weight, up_weight, gain = refs[CHIPS : CHIPS + 3]
    gate_out, up_out, gain_out = refs[-3:]
    shards = gate_weight.shape[1] // ff_local
    width = shards * cut
    for chip in range(CHIPS):

        @pl.when(index[0] == chip)
        def _():
            @pl.loop(0, gate_out.shape[0] // 16)
            def _(n):
                rows = pl.ds(pl.multiple_of(n * 16, 16), 16)
                scale = gain[rows, :1]
                total = jnp.zeros((16, LANES), f32)
                for base, weight, out in ((0, gate_weight, gate_out), (width, up_weight, up_out)):
                    parts = []
                    for s in range(shards):
                        for owner in range(CHIPS):
                            start = base + s * cut
                            parts.append(pieces[owner ^ chip][rows, start : start + cut].astype(f32))
                    wide = jnp.concatenate(parts, axis=1)
                    total = total + lane_sum(wide * weight[rows, :].astype(f32))
                    out[rows, :] = wide * scale
                gain_out[rows, :] = total


def feedforward_result(index, side, pieces, gate_weight, up_weight, gain, ff_local, before):
    local, ff = gate_weight.shape
    half = local // 2
    rows = 64
    steps = half // rows
    row = lambda i, n: ((n[1] ^ side) * steps + i, 0)
    in_specs = [pl.BlockSpec((rows, pieces[0].shape[1]), lambda i, n: (i, 0))] * CHIPS
    in_specs += [pl.BlockSpec((rows, ff), row)] * 2 + [pl.BlockSpec((rows, LANES), row)]
    operands = (*pieces, gate_weight, up_weight, gain)
    aliases = {}
    if before is not None:
        aliases = {1 + len(operands) + n: n for n in range(3)}
        in_specs = in_specs + [pl.BlockSpec(memory_space=pl.ANY)] * 3
        operands = operands + tuple(before)
    return kernel_call(
        functools.partial(feedforward_result_body, ff_local, ff_local // CHIPS),
        (shape((local, ff), f32), shape((local, ff), f32), shape((local, LANES), f32)),
        in_specs,
        (pl.BlockSpec((rows, ff), row), pl.BlockSpec((rows, ff), row), pl.BlockSpec((rows, LANES), row)),
        operands,
        index=index,
        grid=(steps,),
        aliases=aliases,
        name="feedforward_result",
    )


def qkv_result_body(local, group_shards, index, *refs):
    pieces = refs[:PIECES]
    weights, gain = refs[PIECES : PIECES + 3], refs[PIECES + 3]
    outs, gain_out = refs[PIECES + 4 : PIECES + 7], refs[PIECES + 7]
    q_width = GROUP * HEAD
    cut = local // CHIPS
    scale = gain[:, :1]
    for chip in range(CHIPS):
        for side in range(2):

            @pl.when((index[0] == chip) & (pl.program_id(0) == side))
            def _():
                parts, k_parts, v_parts = [], [], []
                for group in range(CHIPS):
                    owner = (group >> 1) + 2 * (group & 1)
                    piece = pieces[2 * (owner ^ chip) + side]
                    for s in range(group_shards):
                        for j in range(CHIPS):
                            start = ((j ^ owner) * group_shards + s) * cut
                            parts.append(piece[:, start : start + cut].astype(f32))
                    k_parts.append(piece[:, q_width : q_width + HEAD].astype(f32))
                    v_parts.append(piece[:, q_width + HEAD : q_width + 2 * HEAD].astype(f32))
                total = jnp.zeros((gain.shape[0], LANES), f32)
                for part, weight, out in zip((parts, k_parts, v_parts), weights, outs):
                    wide = jnp.concatenate(part, axis=1)
                    total = total + lane_sum(wide * weight[...].astype(f32))
                    out[...] = wide * scale
                gain_out[...] = total


def qkv_result(index, pieces, query, key, value, gain):
    local, width = query.shape
    half = local // 2
    group_shards = width // local // CHIPS
    row = lambda i, n: (n[1] ^ i, 0)
    kv_width = key.shape[1]
    return kernel_call(
        functools.partial(qkv_result_body, local, group_shards),
        (
            shape((local, width), f32),
            shape((local, kv_width), f32),
            shape((local, kv_width), f32),
            shape((local, LANES), f32),
        ),
        [pl.BlockSpec(pieces[0].shape, lambda i, n: (0, 0))] * PIECES
        + [
            pl.BlockSpec((half, width), row),
            pl.BlockSpec((half, kv_width), row),
            pl.BlockSpec((half, kv_width), row),
            pl.BlockSpec((half, LANES), row),
        ],
        (
            pl.BlockSpec((half, width), row),
            pl.BlockSpec((half, kv_width), row),
            pl.BlockSpec((half, kv_width), row),
            pl.BlockSpec((half, LANES), row),
        ),
        (*pieces, query, key, value, gain),
        index=index,
        grid=(2,),
        name="qkv_result",
    )


def per_device(
    hidden_in,
    attention_gain,
    query_weight,
    key_weight,
    value_weight,
    output_weight,
    feedforward_gain,
    gate_weight,
    up_weight,
    down_weight,
    out_grad,
):
    rows, width = hidden_in.shape
    shards = lax.axis_size("shard")
    replicas = lax.axis_size("replica")
    place = lax.axis_index("replica")
    depth = lax.axis_index("shard")
    core = place & 1
    chip = (place >> 1) & (CHIPS - 1)
    local = width // shards
    half = local // 2
    ff_local = down_weight.shape[0]
    group_shards = shards // CHIPS
    q_width = GROUP * HEAD
    qkv_width = q_width + 2 * HEAD
    index = jnp.stack([chip, core, depth]).astype(jnp.int32)

    gain_one = jnp.broadcast_to(attention_gain.astype(f32)[:, None], (local, LANES))
    gain_two = jnp.broadcast_to(feedforward_gain.astype(f32)[:, None], (local, LANES))


    at_block, out_block = attention_block(
        index, query_weight, key_weight, value_weight, output_weight, gain_one
    )
    x = own_first(index, (after(hidden_in, at_block),), local)[0]
    xs = [x, swap(x, 2)]
    at_own = lax.all_gather(at_block, "shard", axis=0, tiled=True)
    out_all = lax.all_gather(out_block, "shard", axis=0, tiled=True)
    gu_block = feedforward_block(index, gate_weight, up_weight, after(gain_two, at_block), ff_local)
    gu_own = lax.all_gather(gu_block, "shard", axis=0, tiled=True)
    down_own = lax.all_gather(down_block(index, down_weight, local), "shard", axis=0, tiled=True)
    g = own_first(index, (after(out_grad, x),), local)[0]
    g_blocks = [g, swap(g, 2), swap(g, 4)]
    at_own = after(at_own, gu_block, xs[1], *g_blocks[1:])

    qkv_own = [at_own]
    qkv_own.append(swap(qkv_own[0], 4))
    qkv_other = [swap(qkv_own[0], 1)]
    inverse = rope_base ** (-jnp.arange(0, HEAD, 2, dtype=f32) / HEAD)
    places = (depth * rows + jnp.arange(rows, dtype=jnp.int32)).astype(f32)
    angles = inverse[:, None] * places[None, :]
    angles = jnp.concatenate([angles, angles], axis=0)
    cosine, sine = jnp.cos(angles), jnp.sin(angles)

    def shifted(kv):
        return [kv] + [shift(kv, d) for d in range(1, shards)]

    queries, kv, xhat = qkv_call(xs, qkv_own[0], qkv_other[0], cosine, sine)
    kvs = shifted(kv)
    qkv_own[1] = after(qkv_own[1], *kvs[1:])
    qkv_other.append(swap(qkv_own[1], 1))
    queries_two, kv_two = qkv_call(xhat, qkv_own[1], qkv_other[1], cosine, sine)
    kvs_two = shifted(kv_two)
    groups = [(queries, *attention_call(index, queries, kvs), kvs)]
    groups.append((queries_two, *attention_call(index, queries_two, kvs_two), kvs_two))
    attended = [group[2] for group in groups]
    groups = [(group[0], group[1], group[3], group[4]) for group in groups]

    out_all = after(out_all, qkv_own[1])
    x_place = chip & 1
    low_group = (chip >> 1) == 0
    pair_rows = PAIR * group_shards * half // 2

    def out_for(mask):
        return lax.dynamic_slice_in_dim(out_all, ((chip ^ mask) & 1) * pair_rows, pair_rows, 0)

    out_pieces = [out_for(0)] + [swap(out_for(m), 2 * m) for m in range(1, CHIPS)]
    wo_own = out_rows_call(index, [after(piece, *kvs_two[1:]) for piece in out_pieces])
    wo_other = swap(wo_own, 1)

    mid_terms = [(attended[n], wo_own, wo_other, n) for n in range(PAIR)]
    g_blocks.append(swap(after(g, *out_pieces[1:]), 6))
    mid_out = parts_call(mid_terms, rows, False, "attention_out")
    g_all = jnp.concatenate([after(block, mid_out[0]) for block in g_blocks], axis=0)
    middle, two = middle_call(plane_send(mid_out), after(x, g_all))
    twos = plane_gather_forward(two)

    gu_own = after(gu_own, *twos[1:])
    gu_other = swap(gu_own, 1)
    act, for_gate, for_up, two_all = gate_call(twos, gu_own, gu_other)

    def over_groups(kept):
        if replicas > PIECES:
            groups = [
                [e * PIECES + i for e in range(replicas // PIECES)] for i in range(PIECES)
            ]
            kept = lax.psum(kept, "replica", axis_index_groups=groups)
        return kept

    def reduced(term):
        kept = lax.psum_scatter(term, "shard", scatter_dimension=0, tiled=True)
        return over_groups(kept)

    def plane_pieces(kept):
        mine = plane_gather(kept)
        return mine, [swap(part, 1) for part in mine]

    def mixed(mine, theirs):
        return [part for pair in zip(mine, theirs) for part in pair]

    down_sent = weight_grad(act, None, g_all, 1, width // 2, 1, (), "down_grad_other")
    down_sent = [swap(down_sent[0], 1)]
    down_sent[0] = after(down_sent[0], down_own)
    down_term = weight_grad(act, None, g_all, 0, width // 2, 1, (down_sent,), "down_grad")[0]
    down_kept = reduced(down_term)
    down_other = swap(down_own, 1)

    grads = hidden_back_call(after(g_all, down_term), down_own, down_other, for_gate, for_up)
    grads_wide = grads.shape[1]
    gu_sent = weight_grad(two_all, 1, grads, 0, grads_wide, 1, (), "gate_grad_other")
    gu_sent = [swap(gu_sent[0], 1)]
    gu_term = weight_grad(two_all, 0, grads, 0, grads_wide, 1, (gu_sent,), "gate_grad")[0]
    gu_kept = reduced(gu_term)
    grads_late = after(grads, gu_term)
    e_terms = parts_call([(grads_late, gu_own, gu_other, 0)], rows, True, "feedforward_back")
    e_parts = plane_send(e_terms)
    act_late = after(act, e_terms[0])
    out_terms = parts_call([(act_late, down_own, down_other, 0)], rows, False, "feedforward_out")

    middle_late = after(middle, out_terms[0], down_kept)
    grad_middle, branch = grad_middle_call(e_parts, middle_late, g)
    branches = [branch, swap(branch, 2)]

    def back_block(m, block, before):
        return attention_back_call(index, m, block, wo_own, wo_other, cosine, sine, groups, before)

    before = back_block(0, branch, None)
    out_parts = plane_send(after(out_terms, branches[1], before[1]))
    half_wide = width // 2
    branch_all = jnp.concatenate([branch, after(branches[1], before[1])], axis=0)
    both_attended = jnp.concatenate(attended, axis=1)
    wo_sent = weight_grad(both_attended, None, branch_all, 1, half_wide, 1, (), "out_grad_other")
    wo_other_term = wo_sent[0]
    wo_sent = [swap(wo_other_term, 1)]
    before = back_block(1, after(branches[1], before[1], wo_other_term), before)
    output = output_call(index, out_parts, middle, local)
    grad_q, grad_first, grad_rest = before
    grad_rest = after(grad_rest, *out_parts[1:3])
    rest = [shift(grad_rest[d - 1], -d) for d in range(1, shards)]

    wo_term = weight_grad(both_attended, None, branch_all, 0, half_wide, 1, (wo_sent,), "out_grad")[0]
    wo_terms = out_sends(index, after(wo_term, *rest))
    wo_parts = plane_send(wo_terms)
    wo_wide = out_block_call(index, [after(wo_parts[0], gu_kept), *wo_parts[1:]], shards)
    grad_first = after(grad_first, out_parts[3], wo_parts[1], wo_parts[2])
    grad_qkv = grad_qkv_call(grad_q, grad_first, rest, cosine, sine)

    def qkv_grad(n, side, added, name):
        return weight_grad(xhat, side, grad_qkv[n], 0, qkv_width, 1, added, name)

    qkv_sent = [swap(qkv_grad(n, 1, (), "qkv_grad_other")[0], 1) for n in (1, 0)]
    back_terms = [(grad_qkv[n], qkv_own[n], qkv_other[n], 0) for n in range(PAIR)]
    qkv_sent[0] = after(qkv_sent[0], *wo_parts[1:3])
    qkv_second = qkv_grad(1, 0, ([qkv_sent[0]],), "qkv_grad")[0]
    qkv_term = qkv_grad(0, 0, ([qkv_sent[1]],), "qkv_grad")[0]
    at_term = jnp.concatenate([qkv_term, qkv_second, wo_wide], axis=1)
    at_kept = reduced(after(at_term, gu_kept))
    back_terms[0] = (after(grad_qkv[0], qkv_term, qkv_second), *back_terms[0][1:])
    back_parts = parts_call(back_terms, rows, True, "qkv_back")
    e_one = plane_send(back_parts)
    gu_mine = plane_gather_forward(gu_kept, back_parts[0])
    gu_mine = gu_mine[:3] + [jnp.concatenate(gu_mine[3:], axis=0)]
    gu_theirs = [swap(after(part, output), 1) for part in gu_mine]
    gu_mine[0] = after(gu_mine[0], *gu_theirs)
    gu_out = feedforward_result(index, 0, gu_mine, gate_weight, up_weight, gain_two, ff_local, None)
    gu_out = feedforward_result(index, 1, gu_theirs, gate_weight, up_weight, gain_two, ff_local, gu_out)

    down_mine = plane_gather(after(down_kept, *gu_mine[1:]))
    down_theirs = [swap(part, 1) for part in down_mine]
    down_out = rows_result(index, mixed(down_mine, down_theirs), local, "down_result")
    grad_input = grad_input_call(index, e_one, x, grad_middle, local)

    at_kept = after(at_kept, gu_out[0], down_out, grad_input)
    second = swap(at_kept[:, qkv_width : 2 * qkv_width], 4)
    first = at_kept[:, :qkv_width].astype(f32) + second.astype(f32)
    at_kept = jnp.concatenate([first.astype(bf16), at_kept[:, 2 * qkv_width :]], axis=1)
    at_pieces = mixed(*plane_pieces(at_kept))
    at_pieces[0] = after(at_pieces[0], gu_out[0], down_out, grad_input)
    wo_out = out_result(index, at_pieces, local, width, qkv_width)
    q_out, k_out, v_out, gain_one_sums = qkv_result(
        index, at_pieces, query_weight, key_weight, value_weight, gain_one
    )
    return (
        output,
        grad_input,
        jnp.sum(gain_one_sums, axis=1),
        q_out,
        k_out,
        v_out,
        wo_out,
        jnp.sum(gu_out[2], axis=1),
        gu_out[0],
        gu_out[1],
        down_out,
    )


def solution(mesh):
    return jax.shard_map(
        per_device,
        mesh=mesh,
        in_specs=(
            P(("replica", "shard"), None),
            P("shard"),
            P("shard", None),
            P("shard", None),
            P("shard", None),
            P("shard", None),
            P("shard"),
            P("shard", None),
            P("shard", None),
            P("shard", None),
            P(("replica", "shard"), None),
        ),
        out_specs=(
            P(("replica", "shard"), None),
            P(("replica", "shard"), None),
            P("shard"),
            P("shard", None),
            P("shard", None),
            P("shard", None),
            P("shard", None),
            P("shard"),
            P("shard", None),
            P("shard", None),
            P("shard", None),
        ),
        check_vma=False,
    )
```

```python
import functools

import jax
import jax.numpy as jnp
from jax import lax
from jax.experimental import pallas as pl
from jax.experimental.pallas import tpu as pltpu
from jax.sharding import PartitionSpec as P

HEADS = 32
KV_HEADS = 4
HEAD = 64
GROUP = HEADS // KV_HEADS
CHIPS = 4
PIECES = 2 * CHIPS
PAIR = 2
LANES = 128

norm_eps = 1e-05
rope_base = 10000.0
masked_score = -1e30

f32 = jnp.float32
bf16 = jnp.bfloat16
VMEM = pltpu.VMEM
NT = (((1,), (1,)), ((), ()))
TN = (((0,), (0,)), ((), ()))


def dot(left, right):
    return jnp.dot(left, right, preferred_element_type=f32)


def dot_nt(left, right):
    return lax.dot_general(left, right, NT, preferred_element_type=f32)


def dot_tn(left, right):
    return lax.dot_general(left, right, TN, preferred_element_type=f32)


def shape(dims, kind):
    return jax.ShapeDtypeStruct(dims, kind)


def whole():
    return pl.BlockSpec(memory_space=VMEM)


TIMES = {"attention_back": 13.0}


def kernel_call(body, out_shape, in_specs, out_specs, operands, *, index=None, grid=(), scratch=(),
                aliases=None, name=None):
    params = pltpu.CompilerParams(
        vmem_limit_bytes=52 * 2**20, dimension_semantics=("arbitrary",) * len(grid)
    )
    moved = int(TIMES.get(name, 0.0) * 3.69e6)
    cost = pl.CostEstimate(flops=0, bytes_accessed=moved, transcendentals=0)
    common = dict(
        out_shape=out_shape,
        compiler_params=params,
        cost_estimate=cost,
        input_output_aliases=aliases or {},
        name=name,
    )
    if index is None:
        spec = pl.GridSpec(grid=grid, in_specs=in_specs, out_specs=out_specs, scratch_shapes=scratch)
        return pl.pallas_call(body, grid_spec=spec, **common)(*operands)
    spec = pltpu.PrefetchScalarGridSpec(
        num_scalar_prefetch=1, grid=grid, in_specs=in_specs, out_specs=out_specs,
        scratch_shapes=scratch,
    )
    return pl.pallas_call(body, grid_spec=spec, **common)(index, *operands)


def swap(value, mask):
    size = lax.axis_size("replica")
    return lax.ppermute(value, "replica", [(i, i ^ mask) for i in range(size)])


def shift(value, step):
    size = lax.axis_size("shard")
    pairs = [(i, i + step) for i in range(size) if 0 <= i + step < size]
    return lax.ppermute(value, "shard", pairs)


def plane_gather(value):
    return [value] + [swap(value, 2 * m) for m in range(1, CHIPS)]


def plane_gather_near(value):
    return swap(value, 2), swap(value, 4)


def plane_gather_far(value, across, along):
    middle = value.shape[0] // 2
    return [value, across, along, swap(across[:middle], 4), swap(along[middle:], 2)]


def plane_send(parts):
    return [parts[0]] + [swap(parts[m], 2 * m) for m in range(1, len(parts))]


def group_of(chip):
    return 2 * (chip & 1) + (chip >> 1)


def after(value, *others):
    return lax.optimization_barrier((value, *others))[0]


def attention_block_body(local, group_shards, index, q, k, v, o, gain, out, wo_out):
    scale = gain[:, :1]
    q_width = GROUP * HEAD
    cut = local // CHIPS
    for chip in range(CHIPS):

        group = group_of(chip)

        @pl.when(index[0] == chip)
        def _(group=group):
            parts = []
            for m in range(CHIPS):
                for s in range(group_shards):
                    start = group * q_width + s * local + (m ^ chip) * cut
                    parts.append(q[:, start : start + cut])
            parts.append(k[:, group * HEAD : (group + 1) * HEAD])
            parts.append(v[:, group * HEAD : (group + 1) * HEAD])
            wide = jnp.concatenate([part.astype(f32) for part in parts], axis=1)
            out[...] = (wide * scale).astype(bf16)

    half = local // 2
    shards = o.shape[1] // local
    for core in range(2):

        @pl.when(index[1] == core)
        def _():
            for s in range(shards):
                piece = o[:, s * local + core * half : s * local + (core + 1) * half]
                wo_out[:, s * half : (s + 1) * half] = piece


def attention_block(index, query, key, value, output, gain):
    local, width = query.shape
    half = local // 2
    shards = width // local
    return kernel_call(
        functools.partial(attention_block_body, local, shards // CHIPS),
        (
            shape((half, GROUP * HEAD + 2 * HEAD), bf16),
            shape((local // CHIPS, width // 2), bf16),
        ),
        [
            pl.BlockSpec((half, width), lambda i, n: (n[1], 0)),
            pl.BlockSpec((half, key.shape[1]), lambda i, n: (n[1], 0)),
            pl.BlockSpec((half, key.shape[1]), lambda i, n: (n[1], 0)),
            pl.BlockSpec((local // CHIPS, width), lambda i, n: (n[0], 0)),
            pl.BlockSpec((half, LANES), lambda i, n: (n[1], 0)),
        ],
        (
            pl.BlockSpec((half, GROUP * HEAD + 2 * HEAD), lambda i, n: (0, 0)),
            pl.BlockSpec((local // CHIPS, width // 2), lambda i, n: (0, 0)),
        ),
        (query, key, value, output, gain),
        index=index,
        grid=(1,),
        name="attention_block",
    )


def feedforward_block_body(ff_local, cut, index, gate, up, gain, out):
    scale = gain[:, :1]
    shards = gate.shape[1] // ff_local
    width = shards * cut
    for chip in range(CHIPS):

        @pl.when(index[0] == chip)
        def _():
            for n, source in enumerate((gate, up)):
                parts = [
                    source[:, s * ff_local + chip * cut : s * ff_local + (chip + 1) * cut].astype(f32)
                    for s in range(shards)
                ]
                wide = jnp.concatenate(parts, axis=1)
                out[:, n * width : (n + 1) * width] = (wide * scale).astype(bf16)


def feedforward_block(index, gate, up, gain, ff_local):
    local, ff = gate.shape
    half = local // 2
    rows = 64
    steps = half // rows
    cut = ff_local // CHIPS
    width = 2 * (ff // CHIPS)
    return kernel_call(
        functools.partial(feedforward_block_body, ff_local, cut),
        shape((half, width), bf16),
        [
            pl.BlockSpec((rows, ff), lambda i, n: (n[1] * steps + i, 0)),
            pl.BlockSpec((rows, ff), lambda i, n: (n[1] * steps + i, 0)),
            pl.BlockSpec((rows, LANES), lambda i, n: (n[1] * steps + i, 0)),
        ],
        pl.BlockSpec((rows, width), lambda i, n: (i, 0)),
        (gate, up, gain),
        index=index,
        grid=(steps,),
        name="feedforward_block",
    )


def own_first_body(local, index, *refs):
    count = len(refs) // 2
    half = local // 2
    for core in range(2):

        @pl.when(index[1] == core)
        def _():
            for source, out in zip(refs[:count], refs[count:]):
                shards = source.shape[1] // local
                sides = out.shape[1] // (shards * half)
                for side in range(sides):
                    for s in range(shards):
                        start = s * local + (core ^ side) * half
                        spot = (side * shards + s) * half
                        out[:, spot : spot + half] = source[:, start : start + half]


def own_first(index, sources, local, halves=2):
    return kernel_call(
        functools.partial(own_first_body, local),
        tuple(shape((v.shape[0], v.shape[1] * halves // 2), bf16) for v in sources),
        [pl.BlockSpec(v.shape, lambda i, n: (0, 0)) for v in sources],
        tuple(
            pl.BlockSpec((v.shape[0], v.shape[1] * halves // 2), lambda i, n: (0, 0)) for v in sources
        ),
        tuple(sources),
        index=index,
        grid=(1,),
        name="own_first",
    )


def down_block_body(local, index, source, out):
    own_first_body(local, index, source, out)


def down_block(index, down, local):
    ff_local, width = down.shape
    cut = ff_local // CHIPS
    return kernel_call(
        functools.partial(down_block_body, local),
        shape((cut, width // 2), bf16),
        [pl.BlockSpec((cut, width), lambda i, n: (n[0], 0))],
        pl.BlockSpec((cut, width // 2), lambda i, n: (0, 0)),
        (down,),
        index=index,
        grid=(1,),
        name="down_block",
    )


def part_sum(parts):
    total = parts[0][...]
    for part in parts[1:]:
        total = total + part[...].astype(f32)
    return total


def mean_of(values):
    return jnp.mean(values, axis=1, keepdims=True)


def middle_body(*refs):
    parts, (x, middle, two) = refs[:PAIR], refs[PAIR:]
    total = x[...].astype(f32) + part_sum(parts)
    middle[...] = total
    two[...] = (total * lax.rsqrt(mean_of(total * total) + norm_eps)).astype(bf16)


def middle_call(parts, x):
    return kernel_call(
        middle_body,
        (shape(x.shape, f32), shape(x.shape, bf16)),
        [whole()] * (PAIR + 1),
        (whole(), whole()),
        (*parts, x),
        name="middle",
    )


def norm_back(e, values):
    inverse = lax.rsqrt(mean_of(values * values) + norm_eps)
    return inverse * e - values * (inverse * inverse * inverse) * mean_of(e * values)


def grad_middle_body(*refs):
    parts, (middle, g, grad, low) = refs[:CHIPS], refs[CHIPS:]
    total = g[...].astype(f32) + norm_back(part_sum(parts), middle[...])
    grad[...] = total
    low[...] = total.astype(bf16)


def grad_middle_call(parts, middle, g):
    return kernel_call(
        grad_middle_body,
        (shape(g.shape, f32), shape(g.shape, bf16)),
        [whole()] * (CHIPS + 2),
        (whole(), whole()),
        (*parts, middle, g),
        name="grad_middle",
    )


def store_in_order(local, index, value, out):
    half = local // 2
    shards = out.shape[1] // local
    for core in range(2):

        @pl.when(index[1] == core)
        def _():
            for side in range(2):
                for s in range(shards):
                    spot = s * local + (core ^ side) * half
                    start = (side * shards + s) * half
                    out[:, spot : spot + half] = value[:, start : start + half].astype(bf16)


def output_body(local, index, *refs):
    parts, (middle, out) = refs[:CHIPS], refs[CHIPS:]
    store_in_order(local, index, middle[...] + part_sum(parts), out)


def output_call(index, parts, middle, local):
    spec = pl.BlockSpec(middle.shape, lambda i, n: (0, 0))
    return kernel_call(
        functools.partial(output_body, local),
        shape(middle.shape, bf16),
        [spec] * (CHIPS + 1),
        spec,
        (*parts, middle),
        index=index,
        grid=(1,),
        name="output",
    )


def grad_input_body(local, index, *refs):
    parts, (x, grad, out) = refs[:PAIR], refs[PAIR:]
    total = grad[...] + norm_back(part_sum(parts), x[...].astype(f32))
    store_in_order(local, index, total, out)


def grad_input_call(index, parts, x, grad, local):
    spec = pl.BlockSpec(x.shape, lambda i, n: (0, 0))
    return kernel_call(
        functools.partial(grad_input_body, local),
        shape(x.shape, bf16),
        [spec] * (PAIR + 2),
        spec,
        (*parts, x, grad),
        index=index,
        grid=(1,),
        name="grad_input",
    )


def grad_qkv_body(shards, grad_q, first, *refs):
    rest, (cosine, sine), outs = refs[: shards - 1], refs[shards - 1 : shards + 1], refs[shards + 1 :]
    total = first[...]
    for term in rest:
        total = total + term[...].astype(f32)
    rows = cosine.shape[1]
    width = GROUP * HEAD
    cos, sin = cosine[...], sine[...]
    for n, out in enumerate(outs):
        out[:, :width] = grad_q[:, n * width : (n + 1) * width]
        for m in range(PAIR):
            span = slice(m * rows, (m + 1) * rows)
            turned = total[span, n * 2 * HEAD : (n + 1) * 2 * HEAD].T
            k = turned[:HEAD]
            k = k * cos - half_rotated(k) * sin
            both = jnp.concatenate([k, turned[HEAD:]], axis=0)
            out[span, width:] = both.T.astype(bf16)


def grad_qkv_call(grad_q, first, rest, cosine, sine):
    tokens = grad_q.shape[0]
    return kernel_call(
        functools.partial(grad_qkv_body, len(rest) + 1),
        (shape((tokens, GROUP * HEAD + 2 * HEAD), bf16),) * PAIR,
        [whole()] * (len(rest) + 4),
        (whole(),) * PAIR,
        (grad_q, first, *rest, cosine, sine),
        name="grad_qkv",
    )


def out_sends_body(index, term, *outs):
    cut = outs[0].shape[0] // PAIR
    for row in range(2):

        @pl.when(index[0] >> 1 == row)
        def _():
            for n in range(PAIR):
                for m in range(CHIPS):
                    spot = (n * CHIPS + m) * cut
                    start = (n ^ row) * cut
                    outs[m ^ (2 * n)][start : start + cut, :] = term[spot : spot + cut, :]


def out_sends(index, term):
    rows, width = term.shape
    rows //= CHIPS
    return kernel_call(
        out_sends_body,
        (shape((rows, width), bf16),) * CHIPS,
        [pl.BlockSpec(term.shape, lambda i, n: (0, 0))],
        (pl.BlockSpec((rows, width), lambda i, n: (0, 0)),) * CHIPS,
        (term,),
        index=index,
        grid=(1,),
        name="out_sends",
    )


def out_block_body(index, *refs):
    parts, out = refs[:CHIPS], refs[CHIPS]
    sums = [parts[m][...].astype(f32) + parts[m + 2][...].astype(f32) for m in range(2)]
    for side in range(2):

        @pl.when(index[0] & 1 == side)
        def _():
            for m in range(2):
                rows = sums[m].shape[0]
                spot = (m ^ side) * rows
                out[spot : spot + rows, :] = sums[m].astype(bf16)


def out_block_call(index, parts):
    rows, width = parts[0].shape
    return kernel_call(
        out_block_body,
        shape((PAIR * rows, width), bf16),
        [pl.BlockSpec((rows, width), lambda i, n: (0, 0))] * CHIPS,
        pl.BlockSpec((PAIR * rows, width), lambda i, n: (0, 0)),
        tuple(parts),
        index=index,
        grid=(1,),
        name="out_block",
    )


def half_rotated(values):
    middle = values.shape[0] // 2
    return jnp.concatenate([-values[middle:], values[:middle]], axis=0)


def qkv_body(make, *refs):
    if make:
        xs, (own, other, cosine, sine, queries, kv, xhat) = refs[:PAIR], refs[PAIR:]
        rows, width = xs[0].shape
        for m in range(PAIR):
            x = xs[m][...].astype(f32)
            inverse = lax.rsqrt(mean_of(x * x) + norm_eps)
            xhat[m * rows : (m + 1) * rows, :] = (x * inverse).astype(bf16)
    else:
        xhat, own, other, cosine, sine, queries, kv = refs
        rows, width = cosine.shape[1], xhat.shape[1]
    cos, sin = cosine[...], sine[...]
    total = dot(xhat[:, : width // 2], own[...]) + dot(xhat[:, width // 2 :], other[...])
    for m in range(PAIR):
        turned = total[m * rows : (m + 1) * rows].T
        for h in range(GROUP + 1):
            u = turned[h * HEAD : (h + 1) * HEAD]
            u = u * cos + half_rotated(u) * sin
            if h < GROUP:
                queries[m, :, h * rows : (h + 1) * rows] = (u * HEAD ** (-0.5)).astype(bf16)
            else:
                both = jnp.concatenate([u, turned[(h + 1) * HEAD :]], axis=0)
                kv[m * rows : (m + 1) * rows, :] = both.T.astype(bf16)


def qkv_call(xs, own, other, cosine, sine):
    make = isinstance(xs, list)
    rows = cosine.shape[1]
    tokens = PAIR * rows
    outs = (shape((PAIR, HEAD, GROUP * rows), bf16), shape((tokens, 2 * HEAD), bf16))
    if make:
        outs = outs + (shape((tokens, xs[0].shape[1]), bf16),)
    operands = (*(xs if make else (xs,)), own, other, cosine, sine)
    return kernel_call(
        functools.partial(qkv_body, make),
        outs,
        [whole()] * len(operands),
        tuple(whole() for _ in outs),
        operands,
        name="qkv",
    )


def out_rows_body(index, *refs):
    pieces, out = refs[:CHIPS], refs[CHIPS]
    cut = pieces[0].shape[0] // PAIR
    for row in range(2):

        @pl.when(index[0] >> 1 == row)
        def _():
            for n in range(PAIR):
                for m in range(CHIPS):
                    spot = (n * CHIPS + m) * cut
                    start = (n ^ row) * cut
                    out[spot : spot + cut, :] = pieces[m ^ (2 * n)][start : start + cut, :]


def out_rows_call(index, pieces):
    rows, width = pieces[0].shape
    return kernel_call(
        out_rows_body,
        shape((CHIPS * rows, width), bf16),
        [pl.BlockSpec((rows, width), lambda i, n: (0, 0))] * CHIPS,
        pl.BlockSpec((CHIPS * rows, width), lambda i, n: (0, 0)),
        tuple(pieces),
        index=index,
        grid=(1,),
        name="out_rows",
    )


LANE_HEADS = 4


def own_block_bias(rows):
    key = lax.broadcasted_iota(jnp.int32, (rows, rows), 0)
    mine = lax.broadcasted_iota(jnp.int32, (rows, rows), 1)
    return jnp.where(key <= mine, 0.0, masked_score)


def set_bias(bias):
    rows = bias.shape[0]
    value = own_block_bias(rows)
    for h in range(LANE_HEADS):
        bias[:, h * rows : (h + 1) * rows] = value


def far_bias(depth, d):
    return jnp.where(d <= depth, 0.0, masked_score) if d else 0.0


def attention_body(shards, index, queries, *refs):
    kvs = refs[:shards]
    turned_out, out, stats, bias, terms, out_turned = refs[shards:]
    rows = bias.shape[0]
    wide = LANE_HEADS * rows

    @pl.when(pl.program_id(0) == 0)
    def _():
        set_bias(bias)

    ks = [kv[:, :HEAD] for kv in kvs]
    v_turned = jnp.concatenate([kv[...] for kv in kvs], axis=0).astype(f32).T[HEAD:].astype(bf16)
    for n in range(GROUP // LANE_HEADS):
        span = slice(n * wide, (n + 1) * wide)
        q = queries[0, :, span]
        scores, top = [], None
        for d in range(shards):
            score = dot(ks[d], q)
            if d == 0:
                score = score + bias[...]
            scores.append(score)
            highest = jnp.max(score, axis=0, keepdims=True) + far_bias(index[2], d)
            top = highest if top is None else jnp.maximum(top, highest)
        total = None
        for d in range(shards):
            term = jnp.exp(scores[d] - (top - far_bias(index[2], d)))
            part = jnp.sum(term, axis=0, keepdims=True)
            total = part if total is None else total + part
            terms[d * rows : (d + 1) * rows, :] = term.astype(bf16)
        out_turned[:, span] = dot(v_turned, terms[...]) / total
        stats[0, :, span] = top + jnp.log(total)
    turned_out[0] = out_turned[...].astype(bf16)
    straight = out_turned[...].T
    for h in range(GROUP):
        out[:, h * HEAD : (h + 1) * HEAD] = straight[h * rows : (h + 1) * rows].astype(bf16)


def attention_call(index, queries, kvs):
    chips, _, wide = queries.shape
    rows = wide // GROUP
    shards = len(kvs)
    keys = shards * rows
    block = pl.BlockSpec((1, HEAD, wide), lambda i, n: (i, 0, 0))
    return kernel_call(
        functools.partial(attention_body, shards),
        (
            shape((chips, HEAD, wide), bf16),
            shape((chips * rows, GROUP * HEAD), bf16),
            shape((chips, 1, wide), f32),
        ),
        [block] + [pl.BlockSpec((rows, 2 * HEAD), lambda i, n: (i, 0))] * shards,
        (
            block,
            pl.BlockSpec((rows, GROUP * HEAD), lambda i, n: (i, 0)),
            pl.BlockSpec((1, 1, wide), lambda i, n: (i, 0, 0)),
        ),
        (queries, *kvs),
        index=index,
        grid=(chips,),
        scratch=(
            VMEM((rows, LANE_HEADS * rows), f32),
            VMEM((keys, LANE_HEADS * rows), bf16),
            VMEM((HEAD, wide), f32),
        ),
        name="attention",
    )


def attention_back_body(shards, index, branch, wo_own, wo_other, cosine, sine, *refs):
    per_group = 3 + shards
    inputs = [refs[n * per_group : (n + 1) * per_group] for n in range(PAIR)]
    grad_q, grad_first, grad_rest = refs[-7:-4]
    bias, probs_low, grads_low, grad_lanes = refs[-4:]
    rows = bias.shape[0]
    wide = LANE_HEADS * rows
    width = branch.shape[1]
    set_bias(bias)
    cos, sin = cosine[...], sine[...]
    for n, (queries, turned_out, stats, *kvs) in enumerate(inputs):
        heads = slice(n * GROUP * HEAD, (n + 1) * GROUP * HEAD)
        grad_out = dot_nt(wo_own[heads, :], branch[:, : width // 2])
        grad_out = grad_out + dot_nt(wo_other[heads, :], branch[:, width // 2 :])
        for h in range(GROUP):
            grad_lanes[:, h * rows : (h + 1) * rows] = grad_out[h * HEAD : (h + 1) * HEAD].astype(bf16)
        ks = [kv[:, :HEAD] for kv in kvs]
        vs = [kv[:, HEAD:] for kv in kvs]
        k_turned = jnp.concatenate([kv[...] for kv in kvs], axis=0).astype(f32).T[:HEAD].astype(bf16)
        k_total, v_total, parts = None, None, []
        for c in range(GROUP // LANE_HEADS):
            span = slice(c * wide, (c + 1) * wide)
            q, mine = queries[0, :, span], grad_lanes[:, span]
            delta = jnp.sum(
                mine.astype(f32) * turned_out[0, :, span].astype(f32), axis=0, keepdims=True
            )
            for d in range(shards):
                score = dot(ks[d], q)
                if d == 0:
                    score = score + bias[...]
                probs = jnp.exp(score - (stats[0, :, span] - far_bias(index[2], d)))
                grad_scores = probs * (dot(vs[d], mine) - delta)
                probs_low[d * rows : (d + 1) * rows, :] = probs.astype(bf16)
                grads_low[d * rows : (d + 1) * rows, :] = grad_scores.astype(bf16)
            u = dot(k_turned, grads_low[...]) * HEAD ** (-0.5)
            parts.append(u * cos - half_rotated(u) * sin)
            k_term = dot_nt(grads_low[...], q)
            v_term = dot_nt(probs_low[...], mine)
            k_total = k_term if k_total is None else k_total + k_term
            v_total = v_term if v_total is None else v_total + v_term
        straight = jnp.concatenate(parts, axis=1).T
        for h in range(GROUP):
            spot = (n * GROUP + h) * HEAD
            grad_q[:, spot : spot + HEAD] = straight[h * rows : (h + 1) * rows].astype(bf16)
        both = jnp.concatenate([k_total, v_total], axis=1)
        spot = slice(n * 2 * HEAD, (n + 1) * 2 * HEAD)
        grad_first[:, spot] = both[:rows, :]
        for d in range(1, shards):
            grad_rest[d - 1, :, spot] = both[d * rows : (d + 1) * rows, :].astype(bf16)


def attention_back_call(index, m, branch, wo_own, wo_other, cosine, sine, groups, before):
    chips, _, wide = groups[0][0].shape
    rows = wide // GROUP
    shards = len(groups[0][3])
    keys = shards * rows
    tokens = chips * rows
    block = pl.BlockSpec((1, HEAD, wide), lambda i, n: (m, 0, 0))
    in_specs = [whole()] * 5
    operands = [branch, wo_own, wo_other, jnp.tile(cosine, (1, LANE_HEADS)), jnp.tile(sine, (1, LANE_HEADS))]
    for queries, turned, stats, kvs in groups:
        in_specs += [block, block, pl.BlockSpec((1, 1, wide), lambda i, n: (m, 0, 0))]
        in_specs += [pl.BlockSpec((rows, 2 * HEAD), lambda i, n: (m, 0))] * shards
        operands += [queries, turned, stats, *kvs]
    aliases = {}
    if before is not None:
        aliases = {1 + len(operands) + n: n for n in range(3)}
        in_specs += [pl.BlockSpec(memory_space=pl.ANY)] * 3
        operands += list(before)
    outs = (
        shape((tokens, PAIR * GROUP * HEAD), bf16),
        shape((tokens, PAIR * 2 * HEAD), f32),
        shape((shards - 1, tokens, PAIR * 2 * HEAD), bf16),
    )
    out_specs = (
        pl.BlockSpec((rows, PAIR * GROUP * HEAD), lambda i, n: (m, 0)),
        pl.BlockSpec((rows, PAIR * 2 * HEAD), lambda i, n: (m, 0)),
        pl.BlockSpec((shards - 1, rows, PAIR * 2 * HEAD), lambda i, n: (0, m, 0)),
    )
    return kernel_call(
        functools.partial(attention_back_body, shards),
        outs,
        in_specs,
        out_specs,
        tuple(operands),
        index=index,
        grid=(1,),
        scratch=(
            VMEM((rows, LANE_HEADS * rows), f32),
            VMEM((keys, LANE_HEADS * rows), bf16),
            VMEM((keys, LANE_HEADS * rows), bf16),
            VMEM((HEAD, wide), bf16),
        ),
        aliases=aliases,
        name="attention_back",
    )


def parts_body(steps, transposed, count, *refs):
    lefts, owns, others = refs[:count], refs[count : 2 * count], refs[2 * count : 3 * count]
    outs = refs[3 * count :]
    rows = outs[0].shape[0]
    step = pl.program_id(0)

    def run(weights):
        total = None
        for left, weight in zip(lefts, weights):
            term = (dot_nt if transposed else dot)(left[...], weight[...])
            total = term if total is None else total + term
        for m, out in enumerate(outs):
            out[...] = total[m * rows : (m + 1) * rows, :].astype(out.dtype)

    @pl.when(step < steps)
    def _():
        run(owns)

    @pl.when(step >= steps)
    def _():
        run(others)


def parts_call(terms, rows, transposed, name):
    tokens = terms[0][0].shape[0]
    half = terms[0][1].shape[0] if transposed else terms[0][1].shape[1]
    tile = 256
    steps = half // tile
    last = steps - 1
    specs = [pl.BlockSpec((tokens, term[0].shape[1]), lambda j: (0, 0)) for term in terms]
    for side in range(2):
        for left, _, _, spot in terms:
            depth = left.shape[1]

            def place(side, spot, j):
                step = jnp.maximum(j - steps, 0) if side else jnp.minimum(j, last)
                return (step, spot) if transposed else (spot, step)

            block = (tile, depth) if transposed else (depth, tile)
            specs.append(pl.BlockSpec(block, functools.partial(place, side, spot)))
    count = tokens // rows
    return kernel_call(
        functools.partial(parts_body, steps, transposed, len(terms)),
        tuple(shape((rows, 2 * half), f32 if m == 0 else bf16) for m in range(count)),
        specs,
        tuple(pl.BlockSpec((rows, tile), lambda j: (0, j)) for _ in range(count)),
        (*(term[0] for term in terms), *(term[1] for term in terms), *(term[2] for term in terms)),
        grid=(2 * steps,),
        name=name,
    )


def gate_body(count, *refs):
    twos = refs[:count]
    gate_own, up_own, gate_other, up_other, act, for_gate, for_up, two_all = refs[count:]
    half = two_all.shape[1] // 2

    @pl.when(pl.program_id(0) == 0)
    def _():
        start = 0
        for two in twos:
            two_all[start : start + two.shape[0], :] = two[...]
            start += two.shape[0]

    own = jnp.concatenate([gate_own[...], up_own[...]], axis=1)
    other = jnp.concatenate([gate_other[...], up_other[...]], axis=1)
    both = dot(two_all[:, :half], own) + dot(two_all[:, half:], other)
    wide = gate_own.shape[1]
    gate, up = both[:, :wide], both[:, wide:]
    sig = 1.0 / (1.0 + jnp.exp(-gate))
    silu = gate * sig
    act[...] = (silu * up).astype(bf16)
    for_gate[...] = (up * sig * (1.0 + gate * (1.0 - sig))).astype(bf16)
    for_up[...] = silu.astype(bf16)


def gate_call(twos, own, other):
    rows, width = twos[0].shape
    tokens = CHIPS * rows
    half = width // 2
    ff = own.shape[1] // 2
    tile = LANES
    steps = ff // tile
    weight = [
        pl.BlockSpec((half, tile), lambda j: (0, j)),
        pl.BlockSpec((half, tile), lambda j: (0, j + steps)),
    ]
    column = pl.BlockSpec((tokens, tile), lambda j: (0, j))
    return kernel_call(
        functools.partial(gate_body, len(twos)),
        tuple(shape((tokens, ff), bf16) for _ in range(3)) + (shape((tokens, width), bf16),),
        [pl.BlockSpec(two.shape, lambda j: (0, 0)) for two in twos] + weight + weight,
        (column, column, column, pl.BlockSpec((tokens, width), lambda j: (0, 0))),
        (*twos, own, own, other, other),
        grid=(steps,),
        name="gate",
    )


def hidden_back_body(g, own, other, for_gate, for_up, grads):
    half = g.shape[1] // 2
    ff = own.shape[0]
    hidden = dot_nt(g[:, :half], own[...]) + dot_nt(g[:, half:], other[...])
    grads[:, :ff] = (hidden * for_gate[...].astype(f32)).astype(bf16)
    grads[:, ff:] = (hidden * for_up[...].astype(f32)).astype(bf16)


def hidden_back_call(g, own, other, for_gate, for_up):
    tokens, width = g.shape
    ff, half = own.shape
    block = tokens // 2
    row = lambda i: (i, 0)
    fixed = lambda i: (0, 0)
    return kernel_call(
        hidden_back_body,
        shape((tokens, 2 * ff), bf16),
        [
            pl.BlockSpec((block, width), row),
            pl.BlockSpec((ff, half), fixed),
            pl.BlockSpec((ff, half), fixed),
            pl.BlockSpec((block, ff), row),
            pl.BlockSpec((block, ff), row),
        ],
        pl.BlockSpec((block, 2 * ff), row),
        (g, own, other, for_gate, for_up),
        grid=(2,),
        name="hidden_back",
    )


def weight_grad_body(per, outputs, adds, left, right, *refs):
    added = [refs[n * outputs : (n + 1) * outputs] for n in range(adds)]
    outs, turned = refs[adds * outputs : -1], refs[-1]
    step = pl.program_id(0)

    @pl.when(step == 0)
    def _():
        turned[...] = left[...].T

    for n in range(outputs):

        @pl.when(step // per == n)
        def _(n=n):
            total = dot(turned[...], right[...])
            for terms in added:
                total = total + terms[n][...].astype(f32)
            outs[n][...] = total.astype(bf16)


def weight_grad(left, left_side, right, place, width, outputs, added, name):
    tokens = left.shape[0]
    rows = left.shape[1] // (1 if left_side is None else 2)
    tile = 256 if width % 256 == 0 else width
    per = width // tile
    first = place * width // tile
    side = left_side or 0

    def spot(n, j):
        return (0, jnp.clip(j - n * per, 0, per - 1))

    tiles = [pl.BlockSpec((rows, tile), functools.partial(spot, n)) for n in range(outputs)]
    return kernel_call(
        functools.partial(weight_grad_body, per, outputs, len(added)),
        tuple(shape((rows, width), bf16) for _ in range(outputs)),
        [
            pl.BlockSpec((tokens, rows), lambda j: (0, side)),
            pl.BlockSpec((tokens, tile), lambda j: (0, first + j)),
        ]
        + tiles * len(added),
        tuple(tiles),
        (left, right, *(term for terms in added for term in terms)),
        grid=(per * outputs,),
        scratch=(VMEM((rows, tokens), bf16),),
        name=name,
    )


def rows_result_body(local, index, *refs):
    pieces, out = refs[:PIECES], refs[PIECES]
    half = local // 2
    shards = out.shape[1] // local
    for m in range(CHIPS):
        for core in range(2):

            @pl.when((pl.program_id(0) == m) & (index[1] == core))
            def _():
                for side in range(2):
                    piece = pieces[2 * m + side]
                    for s in range(shards):
                        spot = s * local + (core ^ side) * half
                        out[:, spot : spot + half] = piece[:, s * half : (s + 1) * half].astype(f32)


def rows_result(index, pieces, local, name):
    cut, half_width = pieces[0].shape
    return kernel_call(
        functools.partial(rows_result_body, local),
        shape((CHIPS * cut, 2 * half_width), f32),
        [pl.BlockSpec((cut, half_width), lambda i, n: (0, 0))] * PIECES,
        pl.BlockSpec((cut, 2 * half_width), lambda i, n: (n[0] ^ i, 0)),
        tuple(pieces),
        index=index,
        grid=(CHIPS,),
        name=name,
    )


def lane_sum(value):
    total = value[:, :LANES]
    for n in range(1, value.shape[1] // LANES):
        total = total + value[:, n * LANES : (n + 1) * LANES]
    return total


def feedforward_result_body(ff_local, cut, index, *refs):
    pieces = refs[:CHIPS]
    gate_weight, up_weight, gain = refs[CHIPS : CHIPS + 3]
    gate_out, up_out, gain_out = refs[-3:]
    shards = gate_weight.shape[1] // ff_local
    width = shards * cut
    for chip in range(CHIPS):

        @pl.when(index[0] == chip)
        def _():
            @pl.loop(0, gate_out.shape[0] // 16)
            def _(n):
                rows = pl.ds(pl.multiple_of(n * 16, 16), 16)
                scale = gain[rows, :1]
                total = jnp.zeros((16, LANES), f32)
                for base, weight, out in ((0, gate_weight, gate_out), (width, up_weight, up_out)):
                    parts = []
                    for s in range(shards):
                        for owner in range(CHIPS):
                            start = base + s * cut
                            parts.append(pieces[owner ^ chip][rows, start : start + cut].astype(f32))
                    wide = jnp.concatenate(parts, axis=1)
                    total = total + lane_sum(wide * weight[rows, :].astype(f32))
                    out[rows, :] = wide * scale
                gain_out[rows, :] = total


def feedforward_result(index, side, pieces, gate_weight, up_weight, gain, ff_local, before):
    local, ff = gate_weight.shape
    half = local // 2
    rows = 64
    steps = half // rows
    row = lambda i, n: ((n[1] ^ side) * steps + i, 0)
    in_specs = [pl.BlockSpec((rows, pieces[0].shape[1]), lambda i, n: (i, 0))] * CHIPS
    in_specs += [pl.BlockSpec((rows, ff), row)] * 2 + [pl.BlockSpec((rows, LANES), row)]
    operands = (*pieces, gate_weight, up_weight, gain)
    aliases = {}
    if before is not None:
        aliases = {1 + len(operands) + n: n for n in range(3)}
        in_specs = in_specs + [pl.BlockSpec(memory_space=pl.ANY)] * 3
        operands = operands + tuple(before)
    return kernel_call(
        functools.partial(feedforward_result_body, ff_local, ff_local // CHIPS),
        (shape((local, ff), f32), shape((local, ff), f32), shape((local, LANES), f32)),
        in_specs,
        (pl.BlockSpec((rows, ff), row), pl.BlockSpec((rows, ff), row), pl.BlockSpec((rows, LANES), row)),
        operands,
        index=index,
        grid=(steps,),
        aliases=aliases,
        name="feedforward_result",
    )


def qkv_result_body(local, group_shards, index, *refs):
    pieces = refs[:PIECES]
    weights, gain = refs[PIECES : PIECES + 3], refs[PIECES + 3]
    outs, gain_out = refs[PIECES + 4 : PIECES + 7], refs[PIECES + 7]
    q_width = GROUP * HEAD
    cut = local // CHIPS
    scale = gain[:, :1]
    for chip in range(CHIPS):
        for side in range(2):

            @pl.when((index[0] == chip) & (pl.program_id(0) == side))
            def _():
                parts, k_parts, v_parts = [], [], []
                for group in range(CHIPS):
                    owner = (group >> 1) + 2 * (group & 1)
                    piece = pieces[2 * (owner ^ chip) + side]
                    for s in range(group_shards):
                        for j in range(CHIPS):
                            start = ((j ^ owner) * group_shards + s) * cut
                            parts.append(piece[:, start : start + cut].astype(f32))
                    k_parts.append(piece[:, q_width : q_width + HEAD].astype(f32))
                    v_parts.append(piece[:, q_width + HEAD : q_width + 2 * HEAD].astype(f32))
                total = jnp.zeros((gain.shape[0], LANES), f32)
                for part, weight, out in zip((parts, k_parts, v_parts), weights, outs):
                    wide = jnp.concatenate(part, axis=1)
                    total = total + lane_sum(wide * weight[...].astype(f32))
                    out[...] = wide * scale
                gain_out[...] = total


def qkv_result(index, pieces, query, key, value, gain):
    local, width = query.shape
    half = local // 2
    group_shards = width // local // CHIPS
    row = lambda i, n: (n[1] ^ i, 0)
    kv_width = key.shape[1]
    return kernel_call(
        functools.partial(qkv_result_body, local, group_shards),
        (
            shape((local, width), f32),
            shape((local, kv_width), f32),
            shape((local, kv_width), f32),
            shape((local, LANES), f32),
        ),
        [pl.BlockSpec(pieces[0].shape, lambda i, n: (0, 0))] * PIECES
        + [
            pl.BlockSpec((half, width), row),
            pl.BlockSpec((half, kv_width), row),
            pl.BlockSpec((half, kv_width), row),
            pl.BlockSpec((half, LANES), row),
        ],
        (
            pl.BlockSpec((half, width), row),
            pl.BlockSpec((half, kv_width), row),
            pl.BlockSpec((half, kv_width), row),
            pl.BlockSpec((half, LANES), row),
        ),
        (*pieces, query, key, value, gain),
        index=index,
        grid=(2,),
        name="qkv_result",
    )


def per_device(
    hidden_in,
    attention_gain,
    query_weight,
    key_weight,
    value_weight,
    output_weight,
    feedforward_gain,
    gate_weight,
    up_weight,
    down_weight,
    out_grad,
):
    rows, width = hidden_in.shape
    shards = lax.axis_size("shard")
    replicas = lax.axis_size("replica")
    place = lax.axis_index("replica")
    depth = lax.axis_index("shard")
    core = place & 1
    chip = (place >> 1) & (CHIPS - 1)
    local = width // shards
    half = local // 2
    ff_local = down_weight.shape[0]
    group_shards = shards // CHIPS
    q_width = GROUP * HEAD
    qkv_width = q_width + 2 * HEAD
    index = jnp.stack([chip, core, depth]).astype(jnp.int32)

    gain_one = jnp.broadcast_to(attention_gain.astype(f32)[:, None], (local, LANES))
    gain_two = jnp.broadcast_to(feedforward_gain.astype(f32)[:, None], (local, LANES))


    at_block, out_block = attention_block(
        index, query_weight, key_weight, value_weight, output_weight, gain_one
    )
    x = own_first(index, (after(hidden_in, at_block),), local)[0]
    xs = [x, swap(x, 2)]
    at_own = lax.all_gather(at_block, "shard", axis=0, tiled=True)
    out_all = lax.all_gather(out_block, "shard", axis=0, tiled=True)
    gu_block = feedforward_block(index, gate_weight, up_weight, after(gain_two, at_block), ff_local)
    gu_own = lax.all_gather(gu_block, "shard", axis=0, tiled=True)
    down_own = lax.all_gather(down_block(index, down_weight, local), "shard", axis=0, tiled=True)
    g = own_first(index, (after(out_grad, x),), local)[0]
    g_blocks = [g, swap(g, 2), swap(g, 4)]
    at_own = after(at_own, gu_block, xs[1], *g_blocks[1:])

    qkv_own = [at_own]
    qkv_own.append(swap(qkv_own[0], 4))
    qkv_other = [swap(qkv_own[0], 1)]
    inverse = rope_base ** (-jnp.arange(0, HEAD, 2, dtype=f32) / HEAD)
    places = (depth * rows + jnp.arange(rows, dtype=jnp.int32)).astype(f32)
    angles = inverse[:, None] * places[None, :]
    angles = jnp.concatenate([angles, angles], axis=0)
    cosine, sine = jnp.cos(angles), jnp.sin(angles)

    def shifted(kv):
        return [kv] + [shift(kv, d) for d in range(1, shards)]

    queries, kv, xhat = qkv_call(xs, qkv_own[0], qkv_other[0], cosine, sine)
    kvs = shifted(kv)
    qkv_own[1] = after(qkv_own[1], *kvs[1:])
    qkv_other.append(swap(qkv_own[1], 1))
    queries_two, kv_two = qkv_call(xhat, qkv_own[1], qkv_other[1], cosine, sine)
    kvs_two = shifted(kv_two)
    groups = [(queries, *attention_call(index, queries, kvs), kvs)]
    groups.append((queries_two, *attention_call(index, queries_two, kvs_two), kvs_two))
    attended = [group[2] for group in groups]
    groups = [(group[0], group[1], group[3], group[4]) for group in groups]

    out_all = after(out_all, qkv_own[1])
    x_place = chip & 1
    low_group = (chip >> 1) == 0
    pair_rows = PAIR * group_shards * half // 2

    def out_for(mask):
        return lax.dynamic_slice_in_dim(out_all, ((chip ^ mask) & 1) * pair_rows, pair_rows, 0)

    out_pieces = [out_for(0)] + [swap(out_for(m), 2 * m) for m in range(1, CHIPS)]
    wo_own = out_rows_call(index, [after(piece, *kvs_two[1:]) for piece in out_pieces])
    wo_other = swap(wo_own, 1)

    mid_terms = [(attended[n], wo_own, wo_other, n) for n in range(PAIR)]
    g_blocks.append(swap(after(g, *out_pieces[1:]), 6))
    mid_out = parts_call(mid_terms, rows, False, "attention_out")
    g_all = jnp.concatenate([after(block, mid_out[0]) for block in g_blocks], axis=0)
    middle, two = middle_call(plane_send(mid_out), after(x, g_all))
    twos = plane_gather_far(two, *plane_gather_near(two))

    gu_own = after(gu_own, *twos[1:])
    gu_other = swap(gu_own, 1)
    act, for_gate, for_up, two_all = gate_call(twos, gu_own, gu_other)

    def over_groups(kept):
        if replicas > PIECES:
            groups = [
                [e * PIECES + i for e in range(replicas // PIECES)] for i in range(PIECES)
            ]
            kept = lax.psum(kept, "replica", axis_index_groups=groups)
        return kept

    def reduced(term):
        kept = lax.psum_scatter(term, "shard", scatter_dimension=0, tiled=True)
        return over_groups(kept)

    def plane_pieces(kept):
        mine = plane_gather(kept)
        return mine, [swap(part, 1) for part in mine]

    def mixed(mine, theirs):
        return [part for pair in zip(mine, theirs) for part in pair]

    down_sent = weight_grad(act, None, g_all, 1, width // 2, 1, (), "down_grad_other")
    down_sent = [swap(down_sent[0], 1)]
    down_sent[0] = after(down_sent[0], down_own)
    down_term = weight_grad(act, None, g_all, 0, width // 2, 1, (down_sent,), "down_grad")[0]
    down_kept = reduced(down_term)
    down_other = swap(down_own, 1)

    grads = hidden_back_call(after(g_all, down_term), down_own, down_other, for_gate, for_up)
    grads_wide = grads.shape[1]
    gu_sent = weight_grad(two_all, 1, grads, 0, grads_wide, 1, (), "gate_grad_other")
    gu_sent = [swap(gu_sent[0], 1)]
    gu_term = weight_grad(two_all, 0, grads, 0, grads_wide, 1, (gu_sent,), "gate_grad")[0]
    gu_kept = reduced(gu_term)
    grads_late = after(grads, gu_term)
    e_terms = parts_call([(grads_late, gu_own, gu_other, 0)], rows, True, "feedforward_back")
    e_parts = plane_send(e_terms)
    act_late = after(act, e_terms[0])
    out_terms = parts_call([(act_late, down_own, down_other, 0)], rows, False, "feedforward_out")

    middle_late = after(middle, out_terms[0], down_kept)
    grad_middle, branch = grad_middle_call(e_parts, middle_late, g)
    branches = [branch, swap(branch, 2)]

    def back_block(m, block, before):
        return attention_back_call(index, m, block, wo_own, wo_other, cosine, sine, groups, before)

    before = back_block(0, branch, None)
    out_parts = plane_send(after(out_terms, branches[1], before[1]))
    half_wide = width // 2
    branch_all = jnp.concatenate([branch, after(branches[1], before[1])], axis=0)
    both_attended = jnp.concatenate(attended, axis=1)
    wo_sent = weight_grad(both_attended, None, branch_all, 1, half_wide, 1, (), "out_grad_other")
    wo_other_term = wo_sent[0]
    wo_sent = [swap(wo_other_term, 1)]
    before = back_block(1, after(branches[1], before[1], wo_other_term), before)
    output = output_call(index, out_parts, middle, local)
    grad_q, grad_first, grad_rest = before
    grad_rest = after(grad_rest, out_parts[1])
    rest = [shift(grad_rest[d - 1], -d) for d in range(1, shards)]

    wo_term = weight_grad(both_attended, None, branch_all, 0, half_wide, 1, (wo_sent,), "out_grad")[0]
    wo_terms = out_sends(index, after(wo_term, *rest, *out_parts[1:]))
    wo_parts = plane_send(wo_terms)
    wo_block = out_block_call(index, wo_parts)
    wo_kept = reduced(wo_block)
    grad_first = after(grad_first, wo_block)
    grad_qkv = grad_qkv_call(grad_q, grad_first, rest, cosine, sine)

    def qkv_grad(n, side, added, name):
        return weight_grad(xhat, side, grad_qkv[n], 0, qkv_width, 1, added, name)

    qkv_sent = [swap(qkv_grad(n, 1, (), "qkv_grad_other")[0], 1) for n in (1, 0)]
    back_terms = [(grad_qkv[n], qkv_own[n], qkv_other[n], 0) for n in range(PAIR)]
    qkv_second = qkv_grad(1, 0, ([qkv_sent[0]],), "qkv_grad")[0]
    qkv_term = qkv_grad(0, 0, ([qkv_sent[1]],), "qkv_grad")[0]
    gu_near = plane_gather_near(gu_kept)
    at_term = jnp.concatenate([qkv_term, qkv_second], axis=1)
    at_kept = reduced(after(at_term, wo_kept, *gu_near))
    back_terms[0] = (after(grad_qkv[0], qkv_term, qkv_second), *back_terms[0][1:])
    back_parts = parts_call(back_terms, rows, True, "qkv_back")
    e_one = plane_send(back_parts)
    gu_mine = plane_gather_far(gu_kept, *(after(part, back_parts[0]) for part in gu_near))
    gu_mine = gu_mine[:3] + [jnp.concatenate(gu_mine[3:], axis=0)]
    gu_theirs = [swap(after(part, output), 1) for part in gu_mine]
    gu_out = feedforward_result(index, 0, gu_mine, gate_weight, up_weight, gain_two, ff_local, None)
    gu_out = feedforward_result(index, 1, gu_theirs, gate_weight, up_weight, gain_two, ff_local, gu_out)

    down_mine = plane_gather(after(down_kept, *gu_near))
    down_theirs = [swap(part, 1) for part in down_mine]
    down_out = rows_result(index, mixed(down_mine, down_theirs), local, "down_result")
    grad_input = grad_input_call(index, e_one, x, grad_middle, local)

    wo_out = rows_result(index, mixed(*plane_pieces(after(wo_kept, *gu_theirs))), local, "out_result")
    at_kept = after(at_kept, gu_out[0], down_out, grad_input)
    second = swap(at_kept[:, qkv_width:], 4)
    first = at_kept[:, :qkv_width].astype(f32) + second.astype(f32)
    at_pieces = mixed(*plane_pieces(first.astype(bf16)))
    q_out, k_out, v_out, gain_one_sums = qkv_result(
        index, at_pieces, query_weight, key_weight, value_weight, gain_one
    )
    return (
        output,
        grad_input,
        jnp.sum(gain_one_sums, axis=1),
        q_out,
        k_out,
        v_out,
        wo_out,
        jnp.sum(gu_out[2], axis=1),
        gu_out[0],
        gu_out[1],
        down_out,
    )


def solution(mesh):
    return jax.shard_map(
        per_device,
        mesh=mesh,
        in_specs=(
            P(("replica", "shard"), None),
            P("shard"),
            P("shard", None),
            P("shard", None),
            P("shard", None),
            P("shard", None),
            P("shard"),
            P("shard", None),
            P("shard", None),
            P("shard", None),
            P(("replica", "shard"), None),
        ),
        out_specs=(
            P(("replica", "shard"), None),
            P(("replica", "shard"), None),
            P("shard"),
            P("shard", None),
            P("shard", None),
            P("shard", None),
            P("shard", None),
            P("shard"),
            P("shard", None),
            P("shard", None),
            P("shard", None),
        ),
        check_vma=False,
    )
```

```python
import functools

import jax
import jax.numpy as jnp
from jax import lax
from jax.experimental import pallas as pl
from jax.experimental.pallas import tpu as pltpu
from jax.sharding import PartitionSpec as P

HEADS = 32
KV_HEADS = 4
HEAD = 64
GROUP = HEADS // KV_HEADS
CHIPS = 4
PIECES = 2 * CHIPS
PAIR = 2
LANES = 128

norm_eps = 1e-05
rope_base = 10000.0
masked_score = -1e30

f32 = jnp.float32
bf16 = jnp.bfloat16
VMEM = pltpu.VMEM
NT = (((1,), (1,)), ((), ()))
TN = (((0,), (0,)), ((), ()))


def dot(left, right):
    return jnp.dot(left, right, preferred_element_type=f32)


def dot_nt(left, right):
    return lax.dot_general(left, right, NT, preferred_element_type=f32)


def dot_tn(left, right):
    return lax.dot_general(left, right, TN, preferred_element_type=f32)


def shape(dims, kind):
    return jax.ShapeDtypeStruct(dims, kind)


def whole():
    return pl.BlockSpec(memory_space=VMEM)


TIMES = {"attention_back": 13.0}


def kernel_call(body, out_shape, in_specs, out_specs, operands, *, index=None, grid=(), scratch=(),
                aliases=None, name=None):
    params = pltpu.CompilerParams(
        vmem_limit_bytes=52 * 2**20, dimension_semantics=("arbitrary",) * len(grid)
    )
    moved = int(TIMES.get(name, 0.0) * 3.69e6)
    cost = pl.CostEstimate(flops=0, bytes_accessed=moved, transcendentals=0)
    common = dict(
        out_shape=out_shape,
        compiler_params=params,
        cost_estimate=cost,
        input_output_aliases=aliases or {},
        name=name,
    )
    if index is None:
        spec = pl.GridSpec(grid=grid, in_specs=in_specs, out_specs=out_specs, scratch_shapes=scratch)
        return pl.pallas_call(body, grid_spec=spec, **common)(*operands)
    spec = pltpu.PrefetchScalarGridSpec(
        num_scalar_prefetch=1, grid=grid, in_specs=in_specs, out_specs=out_specs,
        scratch_shapes=scratch,
    )
    return pl.pallas_call(body, grid_spec=spec, **common)(index, *operands)


def swap(value, mask):
    size = lax.axis_size("replica")
    return lax.ppermute(value, "replica", [(i, i ^ mask) for i in range(size)])


def shift(value, step):
    size = lax.axis_size("shard")
    pairs = [(i, i + step) for i in range(size) if 0 <= i + step < size]
    return lax.ppermute(value, "shard", pairs)


def plane_gather(value):
    return [value] + [swap(value, 2 * m) for m in range(1, CHIPS)]


def plane_gather_near(value):
    return swap(value, 2), swap(value, 4)


def plane_gather_far(value, across, along):
    middle = value.shape[0] // 2
    return [value, across, along, swap(across[:middle], 4), swap(along[middle:], 2)]


def plane_send(parts):
    return [parts[0]] + [swap(parts[m], 2 * m) for m in range(1, len(parts))]


def group_of(chip):
    return 2 * (chip & 1) + (chip >> 1)


def after(value, *others):
    return lax.optimization_barrier((value, *others))[0]


def attention_block_body(local, group_shards, index, q, k, v, o, gain, out, wo_out):
    scale = gain[:, :1]
    q_width = GROUP * HEAD
    cut = local // CHIPS
    for chip in range(CHIPS):

        group = group_of(chip)

        @pl.when(index[0] == chip)
        def _(group=group):
            parts = []
            for m in range(CHIPS):
                for s in range(group_shards):
                    start = group * q_width + s * local + (m ^ chip) * cut
                    parts.append(q[:, start : start + cut])
            parts.append(k[:, group * HEAD : (group + 1) * HEAD])
            parts.append(v[:, group * HEAD : (group + 1) * HEAD])
            wide = jnp.concatenate([part.astype(f32) for part in parts], axis=1)
            out[...] = (wide * scale).astype(bf16)

    half = local // 2
    shards = o.shape[1] // local
    for core in range(2):

        @pl.when(index[1] == core)
        def _():
            for s in range(shards):
                piece = o[:, s * local + core * half : s * local + (core + 1) * half]
                wo_out[:, s * half : (s + 1) * half] = piece


def attention_block(index, query, key, value, output, gain):
    local, width = query.shape
    half = local // 2
    shards = width // local
    return kernel_call(
        functools.partial(attention_block_body, local, shards // CHIPS),
        (
            shape((half, GROUP * HEAD + 2 * HEAD), bf16),
            shape((local // CHIPS, width // 2), bf16),
        ),
        [
            pl.BlockSpec((half, width), lambda i, n: (n[1], 0)),
            pl.BlockSpec((half, key.shape[1]), lambda i, n: (n[1], 0)),
            pl.BlockSpec((half, key.shape[1]), lambda i, n: (n[1], 0)),
            pl.BlockSpec((local // CHIPS, width), lambda i, n: (n[0], 0)),
            pl.BlockSpec((half, LANES), lambda i, n: (n[1], 0)),
        ],
        (
            pl.BlockSpec((half, GROUP * HEAD + 2 * HEAD), lambda i, n: (0, 0)),
            pl.BlockSpec((local // CHIPS, width // 2), lambda i, n: (0, 0)),
        ),
        (query, key, value, output, gain),
        index=index,
        grid=(1,),
        name="attention_block",
    )


def feedforward_block_body(ff_local, cut, index, gate, up, gain, out):
    scale = gain[:, :1]
    shards = gate.shape[1] // ff_local
    width = shards * cut
    for chip in range(CHIPS):

        @pl.when(index[0] == chip)
        def _():
            for n, source in enumerate((gate, up)):
                parts = [
                    source[:, s * ff_local + chip * cut : s * ff_local + (chip + 1) * cut].astype(f32)
                    for s in range(shards)
                ]
                wide = jnp.concatenate(parts, axis=1)
                out[:, n * width : (n + 1) * width] = (wide * scale).astype(bf16)


def feedforward_block(index, gate, up, gain, ff_local):
    local, ff = gate.shape
    half = local // 2
    rows = 64
    steps = half // rows
    cut = ff_local // CHIPS
    width = 2 * (ff // CHIPS)
    return kernel_call(
        functools.partial(feedforward_block_body, ff_local, cut),
        shape((half, width), bf16),
        [
            pl.BlockSpec((rows, ff), lambda i, n: (n[1] * steps + i, 0)),
            pl.BlockSpec((rows, ff), lambda i, n: (n[1] * steps + i, 0)),
            pl.BlockSpec((rows, LANES), lambda i, n: (n[1] * steps + i, 0)),
        ],
        pl.BlockSpec((rows, width), lambda i, n: (i, 0)),
        (gate, up, gain),
        index=index,
        grid=(steps,),
        name="feedforward_block",
    )


def own_first_body(local, index, *refs):
    count = len(refs) // 2
    half = local // 2
    for core in range(2):

        @pl.when(index[1] == core)
        def _():
            for source, out in zip(refs[:count], refs[count:]):
                shards = source.shape[1] // local
                sides = out.shape[1] // (shards * half)
                for side in range(sides):
                    for s in range(shards):
                        start = s * local + (core ^ side) * half
                        spot = (side * shards + s) * half
                        out[:, spot : spot + half] = source[:, start : start + half]


def own_first(index, sources, local, halves=2):
    return kernel_call(
        functools.partial(own_first_body, local),
        tuple(shape((v.shape[0], v.shape[1] * halves // 2), bf16) for v in sources),
        [pl.BlockSpec(v.shape, lambda i, n: (0, 0)) for v in sources],
        tuple(
            pl.BlockSpec((v.shape[0], v.shape[1] * halves // 2), lambda i, n: (0, 0)) for v in sources
        ),
        tuple(sources),
        index=index,
        grid=(1,),
        name="own_first",
    )


def down_block_body(local, index, source, out):
    own_first_body(local, index, source, out)


def down_block(index, down, local):
    ff_local, width = down.shape
    cut = ff_local // CHIPS
    return kernel_call(
        functools.partial(down_block_body, local),
        shape((cut, width // 2), bf16),
        [pl.BlockSpec((cut, width), lambda i, n: (n[0], 0))],
        pl.BlockSpec((cut, width // 2), lambda i, n: (0, 0)),
        (down,),
        index=index,
        grid=(1,),
        name="down_block",
    )


def part_sum(parts):
    total = parts[0][...]
    for part in parts[1:]:
        total = total + part[...].astype(f32)
    return total


def mean_of(values):
    return jnp.mean(values, axis=1, keepdims=True)


def middle_body(*refs):
    parts, (x, middle, two) = refs[:PAIR], refs[PAIR:]
    total = x[...].astype(f32) + part_sum(parts)
    middle[...] = total
    two[...] = (total * lax.rsqrt(mean_of(total * total) + norm_eps)).astype(bf16)


def middle_call(parts, x):
    return kernel_call(
        middle_body,
        (shape(x.shape, f32), shape(x.shape, bf16)),
        [whole()] * (PAIR + 1),
        (whole(), whole()),
        (*parts, x),
        name="middle",
    )


def norm_back(e, values):
    inverse = lax.rsqrt(mean_of(values * values) + norm_eps)
    return inverse * e - values * (inverse * inverse * inverse) * mean_of(e * values)


def grad_middle_body(*refs):
    parts, (middle, g, grad, low) = refs[:CHIPS], refs[CHIPS:]
    total = g[...].astype(f32) + norm_back(part_sum(parts), middle[...])
    grad[...] = total
    low[...] = total.astype(bf16)


def grad_middle_call(parts, middle, g):
    return kernel_call(
        grad_middle_body,
        (shape(g.shape, f32), shape(g.shape, bf16)),
        [whole()] * (CHIPS + 2),
        (whole(), whole()),
        (*parts, middle, g),
        name="grad_middle",
    )


def store_in_order(local, index, value, out):
    half = local // 2
    shards = out.shape[1] // local
    for core in range(2):

        @pl.when(index[1] == core)
        def _():
            for side in range(2):
                for s in range(shards):
                    spot = s * local + (core ^ side) * half
                    start = (side * shards + s) * half
                    out[:, spot : spot + half] = value[:, start : start + half].astype(bf16)


def output_body(local, index, *refs):
    parts, (middle, out) = refs[:CHIPS], refs[CHIPS:]
    store_in_order(local, index, middle[...] + part_sum(parts), out)


def output_call(index, parts, middle, local):
    spec = pl.BlockSpec(middle.shape, lambda i, n: (0, 0))
    return kernel_call(
        functools.partial(output_body, local),
        shape(middle.shape, bf16),
        [spec] * (CHIPS + 1),
        spec,
        (*parts, middle),
        index=index,
        grid=(1,),
        name="output",
    )


def grad_input_body(local, index, *refs):
    parts, (x, grad, out) = refs[:PAIR], refs[PAIR:]
    total = grad[...] + norm_back(part_sum(parts), x[...].astype(f32))
    store_in_order(local, index, total, out)


def grad_input_call(index, parts, x, grad, local):
    spec = pl.BlockSpec(x.shape, lambda i, n: (0, 0))
    return kernel_call(
        functools.partial(grad_input_body, local),
        shape(x.shape, bf16),
        [spec] * (PAIR + 2),
        spec,
        (*parts, x, grad),
        index=index,
        grid=(1,),
        name="grad_input",
    )


def grad_qkv_body(shards, grad_q, first, *refs):
    rest, (cosine, sine), outs = refs[: shards - 1], refs[shards - 1 : shards + 1], refs[shards + 1 :]
    total = first[...]
    for term in rest:
        total = total + term[...].astype(f32)
    rows = cosine.shape[1]
    width = GROUP * HEAD
    cos, sin = cosine[...], sine[...]
    for n, out in enumerate(outs):
        out[:, :width] = grad_q[:, n * width : (n + 1) * width]
        for m in range(PAIR):
            span = slice(m * rows, (m + 1) * rows)
            turned = total[span, n * 2 * HEAD : (n + 1) * 2 * HEAD].T
            k = turned[:HEAD]
            k = k * cos - half_rotated(k) * sin
            both = jnp.concatenate([k, turned[HEAD:]], axis=0)
            out[span, width:] = both.T.astype(bf16)


def grad_qkv_call(grad_q, first, rest, cosine, sine):
    tokens = grad_q.shape[0]
    return kernel_call(
        functools.partial(grad_qkv_body, len(rest) + 1),
        (shape((tokens, GROUP * HEAD + 2 * HEAD), bf16),) * PAIR,
        [whole()] * (len(rest) + 4),
        (whole(),) * PAIR,
        (grad_q, first, *rest, cosine, sine),
        name="grad_qkv",
    )


def out_sends_body(index, term, *outs):
    cut = outs[0].shape[0] // PAIR
    for row in range(2):

        @pl.when(index[0] >> 1 == row)
        def _():
            for n in range(PAIR):
                for m in range(CHIPS):
                    spot = (n * CHIPS + m) * cut
                    start = (n ^ row) * cut
                    outs[m ^ (2 * n)][start : start + cut, :] = term[spot : spot + cut, :]


def out_sends(index, term):
    rows, width = term.shape
    rows //= CHIPS
    return kernel_call(
        out_sends_body,
        (shape((rows, width), bf16),) * CHIPS,
        [pl.BlockSpec(term.shape, lambda i, n: (0, 0))],
        (pl.BlockSpec((rows, width), lambda i, n: (0, 0)),) * CHIPS,
        (term,),
        index=index,
        grid=(1,),
        name="out_sends",
    )


def out_block_body(index, *refs):
    parts, out = refs[:CHIPS], refs[CHIPS]
    sums = [parts[m][...].astype(f32) + parts[m + 2][...].astype(f32) for m in range(2)]
    for side in range(2):

        @pl.when(index[0] & 1 == side)
        def _():
            for m in range(2):
                rows = sums[m].shape[0]
                spot = (m ^ side) * rows
                out[spot : spot + rows, :] = sums[m].astype(bf16)


def out_block_call(index, parts):
    rows, width = parts[0].shape
    return kernel_call(
        out_block_body,
        shape((PAIR * rows, width), bf16),
        [pl.BlockSpec((rows, width), lambda i, n: (0, 0))] * CHIPS,
        pl.BlockSpec((PAIR * rows, width), lambda i, n: (0, 0)),
        tuple(parts),
        index=index,
        grid=(1,),
        name="out_block",
    )


def half_rotated(values):
    middle = values.shape[0] // 2
    return jnp.concatenate([-values[middle:], values[:middle]], axis=0)


def qkv_body(make, *refs):
    if make:
        xs, (own, other, cosine, sine, queries, kv, xhat) = refs[:PAIR], refs[PAIR:]
        rows, width = xs[0].shape
        for m in range(PAIR):
            x = xs[m][...].astype(f32)
            inverse = lax.rsqrt(mean_of(x * x) + norm_eps)
            xhat[m * rows : (m + 1) * rows, :] = (x * inverse).astype(bf16)
    else:
        xhat, own, other, cosine, sine, queries, kv = refs
        rows, width = cosine.shape[1], xhat.shape[1]
    cos, sin = cosine[...], sine[...]
    total = dot(xhat[:, : width // 2], own[...]) + dot(xhat[:, width // 2 :], other[...])
    for m in range(PAIR):
        turned = total[m * rows : (m + 1) * rows].T
        for h in range(GROUP + 1):
            u = turned[h * HEAD : (h + 1) * HEAD]
            u = u * cos + half_rotated(u) * sin
            if h < GROUP:
                queries[m, :, h * rows : (h + 1) * rows] = (u * HEAD ** (-0.5)).astype(bf16)
            else:
                both = jnp.concatenate([u, turned[(h + 1) * HEAD :]], axis=0)
                kv[m * rows : (m + 1) * rows, :] = both.T.astype(bf16)


def qkv_call(xs, own, other, cosine, sine):
    make = isinstance(xs, list)
    rows = cosine.shape[1]
    tokens = PAIR * rows
    outs = (shape((PAIR, HEAD, GROUP * rows), bf16), shape((tokens, 2 * HEAD), bf16))
    if make:
        outs = outs + (shape((tokens, xs[0].shape[1]), bf16),)
    operands = (*(xs if make else (xs,)), own, other, cosine, sine)
    return kernel_call(
        functools.partial(qkv_body, make),
        outs,
        [whole()] * len(operands),
        tuple(whole() for _ in outs),
        operands,
        name="qkv",
    )


def out_rows_body(index, *refs):
    pieces, out = refs[:CHIPS], refs[CHIPS]
    cut = pieces[0].shape[0] // PAIR
    for row in range(2):

        @pl.when(index[0] >> 1 == row)
        def _():
            for n in range(PAIR):
                for m in range(CHIPS):
                    spot = (n * CHIPS + m) * cut
                    start = (n ^ row) * cut
                    out[spot : spot + cut, :] = pieces[m ^ (2 * n)][start : start + cut, :]


def out_rows_call(index, pieces):
    rows, width = pieces[0].shape
    return kernel_call(
        out_rows_body,
        shape((CHIPS * rows, width), bf16),
        [pl.BlockSpec((rows, width), lambda i, n: (0, 0))] * CHIPS,
        pl.BlockSpec((CHIPS * rows, width), lambda i, n: (0, 0)),
        tuple(pieces),
        index=index,
        grid=(1,),
        name="out_rows",
    )


LANE_HEADS = 4


def own_block_bias(rows):
    key = lax.broadcasted_iota(jnp.int32, (rows, rows), 0)
    mine = lax.broadcasted_iota(jnp.int32, (rows, rows), 1)
    return jnp.where(key <= mine, 0.0, masked_score)


def set_bias(bias):
    rows = bias.shape[0]
    value = own_block_bias(rows)
    for h in range(LANE_HEADS):
        bias[:, h * rows : (h + 1) * rows] = value


def far_bias(depth, d):
    return jnp.where(d <= depth, 0.0, masked_score) if d else 0.0


def attention_body(shards, index, queries, *refs):
    kvs = refs[:shards]
    turned_out, out, stats, bias, terms, out_turned = refs[shards:]
    rows = bias.shape[0]
    wide = LANE_HEADS * rows

    @pl.when(pl.program_id(0) == 0)
    def _():
        set_bias(bias)

    ks = [kv[:, :HEAD] for kv in kvs]
    v_turned = jnp.concatenate([kv[...] for kv in kvs], axis=0).astype(f32).T[HEAD:].astype(bf16)
    for n in range(GROUP // LANE_HEADS):
        span = slice(n * wide, (n + 1) * wide)
        q = queries[0, :, span]
        scores, top = [], None
        for d in range(shards):
            score = dot(ks[d], q)
            if d == 0:
                score = score + bias[...]
            scores.append(score)
            highest = jnp.max(score, axis=0, keepdims=True) + far_bias(index[2], d)
            top = highest if top is None else jnp.maximum(top, highest)
        total = None
        for d in range(shards):
            term = jnp.exp(scores[d] - (top - far_bias(index[2], d)))
            part = jnp.sum(term, axis=0, keepdims=True)
            total = part if total is None else total + part
            terms[d * rows : (d + 1) * rows, :] = term.astype(bf16)
        out_turned[:, span] = dot(v_turned, terms[...]) / total
        stats[0, :, span] = top + jnp.log(total)
    turned_out[0] = out_turned[...].astype(bf16)
    straight = out_turned[...].T
    for h in range(GROUP):
        out[:, h * HEAD : (h + 1) * HEAD] = straight[h * rows : (h + 1) * rows].astype(bf16)


def attention_call(index, queries, kvs):
    chips, _, wide = queries.shape
    rows = wide // GROUP
    shards = len(kvs)
    keys = shards * rows
    block = pl.BlockSpec((1, HEAD, wide), lambda i, n: (i, 0, 0))
    return kernel_call(
        functools.partial(attention_body, shards),
        (
            shape((chips, HEAD, wide), bf16),
            shape((chips * rows, GROUP * HEAD), bf16),
            shape((chips, 1, wide), f32),
        ),
        [block] + [pl.BlockSpec((rows, 2 * HEAD), lambda i, n: (i, 0))] * shards,
        (
            block,
            pl.BlockSpec((rows, GROUP * HEAD), lambda i, n: (i, 0)),
            pl.BlockSpec((1, 1, wide), lambda i, n: (i, 0, 0)),
        ),
        (queries, *kvs),
        index=index,
        grid=(chips,),
        scratch=(
            VMEM((rows, LANE_HEADS * rows), f32),
            VMEM((keys, LANE_HEADS * rows), bf16),
            VMEM((HEAD, wide), f32),
        ),
        name="attention",
    )


def attention_back_body(shards, index, branch, wo_own, wo_other, cosine, sine, *refs):
    per_group = 3 + shards
    inputs = [refs[n * per_group : (n + 1) * per_group] for n in range(PAIR)]
    grad_q, grad_first, grad_rest = refs[-7:-4]
    bias, probs_low, grads_low, grad_lanes = refs[-4:]
    rows = bias.shape[0]
    wide = LANE_HEADS * rows
    width = branch.shape[1]
    set_bias(bias)
    cos, sin = cosine[...], sine[...]
    for n, (queries, turned_out, stats, *kvs) in enumerate(inputs):
        heads = slice(n * GROUP * HEAD, (n + 1) * GROUP * HEAD)
        grad_out = dot_nt(wo_own[heads, :], branch[:, : width // 2])
        grad_out = grad_out + dot_nt(wo_other[heads, :], branch[:, width // 2 :])
        for h in range(GROUP):
            grad_lanes[:, h * rows : (h + 1) * rows] = grad_out[h * HEAD : (h + 1) * HEAD].astype(bf16)
        ks = [kv[:, :HEAD] for kv in kvs]
        vs = [kv[:, HEAD:] for kv in kvs]
        k_turned = jnp.concatenate([kv[...] for kv in kvs], axis=0).astype(f32).T[:HEAD].astype(bf16)
        k_total, v_total, parts = None, None, []
        for c in range(GROUP // LANE_HEADS):
            span = slice(c * wide, (c + 1) * wide)
            q, mine = queries[0, :, span], grad_lanes[:, span]
            delta = jnp.sum(
                mine.astype(f32) * turned_out[0, :, span].astype(f32), axis=0, keepdims=True
            )
            for d in range(shards):
                score = dot(ks[d], q)
                if d == 0:
                    score = score + bias[...]
                probs = jnp.exp(score - (stats[0, :, span] - far_bias(index[2], d)))
                grad_scores = probs * (dot(vs[d], mine) - delta)
                probs_low[d * rows : (d + 1) * rows, :] = probs.astype(bf16)
                grads_low[d * rows : (d + 1) * rows, :] = grad_scores.astype(bf16)
            u = dot(k_turned, grads_low[...]) * HEAD ** (-0.5)
            parts.append(u * cos - half_rotated(u) * sin)
            k_term = dot_nt(grads_low[...], q)
            v_term = dot_nt(probs_low[...], mine)
            k_total = k_term if k_total is None else k_total + k_term
            v_total = v_term if v_total is None else v_total + v_term
        straight = jnp.concatenate(parts, axis=1).T
        for h in range(GROUP):
            spot = (n * GROUP + h) * HEAD
            grad_q[:, spot : spot + HEAD] = straight[h * rows : (h + 1) * rows].astype(bf16)
        both = jnp.concatenate([k_total, v_total], axis=1)
        spot = slice(n * 2 * HEAD, (n + 1) * 2 * HEAD)
        grad_first[:, spot] = both[:rows, :]
        for d in range(1, shards):
            grad_rest[d - 1, :, spot] = both[d * rows : (d + 1) * rows, :].astype(bf16)


def attention_back_call(index, m, branch, wo_own, wo_other, cosine, sine, groups, before):
    chips, _, wide = groups[0][0].shape
    rows = wide // GROUP
    shards = len(groups[0][3])
    keys = shards * rows
    tokens = chips * rows
    block = pl.BlockSpec((1, HEAD, wide), lambda i, n: (m, 0, 0))
    in_specs = [whole()] * 5
    operands = [branch, wo_own, wo_other, jnp.tile(cosine, (1, LANE_HEADS)), jnp.tile(sine, (1, LANE_HEADS))]
    for queries, turned, stats, kvs in groups:
        in_specs += [block, block, pl.BlockSpec((1, 1, wide), lambda i, n: (m, 0, 0))]
        in_specs += [pl.BlockSpec((rows, 2 * HEAD), lambda i, n: (m, 0))] * shards
        operands += [queries, turned, stats, *kvs]
    aliases = {}
    if before is not None:
        aliases = {1 + len(operands) + n: n for n in range(3)}
        in_specs += [pl.BlockSpec(memory_space=pl.ANY)] * 3
        operands += list(before)
    outs = (
        shape((tokens, PAIR * GROUP * HEAD), bf16),
        shape((tokens, PAIR * 2 * HEAD), f32),
        shape((shards - 1, tokens, PAIR * 2 * HEAD), bf16),
    )
    out_specs = (
        pl.BlockSpec((rows, PAIR * GROUP * HEAD), lambda i, n: (m, 0)),
        pl.BlockSpec((rows, PAIR * 2 * HEAD), lambda i, n: (m, 0)),
        pl.BlockSpec((shards - 1, rows, PAIR * 2 * HEAD), lambda i, n: (0, m, 0)),
    )
    return kernel_call(
        functools.partial(attention_back_body, shards),
        outs,
        in_specs,
        out_specs,
        tuple(operands),
        index=index,
        grid=(1,),
        scratch=(
            VMEM((rows, LANE_HEADS * rows), f32),
            VMEM((keys, LANE_HEADS * rows), bf16),
            VMEM((keys, LANE_HEADS * rows), bf16),
            VMEM((HEAD, wide), bf16),
        ),
        aliases=aliases,
        name="attention_back",
    )


def parts_body(steps, transposed, count, *refs):
    lefts, owns, others = refs[:count], refs[count : 2 * count], refs[2 * count : 3 * count]
    outs = refs[3 * count :]
    rows = outs[0].shape[0]
    step = pl.program_id(0)

    def run(weights):
        total = None
        for left, weight in zip(lefts, weights):
            term = (dot_nt if transposed else dot)(left[...], weight[...])
            total = term if total is None else total + term
        for m, out in enumerate(outs):
            out[...] = total[m * rows : (m + 1) * rows, :].astype(out.dtype)

    @pl.when(step < steps)
    def _():
        run(owns)

    @pl.when(step >= steps)
    def _():
        run(others)


def parts_call(terms, rows, transposed, name):
    tokens = terms[0][0].shape[0]
    half = terms[0][1].shape[0] if transposed else terms[0][1].shape[1]
    tile = 256
    steps = half // tile
    last = steps - 1
    specs = [pl.BlockSpec((tokens, term[0].shape[1]), lambda j: (0, 0)) for term in terms]
    for side in range(2):
        for left, _, _, spot in terms:
            depth = left.shape[1]

            def place(side, spot, j):
                step = jnp.maximum(j - steps, 0) if side else jnp.minimum(j, last)
                return (step, spot) if transposed else (spot, step)

            block = (tile, depth) if transposed else (depth, tile)
            specs.append(pl.BlockSpec(block, functools.partial(place, side, spot)))
    count = tokens // rows
    return kernel_call(
        functools.partial(parts_body, steps, transposed, len(terms)),
        tuple(shape((rows, 2 * half), f32 if m == 0 else bf16) for m in range(count)),
        specs,
        tuple(pl.BlockSpec((rows, tile), lambda j: (0, j)) for _ in range(count)),
        (*(term[0] for term in terms), *(term[1] for term in terms), *(term[2] for term in terms)),
        grid=(2 * steps,),
        name=name,
    )


def gate_body(count, *refs):
    twos = refs[:count]
    gate_own, up_own, gate_other, up_other, act, for_gate, for_up, two_all = refs[count:]
    half = two_all.shape[1] // 2

    @pl.when(pl.program_id(0) == 0)
    def _():
        start = 0
        for two in twos:
            two_all[start : start + two.shape[0], :] = two[...]
            start += two.shape[0]

    own = jnp.concatenate([gate_own[...], up_own[...]], axis=1)
    other = jnp.concatenate([gate_other[...], up_other[...]], axis=1)
    both = dot(two_all[:, :half], own) + dot(two_all[:, half:], other)
    wide = gate_own.shape[1]
    gate, up = both[:, :wide], both[:, wide:]
    sig = 1.0 / (1.0 + jnp.exp(-gate))
    silu = gate * sig
    act[...] = (silu * up).astype(bf16)
    for_gate[...] = (up * sig * (1.0 + gate * (1.0 - sig))).astype(bf16)
    for_up[...] = silu.astype(bf16)


def gate_call(twos, own, other):
    rows, width = twos[0].shape
    tokens = CHIPS * rows
    half = width // 2
    ff = own.shape[1] // 2
    tile = LANES
    steps = ff // tile
    weight = [
        pl.BlockSpec((half, tile), lambda j: (0, j)),
        pl.BlockSpec((half, tile), lambda j: (0, j + steps)),
    ]
    column = pl.BlockSpec((tokens, tile), lambda j: (0, j))
    return kernel_call(
        functools.partial(gate_body, len(twos)),
        tuple(shape((tokens, ff), bf16) for _ in range(3)) + (shape((tokens, width), bf16),),
        [pl.BlockSpec(two.shape, lambda j: (0, 0)) for two in twos] + weight + weight,
        (column, column, column, pl.BlockSpec((tokens, width), lambda j: (0, 0))),
        (*twos, own, own, other, other),
        grid=(steps,),
        name="gate",
    )


def hidden_back_body(g, own, other, for_gate, for_up, grads):
    half = g.shape[1] // 2
    ff = own.shape[0]
    hidden = dot_nt(g[:, :half], own[...]) + dot_nt(g[:, half:], other[...])
    grads[:, :ff] = (hidden * for_gate[...].astype(f32)).astype(bf16)
    grads[:, ff:] = (hidden * for_up[...].astype(f32)).astype(bf16)


def hidden_back_call(g, own, other, for_gate, for_up):
    tokens, width = g.shape
    ff, half = own.shape
    block = tokens // 2
    row = lambda i: (i, 0)
    fixed = lambda i: (0, 0)
    return kernel_call(
        hidden_back_body,
        shape((tokens, 2 * ff), bf16),
        [
            pl.BlockSpec((block, width), row),
            pl.BlockSpec((ff, half), fixed),
            pl.BlockSpec((ff, half), fixed),
            pl.BlockSpec((block, ff), row),
            pl.BlockSpec((block, ff), row),
        ],
        pl.BlockSpec((block, 2 * ff), row),
        (g, own, other, for_gate, for_up),
        grid=(2,),
        name="hidden_back",
    )


def weight_grad_body(per, outputs, adds, left, right, *refs):
    added = [refs[n * outputs : (n + 1) * outputs] for n in range(adds)]
    outs, turned = refs[adds * outputs : -1], refs[-1]
    step = pl.program_id(0)

    @pl.when(step == 0)
    def _():
        turned[...] = left[...].T

    for n in range(outputs):

        @pl.when(step // per == n)
        def _(n=n):
            total = dot(turned[...], right[...])
            for terms in added:
                total = total + terms[n][...].astype(f32)
            outs[n][...] = total.astype(bf16)


def weight_grad(left, left_side, right, place, width, outputs, added, name):
    tokens = left.shape[0]
    rows = left.shape[1] // (1 if left_side is None else 2)
    tile = 256 if width % 256 == 0 else width
    per = width // tile
    first = place * width // tile
    side = left_side or 0

    def spot(n, j):
        return (0, jnp.clip(j - n * per, 0, per - 1))

    tiles = [pl.BlockSpec((rows, tile), functools.partial(spot, n)) for n in range(outputs)]
    return kernel_call(
        functools.partial(weight_grad_body, per, outputs, len(added)),
        tuple(shape((rows, width), bf16) for _ in range(outputs)),
        [
            pl.BlockSpec((tokens, rows), lambda j: (0, side)),
            pl.BlockSpec((tokens, tile), lambda j: (0, first + j)),
        ]
        + tiles * len(added),
        tuple(tiles),
        (left, right, *(term for terms in added for term in terms)),
        grid=(per * outputs,),
        scratch=(VMEM((rows, tokens), bf16),),
        name=name,
    )


def rows_result_body(local, index, *refs):
    pieces, out = refs[:PIECES], refs[PIECES]
    half = local // 2
    shards = out.shape[1] // local
    for m in range(CHIPS):
        for core in range(2):

            @pl.when((pl.program_id(0) == m) & (index[1] == core))
            def _():
                for side in range(2):
                    piece = pieces[2 * m + side]
                    for s in range(shards):
                        spot = s * local + (core ^ side) * half
                        out[:, spot : spot + half] = piece[:, s * half : (s + 1) * half].astype(f32)


def rows_result(index, pieces, local, name):
    cut, half_width = pieces[0].shape
    return kernel_call(
        functools.partial(rows_result_body, local),
        shape((CHIPS * cut, 2 * half_width), f32),
        [pl.BlockSpec((cut, half_width), lambda i, n: (0, 0))] * PIECES,
        pl.BlockSpec((cut, 2 * half_width), lambda i, n: (n[0] ^ i, 0)),
        tuple(pieces),
        index=index,
        grid=(CHIPS,),
        name=name,
    )


def lane_sum(value):
    total = value[:, :LANES]
    for n in range(1, value.shape[1] // LANES):
        total = total + value[:, n * LANES : (n + 1) * LANES]
    return total


def feedforward_result_body(ff_local, cut, index, *refs):
    pieces = refs[:CHIPS]
    gate_weight, up_weight, gain = refs[CHIPS : CHIPS + 3]
    gate_out, up_out, gain_out = refs[-3:]
    shards = gate_weight.shape[1] // ff_local
    width = shards * cut
    for chip in range(CHIPS):

        @pl.when(index[0] == chip)
        def _():
            @pl.loop(0, gate_out.shape[0] // 16)
            def _(n):
                rows = pl.ds(pl.multiple_of(n * 16, 16), 16)
                scale = gain[rows, :1]
                total = jnp.zeros((16, LANES), f32)
                for base, weight, out in ((0, gate_weight, gate_out), (width, up_weight, up_out)):
                    parts = []
                    for s in range(shards):
                        for owner in range(CHIPS):
                            start = base + s * cut
                            parts.append(pieces[owner ^ chip][rows, start : start + cut].astype(f32))
                    wide = jnp.concatenate(parts, axis=1)
                    total = total + lane_sum(wide * weight[rows, :].astype(f32))
                    out[rows, :] = wide * scale
                gain_out[rows, :] = total


def feedforward_result(index, side, pieces, gate_weight, up_weight, gain, ff_local, before):
    local, ff = gate_weight.shape
    half = local // 2
    rows = 64
    steps = half // rows
    row = lambda i, n: ((n[1] ^ side) * steps + i, 0)
    in_specs = [pl.BlockSpec((rows, pieces[0].shape[1]), lambda i, n: (i, 0))] * CHIPS
    in_specs += [pl.BlockSpec((rows, ff), row)] * 2 + [pl.BlockSpec((rows, LANES), row)]
    operands = (*pieces, gate_weight, up_weight, gain)
    aliases = {}
    if before is not None:
        aliases = {1 + len(operands) + n: n for n in range(3)}
        in_specs = in_specs + [pl.BlockSpec(memory_space=pl.ANY)] * 3
        operands = operands + tuple(before)
    return kernel_call(
        functools.partial(feedforward_result_body, ff_local, ff_local // CHIPS),
        (shape((local, ff), f32), shape((local, ff), f32), shape((local, LANES), f32)),
        in_specs,
        (pl.BlockSpec((rows, ff), row), pl.BlockSpec((rows, ff), row), pl.BlockSpec((rows, LANES), row)),
        operands,
        index=index,
        grid=(steps,),
        aliases=aliases,
        name="feedforward_result",
    )


def qkv_result_body(local, group_shards, index, *refs):
    pieces = refs[:PIECES]
    weights, gain = refs[PIECES : PIECES + 3], refs[PIECES + 3]
    outs, gain_out = refs[PIECES + 4 : PIECES + 7], refs[PIECES + 7]
    q_width = GROUP * HEAD
    cut = local // CHIPS
    scale = gain[:, :1]
    for chip in range(CHIPS):
        for side in range(2):

            @pl.when((index[0] == chip) & (pl.program_id(0) == side))
            def _():
                parts, k_parts, v_parts = [], [], []
                for group in range(CHIPS):
                    owner = (group >> 1) + 2 * (group & 1)
                    piece = pieces[2 * (owner ^ chip) + side]
                    for s in range(group_shards):
                        for j in range(CHIPS):
                            start = ((j ^ owner) * group_shards + s) * cut
                            parts.append(piece[:, start : start + cut].astype(f32))
                    k_parts.append(piece[:, q_width : q_width + HEAD].astype(f32))
                    v_parts.append(piece[:, q_width + HEAD : q_width + 2 * HEAD].astype(f32))
                total = jnp.zeros((gain.shape[0], LANES), f32)
                for part, weight, out in zip((parts, k_parts, v_parts), weights, outs):
                    wide = jnp.concatenate(part, axis=1)
                    total = total + lane_sum(wide * weight[...].astype(f32))
                    out[...] = wide * scale
                gain_out[...] = total


def qkv_result(index, pieces, query, key, value, gain):
    local, width = query.shape
    half = local // 2
    group_shards = width // local // CHIPS
    row = lambda i, n: (n[1] ^ i, 0)
    kv_width = key.shape[1]
    return kernel_call(
        functools.partial(qkv_result_body, local, group_shards),
        (
            shape((local, width), f32),
            shape((local, kv_width), f32),
            shape((local, kv_width), f32),
            shape((local, LANES), f32),
        ),
        [pl.BlockSpec(pieces[0].shape, lambda i, n: (0, 0))] * PIECES
        + [
            pl.BlockSpec((half, width), row),
            pl.BlockSpec((half, kv_width), row),
            pl.BlockSpec((half, kv_width), row),
            pl.BlockSpec((half, LANES), row),
        ],
        (
            pl.BlockSpec((half, width), row),
            pl.BlockSpec((half, kv_width), row),
            pl.BlockSpec((half, kv_width), row),
            pl.BlockSpec((half, LANES), row),
        ),
        (*pieces, query, key, value, gain),
        index=index,
        grid=(2,),
        name="qkv_result",
    )


def per_device(
    hidden_in,
    attention_gain,
    query_weight,
    key_weight,
    value_weight,
    output_weight,
    feedforward_gain,
    gate_weight,
    up_weight,
    down_weight,
    out_grad,
):
    rows, width = hidden_in.shape
    shards = lax.axis_size("shard")
    replicas = lax.axis_size("replica")
    place = lax.axis_index("replica")
    depth = lax.axis_index("shard")
    core = place & 1
    chip = (place >> 1) & (CHIPS - 1)
    local = width // shards
    half = local // 2
    ff_local = down_weight.shape[0]
    group_shards = shards // CHIPS
    q_width = GROUP * HEAD
    qkv_width = q_width + 2 * HEAD
    index = jnp.stack([chip, core, depth]).astype(jnp.int32)

    gain_one = jnp.broadcast_to(attention_gain.astype(f32)[:, None], (local, LANES))
    gain_two = jnp.broadcast_to(feedforward_gain.astype(f32)[:, None], (local, LANES))


    at_block, out_block = attention_block(
        index, query_weight, key_weight, value_weight, output_weight, gain_one
    )
    x = own_first(index, (after(hidden_in, at_block),), local)[0]
    xs = [x, swap(x, 2)]
    at_own = lax.all_gather(at_block, "shard", axis=0, tiled=True)
    out_all = lax.all_gather(out_block, "shard", axis=0, tiled=True)
    gu_block = feedforward_block(index, gate_weight, up_weight, after(gain_two, at_block), ff_local)
    gu_own = lax.all_gather(gu_block, "shard", axis=0, tiled=True)
    down_own = lax.all_gather(down_block(index, down_weight, local), "shard", axis=0, tiled=True)
    g = own_first(index, (after(out_grad, x),), local)[0]
    g_blocks = [g, swap(g, 2), swap(g, 4)]
    at_own = after(at_own, gu_block, xs[1], *g_blocks[1:])

    qkv_own = [at_own]
    qkv_own.append(swap(qkv_own[0], 4))
    qkv_other = [swap(qkv_own[0], 1)]
    inverse = rope_base ** (-jnp.arange(0, HEAD, 2, dtype=f32) / HEAD)
    places = (depth * rows + jnp.arange(rows, dtype=jnp.int32)).astype(f32)
    angles = inverse[:, None] * places[None, :]
    angles = jnp.concatenate([angles, angles], axis=0)
    cosine, sine = jnp.cos(angles), jnp.sin(angles)

    def shifted(kv):
        return [kv] + [shift(kv, d) for d in range(1, shards)]

    queries, kv, xhat = qkv_call(xs, qkv_own[0], qkv_other[0], cosine, sine)
    kvs = shifted(kv)
    qkv_own[1] = after(qkv_own[1], *kvs[1:])
    qkv_other.append(swap(qkv_own[1], 1))
    queries_two, kv_two = qkv_call(xhat, qkv_own[1], qkv_other[1], cosine, sine)
    kvs_two = shifted(kv_two)
    groups = [(queries, *attention_call(index, queries, kvs), kvs)]
    groups.append((queries_two, *attention_call(index, queries_two, kvs_two), kvs_two))
    attended = [group[2] for group in groups]
    groups = [(group[0], group[1], group[3], group[4]) for group in groups]

    out_all = after(out_all, qkv_own[1])
    x_place = chip & 1
    low_group = (chip >> 1) == 0
    pair_rows = PAIR * group_shards * half // 2

    def out_for(mask):
        return lax.dynamic_slice_in_dim(out_all, ((chip ^ mask) & 1) * pair_rows, pair_rows, 0)

    out_pieces = [out_for(0)] + [swap(out_for(m), 2 * m) for m in range(1, CHIPS)]
    wo_own = out_rows_call(index, [after(piece, *kvs_two[1:]) for piece in out_pieces])
    wo_other = swap(wo_own, 1)

    mid_terms = [(attended[n], wo_own, wo_other, n) for n in range(PAIR)]
    g_blocks.append(swap(after(g, *out_pieces[1:]), 6))
    mid_out = parts_call(mid_terms, rows, False, "attention_out")
    g_all = jnp.concatenate([after(block, mid_out[0]) for block in g_blocks], axis=0)
    middle, two = middle_call(plane_send(mid_out), after(x, g_all))
    twos = plane_gather_far(two, *plane_gather_near(two))

    gu_own = after(gu_own, *twos[1:])
    gu_other = swap(gu_own, 1)
    act, for_gate, for_up, two_all = gate_call(twos, gu_own, gu_other)

    def over_groups(kept):
        if replicas > PIECES:
            groups = [
                [e * PIECES + i for e in range(replicas // PIECES)] for i in range(PIECES)
            ]
            kept = lax.psum(kept, "replica", axis_index_groups=groups)
        return kept

    def reduced(term):
        kept = lax.psum_scatter(term, "shard", scatter_dimension=0, tiled=True)
        return over_groups(kept)

    def plane_pieces(kept):
        mine = plane_gather(kept)
        return mine, [swap(part, 1) for part in mine]

    def mixed(mine, theirs):
        return [part for pair in zip(mine, theirs) for part in pair]

    down_sent = weight_grad(act, None, g_all, 1, width // 2, 1, (), "down_grad_other")
    down_sent = [swap(down_sent[0], 1)]
    down_sent[0] = after(down_sent[0], down_own)
    down_term = weight_grad(act, None, g_all, 0, width // 2, 1, (down_sent,), "down_grad")[0]
    down_other = swap(down_own, 1)

    grads = hidden_back_call(after(g_all, down_term), down_own, down_other, for_gate, for_up)
    grads_wide = grads.shape[1]
    gu_sent = weight_grad(two_all, 1, grads, 0, grads_wide, 1, (), "gate_grad_other")
    gu_sent = [swap(gu_sent[0], 1)]
    gu_term = weight_grad(two_all, 0, grads, 0, grads_wide, 1, (gu_sent,), "gate_grad")[0]
    gu_kept = reduced(gu_term)
    down_kept = reduced(after(down_term, gu_term))
    grads_late = after(grads, gu_term)
    e_terms = parts_call([(grads_late, gu_own, gu_other, 0)], rows, True, "feedforward_back")
    e_parts = plane_send(e_terms)
    act_late = after(act, e_terms[0])
    out_terms = parts_call([(act_late, down_own, down_other, 0)], rows, False, "feedforward_out")

    middle_late = after(middle, out_terms[0])
    grad_middle, branch = grad_middle_call(e_parts, middle_late, g)
    branches = [branch, swap(branch, 2)]

    def back_block(m, block, before):
        return attention_back_call(index, m, block, wo_own, wo_other, cosine, sine, groups, before)

    before = back_block(0, branch, None)
    out_parts = plane_send(after(out_terms, branches[1], before[1]))
    half_wide = width // 2
    branch_all = jnp.concatenate([branch, after(branches[1], before[1])], axis=0)
    both_attended = jnp.concatenate(attended, axis=1)
    wo_sent = weight_grad(both_attended, None, branch_all, 1, half_wide, 1, (), "out_grad_other")
    wo_other_term = wo_sent[0]
    wo_sent = [swap(wo_other_term, 1)]
    before = back_block(1, after(branches[1], before[1], wo_other_term), before)
    output = output_call(index, out_parts, middle, local)
    grad_q, grad_first, grad_rest = before
    grad_rest = after(grad_rest, out_parts[1])
    rest = [shift(grad_rest[d - 1], -d) for d in range(1, shards)]

    wo_term = weight_grad(both_attended, None, branch_all, 0, half_wide, 1, (wo_sent,), "out_grad")[0]
    wo_terms = out_sends(index, after(wo_term, *rest, *out_parts[1:]))
    wo_parts = plane_send(wo_terms)
    wo_block = out_block_call(index, wo_parts)
    wo_kept = reduced(after(wo_block, down_kept))
    gu_near = plane_gather_near(after(gu_kept, wo_parts[1]))
    grad_first = after(grad_first, wo_block, *gu_near)
    grad_qkv = grad_qkv_call(grad_q, grad_first, rest, cosine, sine)

    def qkv_grad(n, side, added, name):
        return weight_grad(xhat, side, grad_qkv[n], 0, qkv_width, 1, added, name)

    qkv_sent = [swap(qkv_grad(n, 1, (), "qkv_grad_other")[0], 1) for n in (1, 0)]
    back_terms = [(grad_qkv[n], qkv_own[n], qkv_other[n], 0) for n in range(PAIR)]
    qkv_second = qkv_grad(1, 0, ([qkv_sent[0]],), "qkv_grad")[0]
    qkv_term = qkv_grad(0, 0, ([qkv_sent[1]],), "qkv_grad")[0]
    at_term = jnp.concatenate([qkv_term, qkv_second], axis=1)
    at_kept = reduced(after(at_term, wo_kept))
    back_terms[0] = (after(grad_qkv[0], qkv_term, qkv_second), *back_terms[0][1:])
    back_parts = parts_call(back_terms, rows, True, "qkv_back")
    e_one = plane_send(back_parts)
    gu_mine = plane_gather_far(gu_kept, *gu_near)
    gu_mine = gu_mine[:3] + [jnp.concatenate(gu_mine[3:], axis=0)]
    gu_theirs = [swap(after(part, output, back_parts[0]), 1) for part in gu_mine]
    gu_out = feedforward_result(index, 0, gu_mine, gate_weight, up_weight, gain_two, ff_local, None)
    gu_out = feedforward_result(index, 1, gu_theirs, gate_weight, up_weight, gain_two, ff_local, gu_out)

    down_mine = plane_gather_far(down_kept, *plane_gather_near(after(down_kept, *gu_near)))
    down_mine = down_mine[:3] + [jnp.concatenate(down_mine[3:], axis=0)]
    down_theirs = [swap(part, 1) for part in down_mine]
    down_out = rows_result(index, mixed(down_mine, down_theirs), local, "down_result")
    grad_input = grad_input_call(index, e_one, x, grad_middle, local)

    wo_out = rows_result(index, mixed(*plane_pieces(after(wo_kept, *gu_theirs))), local, "out_result")
    at_kept = after(at_kept, gu_out[0], down_out, grad_input)
    second = swap(at_kept[:, qkv_width:], 4)
    first = at_kept[:, :qkv_width].astype(f32) + second.astype(f32)
    at_pieces = mixed(*plane_pieces(first.astype(bf16)))
    q_out, k_out, v_out, gain_one_sums = qkv_result(
        index, at_pieces, query_weight, key_weight, value_weight, gain_one
    )
    return (
        output,
        grad_input,
        jnp.sum(gain_one_sums, axis=1),
        q_out,
        k_out,
        v_out,
        wo_out,
        jnp.sum(gu_out[2], axis=1),
        gu_out[0],
        gu_out[1],
        down_out,
    )


def solution(mesh):
    return jax.shard_map(
        per_device,
        mesh=mesh,
        in_specs=(
            P(("replica", "shard"), None),
            P("shard"),
            P("shard", None),
            P("shard", None),
            P("shard", None),
            P("shard", None),
            P("shard"),
            P("shard", None),
            P("shard", None),
            P("shard", None),
            P(("replica", "shard"), None),
        ),
        out_specs=(
            P(("replica", "shard"), None),
            P(("replica", "shard"), None),
            P("shard"),
            P("shard", None),
            P("shard", None),
            P("shard", None),
            P("shard", None),
            P("shard"),
            P("shard", None),
            P("shard", None),
            P("shard", None),
        ),
        check_vma=False,
    )
```

```python
import functools

import jax
import jax.numpy as jnp
from jax import lax
from jax.experimental import pallas as pl
from jax.experimental.pallas import tpu as pltpu
from jax.sharding import PartitionSpec as P

HEADS = 32
KV_HEADS = 4
HEAD = 64
GROUP = HEADS // KV_HEADS
CHIPS = 4
PIECES = 2 * CHIPS
PAIR = 2
LANES = 128

norm_eps = 1e-05
rope_base = 10000.0
masked_score = -1e30

f32 = jnp.float32
bf16 = jnp.bfloat16
VMEM = pltpu.VMEM
NT = (((1,), (1,)), ((), ()))
TN = (((0,), (0,)), ((), ()))


def dot(left, right):
    return jnp.dot(left, right, preferred_element_type=f32)


def dot_nt(left, right):
    return lax.dot_general(left, right, NT, preferred_element_type=f32)


def dot_tn(left, right):
    return lax.dot_general(left, right, TN, preferred_element_type=f32)


def shape(dims, kind):
    return jax.ShapeDtypeStruct(dims, kind)


def whole():
    return pl.BlockSpec(memory_space=VMEM)


TIMES = {"attention_back": 13.0}


def kernel_call(body, out_shape, in_specs, out_specs, operands, *, index=None, grid=(), scratch=(),
                aliases=None, name=None):
    params = pltpu.CompilerParams(
        vmem_limit_bytes=52 * 2**20, dimension_semantics=("arbitrary",) * len(grid)
    )
    moved = int(TIMES.get(name, 0.0) * 3.69e6)
    cost = pl.CostEstimate(flops=0, bytes_accessed=moved, transcendentals=0)
    common = dict(
        out_shape=out_shape,
        compiler_params=params,
        cost_estimate=cost,
        input_output_aliases=aliases or {},
        name=name,
    )
    if index is None:
        spec = pl.GridSpec(grid=grid, in_specs=in_specs, out_specs=out_specs, scratch_shapes=scratch)
        return pl.pallas_call(body, grid_spec=spec, **common)(*operands)
    spec = pltpu.PrefetchScalarGridSpec(
        num_scalar_prefetch=1, grid=grid, in_specs=in_specs, out_specs=out_specs,
        scratch_shapes=scratch,
    )
    return pl.pallas_call(body, grid_spec=spec, **common)(index, *operands)


def swap(value, mask):
    size = lax.axis_size("replica")
    return lax.ppermute(value, "replica", [(i, i ^ mask) for i in range(size)])


def shift(value, step):
    size = lax.axis_size("shard")
    pairs = [(i, i + step) for i in range(size) if 0 <= i + step < size]
    return lax.ppermute(value, "shard", pairs)


def plane_gather(value):
    return [value] + [swap(value, 2 * m) for m in range(1, CHIPS)]


def plane_gather_near(value):
    return swap(value, 2), swap(value, 4)


def plane_gather_far(value, across, along):
    middle = value.shape[0] // 2
    return [value, across, along, swap(across[:middle], 4), swap(along[middle:], 2)]


def plane_send(parts):
    return [parts[0]] + [swap(parts[m], 2 * m) for m in range(1, len(parts))]


def group_of(chip):
    return 2 * (chip & 1) + (chip >> 1)


def after(value, *others):
    return lax.optimization_barrier((value, *others))[0]


def attention_block_body(local, group_shards, index, q, k, v, o, gain, out, wo_out):
    scale = gain[:, :1]
    q_width = GROUP * HEAD
    cut = local // CHIPS
    for chip in range(CHIPS):

        group = group_of(chip)

        @pl.when(index[0] == chip)
        def _(group=group):
            parts = []
            for m in range(CHIPS):
                for s in range(group_shards):
                    start = group * q_width + s * local + (m ^ chip) * cut
                    parts.append(q[:, start : start + cut])
            parts.append(k[:, group * HEAD : (group + 1) * HEAD])
            parts.append(v[:, group * HEAD : (group + 1) * HEAD])
            wide = jnp.concatenate([part.astype(f32) for part in parts], axis=1)
            out[...] = (wide * scale).astype(bf16)

    half = local // 2
    shards = o.shape[1] // local
    for core in range(2):

        @pl.when(index[1] == core)
        def _():
            for s in range(shards):
                piece = o[:, s * local + core * half : s * local + (core + 1) * half]
                wo_out[:, s * half : (s + 1) * half] = piece


def attention_block(index, query, key, value, output, gain):
    local, width = query.shape
    half = local // 2
    shards = width // local
    return kernel_call(
        functools.partial(attention_block_body, local, shards // CHIPS),
        (
            shape((half, GROUP * HEAD + 2 * HEAD), bf16),
            shape((local // CHIPS, width // 2), bf16),
        ),
        [
            pl.BlockSpec((half, width), lambda i, n: (n[1], 0)),
            pl.BlockSpec((half, key.shape[1]), lambda i, n: (n[1], 0)),
            pl.BlockSpec((half, key.shape[1]), lambda i, n: (n[1], 0)),
            pl.BlockSpec((local // CHIPS, width), lambda i, n: (n[0], 0)),
            pl.BlockSpec((half, LANES), lambda i, n: (n[1], 0)),
        ],
        (
            pl.BlockSpec((half, GROUP * HEAD + 2 * HEAD), lambda i, n: (0, 0)),
            pl.BlockSpec((local // CHIPS, width // 2), lambda i, n: (0, 0)),
        ),
        (query, key, value, output, gain),
        index=index,
        grid=(1,),
        name="attention_block",
    )


def feedforward_block_body(ff_local, cut, index, gate, up, gain, out):
    scale = gain[:, :1]
    shards = gate.shape[1] // ff_local
    width = shards * cut
    for chip in range(CHIPS):

        @pl.when(index[0] == chip)
        def _():
            for n, source in enumerate((gate, up)):
                parts = [
                    source[:, s * ff_local + chip * cut : s * ff_local + (chip + 1) * cut].astype(f32)
                    for s in range(shards)
                ]
                wide = jnp.concatenate(parts, axis=1)
                out[:, n * width : (n + 1) * width] = (wide * scale).astype(bf16)


def feedforward_block(index, gate, up, gain, ff_local):
    local, ff = gate.shape
    half = local // 2
    rows = 64
    steps = half // rows
    cut = ff_local // CHIPS
    width = 2 * (ff // CHIPS)
    return kernel_call(
        functools.partial(feedforward_block_body, ff_local, cut),
        shape((half, width), bf16),
        [
            pl.BlockSpec((rows, ff), lambda i, n: (n[1] * steps + i, 0)),
            pl.BlockSpec((rows, ff), lambda i, n: (n[1] * steps + i, 0)),
            pl.BlockSpec((rows, LANES), lambda i, n: (n[1] * steps + i, 0)),
        ],
        pl.BlockSpec((rows, width), lambda i, n: (i, 0)),
        (gate, up, gain),
        index=index,
        grid=(steps,),
        name="feedforward_block",
    )


def own_first_body(local, index, *refs):
    count = len(refs) // 2
    half = local // 2
    for core in range(2):

        @pl.when(index[1] == core)
        def _():
            for source, out in zip(refs[:count], refs[count:]):
                shards = source.shape[1] // local
                sides = out.shape[1] // (shards * half)
                for side in range(sides):
                    for s in range(shards):
                        start = s * local + (core ^ side) * half
                        spot = (side * shards + s) * half
                        out[:, spot : spot + half] = source[:, start : start + half]


def own_first(index, sources, local, halves=2):
    return kernel_call(
        functools.partial(own_first_body, local),
        tuple(shape((v.shape[0], v.shape[1] * halves // 2), bf16) for v in sources),
        [pl.BlockSpec(v.shape, lambda i, n: (0, 0)) for v in sources],
        tuple(
            pl.BlockSpec((v.shape[0], v.shape[1] * halves // 2), lambda i, n: (0, 0)) for v in sources
        ),
        tuple(sources),
        index=index,
        grid=(1,),
        name="own_first",
    )


def down_block_body(local, index, source, out):
    own_first_body(local, index, source, out)


def down_block(index, down, local):
    ff_local, width = down.shape
    cut = ff_local // CHIPS
    return kernel_call(
        functools.partial(down_block_body, local),
        shape((cut, width // 2), bf16),
        [pl.BlockSpec((cut, width), lambda i, n: (n[0], 0))],
        pl.BlockSpec((cut, width // 2), lambda i, n: (0, 0)),
        (down,),
        index=index,
        grid=(1,),
        name="down_block",
    )


def part_sum(parts):
    total = parts[0][...]
    for part in parts[1:]:
        total = total + part[...].astype(f32)
    return total


def mean_of(values):
    return jnp.mean(values, axis=1, keepdims=True)


def middle_body(*refs):
    parts, (x, middle, two) = refs[:PAIR], refs[PAIR:]
    total = x[...].astype(f32) + part_sum(parts)
    middle[...] = total
    two[...] = (total * lax.rsqrt(mean_of(total * total) + norm_eps)).astype(bf16)


def middle_call(parts, x):
    return kernel_call(
        middle_body,
        (shape(x.shape, f32), shape(x.shape, bf16)),
        [whole()] * (PAIR + 1),
        (whole(), whole()),
        (*parts, x),
        name="middle",
    )


def norm_back(e, values):
    inverse = lax.rsqrt(mean_of(values * values) + norm_eps)
    return inverse * e - values * (inverse * inverse * inverse) * mean_of(e * values)


def grad_middle_body(*refs):
    parts, (middle, g, grad, low) = refs[:CHIPS], refs[CHIPS:]
    total = g[...].astype(f32) + norm_back(part_sum(parts), middle[...])
    grad[...] = total
    low[...] = total.astype(bf16)


def grad_middle_call(parts, middle, g):
    return kernel_call(
        grad_middle_body,
        (shape(g.shape, f32), shape(g.shape, bf16)),
        [whole()] * (CHIPS + 2),
        (whole(), whole()),
        (*parts, middle, g),
        name="grad_middle",
    )


def store_in_order(local, index, value, out):
    half = local // 2
    shards = out.shape[1] // local
    for core in range(2):

        @pl.when(index[1] == core)
        def _():
            for side in range(2):
                for s in range(shards):
                    spot = s * local + (core ^ side) * half
                    start = (side * shards + s) * half
                    out[:, spot : spot + half] = value[:, start : start + half].astype(bf16)


def output_body(local, index, *refs):
    parts, (middle, out) = refs[:CHIPS], refs[CHIPS:]
    store_in_order(local, index, middle[...] + part_sum(parts), out)


def output_call(index, parts, middle, local):
    spec = pl.BlockSpec(middle.shape, lambda i, n: (0, 0))
    return kernel_call(
        functools.partial(output_body, local),
        shape(middle.shape, bf16),
        [spec] * (CHIPS + 1),
        spec,
        (*parts, middle),
        index=index,
        grid=(1,),
        name="output",
    )


def grad_input_body(local, index, *refs):
    parts, (x, grad, out) = refs[:PAIR], refs[PAIR:]
    total = grad[...] + norm_back(part_sum(parts), x[...].astype(f32))
    store_in_order(local, index, total, out)


def grad_input_call(index, parts, x, grad, local):
    spec = pl.BlockSpec(x.shape, lambda i, n: (0, 0))
    return kernel_call(
        functools.partial(grad_input_body, local),
        shape(x.shape, bf16),
        [spec] * (PAIR + 2),
        spec,
        (*parts, x, grad),
        index=index,
        grid=(1,),
        name="grad_input",
    )


def grad_qkv_body(shards, grad_q, first, *refs):
    rest, (cosine, sine), outs = refs[: shards - 1], refs[shards - 1 : shards + 1], refs[shards + 1 :]
    total = first[...]
    for term in rest:
        total = total + term[...].astype(f32)
    rows = cosine.shape[1]
    width = GROUP * HEAD
    cos, sin = cosine[...], sine[...]
    for n, out in enumerate(outs):
        out[:, :width] = grad_q[:, n * width : (n + 1) * width]
        for m in range(PAIR):
            span = slice(m * rows, (m + 1) * rows)
            turned = total[span, n * 2 * HEAD : (n + 1) * 2 * HEAD].T
            k = turned[:HEAD]
            k = k * cos - half_rotated(k) * sin
            both = jnp.concatenate([k, turned[HEAD:]], axis=0)
            out[span, width:] = both.T.astype(bf16)


def grad_qkv_call(grad_q, first, rest, cosine, sine):
    tokens = grad_q.shape[0]
    return kernel_call(
        functools.partial(grad_qkv_body, len(rest) + 1),
        (shape((tokens, GROUP * HEAD + 2 * HEAD), bf16),) * PAIR,
        [whole()] * (len(rest) + 4),
        (whole(),) * PAIR,
        (grad_q, first, *rest, cosine, sine),
        name="grad_qkv",
    )


def out_sends_body(index, term, *outs):
    cut = outs[0].shape[0] // PAIR
    for row in range(2):

        @pl.when(index[0] >> 1 == row)
        def _():
            for n in range(PAIR):
                for m in range(CHIPS):
                    spot = (n * CHIPS + m) * cut
                    start = (n ^ row) * cut
                    outs[m ^ (2 * n)][start : start + cut, :] = term[spot : spot + cut, :]


def out_sends(index, term):
    rows, width = term.shape
    rows //= CHIPS
    return kernel_call(
        out_sends_body,
        (shape((rows, width), bf16),) * CHIPS,
        [pl.BlockSpec(term.shape, lambda i, n: (0, 0))],
        (pl.BlockSpec((rows, width), lambda i, n: (0, 0)),) * CHIPS,
        (term,),
        index=index,
        grid=(1,),
        name="out_sends",
    )


def out_block_body(index, *refs):
    parts, out = refs[:CHIPS], refs[CHIPS]
    sums = [parts[m][...].astype(f32) + parts[m + 2][...].astype(f32) for m in range(2)]
    for side in range(2):

        @pl.when(index[0] & 1 == side)
        def _():
            for m in range(2):
                rows = sums[m].shape[0]
                spot = (m ^ side) * rows
                out[spot : spot + rows, :] = sums[m].astype(bf16)


def out_block_call(index, parts):
    rows, width = parts[0].shape
    return kernel_call(
        out_block_body,
        shape((PAIR * rows, width), bf16),
        [pl.BlockSpec((rows, width), lambda i, n: (0, 0))] * CHIPS,
        pl.BlockSpec((PAIR * rows, width), lambda i, n: (0, 0)),
        tuple(parts),
        index=index,
        grid=(1,),
        name="out_block",
    )


def half_rotated(values):
    middle = values.shape[0] // 2
    return jnp.concatenate([-values[middle:], values[:middle]], axis=0)


def qkv_body(make, *refs):
    if make:
        xs, (own, other, cosine, sine, queries, kv, xhat) = refs[:PAIR], refs[PAIR:]
        rows, width = xs[0].shape
        for m in range(PAIR):
            x = xs[m][...].astype(f32)
            inverse = lax.rsqrt(mean_of(x * x) + norm_eps)
            xhat[m * rows : (m + 1) * rows, :] = (x * inverse).astype(bf16)
    else:
        xhat, own, other, cosine, sine, queries, kv = refs
        rows, width = cosine.shape[1], xhat.shape[1]
    cos, sin = cosine[...], sine[...]
    total = dot(xhat[:, : width // 2], own[...]) + dot(xhat[:, width // 2 :], other[...])
    for m in range(PAIR):
        turned = total[m * rows : (m + 1) * rows].T
        for h in range(GROUP + 1):
            u = turned[h * HEAD : (h + 1) * HEAD]
            u = u * cos + half_rotated(u) * sin
            if h < GROUP:
                queries[m, :, h * rows : (h + 1) * rows] = (u * HEAD ** (-0.5)).astype(bf16)
            else:
                both = jnp.concatenate([u, turned[(h + 1) * HEAD :]], axis=0)
                kv[m * rows : (m + 1) * rows, :] = both.T.astype(bf16)


def qkv_call(xs, own, other, cosine, sine):
    make = isinstance(xs, list)
    rows = cosine.shape[1]
    tokens = PAIR * rows
    outs = (shape((PAIR, HEAD, GROUP * rows), bf16), shape((tokens, 2 * HEAD), bf16))
    if make:
        outs = outs + (shape((tokens, xs[0].shape[1]), bf16),)
    operands = (*(xs if make else (xs,)), own, other, cosine, sine)
    return kernel_call(
        functools.partial(qkv_body, make),
        outs,
        [whole()] * len(operands),
        tuple(whole() for _ in outs),
        operands,
        name="qkv",
    )


def out_rows_body(index, *refs):
    pieces, out = refs[:CHIPS], refs[CHIPS]
    cut = pieces[0].shape[0] // PAIR
    for row in range(2):

        @pl.when(index[0] >> 1 == row)
        def _():
            for n in range(PAIR):
                for m in range(CHIPS):
                    spot = (n * CHIPS + m) * cut
                    start = (n ^ row) * cut
                    out[spot : spot + cut, :] = pieces[m ^ (2 * n)][start : start + cut, :]


def out_rows_call(index, pieces):
    rows, width = pieces[0].shape
    return kernel_call(
        out_rows_body,
        shape((CHIPS * rows, width), bf16),
        [pl.BlockSpec((rows, width), lambda i, n: (0, 0))] * CHIPS,
        pl.BlockSpec((CHIPS * rows, width), lambda i, n: (0, 0)),
        tuple(pieces),
        index=index,
        grid=(1,),
        name="out_rows",
    )


LANE_HEADS = 4


def own_block_bias(rows):
    key = lax.broadcasted_iota(jnp.int32, (rows, rows), 0)
    mine = lax.broadcasted_iota(jnp.int32, (rows, rows), 1)
    return jnp.where(key <= mine, 0.0, masked_score)


def set_bias(bias):
    rows = bias.shape[0]
    value = own_block_bias(rows)
    for h in range(LANE_HEADS):
        bias[:, h * rows : (h + 1) * rows] = value


def far_bias(depth, d):
    return jnp.where(d <= depth, 0.0, masked_score) if d else 0.0


def attention_body(shards, index, queries, *refs):
    kvs = refs[:shards]
    turned_out, out, stats, bias, terms, out_turned = refs[shards:]
    rows = bias.shape[0]
    wide = LANE_HEADS * rows

    @pl.when(pl.program_id(0) == 0)
    def _():
        set_bias(bias)

    ks = [kv[:, :HEAD] for kv in kvs]
    v_turned = jnp.concatenate([kv[...] for kv in kvs], axis=0).astype(f32).T[HEAD:].astype(bf16)
    for n in range(GROUP // LANE_HEADS):
        span = slice(n * wide, (n + 1) * wide)
        q = queries[0, :, span]
        scores, top = [], None
        for d in range(shards):
            score = dot(ks[d], q)
            if d == 0:
                score = score + bias[...]
            scores.append(score)
            highest = jnp.max(score, axis=0, keepdims=True) + far_bias(index[2], d)
            top = highest if top is None else jnp.maximum(top, highest)
        total = None
        for d in range(shards):
            term = jnp.exp(scores[d] - (top - far_bias(index[2], d)))
            part = jnp.sum(term, axis=0, keepdims=True)
            total = part if total is None else total + part
            terms[d * rows : (d + 1) * rows, :] = term.astype(bf16)
        out_turned[:, span] = dot(v_turned, terms[...]) / total
        stats[0, :, span] = top + jnp.log(total)
    turned_out[0] = out_turned[...].astype(bf16)
    straight = out_turned[...].T
    for h in range(GROUP):
        out[:, h * HEAD : (h + 1) * HEAD] = straight[h * rows : (h + 1) * rows].astype(bf16)


def attention_call(index, queries, kvs):
    chips, _, wide = queries.shape
    rows = wide // GROUP
    shards = len(kvs)
    keys = shards * rows
    block = pl.BlockSpec((1, HEAD, wide), lambda i, n: (i, 0, 0))
    return kernel_call(
        functools.partial(attention_body, shards),
        (
            shape((chips, HEAD, wide), bf16),
            shape((chips * rows, GROUP * HEAD), bf16),
            shape((chips, 1, wide), f32),
        ),
        [block] + [pl.BlockSpec((rows, 2 * HEAD), lambda i, n: (i, 0))] * shards,
        (
            block,
            pl.BlockSpec((rows, GROUP * HEAD), lambda i, n: (i, 0)),
            pl.BlockSpec((1, 1, wide), lambda i, n: (i, 0, 0)),
        ),
        (queries, *kvs),
        index=index,
        grid=(chips,),
        scratch=(
            VMEM((rows, LANE_HEADS * rows), f32),
            VMEM((keys, LANE_HEADS * rows), bf16),
            VMEM((HEAD, wide), f32),
        ),
        name="attention",
    )


def attention_back_body(shards, index, branch, wo_own, wo_other, cosine, sine, *refs):
    per_group = 3 + shards
    inputs = [refs[n * per_group : (n + 1) * per_group] for n in range(PAIR)]
    grad_q, grad_first, grad_rest = refs[-7:-4]
    bias, probs_low, grads_low, grad_lanes = refs[-4:]
    rows = bias.shape[0]
    wide = LANE_HEADS * rows
    width = branch.shape[1]
    set_bias(bias)
    cos, sin = cosine[...], sine[...]
    for n, (queries, turned_out, stats, *kvs) in enumerate(inputs):
        heads = slice(n * GROUP * HEAD, (n + 1) * GROUP * HEAD)
        grad_out = dot_nt(wo_own[heads, :], branch[:, : width // 2])
        grad_out = grad_out + dot_nt(wo_other[heads, :], branch[:, width // 2 :])
        for h in range(GROUP):
            grad_lanes[:, h * rows : (h + 1) * rows] = grad_out[h * HEAD : (h + 1) * HEAD].astype(bf16)
        ks = [kv[:, :HEAD] for kv in kvs]
        vs = [kv[:, HEAD:] for kv in kvs]
        k_turned = jnp.concatenate([kv[...] for kv in kvs], axis=0).astype(f32).T[:HEAD].astype(bf16)
        k_total, v_total, parts = None, None, []
        for c in range(GROUP // LANE_HEADS):
            span = slice(c * wide, (c + 1) * wide)
            q, mine = queries[0, :, span], grad_lanes[:, span]
            delta = jnp.sum(
                mine.astype(f32) * turned_out[0, :, span].astype(f32), axis=0, keepdims=True
            )
            for d in range(shards):
                score = dot(ks[d], q)
                if d == 0:
                    score = score + bias[...]
                probs = jnp.exp(score - (stats[0, :, span] - far_bias(index[2], d)))
                grad_scores = probs * (dot(vs[d], mine) - delta)
                probs_low[d * rows : (d + 1) * rows, :] = probs.astype(bf16)
                grads_low[d * rows : (d + 1) * rows, :] = grad_scores.astype(bf16)
            u = dot(k_turned, grads_low[...]) * HEAD ** (-0.5)
            parts.append(u * cos - half_rotated(u) * sin)
            k_term = dot_nt(grads_low[...], q)
            v_term = dot_nt(probs_low[...], mine)
            k_total = k_term if k_total is None else k_total + k_term
            v_total = v_term if v_total is None else v_total + v_term
        straight = jnp.concatenate(parts, axis=1).T
        for h in range(GROUP):
            spot = (n * GROUP + h) * HEAD
            grad_q[:, spot : spot + HEAD] = straight[h * rows : (h + 1) * rows].astype(bf16)
        both = jnp.concatenate([k_total, v_total], axis=1)
        spot = slice(n * 2 * HEAD, (n + 1) * 2 * HEAD)
        grad_first[:, spot] = both[:rows, :]
        for d in range(1, shards):
            grad_rest[d - 1, :, spot] = both[d * rows : (d + 1) * rows, :].astype(bf16)


def attention_back_call(index, m, branch, wo_own, wo_other, cosine, sine, groups, before):
    chips, _, wide = groups[0][0].shape
    rows = wide // GROUP
    shards = len(groups[0][3])
    keys = shards * rows
    tokens = chips * rows
    block = pl.BlockSpec((1, HEAD, wide), lambda i, n: (m, 0, 0))
    in_specs = [whole()] * 5
    operands = [branch, wo_own, wo_other, jnp.tile(cosine, (1, LANE_HEADS)), jnp.tile(sine, (1, LANE_HEADS))]
    for queries, turned, stats, kvs in groups:
        in_specs += [block, block, pl.BlockSpec((1, 1, wide), lambda i, n: (m, 0, 0))]
        in_specs += [pl.BlockSpec((rows, 2 * HEAD), lambda i, n: (m, 0))] * shards
        operands += [queries, turned, stats, *kvs]
    aliases = {}
    if before is not None:
        aliases = {1 + len(operands) + n: n for n in range(3)}
        in_specs += [pl.BlockSpec(memory_space=pl.ANY)] * 3
        operands += list(before)
    outs = (
        shape((tokens, PAIR * GROUP * HEAD), bf16),
        shape((tokens, PAIR * 2 * HEAD), f32),
        shape((shards - 1, tokens, PAIR * 2 * HEAD), bf16),
    )
    out_specs = (
        pl.BlockSpec((rows, PAIR * GROUP * HEAD), lambda i, n: (m, 0)),
        pl.BlockSpec((rows, PAIR * 2 * HEAD), lambda i, n: (m, 0)),
        pl.BlockSpec((shards - 1, rows, PAIR * 2 * HEAD), lambda i, n: (0, m, 0)),
    )
    return kernel_call(
        functools.partial(attention_back_body, shards),
        outs,
        in_specs,
        out_specs,
        tuple(operands),
        index=index,
        grid=(1,),
        scratch=(
            VMEM((rows, LANE_HEADS * rows), f32),
            VMEM((keys, LANE_HEADS * rows), bf16),
            VMEM((keys, LANE_HEADS * rows), bf16),
            VMEM((HEAD, wide), bf16),
        ),
        aliases=aliases,
        name="attention_back",
    )


def parts_body(steps, transposed, count, *refs):
    lefts, owns, others = refs[:count], refs[count : 2 * count], refs[2 * count : 3 * count]
    outs = refs[3 * count :]
    rows = outs[0].shape[0]
    step = pl.program_id(0)

    def run(weights):
        total = None
        for left, weight in zip(lefts, weights):
            term = (dot_nt if transposed else dot)(left[...], weight[...])
            total = term if total is None else total + term
        for m, out in enumerate(outs):
            out[...] = total[m * rows : (m + 1) * rows, :].astype(out.dtype)

    @pl.when(step < steps)
    def _():
        run(owns)

    @pl.when(step >= steps)
    def _():
        run(others)


def parts_call(terms, rows, transposed, name):
    tokens = terms[0][0].shape[0]
    half = terms[0][1].shape[0] if transposed else terms[0][1].shape[1]
    tile = 256
    steps = half // tile
    last = steps - 1
    specs = [pl.BlockSpec((tokens, term[0].shape[1]), lambda j: (0, 0)) for term in terms]
    for side in range(2):
        for left, _, _, spot in terms:
            depth = left.shape[1]

            def place(side, spot, j):
                step = jnp.maximum(j - steps, 0) if side else jnp.minimum(j, last)
                return (step, spot) if transposed else (spot, step)

            block = (tile, depth) if transposed else (depth, tile)
            specs.append(pl.BlockSpec(block, functools.partial(place, side, spot)))
    count = tokens // rows
    return kernel_call(
        functools.partial(parts_body, steps, transposed, len(terms)),
        tuple(shape((rows, 2 * half), f32 if m == 0 else bf16) for m in range(count)),
        specs,
        tuple(pl.BlockSpec((rows, tile), lambda j: (0, j)) for _ in range(count)),
        (*(term[0] for term in terms), *(term[1] for term in terms), *(term[2] for term in terms)),
        grid=(2 * steps,),
        name=name,
    )


def gate_body(count, *refs):
    twos = refs[:count]
    gate_own, up_own, gate_other, up_other, act, for_gate, for_up, two_all = refs[count:]
    half = two_all.shape[1] // 2

    @pl.when(pl.program_id(0) == 0)
    def _():
        start = 0
        for two in twos:
            two_all[start : start + two.shape[0], :] = two[...]
            start += two.shape[0]

    own = jnp.concatenate([gate_own[...], up_own[...]], axis=1)
    other = jnp.concatenate([gate_other[...], up_other[...]], axis=1)
    both = dot(two_all[:, :half], own) + dot(two_all[:, half:], other)
    wide = gate_own.shape[1]
    gate, up = both[:, :wide], both[:, wide:]
    sig = 1.0 / (1.0 + jnp.exp(-gate))
    silu = gate * sig
    act[...] = (silu * up).astype(bf16)
    for_gate[...] = (up * sig * (1.0 + gate * (1.0 - sig))).astype(bf16)
    for_up[...] = silu.astype(bf16)


def gate_call(twos, own, other):
    rows, width = twos[0].shape
    tokens = CHIPS * rows
    half = width // 2
    ff = own.shape[1] // 2
    tile = LANES
    steps = ff // tile
    weight = [
        pl.BlockSpec((half, tile), lambda j: (0, j)),
        pl.BlockSpec((half, tile), lambda j: (0, j + steps)),
    ]
    column = pl.BlockSpec((tokens, tile), lambda j: (0, j))
    return kernel_call(
        functools.partial(gate_body, len(twos)),
        tuple(shape((tokens, ff), bf16) for _ in range(3)) + (shape((tokens, width), bf16),),
        [pl.BlockSpec(two.shape, lambda j: (0, 0)) for two in twos] + weight + weight,
        (column, column, column, pl.BlockSpec((tokens, width), lambda j: (0, 0))),
        (*twos, own, own, other, other),
        grid=(steps,),
        name="gate",
    )


def hidden_back_body(g, own, other, for_gate, for_up, grads):
    half = g.shape[1] // 2
    ff = own.shape[0]
    hidden = dot_nt(g[:, :half], own[...]) + dot_nt(g[:, half:], other[...])
    grads[:, :ff] = (hidden * for_gate[...].astype(f32)).astype(bf16)
    grads[:, ff:] = (hidden * for_up[...].astype(f32)).astype(bf16)


def hidden_back_call(g, own, other, for_gate, for_up):
    tokens, width = g.shape
    ff, half = own.shape
    block = tokens // 2
    row = lambda i: (i, 0)
    fixed = lambda i: (0, 0)
    return kernel_call(
        hidden_back_body,
        shape((tokens, 2 * ff), bf16),
        [
            pl.BlockSpec((block, width), row),
            pl.BlockSpec((ff, half), fixed),
            pl.BlockSpec((ff, half), fixed),
            pl.BlockSpec((block, ff), row),
            pl.BlockSpec((block, ff), row),
        ],
        pl.BlockSpec((block, 2 * ff), row),
        (g, own, other, for_gate, for_up),
        grid=(2,),
        name="hidden_back",
    )


def weight_grad_body(per, outputs, adds, left, right, *refs):
    added = [refs[n * outputs : (n + 1) * outputs] for n in range(adds)]
    outs, turned = refs[adds * outputs : -1], refs[-1]
    step = pl.program_id(0)

    @pl.when(step == 0)
    def _():
        turned[...] = left[...].T

    for n in range(outputs):

        @pl.when(step // per == n)
        def _(n=n):
            total = dot(turned[...], right[...])
            for terms in added:
                total = total + terms[n][...].astype(f32)
            outs[n][...] = total.astype(bf16)


def weight_grad(left, left_side, right, place, width, outputs, added, name):
    tokens = left.shape[0]
    rows = left.shape[1] // (1 if left_side is None else 2)
    tile = 256 if width % 256 == 0 else width
    per = width // tile
    first = place * width // tile
    side = left_side or 0

    def spot(n, j):
        return (0, jnp.clip(j - n * per, 0, per - 1))

    tiles = [pl.BlockSpec((rows, tile), functools.partial(spot, n)) for n in range(outputs)]
    return kernel_call(
        functools.partial(weight_grad_body, per, outputs, len(added)),
        tuple(shape((rows, width), bf16) for _ in range(outputs)),
        [
            pl.BlockSpec((tokens, rows), lambda j: (0, side)),
            pl.BlockSpec((tokens, tile), lambda j: (0, first + j)),
        ]
        + tiles * len(added),
        tuple(tiles),
        (left, right, *(term for terms in added for term in terms)),
        grid=(per * outputs,),
        scratch=(VMEM((rows, tokens), bf16),),
        name=name,
    )


def rows_result_body(local, index, *refs):
    pieces, out = refs[:PIECES], refs[PIECES]
    half = local // 2
    shards = out.shape[1] // local
    for m in range(CHIPS):
        for core in range(2):

            @pl.when((pl.program_id(0) == m) & (index[1] == core))
            def _():
                for side in range(2):
                    piece = pieces[2 * m + side]
                    for s in range(shards):
                        spot = s * local + (core ^ side) * half
                        out[:, spot : spot + half] = piece[:, s * half : (s + 1) * half].astype(f32)


def rows_result(index, pieces, local, name):
    cut, half_width = pieces[0].shape
    return kernel_call(
        functools.partial(rows_result_body, local),
        shape((CHIPS * cut, 2 * half_width), f32),
        [pl.BlockSpec((cut, half_width), lambda i, n: (0, 0))] * PIECES,
        pl.BlockSpec((cut, 2 * half_width), lambda i, n: (n[0] ^ i, 0)),
        tuple(pieces),
        index=index,
        grid=(CHIPS,),
        name=name,
    )


def lane_sum(value):
    total = value[:, :LANES]
    for n in range(1, value.shape[1] // LANES):
        total = total + value[:, n * LANES : (n + 1) * LANES]
    return total


def feedforward_result_body(ff_local, cut, index, *refs):
    pieces = refs[:CHIPS]
    gate_weight, up_weight, gain = refs[CHIPS : CHIPS + 3]
    gate_out, up_out, gain_out = refs[-3:]
    shards = gate_weight.shape[1] // ff_local
    width = shards * cut
    for chip in range(CHIPS):

        @pl.when(index[0] == chip)
        def _():
            @pl.loop(0, gate_out.shape[0] // 16)
            def _(n):
                rows = pl.ds(pl.multiple_of(n * 16, 16), 16)
                scale = gain[rows, :1]
                total = jnp.zeros((16, LANES), f32)
                for base, weight, out in ((0, gate_weight, gate_out), (width, up_weight, up_out)):
                    parts = []
                    for s in range(shards):
                        for owner in range(CHIPS):
                            start = base + s * cut
                            parts.append(pieces[owner ^ chip][rows, start : start + cut].astype(f32))
                    wide = jnp.concatenate(parts, axis=1)
                    total = total + lane_sum(wide * weight[rows, :].astype(f32))
                    out[rows, :] = wide * scale
                gain_out[rows, :] = total


def feedforward_result(index, side, pieces, gate_weight, up_weight, gain, ff_local, before):
    local, ff = gate_weight.shape
    half = local // 2
    rows = 64
    steps = half // rows
    row = lambda i, n: ((n[1] ^ side) * steps + i, 0)
    in_specs = [pl.BlockSpec((rows, pieces[0].shape[1]), lambda i, n: (i, 0))] * CHIPS
    in_specs += [pl.BlockSpec((rows, ff), row)] * 2 + [pl.BlockSpec((rows, LANES), row)]
    operands = (*pieces, gate_weight, up_weight, gain)
    aliases = {}
    if before is not None:
        aliases = {1 + len(operands) + n: n for n in range(3)}
        in_specs = in_specs + [pl.BlockSpec(memory_space=pl.ANY)] * 3
        operands = operands + tuple(before)
    return kernel_call(
        functools.partial(feedforward_result_body, ff_local, ff_local // CHIPS),
        (shape((local, ff), f32), shape((local, ff), f32), shape((local, LANES), f32)),
        in_specs,
        (pl.BlockSpec((rows, ff), row), pl.BlockSpec((rows, ff), row), pl.BlockSpec((rows, LANES), row)),
        operands,
        index=index,
        grid=(steps,),
        aliases=aliases,
        name="feedforward_result",
    )


def qkv_result_body(local, group_shards, index, *refs):
    pieces = refs[:PIECES]
    weights, gain = refs[PIECES : PIECES + 3], refs[PIECES + 3]
    outs, gain_out = refs[PIECES + 4 : PIECES + 7], refs[PIECES + 7]
    q_width = GROUP * HEAD
    cut = local // CHIPS
    scale = gain[:, :1]
    for chip in range(CHIPS):
        for side in range(2):

            @pl.when((index[0] == chip) & (pl.program_id(0) == side))
            def _():
                parts, k_parts, v_parts = [], [], []
                for group in range(CHIPS):
                    owner = (group >> 1) + 2 * (group & 1)
                    piece = pieces[2 * (owner ^ chip) + side]
                    for s in range(group_shards):
                        for j in range(CHIPS):
                            start = ((j ^ owner) * group_shards + s) * cut
                            parts.append(piece[:, start : start + cut].astype(f32))
                    k_parts.append(piece[:, q_width : q_width + HEAD].astype(f32))
                    v_parts.append(piece[:, q_width + HEAD : q_width + 2 * HEAD].astype(f32))
                total = jnp.zeros((gain.shape[0], LANES), f32)
                for part, weight, out in zip((parts, k_parts, v_parts), weights, outs):
                    wide = jnp.concatenate(part, axis=1)
                    total = total + lane_sum(wide * weight[...].astype(f32))
                    out[...] = wide * scale
                gain_out[...] = total


def qkv_result(index, pieces, query, key, value, gain):
    local, width = query.shape
    half = local // 2
    group_shards = width // local // CHIPS
    row = lambda i, n: (n[1] ^ i, 0)
    kv_width = key.shape[1]
    return kernel_call(
        functools.partial(qkv_result_body, local, group_shards),
        (
            shape((local, width), f32),
            shape((local, kv_width), f32),
            shape((local, kv_width), f32),
            shape((local, LANES), f32),
        ),
        [pl.BlockSpec(pieces[0].shape, lambda i, n: (0, 0))] * PIECES
        + [
            pl.BlockSpec((half, width), row),
            pl.BlockSpec((half, kv_width), row),
            pl.BlockSpec((half, kv_width), row),
            pl.BlockSpec((half, LANES), row),
        ],
        (
            pl.BlockSpec((half, width), row),
            pl.BlockSpec((half, kv_width), row),
            pl.BlockSpec((half, kv_width), row),
            pl.BlockSpec((half, LANES), row),
        ),
        (*pieces, query, key, value, gain),
        index=index,
        grid=(2,),
        name="qkv_result",
    )


def per_device(
    hidden_in,
    attention_gain,
    query_weight,
    key_weight,
    value_weight,
    output_weight,
    feedforward_gain,
    gate_weight,
    up_weight,
    down_weight,
    out_grad,
):
    rows, width = hidden_in.shape
    shards = lax.axis_size("shard")
    replicas = lax.axis_size("replica")
    place = lax.axis_index("replica")
    depth = lax.axis_index("shard")
    core = place & 1
    chip = (place >> 1) & (CHIPS - 1)
    local = width // shards
    half = local // 2
    ff_local = down_weight.shape[0]
    group_shards = shards // CHIPS
    q_width = GROUP * HEAD
    qkv_width = q_width + 2 * HEAD
    index = jnp.stack([chip, core, depth]).astype(jnp.int32)

    gain_one = jnp.broadcast_to(attention_gain.astype(f32)[:, None], (local, LANES))
    gain_two = jnp.broadcast_to(feedforward_gain.astype(f32)[:, None], (local, LANES))


    at_block, out_block = attention_block(
        index, query_weight, key_weight, value_weight, output_weight, gain_one
    )
    x = own_first(index, (after(hidden_in, at_block),), local)[0]
    xs = [x, swap(x, 2)]
    at_own = lax.all_gather(at_block, "shard", axis=0, tiled=True)
    out_all = lax.all_gather(out_block, "shard", axis=0, tiled=True)
    gu_block = feedforward_block(index, gate_weight, up_weight, after(gain_two, at_block), ff_local)
    gu_own = lax.all_gather(gu_block, "shard", axis=0, tiled=True)
    down_own = lax.all_gather(down_block(index, down_weight, local), "shard", axis=0, tiled=True)
    g = own_first(index, (after(out_grad, x),), local)[0]
    g_blocks = [g, swap(g, 2), swap(g, 4)]
    at_own = after(at_own, gu_block, xs[1], *g_blocks[1:])

    qkv_own = [at_own]
    qkv_own.append(swap(qkv_own[0], 4))
    qkv_other = [swap(qkv_own[0], 1)]
    inverse = rope_base ** (-jnp.arange(0, HEAD, 2, dtype=f32) / HEAD)
    places = (depth * rows + jnp.arange(rows, dtype=jnp.int32)).astype(f32)
    angles = inverse[:, None] * places[None, :]
    angles = jnp.concatenate([angles, angles], axis=0)
    cosine, sine = jnp.cos(angles), jnp.sin(angles)

    def shifted(kv):
        return [kv] + [shift(kv, d) for d in range(1, shards)]

    queries, kv, xhat = qkv_call(xs, qkv_own[0], qkv_other[0], cosine, sine)
    kvs = shifted(kv)
    qkv_own[1] = after(qkv_own[1], *kvs[1:])
    qkv_other.append(swap(qkv_own[1], 1))
    queries_two, kv_two = qkv_call(xhat, qkv_own[1], qkv_other[1], cosine, sine)
    kvs_two = shifted(kv_two)
    groups = [(queries, *attention_call(index, queries, kvs), kvs)]
    groups.append((queries_two, *attention_call(index, queries_two, kvs_two), kvs_two))
    attended = [group[2] for group in groups]
    groups = [(group[0], group[1], group[3], group[4]) for group in groups]

    out_all = after(out_all, qkv_own[1])
    x_place = chip & 1
    low_group = (chip >> 1) == 0
    pair_rows = PAIR * group_shards * half // 2

    def out_for(mask):
        return lax.dynamic_slice_in_dim(out_all, ((chip ^ mask) & 1) * pair_rows, pair_rows, 0)

    out_pieces = [out_for(0)] + [swap(out_for(m), 2 * m) for m in range(1, CHIPS)]
    wo_own = out_rows_call(index, [after(piece, *kvs_two[1:]) for piece in out_pieces])
    wo_other = swap(wo_own, 1)

    mid_terms = [(attended[n], wo_own, wo_other, n) for n in range(PAIR)]
    g_blocks.append(swap(after(g, *out_pieces[1:]), 6))
    mid_out = parts_call(mid_terms, rows, False, "attention_out")
    g_all = jnp.concatenate([after(block, mid_out[0]) for block in g_blocks], axis=0)
    middle, two = middle_call(plane_send(mid_out), after(x, g_all))
    twos = plane_gather_far(two, *plane_gather_near(two))

    gu_own = after(gu_own, *twos[1:])
    gu_other = swap(gu_own, 1)
    act, for_gate, for_up, two_all = gate_call(twos, gu_own, gu_other)

    def over_groups(kept):
        if replicas > PIECES:
            groups = [
                [e * PIECES + i for e in range(replicas // PIECES)] for i in range(PIECES)
            ]
            kept = lax.psum(kept, "replica", axis_index_groups=groups)
        return kept

    def reduced(term):
        kept = lax.psum_scatter(term, "shard", scatter_dimension=0, tiled=True)
        return over_groups(kept)

    def plane_pieces(kept):
        mine = plane_gather(kept)
        return mine, [swap(part, 1) for part in mine]

    def mixed(mine, theirs):
        return [part for pair in zip(mine, theirs) for part in pair]

    down_sent = weight_grad(act, None, g_all, 1, width // 2, 1, (), "down_grad_other")
    down_sent = [swap(down_sent[0], 1)]
    down_sent[0] = after(down_sent[0], down_own)
    down_term = weight_grad(act, None, g_all, 0, width // 2, 1, (down_sent,), "down_grad")[0]
    down_other = swap(down_own, 1)

    grads = hidden_back_call(after(g_all, down_term), down_own, down_other, for_gate, for_up)
    grads_wide = grads.shape[1]
    gu_sent = weight_grad(two_all, 1, grads, 0, grads_wide, 1, (), "gate_grad_other")
    gu_sent = [swap(gu_sent[0], 1)]
    gu_term = weight_grad(two_all, 0, grads, 0, grads_wide, 1, (gu_sent,), "gate_grad")[0]
    gu_kept = reduced(gu_term)
    grads_late = after(grads, gu_term)
    e_terms = parts_call([(grads_late, gu_own, gu_other, 0)], rows, True, "feedforward_back")
    e_parts = plane_send(e_terms)
    act_late = after(act, e_terms[0])
    out_terms = parts_call([(act_late, down_own, down_other, 0)], rows, False, "feedforward_out")

    middle_late = after(middle, out_terms[0])
    grad_middle, branch = grad_middle_call(e_parts, middle_late, g)
    branches = [branch, swap(branch, 2)]

    def back_block(m, block, before):
        return attention_back_call(index, m, block, wo_own, wo_other, cosine, sine, groups, before)

    before = back_block(0, branch, None)
    out_parts = plane_send(after(out_terms, branches[1], before[1]))
    half_wide = width // 2
    branch_all = jnp.concatenate([branch, after(branches[1], before[1])], axis=0)
    both_attended = jnp.concatenate(attended, axis=1)
    wo_sent = weight_grad(both_attended, None, branch_all, 1, half_wide, 1, (), "out_grad_other")
    wo_other_term = wo_sent[0]
    wo_sent = [swap(wo_other_term, 1)]
    before = back_block(1, after(branches[1], before[1], wo_other_term), before)
    output = output_call(index, out_parts, middle, local)
    grad_q, grad_first, grad_rest = before
    grad_rest = after(grad_rest, out_parts[1])
    rest = [shift(grad_rest[d - 1], -d) for d in range(1, shards)]

    wo_term = weight_grad(both_attended, None, branch_all, 0, half_wide, 1, (wo_sent,), "out_grad")[0]
    wo_terms = out_sends(index, after(wo_term, *rest, *out_parts[1:]))
    wo_parts = plane_send(wo_terms)
    wo_block = out_block_call(index, wo_parts)
    down_kept = reduced(after(down_term, *rest))
    gu_near = plane_gather_near(after(gu_kept, *wo_parts[1:]))
    grad_first = after(grad_first, wo_block)
    grad_qkv = grad_qkv_call(grad_q, grad_first, rest, cosine, sine)

    def qkv_grad(n, side, added, name):
        return weight_grad(xhat, side, grad_qkv[n], 0, qkv_width, 1, added, name)

    qkv_sent = [swap(qkv_grad(n, 1, (), "qkv_grad_other")[0], 1) for n in (1, 0)]
    back_terms = [(grad_qkv[n], qkv_own[n], qkv_other[n], 0) for n in range(PAIR)]
    qkv_second = qkv_grad(1, 0, ([qkv_sent[0]],), "qkv_grad")[0]
    qkv_term = qkv_grad(0, 0, ([qkv_sent[1]],), "qkv_grad")[0]
    at_term = jnp.concatenate([qkv_term, qkv_second], axis=1)
    at_kept = reduced(at_term)
    wo_kept = reduced(after(wo_block, at_kept))
    back_terms[0] = (after(grad_qkv[0], qkv_term, qkv_second), *back_terms[0][1:])
    back_parts = parts_call(back_terms, rows, True, "qkv_back")
    e_one = plane_send(back_parts)
    gu_mine = plane_gather_far(gu_kept, *gu_near)
    gu_mine = gu_mine[:3] + [jnp.concatenate(gu_mine[3:], axis=0)]
    gu_theirs = [swap(after(part, output, back_parts[0]), 1) for part in gu_mine]
    gu_out = feedforward_result(index, 0, gu_mine, gate_weight, up_weight, gain_two, ff_local, None)
    gu_out = feedforward_result(index, 1, gu_theirs, gate_weight, up_weight, gain_two, ff_local, gu_out)

    down_mine = plane_gather_far(down_kept, *plane_gather_near(after(down_kept, *gu_near)))
    down_mine = down_mine[:3] + [jnp.concatenate(down_mine[3:], axis=0)]
    down_theirs = [swap(part, 1) for part in down_mine]
    down_out = rows_result(index, mixed(down_mine, down_theirs), local, "down_result")
    grad_input = grad_input_call(index, e_one, x, grad_middle, local)

    wo_out = rows_result(index, mixed(*plane_pieces(wo_kept)), local, "out_result")
    at_kept = after(at_kept, gu_out[0], grad_input)
    second = swap(at_kept[:, qkv_width:], 4)
    first = at_kept[:, :qkv_width].astype(f32) + second.astype(f32)
    at_pieces = mixed(*plane_pieces(first.astype(bf16)))
    q_out, k_out, v_out, gain_one_sums = qkv_result(
        index, at_pieces, query_weight, key_weight, value_weight, gain_one
    )
    return (
        output,
        grad_input,
        jnp.sum(gain_one_sums, axis=1),
        q_out,
        k_out,
        v_out,
        wo_out,
        jnp.sum(gu_out[2], axis=1),
        gu_out[0],
        gu_out[1],
        down_out,
    )


def solution(mesh):
    return jax.shard_map(
        per_device,
        mesh=mesh,
        in_specs=(
            P(("replica", "shard"), None),
            P("shard"),
            P("shard", None),
            P("shard", None),
            P("shard", None),
            P("shard", None),
            P("shard"),
            P("shard", None),
            P("shard", None),
            P("shard", None),
            P(("replica", "shard"), None),
        ),
        out_specs=(
            P(("replica", "shard"), None),
            P(("replica", "shard"), None),
            P("shard"),
            P("shard", None),
            P("shard", None),
            P("shard", None),
            P("shard", None),
            P("shard"),
            P("shard", None),
            P("shard", None),
            P("shard", None),
        ),
        check_vma=False,
    )
```

```python
import functools

import jax
import jax.numpy as jnp
from jax import lax
from jax.experimental import pallas as pl
from jax.experimental.pallas import tpu as pltpu
from jax.sharding import PartitionSpec as P

HEADS = 32
KV_HEADS = 4
HEAD = 64
GROUP = HEADS // KV_HEADS
CHIPS = 4
PIECES = 2 * CHIPS
PAIR = 2
LANES = 128

norm_eps = 1e-05
rope_base = 10000.0
masked_score = -1e30

f32 = jnp.float32
bf16 = jnp.bfloat16
VMEM = pltpu.VMEM
NT = (((1,), (1,)), ((), ()))
TN = (((0,), (0,)), ((), ()))


def dot(left, right):
    return jnp.dot(left, right, preferred_element_type=f32)


def dot_nt(left, right):
    return lax.dot_general(left, right, NT, preferred_element_type=f32)


def dot_tn(left, right):
    return lax.dot_general(left, right, TN, preferred_element_type=f32)


def shape(dims, kind):
    return jax.ShapeDtypeStruct(dims, kind)


def whole():
    return pl.BlockSpec(memory_space=VMEM)


TIMES = {"attention_back": 13.0}


def kernel_call(body, out_shape, in_specs, out_specs, operands, *, index=None, grid=(), scratch=(),
                aliases=None, name=None):
    params = pltpu.CompilerParams(
        vmem_limit_bytes=52 * 2**20, dimension_semantics=("arbitrary",) * len(grid)
    )
    moved = int(TIMES.get(name, 0.0) * 3.69e6)
    cost = pl.CostEstimate(flops=0, bytes_accessed=moved, transcendentals=0)
    common = dict(
        out_shape=out_shape,
        compiler_params=params,
        cost_estimate=cost,
        input_output_aliases=aliases or {},
        name=name,
    )
    if index is None:
        spec = pl.GridSpec(grid=grid, in_specs=in_specs, out_specs=out_specs, scratch_shapes=scratch)
        return pl.pallas_call(body, grid_spec=spec, **common)(*operands)
    spec = pltpu.PrefetchScalarGridSpec(
        num_scalar_prefetch=1, grid=grid, in_specs=in_specs, out_specs=out_specs,
        scratch_shapes=scratch,
    )
    return pl.pallas_call(body, grid_spec=spec, **common)(index, *operands)


def swap(value, mask):
    size = lax.axis_size("replica")
    return lax.ppermute(value, "replica", [(i, i ^ mask) for i in range(size)])


def shift(value, step):
    size = lax.axis_size("shard")
    pairs = [(i, i + step) for i in range(size) if 0 <= i + step < size]
    return lax.ppermute(value, "shard", pairs)


def plane_gather(value):
    return [value] + [swap(value, 2 * m) for m in range(1, CHIPS)]


def plane_gather_near(value):
    return swap(value, 2), swap(value, 4)


def plane_gather_far(value, across, along):
    middle = value.shape[0] // 2
    return [value, across, along, swap(across[:middle], 4), swap(along[middle:], 2)]


def plane_send(parts):
    return [parts[0]] + [swap(parts[m], 2 * m) for m in range(1, len(parts))]


def group_of(chip):
    return 2 * (chip & 1) + (chip >> 1)


def after(value, *others):
    return lax.optimization_barrier((value, *others))[0]


def attention_block_body(local, group_shards, index, q, k, v, o, gain, out, wo_out):
    scale = gain[:, :1]
    q_width = GROUP * HEAD
    cut = local // CHIPS
    for chip in range(CHIPS):

        group = group_of(chip)

        @pl.when(index[0] == chip)
        def _(group=group):
            parts = []
            for m in range(CHIPS):
                for s in range(group_shards):
                    start = group * q_width + s * local + (m ^ chip) * cut
                    parts.append(q[:, start : start + cut])
            parts.append(k[:, group * HEAD : (group + 1) * HEAD])
            parts.append(v[:, group * HEAD : (group + 1) * HEAD])
            wide = jnp.concatenate([part.astype(f32) for part in parts], axis=1)
            out[...] = (wide * scale).astype(bf16)

    half = local // 2
    shards = o.shape[1] // local
    for core in range(2):

        @pl.when(index[1] == core)
        def _():
            for s in range(shards):
                piece = o[:, s * local + core * half : s * local + (core + 1) * half]
                wo_out[:, s * half : (s + 1) * half] = piece


def attention_block(index, query, key, value, output, gain):
    local, width = query.shape
    half = local // 2
    shards = width // local
    return kernel_call(
        functools.partial(attention_block_body, local, shards // CHIPS),
        (
            shape((half, GROUP * HEAD + 2 * HEAD), bf16),
            shape((local // CHIPS, width // 2), bf16),
        ),
        [
            pl.BlockSpec((half, width), lambda i, n: (n[1], 0)),
            pl.BlockSpec((half, key.shape[1]), lambda i, n: (n[1], 0)),
            pl.BlockSpec((half, key.shape[1]), lambda i, n: (n[1], 0)),
            pl.BlockSpec((local // CHIPS, width), lambda i, n: (n[0], 0)),
            pl.BlockSpec((half, LANES), lambda i, n: (n[1], 0)),
        ],
        (
            pl.BlockSpec((half, GROUP * HEAD + 2 * HEAD), lambda i, n: (0, 0)),
            pl.BlockSpec((local // CHIPS, width // 2), lambda i, n: (0, 0)),
        ),
        (query, key, value, output, gain),
        index=index,
        grid=(1,),
        name="attention_block",
    )


def feedforward_block_body(ff_local, cut, index, gate, up, gain, out):
    scale = gain[:, :1]
    shards = gate.shape[1] // ff_local
    width = shards * cut
    for chip in range(CHIPS):

        @pl.when(index[0] == chip)
        def _():
            for n, source in enumerate((gate, up)):
                parts = [
                    source[:, s * ff_local + chip * cut : s * ff_local + (chip + 1) * cut].astype(f32)
                    for s in range(shards)
                ]
                wide = jnp.concatenate(parts, axis=1)
                out[:, n * width : (n + 1) * width] = (wide * scale).astype(bf16)


def feedforward_block(index, gate, up, gain, ff_local):
    local, ff = gate.shape
    half = local // 2
    rows = 64
    steps = half // rows
    cut = ff_local // CHIPS
    width = 2 * (ff // CHIPS)
    return kernel_call(
        functools.partial(feedforward_block_body, ff_local, cut),
        shape((half, width), bf16),
        [
            pl.BlockSpec((rows, ff), lambda i, n: (n[1] * steps + i, 0)),
            pl.BlockSpec((rows, ff), lambda i, n: (n[1] * steps + i, 0)),
            pl.BlockSpec((rows, LANES), lambda i, n: (n[1] * steps + i, 0)),
        ],
        pl.BlockSpec((rows, width), lambda i, n: (i, 0)),
        (gate, up, gain),
        index=index,
        grid=(steps,),
        name="feedforward_block",
    )


def own_first_body(local, index, *refs):
    count = len(refs) // 2
    half = local // 2
    for core in range(2):

        @pl.when(index[1] == core)
        def _():
            for source, out in zip(refs[:count], refs[count:]):
                shards = source.shape[1] // local
                sides = out.shape[1] // (shards * half)
                for side in range(sides):
                    for s in range(shards):
                        start = s * local + (core ^ side) * half
                        spot = (side * shards + s) * half
                        out[:, spot : spot + half] = source[:, start : start + half]


def own_first(index, sources, local, halves=2):
    return kernel_call(
        functools.partial(own_first_body, local),
        tuple(shape((v.shape[0], v.shape[1] * halves // 2), bf16) for v in sources),
        [pl.BlockSpec(v.shape, lambda i, n: (0, 0)) for v in sources],
        tuple(
            pl.BlockSpec((v.shape[0], v.shape[1] * halves // 2), lambda i, n: (0, 0)) for v in sources
        ),
        tuple(sources),
        index=index,
        grid=(1,),
        name="own_first",
    )


def down_block_body(local, index, source, out):
    own_first_body(local, index, source, out)


def down_block(index, down, local):
    ff_local, width = down.shape
    cut = ff_local // CHIPS
    return kernel_call(
        functools.partial(down_block_body, local),
        shape((cut, width // 2), bf16),
        [pl.BlockSpec((cut, width), lambda i, n: (n[0], 0))],
        pl.BlockSpec((cut, width // 2), lambda i, n: (0, 0)),
        (down,),
        index=index,
        grid=(1,),
        name="down_block",
    )


def part_sum(parts):
    total = parts[0][...]
    for part in parts[1:]:
        total = total + part[...].astype(f32)
    return total


def mean_of(values):
    return jnp.mean(values, axis=1, keepdims=True)


def middle_body(*refs):
    parts, (x, middle, two) = refs[:PAIR], refs[PAIR:]
    total = x[...].astype(f32) + part_sum(parts)
    middle[...] = total
    two[...] = (total * lax.rsqrt(mean_of(total * total) + norm_eps)).astype(bf16)


def middle_call(parts, x):
    return kernel_call(
        middle_body,
        (shape(x.shape, f32), shape(x.shape, bf16)),
        [whole()] * (PAIR + 1),
        (whole(), whole()),
        (*parts, x),
        name="middle",
    )


def norm_back(e, values):
    inverse = lax.rsqrt(mean_of(values * values) + norm_eps)
    return inverse * e - values * (inverse * inverse * inverse) * mean_of(e * values)


def grad_middle_body(*refs):
    parts, (middle, g, grad, low) = refs[:CHIPS], refs[CHIPS:]
    total = g[...].astype(f32) + norm_back(part_sum(parts), middle[...])
    grad[...] = total
    low[...] = total.astype(bf16)


def grad_middle_call(parts, middle, g):
    return kernel_call(
        grad_middle_body,
        (shape(g.shape, f32), shape(g.shape, bf16)),
        [whole()] * (CHIPS + 2),
        (whole(), whole()),
        (*parts, middle, g),
        name="grad_middle",
    )


def store_in_order(local, index, value, out):
    half = local // 2
    shards = out.shape[1] // local
    for core in range(2):

        @pl.when(index[1] == core)
        def _():
            for side in range(2):
                for s in range(shards):
                    spot = s * local + (core ^ side) * half
                    start = (side * shards + s) * half
                    out[:, spot : spot + half] = value[:, start : start + half].astype(bf16)


def output_body(local, index, *refs):
    parts, (middle, out) = refs[:CHIPS], refs[CHIPS:]
    store_in_order(local, index, middle[...] + part_sum(parts), out)


def output_call(index, parts, middle, local):
    spec = pl.BlockSpec(middle.shape, lambda i, n: (0, 0))
    return kernel_call(
        functools.partial(output_body, local),
        shape(middle.shape, bf16),
        [spec] * (CHIPS + 1),
        spec,
        (*parts, middle),
        index=index,
        grid=(1,),
        name="output",
    )


def grad_input_body(local, index, *refs):
    parts, (x, grad, out) = refs[:PAIR], refs[PAIR:]
    total = grad[...] + norm_back(part_sum(parts), x[...].astype(f32))
    store_in_order(local, index, total, out)


def grad_input_call(index, parts, x, grad, local):
    spec = pl.BlockSpec(x.shape, lambda i, n: (0, 0))
    return kernel_call(
        functools.partial(grad_input_body, local),
        shape(x.shape, bf16),
        [spec] * (PAIR + 2),
        spec,
        (*parts, x, grad),
        index=index,
        grid=(1,),
        name="grad_input",
    )


def grad_qkv_body(shards, grad_q, first, *refs):
    rest, (cosine, sine), outs = refs[: shards - 1], refs[shards - 1 : shards + 1], refs[shards + 1 :]
    total = first[...]
    for term in rest:
        total = total + term[...].astype(f32)
    rows = cosine.shape[1]
    width = GROUP * HEAD
    cos, sin = cosine[...], sine[...]
    for n, out in enumerate(outs):
        out[:, :width] = grad_q[:, n * width : (n + 1) * width]
        for m in range(PAIR):
            span = slice(m * rows, (m + 1) * rows)
            turned = total[span, n * 2 * HEAD : (n + 1) * 2 * HEAD].T
            k = turned[:HEAD]
            k = k * cos - half_rotated(k) * sin
            both = jnp.concatenate([k, turned[HEAD:]], axis=0)
            out[span, width:] = both.T.astype(bf16)


def grad_qkv_call(grad_q, first, rest, cosine, sine):
    tokens = grad_q.shape[0]
    return kernel_call(
        functools.partial(grad_qkv_body, len(rest) + 1),
        (shape((tokens, GROUP * HEAD + 2 * HEAD), bf16),) * PAIR,
        [whole()] * (len(rest) + 4),
        (whole(),) * PAIR,
        (grad_q, first, *rest, cosine, sine),
        name="grad_qkv",
    )


def out_sends_body(index, term, *outs):
    cut = outs[0].shape[0] // PAIR
    for row in range(2):

        @pl.when(index[0] >> 1 == row)
        def _():
            for n in range(PAIR):
                for m in range(CHIPS):
                    spot = (n * CHIPS + m) * cut
                    start = (n ^ row) * cut
                    outs[m ^ (2 * n)][start : start + cut, :] = term[spot : spot + cut, :]


def out_sends(index, term):
    rows, width = term.shape
    rows //= CHIPS
    return kernel_call(
        out_sends_body,
        (shape((rows, width), bf16),) * CHIPS,
        [pl.BlockSpec(term.shape, lambda i, n: (0, 0))],
        (pl.BlockSpec((rows, width), lambda i, n: (0, 0)),) * CHIPS,
        (term,),
        index=index,
        grid=(1,),
        name="out_sends",
    )


def out_block_body(index, *refs):
    parts, out = refs[:CHIPS], refs[CHIPS]
    sums = [parts[m][...].astype(f32) + parts[m + 2][...].astype(f32) for m in range(2)]
    for side in range(2):

        @pl.when(index[0] & 1 == side)
        def _():
            for m in range(2):
                rows = sums[m].shape[0]
                spot = (m ^ side) * rows
                out[spot : spot + rows, :] = sums[m].astype(bf16)


def out_block_call(index, parts):
    rows, width = parts[0].shape
    return kernel_call(
        out_block_body,
        shape((PAIR * rows, width), bf16),
        [pl.BlockSpec((rows, width), lambda i, n: (0, 0))] * CHIPS,
        pl.BlockSpec((PAIR * rows, width), lambda i, n: (0, 0)),
        tuple(parts),
        index=index,
        grid=(1,),
        name="out_block",
    )


def half_rotated(values):
    middle = values.shape[0] // 2
    return jnp.concatenate([-values[middle:], values[:middle]], axis=0)


def qkv_body(make, *refs):
    if make:
        xs, (own, other, cosine, sine, queries, kv, xhat) = refs[:PAIR], refs[PAIR:]
        rows, width = xs[0].shape
        for m in range(PAIR):
            x = xs[m][...].astype(f32)
            inverse = lax.rsqrt(mean_of(x * x) + norm_eps)
            xhat[m * rows : (m + 1) * rows, :] = (x * inverse).astype(bf16)
    else:
        xhat, own, other, cosine, sine, queries, kv = refs
        rows, width = cosine.shape[1], xhat.shape[1]
    cos, sin = cosine[...], sine[...]
    total = dot(xhat[:, : width // 2], own[...]) + dot(xhat[:, width // 2 :], other[...])
    for m in range(PAIR):
        turned = total[m * rows : (m + 1) * rows].T
        for h in range(GROUP + 1):
            u = turned[h * HEAD : (h + 1) * HEAD]
            u = u * cos + half_rotated(u) * sin
            if h < GROUP:
                queries[m, :, h * rows : (h + 1) * rows] = (u * HEAD ** (-0.5)).astype(bf16)
            else:
                both = jnp.concatenate([u, turned[(h + 1) * HEAD :]], axis=0)
                kv[m * rows : (m + 1) * rows, :] = both.T.astype(bf16)


def qkv_call(xs, own, other, cosine, sine):
    make = isinstance(xs, list)
    rows = cosine.shape[1]
    tokens = PAIR * rows
    outs = (shape((PAIR, HEAD, GROUP * rows), bf16), shape((tokens, 2 * HEAD), bf16))
    if make:
        outs = outs + (shape((tokens, xs[0].shape[1]), bf16),)
    operands = (*(xs if make else (xs,)), own, other, cosine, sine)
    return kernel_call(
        functools.partial(qkv_body, make),
        outs,
        [whole()] * len(operands),
        tuple(whole() for _ in outs),
        operands,
        name="qkv",
    )


def out_rows_body(index, *refs):
    pieces, out = refs[:CHIPS], refs[CHIPS]
    cut = pieces[0].shape[0] // PAIR
    for row in range(2):

        @pl.when(index[0] >> 1 == row)
        def _():
            for n in range(PAIR):
                for m in range(CHIPS):
                    spot = (n * CHIPS + m) * cut
                    start = (n ^ row) * cut
                    out[spot : spot + cut, :] = pieces[m ^ (2 * n)][start : start + cut, :]


def out_rows_call(index, pieces):
    rows, width = pieces[0].shape
    return kernel_call(
        out_rows_body,
        shape((CHIPS * rows, width), bf16),
        [pl.BlockSpec((rows, width), lambda i, n: (0, 0))] * CHIPS,
        pl.BlockSpec((CHIPS * rows, width), lambda i, n: (0, 0)),
        tuple(pieces),
        index=index,
        grid=(1,),
        name="out_rows",
    )


LANE_HEADS = 4


def own_block_bias(rows):
    key = lax.broadcasted_iota(jnp.int32, (rows, rows), 0)
    mine = lax.broadcasted_iota(jnp.int32, (rows, rows), 1)
    return jnp.where(key <= mine, 0.0, masked_score)


def set_bias(bias):
    rows = bias.shape[0]
    value = own_block_bias(rows)
    for h in range(LANE_HEADS):
        bias[:, h * rows : (h + 1) * rows] = value


def far_bias(depth, d):
    return jnp.where(d <= depth, 0.0, masked_score) if d else 0.0


def attention_body(shards, index, queries, *refs):
    kvs = refs[:shards]
    turned_out, out, stats, bias, terms, out_turned = refs[shards:]
    rows = bias.shape[0]
    wide = LANE_HEADS * rows

    @pl.when(pl.program_id(0) == 0)
    def _():
        set_bias(bias)

    ks = [kv[:, :HEAD] for kv in kvs]
    v_turned = jnp.concatenate([kv[...] for kv in kvs], axis=0).astype(f32).T[HEAD:].astype(bf16)
    for n in range(GROUP // LANE_HEADS):
        span = slice(n * wide, (n + 1) * wide)
        q = queries[0, :, span]
        scores, top = [], None
        for d in range(shards):
            score = dot(ks[d], q)
            if d == 0:
                score = score + bias[...]
            scores.append(score)
            highest = jnp.max(score, axis=0, keepdims=True) + far_bias(index[2], d)
            top = highest if top is None else jnp.maximum(top, highest)
        total = None
        for d in range(shards):
            term = jnp.exp(scores[d] - (top - far_bias(index[2], d)))
            part = jnp.sum(term, axis=0, keepdims=True)
            total = part if total is None else total + part
            terms[d * rows : (d + 1) * rows, :] = term.astype(bf16)
        out_turned[:, span] = dot(v_turned, terms[...]) / total
        stats[0, :, span] = top + jnp.log(total)
    turned_out[0] = out_turned[...].astype(bf16)
    straight = out_turned[...].T
    for h in range(GROUP):
        out[:, h * HEAD : (h + 1) * HEAD] = straight[h * rows : (h + 1) * rows].astype(bf16)


def attention_call(index, queries, kvs):
    chips, _, wide = queries.shape
    rows = wide // GROUP
    shards = len(kvs)
    keys = shards * rows
    block = pl.BlockSpec((1, HEAD, wide), lambda i, n: (i, 0, 0))
    return kernel_call(
        functools.partial(attention_body, shards),
        (
            shape((chips, HEAD, wide), bf16),
            shape((chips * rows, GROUP * HEAD), bf16),
            shape((chips, 1, wide), f32),
        ),
        [block] + [pl.BlockSpec((rows, 2 * HEAD), lambda i, n: (i, 0))] * shards,
        (
            block,
            pl.BlockSpec((rows, GROUP * HEAD), lambda i, n: (i, 0)),
            pl.BlockSpec((1, 1, wide), lambda i, n: (i, 0, 0)),
        ),
        (queries, *kvs),
        index=index,
        grid=(chips,),
        scratch=(
            VMEM((rows, LANE_HEADS * rows), f32),
            VMEM((keys, LANE_HEADS * rows), bf16),
            VMEM((HEAD, wide), f32),
        ),
        name="attention",
    )


def attention_back_body(shards, index, branch, wo_own, wo_other, cosine, sine, *refs):
    per_group = 3 + shards
    inputs = [refs[n * per_group : (n + 1) * per_group] for n in range(PAIR)]
    grad_q, grad_first, grad_rest = refs[-7:-4]
    bias, probs_low, grads_low, grad_lanes = refs[-4:]
    rows = bias.shape[0]
    wide = LANE_HEADS * rows
    width = branch.shape[1]
    set_bias(bias)
    cos, sin = cosine[...], sine[...]
    for n, (queries, turned_out, stats, *kvs) in enumerate(inputs):
        heads = slice(n * GROUP * HEAD, (n + 1) * GROUP * HEAD)
        grad_out = dot_nt(wo_own[heads, :], branch[:, : width // 2])
        grad_out = grad_out + dot_nt(wo_other[heads, :], branch[:, width // 2 :])
        for h in range(GROUP):
            grad_lanes[:, h * rows : (h + 1) * rows] = grad_out[h * HEAD : (h + 1) * HEAD].astype(bf16)
        ks = [kv[:, :HEAD] for kv in kvs]
        vs = [kv[:, HEAD:] for kv in kvs]
        k_turned = jnp.concatenate([kv[...] for kv in kvs], axis=0).astype(f32).T[:HEAD].astype(bf16)
        k_total, v_total, parts = None, None, []
        for c in range(GROUP // LANE_HEADS):
            span = slice(c * wide, (c + 1) * wide)
            q, mine = queries[0, :, span], grad_lanes[:, span]
            delta = jnp.sum(
                mine.astype(f32) * turned_out[0, :, span].astype(f32), axis=0, keepdims=True
            )
            for d in range(shards):
                score = dot(ks[d], q)
                if d == 0:
                    score = score + bias[...]
                probs = jnp.exp(score - (stats[0, :, span] - far_bias(index[2], d)))
                grad_scores = probs * (dot(vs[d], mine) - delta)
                probs_low[d * rows : (d + 1) * rows, :] = probs.astype(bf16)
                grads_low[d * rows : (d + 1) * rows, :] = grad_scores.astype(bf16)
            u = dot(k_turned, grads_low[...]) * HEAD ** (-0.5)
            parts.append(u * cos - half_rotated(u) * sin)
            k_term = dot_nt(grads_low[...], q)
            v_term = dot_nt(probs_low[...], mine)
            k_total = k_term if k_total is None else k_total + k_term
            v_total = v_term if v_total is None else v_total + v_term
        straight = jnp.concatenate(parts, axis=1).T
        for h in range(GROUP):
            spot = (n * GROUP + h) * HEAD
            grad_q[:, spot : spot + HEAD] = straight[h * rows : (h + 1) * rows].astype(bf16)
        both = jnp.concatenate([k_total, v_total], axis=1)
        spot = slice(n * 2 * HEAD, (n + 1) * 2 * HEAD)
        grad_first[:, spot] = both[:rows, :]
        for d in range(1, shards):
            grad_rest[d - 1, :, spot] = both[d * rows : (d + 1) * rows, :].astype(bf16)


def attention_back_call(index, m, branch, wo_own, wo_other, cosine, sine, groups, before):
    chips, _, wide = groups[0][0].shape
    rows = wide // GROUP
    shards = len(groups[0][3])
    keys = shards * rows
    tokens = chips * rows
    block = pl.BlockSpec((1, HEAD, wide), lambda i, n: (m, 0, 0))
    in_specs = [whole()] * 5
    operands = [branch, wo_own, wo_other, jnp.tile(cosine, (1, LANE_HEADS)), jnp.tile(sine, (1, LANE_HEADS))]
    for queries, turned, stats, kvs in groups:
        in_specs += [block, block, pl.BlockSpec((1, 1, wide), lambda i, n: (m, 0, 0))]
        in_specs += [pl.BlockSpec((rows, 2 * HEAD), lambda i, n: (m, 0))] * shards
        operands += [queries, turned, stats, *kvs]
    aliases = {}
    if before is not None:
        aliases = {1 + len(operands) + n: n for n in range(3)}
        in_specs += [pl.BlockSpec(memory_space=pl.ANY)] * 3
        operands += list(before)
    outs = (
        shape((tokens, PAIR * GROUP * HEAD), bf16),
        shape((tokens, PAIR * 2 * HEAD), f32),
        shape((shards - 1, tokens, PAIR * 2 * HEAD), bf16),
    )
    out_specs = (
        pl.BlockSpec((rows, PAIR * GROUP * HEAD), lambda i, n: (m, 0)),
        pl.BlockSpec((rows, PAIR * 2 * HEAD), lambda i, n: (m, 0)),
        pl.BlockSpec((shards - 1, rows, PAIR * 2 * HEAD), lambda i, n: (0, m, 0)),
    )
    return kernel_call(
        functools.partial(attention_back_body, shards),
        outs,
        in_specs,
        out_specs,
        tuple(operands),
        index=index,
        grid=(1,),
        scratch=(
            VMEM((rows, LANE_HEADS * rows), f32),
            VMEM((keys, LANE_HEADS * rows), bf16),
            VMEM((keys, LANE_HEADS * rows), bf16),
            VMEM((HEAD, wide), bf16),
        ),
        aliases=aliases,
        name="attention_back",
    )


def parts_body(steps, transposed, count, *refs):
    lefts, owns, others = refs[:count], refs[count : 2 * count], refs[2 * count : 3 * count]
    outs = refs[3 * count :]
    rows = outs[0].shape[0]
    step = pl.program_id(0)

    def run(weights):
        total = None
        for left, weight in zip(lefts, weights):
            term = (dot_nt if transposed else dot)(left[...], weight[...])
            total = term if total is None else total + term
        for m, out in enumerate(outs):
            out[...] = total[m * rows : (m + 1) * rows, :].astype(out.dtype)

    @pl.when(step < steps)
    def _():
        run(owns)

    @pl.when(step >= steps)
    def _():
        run(others)


def parts_call(terms, rows, transposed, name):
    tokens = terms[0][0].shape[0]
    half = terms[0][1].shape[0] if transposed else terms[0][1].shape[1]
    tile = 256
    steps = half // tile
    last = steps - 1
    specs = [pl.BlockSpec((tokens, term[0].shape[1]), lambda j: (0, 0)) for term in terms]
    for side in range(2):
        for left, _, _, spot in terms:
            depth = left.shape[1]

            def place(side, spot, j):
                step = jnp.maximum(j - steps, 0) if side else jnp.minimum(j, last)
                return (step, spot) if transposed else (spot, step)

            block = (tile, depth) if transposed else (depth, tile)
            specs.append(pl.BlockSpec(block, functools.partial(place, side, spot)))
    count = tokens // rows
    return kernel_call(
        functools.partial(parts_body, steps, transposed, len(terms)),
        tuple(shape((rows, 2 * half), f32 if m == 0 else bf16) for m in range(count)),
        specs,
        tuple(pl.BlockSpec((rows, tile), lambda j: (0, j)) for _ in range(count)),
        (*(term[0] for term in terms), *(term[1] for term in terms), *(term[2] for term in terms)),
        grid=(2 * steps,),
        name=name,
    )


def gate_body(count, *refs):
    twos = refs[:count]
    gate_own, up_own, gate_other, up_other, act, for_gate, for_up, two_all = refs[count:]
    half = two_all.shape[1] // 2

    @pl.when(pl.program_id(0) == 0)
    def _():
        start = 0
        for two in twos:
            two_all[start : start + two.shape[0], :] = two[...]
            start += two.shape[0]

    own = jnp.concatenate([gate_own[...], up_own[...]], axis=1)
    other = jnp.concatenate([gate_other[...], up_other[...]], axis=1)
    both = dot(two_all[:, :half], own) + dot(two_all[:, half:], other)
    wide = gate_own.shape[1]
    gate, up = both[:, :wide], both[:, wide:]
    sig = 1.0 / (1.0 + jnp.exp(-gate))
    silu = gate * sig
    act[...] = (silu * up).astype(bf16)
    for_gate[...] = (up * sig * (1.0 + gate * (1.0 - sig))).astype(bf16)
    for_up[...] = silu.astype(bf16)


def gate_call(twos, own, other):
    rows, width = twos[0].shape
    tokens = CHIPS * rows
    half = width // 2
    ff = own.shape[1] // 2
    tile = LANES
    steps = ff // tile
    weight = [
        pl.BlockSpec((half, tile), lambda j: (0, j)),
        pl.BlockSpec((half, tile), lambda j: (0, j + steps)),
    ]
    column = pl.BlockSpec((tokens, tile), lambda j: (0, j))
    return kernel_call(
        functools.partial(gate_body, len(twos)),
        tuple(shape((tokens, ff), bf16) for _ in range(3)) + (shape((tokens, width), bf16),),
        [pl.BlockSpec(two.shape, lambda j: (0, 0)) for two in twos] + weight + weight,
        (column, column, column, pl.BlockSpec((tokens, width), lambda j: (0, 0))),
        (*twos, own, own, other, other),
        grid=(steps,),
        name="gate",
    )


def hidden_back_body(g, own, other, for_gate, for_up, grads):
    half = g.shape[1] // 2
    ff = own.shape[0]
    hidden = dot_nt(g[:, :half], own[...]) + dot_nt(g[:, half:], other[...])
    grads[:, :ff] = (hidden * for_gate[...].astype(f32)).astype(bf16)
    grads[:, ff:] = (hidden * for_up[...].astype(f32)).astype(bf16)


def hidden_back_call(g, own, other, for_gate, for_up):
    tokens, width = g.shape
    ff, half = own.shape
    block = tokens // 2
    row = lambda i: (i, 0)
    fixed = lambda i: (0, 0)
    return kernel_call(
        hidden_back_body,
        shape((tokens, 2 * ff), bf16),
        [
            pl.BlockSpec((block, width), row),
            pl.BlockSpec((ff, half), fixed),
            pl.BlockSpec((ff, half), fixed),
            pl.BlockSpec((block, ff), row),
            pl.BlockSpec((block, ff), row),
        ],
        pl.BlockSpec((block, 2 * ff), row),
        (g, own, other, for_gate, for_up),
        grid=(2,),
        name="hidden_back",
    )


def weight_grad_body(per, outputs, adds, left, right, *refs):
    added = [refs[n * outputs : (n + 1) * outputs] for n in range(adds)]
    outs, turned = refs[adds * outputs : -1], refs[-1]
    step = pl.program_id(0)

    @pl.when(step == 0)
    def _():
        turned[...] = left[...].T

    for n in range(outputs):

        @pl.when(step // per == n)
        def _(n=n):
            total = dot(turned[...], right[...])
            for terms in added:
                total = total + terms[n][...].astype(f32)
            outs[n][...] = total.astype(bf16)


def weight_grad(left, left_side, right, place, width, outputs, added, name):
    tokens = left.shape[0]
    rows = left.shape[1] // (1 if left_side is None else 2)
    tile = 256 if width % 256 == 0 else width
    per = width // tile
    first = place * width // tile
    side = left_side or 0

    def spot(n, j):
        return (0, jnp.clip(j - n * per, 0, per - 1))

    tiles = [pl.BlockSpec((rows, tile), functools.partial(spot, n)) for n in range(outputs)]
    return kernel_call(
        functools.partial(weight_grad_body, per, outputs, len(added)),
        tuple(shape((rows, width), bf16) for _ in range(outputs)),
        [
            pl.BlockSpec((tokens, rows), lambda j: (0, side)),
            pl.BlockSpec((tokens, tile), lambda j: (0, first + j)),
        ]
        + tiles * len(added),
        tuple(tiles),
        (left, right, *(term for terms in added for term in terms)),
        grid=(per * outputs,),
        scratch=(VMEM((rows, tokens), bf16),),
        name=name,
    )


def rows_result_body(local, index, *refs):
    pieces, out = refs[:PIECES], refs[PIECES]
    half = local // 2
    shards = out.shape[1] // local
    for m in range(CHIPS):
        for core in range(2):

            @pl.when((pl.program_id(0) == m) & (index[1] == core))
            def _():
                for side in range(2):
                    piece = pieces[2 * m + side]
                    for s in range(shards):
                        spot = s * local + (core ^ side) * half
                        out[:, spot : spot + half] = piece[:, s * half : (s + 1) * half].astype(f32)


def rows_result(index, pieces, local, name):
    cut, half_width = pieces[0].shape
    return kernel_call(
        functools.partial(rows_result_body, local),
        shape((CHIPS * cut, 2 * half_width), f32),
        [pl.BlockSpec((cut, half_width), lambda i, n: (0, 0))] * PIECES,
        pl.BlockSpec((cut, 2 * half_width), lambda i, n: (n[0] ^ i, 0)),
        tuple(pieces),
        index=index,
        grid=(CHIPS,),
        name=name,
    )


def lane_sum(value):
    total = value[:, :LANES]
    for n in range(1, value.shape[1] // LANES):
        total = total + value[:, n * LANES : (n + 1) * LANES]
    return total


def feedforward_result_body(ff_local, cut, index, *refs):
    pieces = refs[:CHIPS]
    gate_weight, up_weight, gain = refs[CHIPS : CHIPS + 3]
    gate_out, up_out, gain_out = refs[-3:]
    shards = gate_weight.shape[1] // ff_local
    width = shards * cut
    for chip in range(CHIPS):

        @pl.when(index[0] == chip)
        def _():
            @pl.loop(0, gate_out.shape[0] // 16)
            def _(n):
                rows = pl.ds(pl.multiple_of(n * 16, 16), 16)
                scale = gain[rows, :1]
                total = jnp.zeros((16, LANES), f32)
                for base, weight, out in ((0, gate_weight, gate_out), (width, up_weight, up_out)):
                    parts = []
                    for s in range(shards):
                        for owner in range(CHIPS):
                            start = base + s * cut
                            parts.append(pieces[owner ^ chip][rows, start : start + cut].astype(f32))
                    wide = jnp.concatenate(parts, axis=1)
                    total = total + lane_sum(wide * weight[rows, :].astype(f32))
                    out[rows, :] = wide * scale
                gain_out[rows, :] = total


def feedforward_result(index, side, pieces, gate_weight, up_weight, gain, ff_local, before):
    local, ff = gate_weight.shape
    half = local // 2
    rows = 64
    steps = half // rows
    row = lambda i, n: ((n[1] ^ side) * steps + i, 0)
    in_specs = [pl.BlockSpec((rows, pieces[0].shape[1]), lambda i, n: (i, 0))] * CHIPS
    in_specs += [pl.BlockSpec((rows, ff), row)] * 2 + [pl.BlockSpec((rows, LANES), row)]
    operands = (*pieces, gate_weight, up_weight, gain)
    aliases = {}
    if before is not None:
        aliases = {1 + len(operands) + n: n for n in range(3)}
        in_specs = in_specs + [pl.BlockSpec(memory_space=pl.ANY)] * 3
        operands = operands + tuple(before)
    return kernel_call(
        functools.partial(feedforward_result_body, ff_local, ff_local // CHIPS),
        (shape((local, ff), f32), shape((local, ff), f32), shape((local, LANES), f32)),
        in_specs,
        (pl.BlockSpec((rows, ff), row), pl.BlockSpec((rows, ff), row), pl.BlockSpec((rows, LANES), row)),
        operands,
        index=index,
        grid=(steps,),
        aliases=aliases,
        name="feedforward_result",
    )


def qkv_result_body(local, group_shards, index, *refs):
    pieces = refs[:PIECES]
    weights, gain = refs[PIECES : PIECES + 3], refs[PIECES + 3]
    outs, gain_out = refs[PIECES + 4 : PIECES + 7], refs[PIECES + 7]
    q_width = GROUP * HEAD
    cut = local // CHIPS
    scale = gain[:, :1]
    for chip in range(CHIPS):
        for side in range(2):

            @pl.when((index[0] == chip) & (pl.program_id(0) == side))
            def _():
                parts, k_parts, v_parts = [], [], []
                for group in range(CHIPS):
                    owner = (group >> 1) + 2 * (group & 1)
                    piece = pieces[2 * (owner ^ chip) + side]
                    for s in range(group_shards):
                        for j in range(CHIPS):
                            start = ((j ^ owner) * group_shards + s) * cut
                            parts.append(piece[:, start : start + cut].astype(f32))
                    k_parts.append(piece[:, q_width : q_width + HEAD].astype(f32))
                    v_parts.append(piece[:, q_width + HEAD : q_width + 2 * HEAD].astype(f32))
                total = jnp.zeros((gain.shape[0], LANES), f32)
                for part, weight, out in zip((parts, k_parts, v_parts), weights, outs):
                    wide = jnp.concatenate(part, axis=1)
                    total = total + lane_sum(wide * weight[...].astype(f32))
                    out[...] = wide * scale
                gain_out[...] = total


def qkv_result(index, pieces, query, key, value, gain):
    local, width = query.shape
    half = local // 2
    group_shards = width // local // CHIPS
    row = lambda i, n: (n[1] ^ i, 0)
    kv_width = key.shape[1]
    return kernel_call(
        functools.partial(qkv_result_body, local, group_shards),
        (
            shape((local, width), f32),
            shape((local, kv_width), f32),
            shape((local, kv_width), f32),
            shape((local, LANES), f32),
        ),
        [pl.BlockSpec(pieces[0].shape, lambda i, n: (0, 0))] * PIECES
        + [
            pl.BlockSpec((half, width), row),
            pl.BlockSpec((half, kv_width), row),
            pl.BlockSpec((half, kv_width), row),
            pl.BlockSpec((half, LANES), row),
        ],
        (
            pl.BlockSpec((half, width), row),
            pl.BlockSpec((half, kv_width), row),
            pl.BlockSpec((half, kv_width), row),
            pl.BlockSpec((half, LANES), row),
        ),
        (*pieces, query, key, value, gain),
        index=index,
        grid=(2,),
        name="qkv_result",
    )


def per_device(
    hidden_in,
    attention_gain,
    query_weight,
    key_weight,
    value_weight,
    output_weight,
    feedforward_gain,
    gate_weight,
    up_weight,
    down_weight,
    out_grad,
):
    rows, width = hidden_in.shape
    shards = lax.axis_size("shard")
    replicas = lax.axis_size("replica")
    place = lax.axis_index("replica")
    depth = lax.axis_index("shard")
    core = place & 1
    chip = (place >> 1) & (CHIPS - 1)
    local = width // shards
    half = local // 2
    ff_local = down_weight.shape[0]
    group_shards = shards // CHIPS
    q_width = GROUP * HEAD
    qkv_width = q_width + 2 * HEAD
    index = jnp.stack([chip, core, depth]).astype(jnp.int32)

    gain_one = jnp.broadcast_to(attention_gain.astype(f32)[:, None], (local, LANES))
    gain_two = jnp.broadcast_to(feedforward_gain.astype(f32)[:, None], (local, LANES))


    at_block, out_block = attention_block(
        index, query_weight, key_weight, value_weight, output_weight, gain_one
    )
    x = own_first(index, (after(hidden_in, at_block),), local)[0]
    xs = [x, swap(x, 2)]
    at_own = lax.all_gather(at_block, "shard", axis=0, tiled=True)
    out_all = lax.all_gather(out_block, "shard", axis=0, tiled=True)
    gu_block = feedforward_block(index, gate_weight, up_weight, after(gain_two, at_block), ff_local)
    gu_own = lax.all_gather(gu_block, "shard", axis=0, tiled=True)
    down_own = lax.all_gather(down_block(index, down_weight, local), "shard", axis=0, tiled=True)
    g = own_first(index, (after(out_grad, x),), local)[0]
    g_blocks = [g, swap(g, 2), swap(g, 4)]
    at_own = after(at_own, gu_block, xs[1], *g_blocks[1:])

    qkv_own = [at_own]
    qkv_own.append(swap(qkv_own[0], 4))
    qkv_other = [swap(qkv_own[0], 1)]
    inverse = rope_base ** (-jnp.arange(0, HEAD, 2, dtype=f32) / HEAD)
    places = (depth * rows + jnp.arange(rows, dtype=jnp.int32)).astype(f32)
    angles = inverse[:, None] * places[None, :]
    angles = jnp.concatenate([angles, angles], axis=0)
    cosine, sine = jnp.cos(angles), jnp.sin(angles)

    def shifted(kv):
        return [kv] + [shift(kv, d) for d in range(1, shards)]

    queries, kv, xhat = qkv_call(xs, qkv_own[0], qkv_other[0], cosine, sine)
    kvs = shifted(kv)
    qkv_own[1] = after(qkv_own[1], *kvs[1:])
    qkv_other.append(swap(qkv_own[1], 1))
    queries_two, kv_two = qkv_call(xhat, qkv_own[1], qkv_other[1], cosine, sine)
    kvs_two = shifted(kv_two)
    groups = [(queries, *attention_call(index, queries, kvs), kvs)]
    groups.append((queries_two, *attention_call(index, queries_two, kvs_two), kvs_two))
    attended = [group[2] for group in groups]
    groups = [(group[0], group[1], group[3], group[4]) for group in groups]

    out_all = after(out_all, qkv_own[1])
    x_place = chip & 1
    low_group = (chip >> 1) == 0
    pair_rows = PAIR * group_shards * half // 2

    def out_for(mask):
        return lax.dynamic_slice_in_dim(out_all, ((chip ^ mask) & 1) * pair_rows, pair_rows, 0)

    out_pieces = [out_for(0)] + [swap(out_for(m), 2 * m) for m in range(1, CHIPS)]
    wo_own = out_rows_call(index, [after(piece, *kvs_two[1:]) for piece in out_pieces])
    wo_other = swap(wo_own, 1)

    mid_terms = [(attended[n], wo_own, wo_other, n) for n in range(PAIR)]
    g_blocks.append(swap(after(g, *out_pieces[1:]), 6))
    mid_out = parts_call(mid_terms, rows, False, "attention_out")
    g_all = jnp.concatenate([after(block, mid_out[0]) for block in g_blocks], axis=0)
    middle, two = middle_call(plane_send(mid_out), after(x, g_all))
    twos = plane_gather_far(two, *plane_gather_near(two))

    gu_own = after(gu_own, *twos[1:])
    gu_other = swap(gu_own, 1)
    act, for_gate, for_up, two_all = gate_call(twos, gu_own, gu_other)

    def over_groups(kept):
        if replicas > PIECES:
            groups = [
                [e * PIECES + i for e in range(replicas // PIECES)] for i in range(PIECES)
            ]
            kept = lax.psum(kept, "replica", axis_index_groups=groups)
        return kept

    def reduced(term):
        kept = lax.psum_scatter(term, "shard", scatter_dimension=0, tiled=True)
        return over_groups(kept)

    def plane_pieces(kept):
        mine = plane_gather(kept)
        return mine, [swap(part, 1) for part in mine]

    def mixed(mine, theirs):
        return [part for pair in zip(mine, theirs) for part in pair]

    down_sent = weight_grad(act, None, g_all, 1, width // 2, 1, (), "down_grad_other")
    down_sent = [swap(down_sent[0], 1)]
    down_sent[0] = after(down_sent[0], down_own)
    down_term = weight_grad(act, None, g_all, 0, width // 2, 1, (down_sent,), "down_grad")[0]
    down_kept = reduced(down_term)
    down_other = swap(down_own, 1)

    grads = hidden_back_call(after(g_all, down_term), down_own, down_other, for_gate, for_up)
    grads_wide = grads.shape[1]
    gu_sent = weight_grad(two_all, 1, grads, 0, grads_wide, 1, (), "gate_grad_other")
    gu_sent = [swap(gu_sent[0], 1)]
    gu_term = weight_grad(two_all, 0, grads, 0, grads_wide, 1, (gu_sent,), "gate_grad")[0]
    gu_kept = reduced(gu_term)
    grads_late = after(grads, gu_term)
    e_terms = parts_call([(grads_late, gu_own, gu_other, 0)], rows, True, "feedforward_back")
    e_parts = plane_send(e_terms)
    act_late = after(act, e_terms[0])
    out_terms = parts_call([(act_late, down_own, down_other, 0)], rows, False, "feedforward_out")

    middle_late = after(middle, out_terms[0], down_kept)
    grad_middle, branch = grad_middle_call(e_parts, middle_late, g)
    branches = [branch, swap(branch, 2)]

    def back_block(m, block, before):
        return attention_back_call(index, m, block, wo_own, wo_other, cosine, sine, groups, before)

    before = back_block(0, branch, None)
    out_parts = plane_send(after(out_terms, branches[1], before[1]))
    half_wide = width // 2
    branch_all = jnp.concatenate([branch, after(branches[1], before[1])], axis=0)
    both_attended = jnp.concatenate(attended, axis=1)
    wo_sent = weight_grad(both_attended, None, branch_all, 1, half_wide, 1, (), "out_grad_other")
    wo_other_term = wo_sent[0]
    wo_sent = [swap(wo_other_term, 1)]
    before = back_block(1, after(branches[1], before[1], wo_other_term), before)
    output = output_call(index, out_parts, middle, local)
    grad_q, grad_first, grad_rest = before
    grad_rest = after(grad_rest, out_parts[1])
    rest = [shift(grad_rest[d - 1], -d) for d in range(1, shards)]

    wo_term = weight_grad(both_attended, None, branch_all, 0, half_wide, 1, (wo_sent,), "out_grad")[0]
    wo_terms = out_sends(index, after(wo_term, *rest, *out_parts[1:]))
    wo_parts = plane_send(wo_terms)
    wo_block = out_block_call(index, [after(wo_parts[0], gu_kept), *wo_parts[1:]])
    wo_kept = reduced(wo_block)
    grad_first = after(grad_first, wo_block)
    grad_qkv = grad_qkv_call(grad_q, grad_first, rest, cosine, sine)

    def qkv_grad(n, side, added, name):
        return weight_grad(xhat, side, grad_qkv[n], 0, qkv_width, 1, added, name)

    qkv_sent = [swap(qkv_grad(n, 1, (), "qkv_grad_other")[0], 1) for n in (1, 0)]
    back_terms = [(grad_qkv[n], qkv_own[n], qkv_other[n], 0) for n in range(PAIR)]
    qkv_second = qkv_grad(1, 0, ([qkv_sent[0]],), "qkv_grad")[0]
    qkv_term = qkv_grad(0, 0, ([qkv_sent[1]],), "qkv_grad")[0]
    gu_near = plane_gather_near(gu_kept)
    at_term = jnp.concatenate([qkv_term, qkv_second], axis=1)
    at_kept = reduced(after(at_term, wo_kept))
    back_terms[0] = (after(grad_qkv[0], at_term), *back_terms[0][1:])
    back_parts = parts_call(back_terms, rows, True, "qkv_back")
    e_one = plane_send(back_parts)
    gu_mine = plane_gather_far(gu_kept, *(after(part, back_parts[0]) for part in gu_near))
    gu_mine = gu_mine[:3] + [jnp.concatenate(gu_mine[3:], axis=0)]
    gu_theirs = [swap(after(part, output), 1) for part in gu_mine]
    gu_out = feedforward_result(index, 0, gu_mine, gate_weight, up_weight, gain_two, ff_local, None)
    gu_out = feedforward_result(index, 1, gu_theirs, gate_weight, up_weight, gain_two, ff_local, gu_out)

    down_mine = plane_gather_far(down_kept, *plane_gather_near(after(down_kept, *gu_near)))
    down_mine = down_mine[:3] + [jnp.concatenate(down_mine[3:], axis=0)]
    down_theirs = [swap(part, 1) for part in down_mine]
    down_out = rows_result(index, mixed(down_mine, down_theirs), local, "down_result")
    grad_input = grad_input_call(index, e_one, x, grad_middle, local)

    wo_out = rows_result(index, mixed(*plane_pieces(wo_kept)), local, "out_result")
    second = swap(at_kept[:, qkv_width:], 4)
    first = at_kept[:, :qkv_width].astype(f32) + second.astype(f32)
    at_mine = plane_gather(first.astype(bf16))
    at_pieces = mixed(at_mine, [swap(after(piece, gu_out[0]), 1) for piece in at_mine])
    q_out, k_out, v_out, gain_one_sums = qkv_result(
        index, at_pieces, query_weight, key_weight, value_weight, gain_one
    )
    return (
        output,
        grad_input,
        jnp.sum(gain_one_sums, axis=1),
        q_out,
        k_out,
        v_out,
        wo_out,
        jnp.sum(gu_out[2], axis=1),
        gu_out[0],
        gu_out[1],
        down_out,
    )


def solution(mesh):
    return jax.shard_map(
        per_device,
        mesh=mesh,
        in_specs=(
            P(("replica", "shard"), None),
            P("shard"),
            P("shard", None),
            P("shard", None),
            P("shard", None),
            P("shard", None),
            P("shard"),
            P("shard", None),
            P("shard", None),
            P("shard", None),
            P(("replica", "shard"), None),
        ),
        out_specs=(
            P(("replica", "shard"), None),
            P(("replica", "shard"), None),
            P("shard"),
            P("shard", None),
            P("shard", None),
            P("shard", None),
            P("shard", None),
            P("shard"),
            P("shard", None),
            P("shard", None),
            P("shard", None),
        ),
        check_vma=False,
    )
```

```python
import functools

import jax
import jax.numpy as jnp
from jax import lax
from jax.experimental import pallas as pl
from jax.experimental.pallas import tpu as pltpu
from jax.sharding import PartitionSpec as P

HEADS = 32
KV_HEADS = 4
HEAD = 64
GROUP = HEADS // KV_HEADS
CHIPS = 4
PIECES = 2 * CHIPS
PAIR = 2
LANES = 128

norm_eps = 1e-05
rope_base = 10000.0
masked_score = -1e30

f32 = jnp.float32
bf16 = jnp.bfloat16
VMEM = pltpu.VMEM
NT = (((1,), (1,)), ((), ()))
TN = (((0,), (0,)), ((), ()))


def dot(left, right):
    return jnp.dot(left, right, preferred_element_type=f32)


def dot_nt(left, right):
    return lax.dot_general(left, right, NT, preferred_element_type=f32)


def dot_tn(left, right):
    return lax.dot_general(left, right, TN, preferred_element_type=f32)


def shape(dims, kind):
    return jax.ShapeDtypeStruct(dims, kind)


def whole():
    return pl.BlockSpec(memory_space=VMEM)


TIMES = {"attention_back": 13.0, "feedforward_result": 10.0, "down_result": 8.0, "grad_input": 4.0}


def kernel_call(body, out_shape, in_specs, out_specs, operands, *, index=None, grid=(), scratch=(),
                aliases=None, name=None):
    params = pltpu.CompilerParams(
        vmem_limit_bytes=52 * 2**20, dimension_semantics=("arbitrary",) * len(grid)
    )
    moved = int(TIMES.get(name, 0.0) * 3.69e6)
    cost = pl.CostEstimate(flops=0, bytes_accessed=moved, transcendentals=0)
    common = dict(
        out_shape=out_shape,
        compiler_params=params,
        cost_estimate=cost,
        input_output_aliases=aliases or {},
        name=name,
    )
    if index is None:
        spec = pl.GridSpec(grid=grid, in_specs=in_specs, out_specs=out_specs, scratch_shapes=scratch)
        return pl.pallas_call(body, grid_spec=spec, **common)(*operands)
    spec = pltpu.PrefetchScalarGridSpec(
        num_scalar_prefetch=1, grid=grid, in_specs=in_specs, out_specs=out_specs,
        scratch_shapes=scratch,
    )
    return pl.pallas_call(body, grid_spec=spec, **common)(index, *operands)


def swap(value, mask):
    size = lax.axis_size("replica")
    return lax.ppermute(value, "replica", [(i, i ^ mask) for i in range(size)])


def shift(value, step):
    size = lax.axis_size("shard")
    pairs = [(i, i + step) for i in range(size) if 0 <= i + step < size]
    return lax.ppermute(value, "shard", pairs)


def plane_gather(value):
    return [value] + [swap(value, 2 * m) for m in range(1, CHIPS)]


def plane_gather_forward(value, *before):
    middle = value.shape[0] // 2
    across, along = swap(value, 2), swap(value, 4)
    if before:
        across, along = after(across, *before), after(along, *before)
    return [value, across, along, swap(across[:middle], 4), swap(along[middle:], 2)]


def plane_send(parts):
    return [parts[0]] + [swap(parts[m], 2 * m) for m in range(1, len(parts))]


def group_of(chip):
    return 2 * (chip & 1) + (chip >> 1)


def after(value, *others):
    return lax.optimization_barrier((value, *others))[0]


def attention_block_body(local, group_shards, index, q, k, v, o, gain, out, wo_out):
    scale = gain[:, :1]
    q_width = GROUP * HEAD
    cut = local // CHIPS
    for chip in range(CHIPS):

        group = group_of(chip)

        @pl.when(index[0] == chip)
        def _(group=group):
            parts = []
            for m in range(CHIPS):
                for s in range(group_shards):
                    start = group * q_width + s * local + (m ^ chip) * cut
                    parts.append(q[:, start : start + cut])
            parts.append(k[:, group * HEAD : (group + 1) * HEAD])
            parts.append(v[:, group * HEAD : (group + 1) * HEAD])
            wide = jnp.concatenate([part.astype(f32) for part in parts], axis=1)
            out[...] = (wide * scale).astype(bf16)

    half = local // 2
    shards = o.shape[1] // local
    for core in range(2):

        @pl.when(index[1] == core)
        def _():
            for s in range(shards):
                piece = o[:, s * local + core * half : s * local + (core + 1) * half]
                wo_out[:, s * half : (s + 1) * half] = piece


def attention_block(index, query, key, value, output, gain):
    local, width = query.shape
    half = local // 2
    shards = width // local
    return kernel_call(
        functools.partial(attention_block_body, local, shards // CHIPS),
        (
            shape((half, GROUP * HEAD + 2 * HEAD), bf16),
            shape((local // CHIPS, width // 2), bf16),
        ),
        [
            pl.BlockSpec((half, width), lambda i, n: (n[1], 0)),
            pl.BlockSpec((half, key.shape[1]), lambda i, n: (n[1], 0)),
            pl.BlockSpec((half, key.shape[1]), lambda i, n: (n[1], 0)),
            pl.BlockSpec((local // CHIPS, width), lambda i, n: (n[0], 0)),
            pl.BlockSpec((half, LANES), lambda i, n: (n[1], 0)),
        ],
        (
            pl.BlockSpec((half, GROUP * HEAD + 2 * HEAD), lambda i, n: (0, 0)),
            pl.BlockSpec((local // CHIPS, width // 2), lambda i, n: (0, 0)),
        ),
        (query, key, value, output, gain),
        index=index,
        grid=(1,),
        name="attention_block",
    )


def feedforward_block_body(ff_local, cut, index, gate, up, gain, out):
    scale = gain[:, :1]
    shards = gate.shape[1] // ff_local
    width = shards * cut
    for chip in range(CHIPS):

        @pl.when(index[0] == chip)
        def _():
            for n, source in enumerate((gate, up)):
                parts = [
                    source[:, s * ff_local + chip * cut : s * ff_local + (chip + 1) * cut].astype(f32)
                    for s in range(shards)
                ]
                wide = jnp.concatenate(parts, axis=1)
                out[:, n * width : (n + 1) * width] = (wide * scale).astype(bf16)


def feedforward_block(index, gate, up, gain, ff_local):
    local, ff = gate.shape
    half = local // 2
    rows = 64
    steps = half // rows
    cut = ff_local // CHIPS
    width = 2 * (ff // CHIPS)
    return kernel_call(
        functools.partial(feedforward_block_body, ff_local, cut),
        shape((half, width), bf16),
        [
            pl.BlockSpec((rows, ff), lambda i, n: (n[1] * steps + i, 0)),
            pl.BlockSpec((rows, ff), lambda i, n: (n[1] * steps + i, 0)),
            pl.BlockSpec((rows, LANES), lambda i, n: (n[1] * steps + i, 0)),
        ],
        pl.BlockSpec((rows, width), lambda i, n: (i, 0)),
        (gate, up, gain),
        index=index,
        grid=(steps,),
        name="feedforward_block",
    )


def own_first_body(local, index, *refs):
    count = len(refs) // 2
    half = local // 2
    for core in range(2):

        @pl.when(index[1] == core)
        def _():
            for source, out in zip(refs[:count], refs[count:]):
                shards = source.shape[1] // local
                sides = out.shape[1] // (shards * half)
                for side in range(sides):
                    for s in range(shards):
                        start = s * local + (core ^ side) * half
                        spot = (side * shards + s) * half
                        out[:, spot : spot + half] = source[:, start : start + half]


def own_first(index, sources, local, halves=2):
    return kernel_call(
        functools.partial(own_first_body, local),
        tuple(shape((v.shape[0], v.shape[1] * halves // 2), bf16) for v in sources),
        [pl.BlockSpec(v.shape, lambda i, n: (0, 0)) for v in sources],
        tuple(
            pl.BlockSpec((v.shape[0], v.shape[1] * halves // 2), lambda i, n: (0, 0)) for v in sources
        ),
        tuple(sources),
        index=index,
        grid=(1,),
        name="own_first",
    )


def down_block_body(local, index, source, out):
    own_first_body(local, index, source, out)


def down_block(index, down, local):
    ff_local, width = down.shape
    cut = ff_local // CHIPS
    return kernel_call(
        functools.partial(down_block_body, local),
        shape((cut, width // 2), bf16),
        [pl.BlockSpec((cut, width), lambda i, n: (n[0], 0))],
        pl.BlockSpec((cut, width // 2), lambda i, n: (0, 0)),
        (down,),
        index=index,
        grid=(1,),
        name="down_block",
    )


def part_sum(parts):
    total = parts[0][...]
    for part in parts[1:]:
        total = total + part[...].astype(f32)
    return total


def mean_of(values):
    return jnp.mean(values, axis=1, keepdims=True)


def middle_body(*refs):
    parts, (x, middle, two) = refs[:PAIR], refs[PAIR:]
    total = x[...].astype(f32) + part_sum(parts)
    middle[...] = total
    two[...] = (total * lax.rsqrt(mean_of(total * total) + norm_eps)).astype(bf16)


def middle_call(parts, x):
    return kernel_call(
        middle_body,
        (shape(x.shape, f32), shape(x.shape, bf16)),
        [whole()] * (PAIR + 1),
        (whole(), whole()),
        (*parts, x),
        name="middle",
    )


def norm_back(e, values):
    inverse = lax.rsqrt(mean_of(values * values) + norm_eps)
    return inverse * e - values * (inverse * inverse * inverse) * mean_of(e * values)


def grad_middle_body(*refs):
    parts, (middle, g, grad, low) = refs[:CHIPS], refs[CHIPS:]
    total = g[...].astype(f32) + norm_back(part_sum(parts), middle[...])
    grad[...] = total
    low[...] = total.astype(bf16)


def grad_middle_call(parts, middle, g):
    return kernel_call(
        grad_middle_body,
        (shape(g.shape, f32), shape(g.shape, bf16)),
        [whole()] * (CHIPS + 2),
        (whole(), whole()),
        (*parts, middle, g),
        name="grad_middle",
    )


def store_in_order(local, index, value, out):
    half = local // 2
    shards = out.shape[1] // local
    for core in range(2):

        @pl.when(index[1] == core)
        def _():
            for side in range(2):
                for s in range(shards):
                    spot = s * local + (core ^ side) * half
                    start = (side * shards + s) * half
                    out[:, spot : spot + half] = value[:, start : start + half].astype(bf16)


def output_body(local, index, *refs):
    parts, (middle, out) = refs[:CHIPS], refs[CHIPS:]
    store_in_order(local, index, middle[...] + part_sum(parts), out)


def output_call(index, parts, middle, local):
    spec = pl.BlockSpec(middle.shape, lambda i, n: (0, 0))
    return kernel_call(
        functools.partial(output_body, local),
        shape(middle.shape, bf16),
        [spec] * (CHIPS + 1),
        spec,
        (*parts, middle),
        index=index,
        grid=(1,),
        name="output",
    )


def grad_input_body(local, index, *refs):
    parts, (x, grad, out) = refs[:PAIR], refs[PAIR:]
    total = grad[...] + norm_back(part_sum(parts), x[...].astype(f32))
    store_in_order(local, index, total, out)


def grad_input_call(index, parts, x, grad, local):
    spec = pl.BlockSpec(x.shape, lambda i, n: (0, 0))
    return kernel_call(
        functools.partial(grad_input_body, local),
        shape(x.shape, bf16),
        [spec] * (PAIR + 2),
        spec,
        (*parts, x, grad),
        index=index,
        grid=(1,),
        name="grad_input",
    )


def grad_qkv_body(shards, grad_q, first, *refs):
    rest, (cosine, sine), outs = refs[: shards - 1], refs[shards - 1 : shards + 1], refs[shards + 1 :]
    total = first[...]
    for term in rest:
        total = total + term[...].astype(f32)
    rows = cosine.shape[1]
    width = GROUP * HEAD
    cos, sin = cosine[...], sine[...]
    for n, out in enumerate(outs):
        out[:, :width] = grad_q[:, n * width : (n + 1) * width]
        for m in range(PAIR):
            span = slice(m * rows, (m + 1) * rows)
            turned = total[span, n * 2 * HEAD : (n + 1) * 2 * HEAD].T
            k = turned[:HEAD]
            k = k * cos - half_rotated(k) * sin
            both = jnp.concatenate([k, turned[HEAD:]], axis=0)
            out[span, width:] = both.T.astype(bf16)


def grad_qkv_call(grad_q, first, rest, cosine, sine):
    tokens = grad_q.shape[0]
    return kernel_call(
        functools.partial(grad_qkv_body, len(rest) + 1),
        (shape((tokens, GROUP * HEAD + 2 * HEAD), bf16),) * PAIR,
        [whole()] * (len(rest) + 4),
        (whole(),) * PAIR,
        (grad_q, first, *rest, cosine, sine),
        name="grad_qkv",
    )


def out_sends_body(index, term, *outs):
    cut = outs[0].shape[0] // PAIR
    for row in range(2):

        @pl.when(index[0] >> 1 == row)
        def _():
            for n in range(PAIR):
                for m in range(CHIPS):
                    spot = (n * CHIPS + m) * cut
                    start = (n ^ row) * cut
                    outs[m ^ (2 * n)][start : start + cut, :] = term[spot : spot + cut, :]


def out_sends(index, term):
    rows, width = term.shape
    rows //= CHIPS
    return kernel_call(
        out_sends_body,
        (shape((rows, width), bf16),) * CHIPS,
        [pl.BlockSpec(term.shape, lambda i, n: (0, 0))],
        (pl.BlockSpec((rows, width), lambda i, n: (0, 0)),) * CHIPS,
        (term,),
        index=index,
        grid=(1,),
        name="out_sends",
    )


def out_block_body(shards, index, *refs):
    parts, out = refs[:CHIPS], refs[CHIPS]
    group_shards = shards // CHIPS
    cut = parts[0].shape[0] // (PAIR * group_shards)
    sums = [parts[m][...].astype(f32) + parts[m + 2][...].astype(f32) for m in range(2)]
    for side in range(2):

        @pl.when(index[0] & 1 == side)
        def _():
            for m in range(2):
                for n in range(PAIR * group_shards):
                    shard = (m ^ side) * PAIR * group_shards + n
                    rows = sums[m][n * cut : (n + 1) * cut].astype(bf16)
                    out[2 * shard * cut : (2 * shard + 1) * cut, :] = rows[:, :512]
                    out[(2 * shard + 1) * cut : (2 * shard + 2) * cut, :] = rows[:, 512:]


def out_block_call(index, parts, shards):
    rows, width = parts[0].shape
    return kernel_call(
        functools.partial(out_block_body, shards),
        shape((2 * PAIR * rows, width // 2), bf16),
        [pl.BlockSpec((rows, width), lambda i, n: (0, 0))] * CHIPS,
        pl.BlockSpec((2 * PAIR * rows, width // 2), lambda i, n: (0, 0)),
        tuple(parts),
        index=index,
        grid=(1,),
        name="out_block",
    )


def half_rotated(values):
    middle = values.shape[0] // 2
    return jnp.concatenate([-values[middle:], values[:middle]], axis=0)


def qkv_body(make, *refs):
    if make:
        xs, (own, other, cosine, sine, queries, kv, xhat) = refs[:PAIR], refs[PAIR:]
        rows, width = xs[0].shape
        for m in range(PAIR):
            x = xs[m][...].astype(f32)
            inverse = lax.rsqrt(mean_of(x * x) + norm_eps)
            xhat[m * rows : (m + 1) * rows, :] = (x * inverse).astype(bf16)
    else:
        xhat, own, other, cosine, sine, queries, kv = refs
        rows, width = cosine.shape[1], xhat.shape[1]
    cos, sin = cosine[...], sine[...]
    total = dot(xhat[:, : width // 2], own[...]) + dot(xhat[:, width // 2 :], other[...])
    for m in range(PAIR):
        turned = total[m * rows : (m + 1) * rows].T
        for h in range(GROUP + 1):
            u = turned[h * HEAD : (h + 1) * HEAD]
            u = u * cos + half_rotated(u) * sin
            if h < GROUP:
                queries[m, :, h * rows : (h + 1) * rows] = (u * HEAD ** (-0.5)).astype(bf16)
            else:
                both = jnp.concatenate([u, turned[(h + 1) * HEAD :]], axis=0)
                kv[m * rows : (m + 1) * rows, :] = both.T.astype(bf16)


def qkv_call(xs, own, other, cosine, sine):
    make = isinstance(xs, list)
    rows = cosine.shape[1]
    tokens = PAIR * rows
    outs = (shape((PAIR, HEAD, GROUP * rows), bf16), shape((tokens, 2 * HEAD), bf16))
    if make:
        outs = outs + (shape((tokens, xs[0].shape[1]), bf16),)
    operands = (*(xs if make else (xs,)), own, other, cosine, sine)
    return kernel_call(
        functools.partial(qkv_body, make),
        outs,
        [whole()] * len(operands),
        tuple(whole() for _ in outs),
        operands,
        name="qkv",
    )


def out_rows_body(index, *refs):
    pieces, out = refs[:CHIPS], refs[CHIPS]
    cut = pieces[0].shape[0] // PAIR
    for row in range(2):

        @pl.when(index[0] >> 1 == row)
        def _():
            for n in range(PAIR):
                for m in range(CHIPS):
                    spot = (n * CHIPS + m) * cut
                    start = (n ^ row) * cut
                    out[spot : spot + cut, :] = pieces[m ^ (2 * n)][start : start + cut, :]


def out_rows_call(index, pieces):
    rows, width = pieces[0].shape
    return kernel_call(
        out_rows_body,
        shape((CHIPS * rows, width), bf16),
        [pl.BlockSpec((rows, width), lambda i, n: (0, 0))] * CHIPS,
        pl.BlockSpec((CHIPS * rows, width), lambda i, n: (0, 0)),
        tuple(pieces),
        index=index,
        grid=(1,),
        name="out_rows",
    )


LANE_HEADS = 4


def own_block_bias(rows):
    key = lax.broadcasted_iota(jnp.int32, (rows, rows), 0)
    mine = lax.broadcasted_iota(jnp.int32, (rows, rows), 1)
    return jnp.where(key <= mine, 0.0, masked_score)


def set_bias(bias):
    rows = bias.shape[0]
    value = own_block_bias(rows)
    for h in range(LANE_HEADS):
        bias[:, h * rows : (h + 1) * rows] = value


def far_bias(depth, d):
    return jnp.where(d <= depth, 0.0, masked_score) if d else 0.0


def attention_body(shards, index, queries, *refs):
    kvs = refs[:shards]
    turned_out, out, stats, bias, terms, out_turned = refs[shards:]
    rows = bias.shape[0]
    wide = LANE_HEADS * rows

    @pl.when(pl.program_id(0) == 0)
    def _():
        set_bias(bias)

    ks = [kv[:, :HEAD] for kv in kvs]
    v_turned = jnp.concatenate([kv[...] for kv in kvs], axis=0).astype(f32).T[HEAD:].astype(bf16)
    for n in range(GROUP // LANE_HEADS):
        span = slice(n * wide, (n + 1) * wide)
        q = queries[0, :, span]
        scores, top = [], None
        for d in range(shards):
            score = dot(ks[d], q)
            if d == 0:
                score = score + bias[...]
            scores.append(score)
            highest = jnp.max(score, axis=0, keepdims=True) + far_bias(index[2], d)
            top = highest if top is None else jnp.maximum(top, highest)
        total = None
        for d in range(shards):
            term = jnp.exp(scores[d] - (top - far_bias(index[2], d)))
            part = jnp.sum(term, axis=0, keepdims=True)
            total = part if total is None else total + part
            terms[d * rows : (d + 1) * rows, :] = term.astype(bf16)
        out_turned[:, span] = dot(v_turned, terms[...]) / total
        stats[0, :, span] = top + jnp.log(total)
    turned_out[0] = out_turned[...].astype(bf16)
    straight = out_turned[...].T
    for h in range(GROUP):
        out[:, h * HEAD : (h + 1) * HEAD] = straight[h * rows : (h + 1) * rows].astype(bf16)


def attention_call(index, queries, kvs):
    chips, _, wide = queries.shape
    rows = wide // GROUP
    shards = len(kvs)
    keys = shards * rows
    block = pl.BlockSpec((1, HEAD, wide), lambda i, n: (i, 0, 0))
    return kernel_call(
        functools.partial(attention_body, shards),
        (
            shape((chips, HEAD, wide), bf16),
            shape((chips * rows, GROUP * HEAD), bf16),
            shape((chips, 1, wide), f32),
        ),
        [block] + [pl.BlockSpec((rows, 2 * HEAD), lambda i, n: (i, 0))] * shards,
        (
            block,
            pl.BlockSpec((rows, GROUP * HEAD), lambda i, n: (i, 0)),
            pl.BlockSpec((1, 1, wide), lambda i, n: (i, 0, 0)),
        ),
        (queries, *kvs),
        index=index,
        grid=(chips,),
        scratch=(
            VMEM((rows, LANE_HEADS * rows), f32),
            VMEM((keys, LANE_HEADS * rows), bf16),
            VMEM((HEAD, wide), f32),
        ),
        name="attention",
    )


def attention_back_body(shards, index, branch, wo_own, wo_other, cosine, sine, *refs):
    per_group = 3 + shards
    inputs = [refs[n * per_group : (n + 1) * per_group] for n in range(PAIR)]
    grad_q, grad_first, grad_rest = refs[-7:-4]
    bias, probs_low, grads_low, grad_lanes = refs[-4:]
    rows = bias.shape[0]
    wide = LANE_HEADS * rows
    width = branch.shape[1]
    set_bias(bias)
    cos, sin = cosine[...], sine[...]
    for n, (queries, turned_out, stats, *kvs) in enumerate(inputs):
        heads = slice(n * GROUP * HEAD, (n + 1) * GROUP * HEAD)
        grad_out = dot_nt(wo_own[heads, :], branch[:, : width // 2])
        grad_out = grad_out + dot_nt(wo_other[heads, :], branch[:, width // 2 :])
        for h in range(GROUP):
            grad_lanes[:, h * rows : (h + 1) * rows] = grad_out[h * HEAD : (h + 1) * HEAD].astype(bf16)
        ks = [kv[:, :HEAD] for kv in kvs]
        vs = [kv[:, HEAD:] for kv in kvs]
        k_turned = jnp.concatenate([kv[...] for kv in kvs], axis=0).astype(f32).T[:HEAD].astype(bf16)
        k_total, v_total, parts = None, None, []
        for c in range(GROUP // LANE_HEADS):
            span = slice(c * wide, (c + 1) * wide)
            q, mine = queries[0, :, span], grad_lanes[:, span]
            delta = jnp.sum(
                mine.astype(f32) * turned_out[0, :, span].astype(f32), axis=0, keepdims=True
            )
            for d in range(shards):
                score = dot(ks[d], q)
                if d == 0:
                    score = score + bias[...]
                probs = jnp.exp(score - (stats[0, :, span] - far_bias(index[2], d)))
                grad_scores = probs * (dot(vs[d], mine) - delta)
                probs_low[d * rows : (d + 1) * rows, :] = probs.astype(bf16)
                grads_low[d * rows : (d + 1) * rows, :] = grad_scores.astype(bf16)
            u = dot(k_turned, grads_low[...]) * HEAD ** (-0.5)
            parts.append(u * cos - half_rotated(u) * sin)
            k_term = dot_nt(grads_low[...], q)
            v_term = dot_nt(probs_low[...], mine)
            k_total = k_term if k_total is None else k_total + k_term
            v_total = v_term if v_total is None else v_total + v_term
        straight = jnp.concatenate(parts, axis=1).T
        for h in range(GROUP):
            spot = (n * GROUP + h) * HEAD
            grad_q[:, spot : spot + HEAD] = straight[h * rows : (h + 1) * rows].astype(bf16)
        both = jnp.concatenate([k_total, v_total], axis=1)
        spot = slice(n * 2 * HEAD, (n + 1) * 2 * HEAD)
        grad_first[:, spot] = both[:rows, :]
        for d in range(1, shards):
            grad_rest[d - 1, :, spot] = both[d * rows : (d + 1) * rows, :].astype(bf16)


def attention_back_call(index, m, branch, wo_own, wo_other, cosine, sine, groups, before):
    chips, _, wide = groups[0][0].shape
    rows = wide // GROUP
    shards = len(groups[0][3])
    keys = shards * rows
    tokens = chips * rows
    block = pl.BlockSpec((1, HEAD, wide), lambda i, n: (m, 0, 0))
    in_specs = [whole()] * 5
    operands = [branch, wo_own, wo_other, jnp.tile(cosine, (1, LANE_HEADS)), jnp.tile(sine, (1, LANE_HEADS))]
    for queries, turned, stats, kvs in groups:
        in_specs += [block, block, pl.BlockSpec((1, 1, wide), lambda i, n: (m, 0, 0))]
        in_specs += [pl.BlockSpec((rows, 2 * HEAD), lambda i, n: (m, 0))] * shards
        operands += [queries, turned, stats, *kvs]
    aliases = {}
    if before is not None:
        aliases = {1 + len(operands) + n: n for n in range(3)}
        in_specs += [pl.BlockSpec(memory_space=pl.ANY)] * 3
        operands += list(before)
    outs = (
        shape((tokens, PAIR * GROUP * HEAD), bf16),
        shape((tokens, PAIR * 2 * HEAD), f32),
        shape((shards - 1, tokens, PAIR * 2 * HEAD), bf16),
    )
    out_specs = (
        pl.BlockSpec((rows, PAIR * GROUP * HEAD), lambda i, n: (m, 0)),
        pl.BlockSpec((rows, PAIR * 2 * HEAD), lambda i, n: (m, 0)),
        pl.BlockSpec((shards - 1, rows, PAIR * 2 * HEAD), lambda i, n: (0, m, 0)),
    )
    return kernel_call(
        functools.partial(attention_back_body, shards),
        outs,
        in_specs,
        out_specs,
        tuple(operands),
        index=index,
        grid=(1,),
        scratch=(
            VMEM((rows, LANE_HEADS * rows), f32),
            VMEM((keys, LANE_HEADS * rows), bf16),
            VMEM((keys, LANE_HEADS * rows), bf16),
            VMEM((HEAD, wide), bf16),
        ),
        aliases=aliases,
        name="attention_back",
    )


def parts_body(steps, transposed, count, *refs):
    lefts, owns, others = refs[:count], refs[count : 2 * count], refs[2 * count : 3 * count]
    outs = refs[3 * count :]
    rows = outs[0].shape[0]
    step = pl.program_id(0)

    def run(weights):
        total = None
        for left, weight in zip(lefts, weights):
            term = (dot_nt if transposed else dot)(left[...], weight[...])
            total = term if total is None else total + term
        for m, out in enumerate(outs):
            out[...] = total[m * rows : (m + 1) * rows, :].astype(out.dtype)

    @pl.when(step < steps)
    def _():
        run(owns)

    @pl.when(step >= steps)
    def _():
        run(others)


def parts_call(terms, rows, transposed, name):
    tokens = terms[0][0].shape[0]
    half = terms[0][1].shape[0] if transposed else terms[0][1].shape[1]
    tile = 256
    steps = half // tile
    last = steps - 1
    specs = [pl.BlockSpec((tokens, term[0].shape[1]), lambda j: (0, 0)) for term in terms]
    for side in range(2):
        for left, _, _, spot in terms:
            depth = left.shape[1]

            def place(side, spot, j):
                step = jnp.maximum(j - steps, 0) if side else jnp.minimum(j, last)
                return (step, spot) if transposed else (spot, step)

            block = (tile, depth) if transposed else (depth, tile)
            specs.append(pl.BlockSpec(block, functools.partial(place, side, spot)))
    count = tokens // rows
    return kernel_call(
        functools.partial(parts_body, steps, transposed, len(terms)),
        tuple(shape((rows, 2 * half), f32 if m == 0 else bf16) for m in range(count)),
        specs,
        tuple(pl.BlockSpec((rows, tile), lambda j: (0, j)) for _ in range(count)),
        (*(term[0] for term in terms), *(term[1] for term in terms), *(term[2] for term in terms)),
        grid=(2 * steps,),
        name=name,
    )


def gate_body(count, *refs):
    twos = refs[:count]
    gate_own, up_own, gate_other, up_other, act, for_gate, for_up, two_all = refs[count:]
    half = two_all.shape[1] // 2

    @pl.when(pl.program_id(0) == 0)
    def _():
        start = 0
        for two in twos:
            two_all[start : start + two.shape[0], :] = two[...]
            start += two.shape[0]

    own = jnp.concatenate([gate_own[...], up_own[...]], axis=1)
    other = jnp.concatenate([gate_other[...], up_other[...]], axis=1)
    both = dot(two_all[:, :half], own) + dot(two_all[:, half:], other)
    wide = gate_own.shape[1]
    gate, up = both[:, :wide], both[:, wide:]
    sig = 1.0 / (1.0 + jnp.exp(-gate))
    silu = gate * sig
    act[...] = (silu * up).astype(bf16)
    for_gate[...] = (up * sig * (1.0 + gate * (1.0 - sig))).astype(bf16)
    for_up[...] = silu.astype(bf16)


def gate_call(twos, own, other):
    rows, width = twos[0].shape
    tokens = CHIPS * rows
    half = width // 2
    ff = own.shape[1] // 2
    tile = LANES
    steps = ff // tile
    weight = [
        pl.BlockSpec((half, tile), lambda j: (0, j)),
        pl.BlockSpec((half, tile), lambda j: (0, j + steps)),
    ]
    column = pl.BlockSpec((tokens, tile), lambda j: (0, j))
    return kernel_call(
        functools.partial(gate_body, len(twos)),
        tuple(shape((tokens, ff), bf16) for _ in range(3)) + (shape((tokens, width), bf16),),
        [pl.BlockSpec(two.shape, lambda j: (0, 0)) for two in twos] + weight + weight,
        (column, column, column, pl.BlockSpec((tokens, width), lambda j: (0, 0))),
        (*twos, own, own, other, other),
        grid=(steps,),
        name="gate",
    )


def hidden_back_body(g, own, other, for_gate, for_up, grads):
    half = g.shape[1] // 2
    ff = own.shape[0]
    hidden = dot_nt(g[:, :half], own[...]) + dot_nt(g[:, half:], other[...])
    grads[:, :ff] = (hidden * for_gate[...].astype(f32)).astype(bf16)
    grads[:, ff:] = (hidden * for_up[...].astype(f32)).astype(bf16)


def hidden_back_call(g, own, other, for_gate, for_up):
    tokens, width = g.shape
    ff, half = own.shape
    block = tokens // 2
    row = lambda i: (i, 0)
    fixed = lambda i: (0, 0)
    return kernel_call(
        hidden_back_body,
        shape((tokens, 2 * ff), bf16),
        [
            pl.BlockSpec((block, width), row),
            pl.BlockSpec((ff, half), fixed),
            pl.BlockSpec((ff, half), fixed),
            pl.BlockSpec((block, ff), row),
            pl.BlockSpec((block, ff), row),
        ],
        pl.BlockSpec((block, 2 * ff), row),
        (g, own, other, for_gate, for_up),
        grid=(2,),
        name="hidden_back",
    )


def weight_grad_body(per, outputs, adds, left, right, *refs):
    added = [refs[n * outputs : (n + 1) * outputs] for n in range(adds)]
    outs, turned = refs[adds * outputs : -1], refs[-1]
    step = pl.program_id(0)

    @pl.when(step == 0)
    def _():
        turned[...] = left[...].T

    for n in range(outputs):

        @pl.when(step // per == n)
        def _(n=n):
            total = dot(turned[...], right[...])
            for terms in added:
                total = total + terms[n][...].astype(f32)
            outs[n][...] = total.astype(bf16)


def weight_grad(left, left_side, right, place, width, outputs, added, name):
    tokens = left.shape[0]
    rows = left.shape[1] // (1 if left_side is None else 2)
    tile = 256 if width % 256 == 0 else width
    per = width // tile
    first = place * width // tile
    side = left_side or 0

    def spot(n, j):
        return (0, jnp.clip(j - n * per, 0, per - 1))

    tiles = [pl.BlockSpec((rows, tile), functools.partial(spot, n)) for n in range(outputs)]
    return kernel_call(
        functools.partial(weight_grad_body, per, outputs, len(added)),
        tuple(shape((rows, width), bf16) for _ in range(outputs)),
        [
            pl.BlockSpec((tokens, rows), lambda j: (0, side)),
            pl.BlockSpec((tokens, tile), lambda j: (0, first + j)),
        ]
        + tiles * len(added),
        tuple(tiles),
        (left, right, *(term for terms in added for term in terms)),
        grid=(per * outputs,),
        scratch=(VMEM((rows, tokens), bf16),),
        name=name,
    )


def rows_result_body(local, index, *refs):
    pieces, out = refs[:PIECES], refs[PIECES]
    half = local // 2
    shards = out.shape[1] // local
    for m in range(CHIPS):
        for core in range(2):

            @pl.when((pl.program_id(0) == m) & (index[1] == core))
            def _():
                for side in range(2):
                    piece = pieces[2 * m + side]
                    for s in range(shards):
                        spot = s * local + (core ^ side) * half
                        out[:, spot : spot + half] = piece[:, s * half : (s + 1) * half].astype(f32)


def rows_result(index, pieces, local, name):
    cut, half_width = pieces[0].shape
    return kernel_call(
        functools.partial(rows_result_body, local),
        shape((CHIPS * cut, 2 * half_width), f32),
        [pl.BlockSpec((cut, half_width), lambda i, n: (0, 0))] * PIECES,
        pl.BlockSpec((cut, 2 * half_width), lambda i, n: (n[0] ^ i, 0)),
        tuple(pieces),
        index=index,
        grid=(CHIPS,),
        name=name,
    )


def out_result_body(local, base, index, *refs):
    pieces, out = refs[:PIECES], refs[PIECES]
    half = local // 2
    cut = local // CHIPS
    shards = out.shape[1] // local
    for m in range(CHIPS):
        for core in range(2):

            @pl.when((pl.program_id(0) == m) & (index[1] == core))
            def _():
                for side in range(2):
                    piece = pieces[2 * m + side]
                    for s in range(shards):
                        spot = s * local + (core ^ side) * half
                        row, column = (0, s * half) if s * half < 512 else (cut, s * half - 512)
                        column += base
                        out[:, spot : spot + half] = piece[row : row + cut, column : column + half].astype(f32)


def out_result(index, pieces, local, width, base):
    cut = local // CHIPS
    return kernel_call(
        functools.partial(out_result_body, local, base),
        shape((local, width), f32),
        [pl.BlockSpec(pieces[0].shape, lambda i, n: (0, 0))] * PIECES,
        pl.BlockSpec((cut, width), lambda i, n: (n[0] ^ i, 0)),
        tuple(pieces),
        index=index,
        grid=(CHIPS,),
        name="out_result",
    )


def lane_sum(value):
    total = value[:, :LANES]
    for n in range(1, value.shape[1] // LANES):
        total = total + value[:, n * LANES : (n + 1) * LANES]
    return total


def feedforward_result_body(ff_local, cut, index, *refs):
    pieces = refs[:CHIPS]
    gate_weight, up_weight, gain = refs[CHIPS : CHIPS + 3]
    gate_out, up_out, gain_out = refs[-3:]
    shards = gate_weight.shape[1] // ff_local
    width = shards * cut
    for chip in range(CHIPS):

        @pl.when(index[0] == chip)
        def _():
            @pl.loop(0, gate_out.shape[0] // 16)
            def _(n):
                rows = pl.ds(pl.multiple_of(n * 16, 16), 16)
                scale = gain[rows, :1]
                total = jnp.zeros((16, LANES), f32)
                for base, weight, out in ((0, gate_weight, gate_out), (width, up_weight, up_out)):
                    parts = []
                    for s in range(shards):
                        for owner in range(CHIPS):
                            start = base + s * cut
                            parts.append(pieces[owner ^ chip][rows, start : start + cut].astype(f32))
                    wide = jnp.concatenate(parts, axis=1)
                    total = total + lane_sum(wide * weight[rows, :].astype(f32))
                    out[rows, :] = wide * scale
                gain_out[rows, :] = total


def feedforward_result(index, side, pieces, gate_weight, up_weight, gain, ff_local, before):
    local, ff = gate_weight.shape
    half = local // 2
    rows = 64
    steps = half // rows
    row = lambda i, n: ((n[1] ^ side) * steps + i, 0)
    in_specs = [pl.BlockSpec((rows, pieces[0].shape[1]), lambda i, n: (i, 0))] * CHIPS
    in_specs += [pl.BlockSpec((rows, ff), row)] * 2 + [pl.BlockSpec((rows, LANES), row)]
    operands = (*pieces, gate_weight, up_weight, gain)
    aliases = {}
    if before is not None:
        aliases = {1 + len(operands) + n: n for n in range(3)}
        in_specs = in_specs + [pl.BlockSpec(memory_space=pl.ANY)] * 3
        operands = operands + tuple(before)
    return kernel_call(
        functools.partial(feedforward_result_body, ff_local, ff_local // CHIPS),
        (shape((local, ff), f32), shape((local, ff), f32), shape((local, LANES), f32)),
        in_specs,
        (pl.BlockSpec((rows, ff), row), pl.BlockSpec((rows, ff), row), pl.BlockSpec((rows, LANES), row)),
        operands,
        index=index,
        grid=(steps,),
        aliases=aliases,
        name="feedforward_result",
    )


def qkv_result_body(local, group_shards, index, *refs):
    pieces = refs[:PIECES]
    weights, gain = refs[PIECES : PIECES + 3], refs[PIECES + 3]
    outs, gain_out = refs[PIECES + 4 : PIECES + 7], refs[PIECES + 7]
    q_width = GROUP * HEAD
    cut = local // CHIPS
    scale = gain[:, :1]
    for chip in range(CHIPS):
        for side in range(2):

            @pl.when((index[0] == chip) & (pl.program_id(0) == side))
            def _():
                parts, k_parts, v_parts = [], [], []
                for group in range(CHIPS):
                    owner = (group >> 1) + 2 * (group & 1)
                    piece = pieces[2 * (owner ^ chip) + side]
                    for s in range(group_shards):
                        for j in range(CHIPS):
                            start = ((j ^ owner) * group_shards + s) * cut
                            parts.append(piece[:, start : start + cut].astype(f32))
                    k_parts.append(piece[:, q_width : q_width + HEAD].astype(f32))
                    v_parts.append(piece[:, q_width + HEAD : q_width + 2 * HEAD].astype(f32))
                total = jnp.zeros((gain.shape[0], LANES), f32)
                for part, weight, out in zip((parts, k_parts, v_parts), weights, outs):
                    wide = jnp.concatenate(part, axis=1)
                    total = total + lane_sum(wide * weight[...].astype(f32))
                    out[...] = wide * scale
                gain_out[...] = total


def qkv_result(index, pieces, query, key, value, gain):
    local, width = query.shape
    half = local // 2
    group_shards = width // local // CHIPS
    row = lambda i, n: (n[1] ^ i, 0)
    kv_width = key.shape[1]
    return kernel_call(
        functools.partial(qkv_result_body, local, group_shards),
        (
            shape((local, width), f32),
            shape((local, kv_width), f32),
            shape((local, kv_width), f32),
            shape((local, LANES), f32),
        ),
        [pl.BlockSpec(pieces[0].shape, lambda i, n: (0, 0))] * PIECES
        + [
            pl.BlockSpec((half, width), row),
            pl.BlockSpec((half, kv_width), row),
            pl.BlockSpec((half, kv_width), row),
            pl.BlockSpec((half, LANES), row),
        ],
        (
            pl.BlockSpec((half, width), row),
            pl.BlockSpec((half, kv_width), row),
            pl.BlockSpec((half, kv_width), row),
            pl.BlockSpec((half, LANES), row),
        ),
        (*pieces, query, key, value, gain),
        index=index,
        grid=(2,),
        name="qkv_result",
    )


def per_device(
    hidden_in,
    attention_gain,
    query_weight,
    key_weight,
    value_weight,
    output_weight,
    feedforward_gain,
    gate_weight,
    up_weight,
    down_weight,
    out_grad,
):
    rows, width = hidden_in.shape
    shards = lax.axis_size("shard")
    replicas = lax.axis_size("replica")
    place = lax.axis_index("replica")
    depth = lax.axis_index("shard")
    core = place & 1
    chip = (place >> 1) & (CHIPS - 1)
    local = width // shards
    half = local // 2
    ff_local = down_weight.shape[0]
    group_shards = shards // CHIPS
    q_width = GROUP * HEAD
    qkv_width = q_width + 2 * HEAD
    index = jnp.stack([chip, core, depth]).astype(jnp.int32)

    gain_one = jnp.broadcast_to(attention_gain.astype(f32)[:, None], (local, LANES))
    gain_two = jnp.broadcast_to(feedforward_gain.astype(f32)[:, None], (local, LANES))


    at_block, out_block = attention_block(
        index, query_weight, key_weight, value_weight, output_weight, gain_one
    )
    x = own_first(index, (after(hidden_in, at_block),), local)[0]
    xs = [x, swap(x, 2)]
    at_own = lax.all_gather(at_block, "shard", axis=0, tiled=True)
    out_all = lax.all_gather(out_block, "shard", axis=0, tiled=True)
    gu_block = feedforward_block(index, gate_weight, up_weight, after(gain_two, at_block), ff_local)
    gu_own = lax.all_gather(gu_block, "shard", axis=0, tiled=True)
    down_own = lax.all_gather(down_block(index, down_weight, local), "shard", axis=0, tiled=True)
    g = own_first(index, (after(out_grad, x),), local)[0]
    g_blocks = [g, swap(g, 2), swap(g, 4)]
    at_own = after(at_own, gu_block, xs[1], *g_blocks[1:])

    qkv_own = [at_own]
    qkv_own.append(swap(qkv_own[0], 4))
    qkv_other = [swap(qkv_own[0], 1)]
    inverse = rope_base ** (-jnp.arange(0, HEAD, 2, dtype=f32) / HEAD)
    places = (depth * rows + jnp.arange(rows, dtype=jnp.int32)).astype(f32)
    angles = inverse[:, None] * places[None, :]
    angles = jnp.concatenate([angles, angles], axis=0)
    cosine, sine = jnp.cos(angles), jnp.sin(angles)

    def shifted(kv):
        return [kv] + [shift(kv, d) for d in range(1, shards)]

    queries, kv, xhat = qkv_call(xs, qkv_own[0], qkv_other[0], cosine, sine)
    kvs = shifted(kv)
    qkv_own[1] = after(qkv_own[1], *kvs[1:])
    qkv_other.append(swap(qkv_own[1], 1))
    queries_two, kv_two = qkv_call(xhat, qkv_own[1], qkv_other[1], cosine, sine)
    kvs_two = shifted(kv_two)
    groups = [(queries, *attention_call(index, queries, kvs), kvs)]
    groups.append((queries_two, *attention_call(index, queries_two, kvs_two), kvs_two))
    attended = [group[2] for group in groups]
    groups = [(group[0], group[1], group[3], group[4]) for group in groups]

    out_all = after(out_all, qkv_own[1])
    x_place = chip & 1
    low_group = (chip >> 1) == 0
    pair_rows = PAIR * group_shards * half // 2

    def out_for(mask):
        return lax.dynamic_slice_in_dim(out_all, ((chip ^ mask) & 1) * pair_rows, pair_rows, 0)

    out_pieces = [out_for(0)] + [swap(out_for(m), 2 * m) for m in range(1, CHIPS)]
    wo_own = out_rows_call(index, [after(piece, *kvs_two[1:]) for piece in out_pieces])
    wo_other = swap(wo_own, 1)

    mid_terms = [(attended[n], wo_own, wo_other, n) for n in range(PAIR)]
    g_blocks.append(swap(after(g, *out_pieces[1:]), 6))
    mid_out = parts_call(mid_terms, rows, False, "attention_out")
    g_all = jnp.concatenate([after(block, mid_out[0]) for block in g_blocks], axis=0)
    middle, two = middle_call(plane_send(mid_out), after(x, g_all))
    twos = plane_gather_forward(two)

    gu_own = after(gu_own, *twos[1:])
    gu_other = swap(gu_own, 1)
    act, for_gate, for_up, two_all = gate_call(twos, gu_own, gu_other)

    def over_groups(kept):
        if replicas > PIECES:
            groups = [
                [e * PIECES + i for e in range(replicas // PIECES)] for i in range(PIECES)
            ]
            kept = lax.psum(kept, "replica", axis_index_groups=groups)
        return kept

    def reduced(term):
        kept = lax.psum_scatter(term, "shard", scatter_dimension=0, tiled=True)
        return over_groups(kept)

    def plane_pieces(kept):
        mine = plane_gather(kept)
        return mine, [swap(part, 1) for part in mine]

    def mixed(mine, theirs):
        return [part for pair in zip(mine, theirs) for part in pair]

    down_sent = weight_grad(act, None, g_all, 1, width // 2, 1, (), "down_grad_other")
    down_sent = [swap(down_sent[0], 1)]
    down_sent[0] = after(down_sent[0], down_own)
    down_term = weight_grad(act, None, g_all, 0, width // 2, 1, (down_sent,), "down_grad")[0]
    down_kept = reduced(down_term)
    down_other = swap(down_own, 1)

    grads = hidden_back_call(after(g_all, down_term), down_own, down_other, for_gate, for_up)
    grads_wide = grads.shape[1]
    gu_sent = weight_grad(two_all, 1, grads, 0, grads_wide, 1, (), "gate_grad_other")
    gu_sent = [swap(gu_sent[0], 1)]
    gu_term = weight_grad(two_all, 0, grads, 0, grads_wide, 1, (gu_sent,), "gate_grad")[0]
    gu_kept = reduced(gu_term)
    grads_late = after(grads, gu_term)
    e_terms = parts_call([(grads_late, gu_own, gu_other, 0)], rows, True, "feedforward_back")
    e_parts = plane_send(e_terms)
    act_late = after(act, e_terms[0])
    out_terms = parts_call([(act_late, down_own, down_other, 0)], rows, False, "feedforward_out")

    middle_late = after(middle, out_terms[0], down_kept)
    grad_middle, branch = grad_middle_call(e_parts, middle_late, g)
    branches = [branch, swap(branch, 2)]

    def back_block(m, block, before):
        return attention_back_call(index, m, block, wo_own, wo_other, cosine, sine, groups, before)

    before = back_block(0, branch, None)
    out_parts = plane_send(after(out_terms, branches[1], before[1]))
    before = back_block(1, after(branches[1], before[1]), before)
    output = output_call(index, out_parts, middle, local)
    grad_q, grad_first, grad_rest = before
    grad_rest = after(grad_rest, *out_parts[1:3])
    rest = [shift(grad_rest[d - 1], -d) for d in range(1, shards)]

    half_wide = width // 2
    branch_all = jnp.concatenate([after(block, grad_first, *out_parts[1:3]) for block in branches], axis=0)
    both_attended = jnp.concatenate(attended, axis=1)
    wo_sent = weight_grad(both_attended, None, branch_all, 1, half_wide, 1, (), "out_grad_other")
    wo_sent = [after(swap(wo_sent[0], 1), rest[-1])]
    wo_term = weight_grad(both_attended, None, branch_all, 0, half_wide, 1, (wo_sent,), "out_grad")[0]
    wo_terms = out_sends(index, wo_term)
    wo_parts = plane_send(wo_terms)
    wo_wide = out_block_call(index, [after(wo_parts[0], gu_kept), *wo_parts[1:]], shards)
    grad_first = after(grad_first, out_parts[3], wo_terms[0])
    grad_qkv = grad_qkv_call(grad_q, grad_first, rest, cosine, sine)

    def qkv_grad(n, side, added, name):
        return weight_grad(xhat, side, grad_qkv[n], 0, qkv_width, 1, added, name)

    qkv_sent = [swap(qkv_grad(n, 1, (), "qkv_grad_other")[0], 1) for n in (1, 0)]
    back_terms = [(grad_qkv[n], qkv_own[n], qkv_other[n], 0) for n in range(PAIR)]
    qkv_sent[0] = after(qkv_sent[0], *wo_parts[1:3])
    qkv_second = qkv_grad(1, 0, ([qkv_sent[0]],), "qkv_grad")[0]
    qkv_term = qkv_grad(0, 0, ([qkv_sent[1]],), "qkv_grad")[0]
    at_term = jnp.concatenate([qkv_term, qkv_second, wo_wide], axis=1)
    at_kept = reduced(after(at_term, gu_kept))
    back_terms[0] = (after(grad_qkv[0], qkv_term, qkv_second), *back_terms[0][1:])
    back_parts = parts_call(back_terms, rows, True, "qkv_back")
    e_one = plane_send(back_parts)
    gu_mine = plane_gather_forward(gu_kept, back_parts[0])
    gu_mine = gu_mine[:3] + [jnp.concatenate(gu_mine[3:], axis=0)]
    gu_theirs = [swap(after(part, output), 1) for part in gu_mine]
    gu_out = feedforward_result(index, 0, gu_mine, gate_weight, up_weight, gain_two, ff_local, None)
    gu_out = feedforward_result(index, 1, gu_theirs, gate_weight, up_weight, gain_two, ff_local, gu_out)

    down_mine = plane_gather(after(down_kept, *gu_mine[1:]))
    down_theirs = [swap(part, 1) for part in down_mine]
    down_out = rows_result(index, mixed(down_mine, down_theirs), local, "down_result")
    grad_input = grad_input_call(index, e_one, x, grad_middle, local)

    second = swap(at_kept[:, qkv_width : 2 * qkv_width], 4)
    first = at_kept[:, :qkv_width].astype(f32) + second.astype(f32)
    at_kept = jnp.concatenate([first.astype(bf16), at_kept[:, 2 * qkv_width :]], axis=1)
    at_mine = plane_gather(at_kept)
    at_near = [after(piece, gu_out[0], down_out, grad_input) for piece in at_mine]
    at_pieces = mixed(at_mine, [swap(piece, 1) for piece in at_near])
    wo_out = out_result(index, at_pieces, local, width, qkv_width)
    q_out, k_out, v_out, gain_one_sums = qkv_result(
        index, at_pieces, query_weight, key_weight, value_weight, gain_one
    )
    return (
        output,
        grad_input,
        jnp.sum(gain_one_sums, axis=1),
        q_out,
        k_out,
        v_out,
        wo_out,
        jnp.sum(gu_out[2], axis=1),
        gu_out[0],
        gu_out[1],
        down_out,
    )


def solution(mesh):
    return jax.shard_map(
        per_device,
        mesh=mesh,
        in_specs=(
            P(("replica", "shard"), None),
            P("shard"),
            P("shard", None),
            P("shard", None),
            P("shard", None),
            P("shard", None),
            P("shard"),
            P("shard", None),
            P("shard", None),
            P("shard", None),
            P(("replica", "shard"), None),
        ),
        out_specs=(
            P(("replica", "shard"), None),
            P(("replica", "shard"), None),
            P("shard"),
            P("shard", None),
            P("shard", None),
            P("shard", None),
            P("shard", None),
            P("shard"),
            P("shard", None),
            P("shard", None),
            P("shard", None),
        ),
        check_vma=False,
    )
```

```python
import functools

import jax
import jax.numpy as jnp
from jax import lax
from jax.experimental import pallas as pl
from jax.experimental.pallas import tpu as pltpu
from jax.sharding import PartitionSpec as P

HEADS = 32
KV_HEADS = 4
HEAD = 64
GROUP = HEADS // KV_HEADS
CHIPS = 4
PIECES = 2 * CHIPS
PAIR = 2
LANES = 128

norm_eps = 1e-05
rope_base = 10000.0
masked_score = -1e30

f32 = jnp.float32
bf16 = jnp.bfloat16
VMEM = pltpu.VMEM
NT = (((1,), (1,)), ((), ()))
TN = (((0,), (0,)), ((), ()))


def dot(left, right):
    return jnp.dot(left, right, preferred_element_type=f32)


def dot_nt(left, right):
    return lax.dot_general(left, right, NT, preferred_element_type=f32)


def dot_tn(left, right):
    return lax.dot_general(left, right, TN, preferred_element_type=f32)


def shape(dims, kind):
    return jax.ShapeDtypeStruct(dims, kind)


def whole():
    return pl.BlockSpec(memory_space=VMEM)


TIMES = {"attention_back": 13.0, "feedforward_result": 10.0, "down_result": 8.0, "grad_input": 4.0}


def kernel_call(body, out_shape, in_specs, out_specs, operands, *, index=None, grid=(), scratch=(),
                aliases=None, name=None):
    params = pltpu.CompilerParams(
        vmem_limit_bytes=52 * 2**20, dimension_semantics=("arbitrary",) * len(grid)
    )
    moved = int(TIMES.get(name, 0.0) * 3.69e6)
    cost = pl.CostEstimate(flops=0, bytes_accessed=moved, transcendentals=0)
    common = dict(
        out_shape=out_shape,
        compiler_params=params,
        cost_estimate=cost,
        input_output_aliases=aliases or {},
        name=name,
    )
    if index is None:
        spec = pl.GridSpec(grid=grid, in_specs=in_specs, out_specs=out_specs, scratch_shapes=scratch)
        return pl.pallas_call(body, grid_spec=spec, **common)(*operands)
    spec = pltpu.PrefetchScalarGridSpec(
        num_scalar_prefetch=1, grid=grid, in_specs=in_specs, out_specs=out_specs,
        scratch_shapes=scratch,
    )
    return pl.pallas_call(body, grid_spec=spec, **common)(index, *operands)


def swap(value, mask):
    size = lax.axis_size("replica")
    return lax.ppermute(value, "replica", [(i, i ^ mask) for i in range(size)])


def shift(value, step):
    size = lax.axis_size("shard")
    pairs = [(i, i + step) for i in range(size) if 0 <= i + step < size]
    return lax.ppermute(value, "shard", pairs)


def plane_gather(value):
    return [value] + [swap(value, 2 * m) for m in range(1, CHIPS)]


def plane_gather_forward(value, *before):
    middle = value.shape[0] // 2
    across, along = swap(value, 2), swap(value, 4)
    if before:
        across, along = after(across, *before), after(along, *before)
    return [value, across, along, swap(across[:middle], 4), swap(along[middle:], 2)]


def plane_send(parts):
    return [parts[0]] + [swap(parts[m], 2 * m) for m in range(1, len(parts))]


def group_of(chip):
    return 2 * (chip & 1) + (chip >> 1)


def after(value, *others):
    return lax.optimization_barrier((value, *others))[0]


def attention_block_body(local, group_shards, index, q, k, v, o, gain, out, wo_out):
    scale = gain[:, :1]
    q_width = GROUP * HEAD
    cut = local // CHIPS
    for chip in range(CHIPS):

        group = group_of(chip)

        @pl.when(index[0] == chip)
        def _(group=group):
            parts = []
            for m in range(CHIPS):
                for s in range(group_shards):
                    start = group * q_width + s * local + (m ^ chip) * cut
                    parts.append(q[:, start : start + cut])
            parts.append(k[:, group * HEAD : (group + 1) * HEAD])
            parts.append(v[:, group * HEAD : (group + 1) * HEAD])
            wide = jnp.concatenate([part.astype(f32) for part in parts], axis=1)
            out[...] = (wide * scale).astype(bf16)

    half = local // 2
    shards = o.shape[1] // local
    for core in range(2):

        @pl.when(index[1] == core)
        def _():
            for s in range(shards):
                piece = o[:, s * local + core * half : s * local + (core + 1) * half]
                wo_out[:, s * half : (s + 1) * half] = piece


def attention_block(index, query, key, value, output, gain):
    local, width = query.shape
    half = local // 2
    shards = width // local
    return kernel_call(
        functools.partial(attention_block_body, local, shards // CHIPS),
        (
            shape((half, GROUP * HEAD + 2 * HEAD), bf16),
            shape((local // CHIPS, width // 2), bf16),
        ),
        [
            pl.BlockSpec((half, width), lambda i, n: (n[1], 0)),
            pl.BlockSpec((half, key.shape[1]), lambda i, n: (n[1], 0)),
            pl.BlockSpec((half, key.shape[1]), lambda i, n: (n[1], 0)),
            pl.BlockSpec((local // CHIPS, width), lambda i, n: (n[0], 0)),
            pl.BlockSpec((half, LANES), lambda i, n: (n[1], 0)),
        ],
        (
            pl.BlockSpec((half, GROUP * HEAD + 2 * HEAD), lambda i, n: (0, 0)),
            pl.BlockSpec((local // CHIPS, width // 2), lambda i, n: (0, 0)),
        ),
        (query, key, value, output, gain),
        index=index,
        grid=(1,),
        name="attention_block",
    )


def feedforward_block_body(ff_local, cut, index, gate, up, gain, out):
    scale = gain[:, :1]
    shards = gate.shape[1] // ff_local
    width = shards * cut
    for chip in range(CHIPS):

        @pl.when(index[0] == chip)
        def _():
            for n, source in enumerate((gate, up)):
                parts = [
                    source[:, s * ff_local + chip * cut : s * ff_local + (chip + 1) * cut].astype(f32)
                    for s in range(shards)
                ]
                wide = jnp.concatenate(parts, axis=1)
                out[:, n * width : (n + 1) * width] = (wide * scale).astype(bf16)


def feedforward_block(index, gate, up, gain, ff_local):
    local, ff = gate.shape
    half = local // 2
    rows = 64
    steps = half // rows
    cut = ff_local // CHIPS
    width = 2 * (ff // CHIPS)
    return kernel_call(
        functools.partial(feedforward_block_body, ff_local, cut),
        shape((half, width), bf16),
        [
            pl.BlockSpec((rows, ff), lambda i, n: (n[1] * steps + i, 0)),
            pl.BlockSpec((rows, ff), lambda i, n: (n[1] * steps + i, 0)),
            pl.BlockSpec((rows, LANES), lambda i, n: (n[1] * steps + i, 0)),
        ],
        pl.BlockSpec((rows, width), lambda i, n: (i, 0)),
        (gate, up, gain),
        index=index,
        grid=(steps,),
        name="feedforward_block",
    )


def own_first_body(local, index, *refs):
    count = len(refs) // 2
    half = local // 2
    for core in range(2):

        @pl.when(index[1] == core)
        def _():
            for source, out in zip(refs[:count], refs[count:]):
                shards = source.shape[1] // local
                sides = out.shape[1] // (shards * half)
                for side in range(sides):
                    for s in range(shards):
                        start = s * local + (core ^ side) * half
                        spot = (side * shards + s) * half
                        out[:, spot : spot + half] = source[:, start : start + half]


def own_first(index, sources, local, halves=2):
    return kernel_call(
        functools.partial(own_first_body, local),
        tuple(shape((v.shape[0], v.shape[1] * halves // 2), bf16) for v in sources),
        [pl.BlockSpec(v.shape, lambda i, n: (0, 0)) for v in sources],
        tuple(
            pl.BlockSpec((v.shape[0], v.shape[1] * halves // 2), lambda i, n: (0, 0)) for v in sources
        ),
        tuple(sources),
        index=index,
        grid=(1,),
        name="own_first",
    )


def down_block_body(local, index, source, out):
    own_first_body(local, index, source, out)


def down_block(index, down, local):
    ff_local, width = down.shape
    cut = ff_local // CHIPS
    return kernel_call(
        functools.partial(down_block_body, local),
        shape((cut, width // 2), bf16),
        [pl.BlockSpec((cut, width), lambda i, n: (n[0], 0))],
        pl.BlockSpec((cut, width // 2), lambda i, n: (0, 0)),
        (down,),
        index=index,
        grid=(1,),
        name="down_block",
    )


def part_sum(parts):
    total = parts[0][...]
    for part in parts[1:]:
        total = total + part[...].astype(f32)
    return total


def mean_of(values):
    return jnp.mean(values, axis=1, keepdims=True)


def middle_body(*refs):
    parts, (x, middle, two) = refs[:PAIR], refs[PAIR:]
    total = x[...].astype(f32) + part_sum(parts)
    middle[...] = total
    two[...] = (total * lax.rsqrt(mean_of(total * total) + norm_eps)).astype(bf16)


def middle_call(parts, x):
    return kernel_call(
        middle_body,
        (shape(x.shape, f32), shape(x.shape, bf16)),
        [whole()] * (PAIR + 1),
        (whole(), whole()),
        (*parts, x),
        name="middle",
    )


def norm_back(e, values):
    inverse = lax.rsqrt(mean_of(values * values) + norm_eps)
    return inverse * e - values * (inverse * inverse * inverse) * mean_of(e * values)


def grad_middle_body(*refs):
    parts, (middle, g, grad, low) = refs[:CHIPS], refs[CHIPS:]
    total = g[...].astype(f32) + norm_back(part_sum(parts), middle[...])
    grad[...] = total
    low[...] = total.astype(bf16)


def grad_middle_call(parts, middle, g):
    return kernel_call(
        grad_middle_body,
        (shape(g.shape, f32), shape(g.shape, bf16)),
        [whole()] * (CHIPS + 2),
        (whole(), whole()),
        (*parts, middle, g),
        name="grad_middle",
    )


def store_in_order(local, index, value, out):
    half = local // 2
    shards = out.shape[1] // local
    for core in range(2):

        @pl.when(index[1] == core)
        def _():
            for side in range(2):
                for s in range(shards):
                    spot = s * local + (core ^ side) * half
                    start = (side * shards + s) * half
                    out[:, spot : spot + half] = value[:, start : start + half].astype(bf16)


def output_body(local, index, *refs):
    parts, (middle, out) = refs[:CHIPS], refs[CHIPS:]
    store_in_order(local, index, middle[...] + part_sum(parts), out)


def output_call(index, parts, middle, local):
    spec = pl.BlockSpec(middle.shape, lambda i, n: (0, 0))
    return kernel_call(
        functools.partial(output_body, local),
        shape(middle.shape, bf16),
        [spec] * (CHIPS + 1),
        spec,
        (*parts, middle),
        index=index,
        grid=(1,),
        name="output",
    )


def grad_input_body(local, index, *refs):
    parts, (x, grad, out) = refs[:PAIR], refs[PAIR:]
    total = grad[...] + norm_back(part_sum(parts), x[...].astype(f32))
    store_in_order(local, index, total, out)


def grad_input_call(index, parts, x, grad, local):
    spec = pl.BlockSpec(x.shape, lambda i, n: (0, 0))
    return kernel_call(
        functools.partial(grad_input_body, local),
        shape(x.shape, bf16),
        [spec] * (PAIR + 2),
        spec,
        (*parts, x, grad),
        index=index,
        grid=(1,),
        name="grad_input",
    )


def grad_qkv_body(shards, grad_q, first, *refs):
    rest, (cosine, sine), outs = refs[: shards - 1], refs[shards - 1 : shards + 1], refs[shards + 1 :]
    total = first[...]
    for term in rest:
        total = total + term[...].astype(f32)
    rows = cosine.shape[1]
    width = GROUP * HEAD
    cos, sin = cosine[...], sine[...]
    for n, out in enumerate(outs):
        out[:, :width] = grad_q[:, n * width : (n + 1) * width]
        for m in range(PAIR):
            span = slice(m * rows, (m + 1) * rows)
            turned = total[span, n * 2 * HEAD : (n + 1) * 2 * HEAD].T
            k = turned[:HEAD]
            k = k * cos - half_rotated(k) * sin
            both = jnp.concatenate([k, turned[HEAD:]], axis=0)
            out[span, width:] = both.T.astype(bf16)


def grad_qkv_call(grad_q, first, rest, cosine, sine):
    tokens = grad_q.shape[0]
    return kernel_call(
        functools.partial(grad_qkv_body, len(rest) + 1),
        (shape((tokens, GROUP * HEAD + 2 * HEAD), bf16),) * PAIR,
        [whole()] * (len(rest) + 4),
        (whole(),) * PAIR,
        (grad_q, first, *rest, cosine, sine),
        name="grad_qkv",
    )


def out_sends_body(index, term, *outs):
    cut = outs[0].shape[0] // PAIR
    for row in range(2):

        @pl.when(index[0] >> 1 == row)
        def _():
            for n in range(PAIR):
                for m in range(CHIPS):
                    spot = (n * CHIPS + m) * cut
                    start = (n ^ row) * cut
                    outs[m ^ (2 * n)][start : start + cut, :] = term[spot : spot + cut, :]


def out_sends(index, term):
    rows, width = term.shape
    rows //= CHIPS
    return kernel_call(
        out_sends_body,
        (shape((rows, width), bf16),) * CHIPS,
        [pl.BlockSpec(term.shape, lambda i, n: (0, 0))],
        (pl.BlockSpec((rows, width), lambda i, n: (0, 0)),) * CHIPS,
        (term,),
        index=index,
        grid=(1,),
        name="out_sends",
    )


def out_block_body(shards, index, *refs):
    parts, out = refs[:CHIPS], refs[CHIPS]
    group_shards = shards // CHIPS
    cut = parts[0].shape[0] // (PAIR * group_shards)
    sums = [parts[m][...].astype(f32) + parts[m + 2][...].astype(f32) for m in range(2)]
    for side in range(2):

        @pl.when(index[0] & 1 == side)
        def _():
            for m in range(2):
                for n in range(PAIR * group_shards):
                    shard = (m ^ side) * PAIR * group_shards + n
                    rows = sums[m][n * cut : (n + 1) * cut].astype(bf16)
                    out[2 * shard * cut : (2 * shard + 1) * cut, :] = rows[:, :512]
                    out[(2 * shard + 1) * cut : (2 * shard + 2) * cut, :] = rows[:, 512:]


def out_block_call(index, parts, shards):
    rows, width = parts[0].shape
    return kernel_call(
        functools.partial(out_block_body, shards),
        shape((2 * PAIR * rows, width // 2), bf16),
        [pl.BlockSpec((rows, width), lambda i, n: (0, 0))] * CHIPS,
        pl.BlockSpec((2 * PAIR * rows, width // 2), lambda i, n: (0, 0)),
        tuple(parts),
        index=index,
        grid=(1,),
        name="out_block",
    )


def half_rotated(values):
    middle = values.shape[0] // 2
    return jnp.concatenate([-values[middle:], values[:middle]], axis=0)


def qkv_body(make, *refs):
    if make:
        xs, (own, other, cosine, sine, queries, kv, xhat) = refs[:PAIR], refs[PAIR:]
        rows, width = xs[0].shape
        for m in range(PAIR):
            x = xs[m][...].astype(f32)
            inverse = lax.rsqrt(mean_of(x * x) + norm_eps)
            xhat[m * rows : (m + 1) * rows, :] = (x * inverse).astype(bf16)
    else:
        xhat, own, other, cosine, sine, queries, kv = refs
        rows, width = cosine.shape[1], xhat.shape[1]
    cos, sin = cosine[...], sine[...]
    total = dot(xhat[:, : width // 2], own[...]) + dot(xhat[:, width // 2 :], other[...])
    for m in range(PAIR):
        turned = total[m * rows : (m + 1) * rows].T
        for h in range(GROUP + 1):
            u = turned[h * HEAD : (h + 1) * HEAD]
            u = u * cos + half_rotated(u) * sin
            if h < GROUP:
                queries[m, :, h * rows : (h + 1) * rows] = (u * HEAD ** (-0.5)).astype(bf16)
            else:
                both = jnp.concatenate([u, turned[(h + 1) * HEAD :]], axis=0)
                kv[m * rows : (m + 1) * rows, :] = both.T.astype(bf16)


def qkv_call(xs, own, other, cosine, sine):
    make = isinstance(xs, list)
    rows = cosine.shape[1]
    tokens = PAIR * rows
    outs = (shape((PAIR, HEAD, GROUP * rows), bf16), shape((tokens, 2 * HEAD), bf16))
    if make:
        outs = outs + (shape((tokens, xs[0].shape[1]), bf16),)
    operands = (*(xs if make else (xs,)), own, other, cosine, sine)
    return kernel_call(
        functools.partial(qkv_body, make),
        outs,
        [whole()] * len(operands),
        tuple(whole() for _ in outs),
        operands,
        name="qkv",
    )


def out_rows_body(index, *refs):
    pieces, out = refs[:CHIPS], refs[CHIPS]
    cut = pieces[0].shape[0] // PAIR
    for row in range(2):

        @pl.when(index[0] >> 1 == row)
        def _():
            for n in range(PAIR):
                for m in range(CHIPS):
                    spot = (n * CHIPS + m) * cut
                    start = (n ^ row) * cut
                    out[spot : spot + cut, :] = pieces[m ^ (2 * n)][start : start + cut, :]


def out_rows_call(index, pieces):
    rows, width = pieces[0].shape
    return kernel_call(
        out_rows_body,
        shape((CHIPS * rows, width), bf16),
        [pl.BlockSpec((rows, width), lambda i, n: (0, 0))] * CHIPS,
        pl.BlockSpec((CHIPS * rows, width), lambda i, n: (0, 0)),
        tuple(pieces),
        index=index,
        grid=(1,),
        name="out_rows",
    )


LANE_HEADS = 4


def own_block_bias(rows):
    key = lax.broadcasted_iota(jnp.int32, (rows, rows), 0)
    mine = lax.broadcasted_iota(jnp.int32, (rows, rows), 1)
    return jnp.where(key <= mine, 0.0, masked_score)


def set_bias(bias):
    rows = bias.shape[0]
    value = own_block_bias(rows)
    for h in range(LANE_HEADS):
        bias[:, h * rows : (h + 1) * rows] = value


def far_bias(depth, d):
    return jnp.where(d <= depth, 0.0, masked_score) if d else 0.0


def attention_body(shards, index, queries, *refs):
    kvs = refs[:shards]
    turned_out, out, stats, bias, terms, out_turned = refs[shards:]
    rows = bias.shape[0]
    wide = LANE_HEADS * rows

    @pl.when(pl.program_id(0) == 0)
    def _():
        set_bias(bias)

    ks = [kv[:, :HEAD] for kv in kvs]
    v_turned = jnp.concatenate([kv[...] for kv in kvs], axis=0).astype(f32).T[HEAD:].astype(bf16)
    for n in range(GROUP // LANE_HEADS):
        span = slice(n * wide, (n + 1) * wide)
        q = queries[0, :, span]
        scores, top = [], None
        for d in range(shards):
            score = dot(ks[d], q)
            if d == 0:
                score = score + bias[...]
            scores.append(score)
            highest = jnp.max(score, axis=0, keepdims=True) + far_bias(index[2], d)
            top = highest if top is None else jnp.maximum(top, highest)
        total = None
        for d in range(shards):
            term = jnp.exp(scores[d] - (top - far_bias(index[2], d)))
            part = jnp.sum(term, axis=0, keepdims=True)
            total = part if total is None else total + part
            terms[d * rows : (d + 1) * rows, :] = term.astype(bf16)
        out_turned[:, span] = dot(v_turned, terms[...]) / total
        stats[0, :, span] = top + jnp.log(total)
    turned_out[0] = out_turned[...].astype(bf16)
    straight = out_turned[...].T
    for h in range(GROUP):
        out[:, h * HEAD : (h + 1) * HEAD] = straight[h * rows : (h + 1) * rows].astype(bf16)


def attention_call(index, queries, kvs):
    chips, _, wide = queries.shape
    rows = wide // GROUP
    shards = len(kvs)
    keys = shards * rows
    block = pl.BlockSpec((1, HEAD, wide), lambda i, n: (i, 0, 0))
    return kernel_call(
        functools.partial(attention_body, shards),
        (
            shape((chips, HEAD, wide), bf16),
            shape((chips * rows, GROUP * HEAD), bf16),
            shape((chips, 1, wide), f32),
        ),
        [block] + [pl.BlockSpec((rows, 2 * HEAD), lambda i, n: (i, 0))] * shards,
        (
            block,
            pl.BlockSpec((rows, GROUP * HEAD), lambda i, n: (i, 0)),
            pl.BlockSpec((1, 1, wide), lambda i, n: (i, 0, 0)),
        ),
        (queries, *kvs),
        index=index,
        grid=(chips,),
        scratch=(
            VMEM((rows, LANE_HEADS * rows), f32),
            VMEM((keys, LANE_HEADS * rows), bf16),
            VMEM((HEAD, wide), f32),
        ),
        name="attention",
    )


def attention_back_body(shards, index, branch, wo_own, wo_other, cosine, sine, *refs):
    per_group = 3 + shards
    inputs = [refs[n * per_group : (n + 1) * per_group] for n in range(PAIR)]
    grad_q, grad_first, grad_rest = refs[-7:-4]
    bias, probs_low, grads_low, grad_lanes = refs[-4:]
    rows = bias.shape[0]
    wide = LANE_HEADS * rows
    width = branch.shape[1]
    set_bias(bias)
    cos, sin = cosine[...], sine[...]
    for n, (queries, turned_out, stats, *kvs) in enumerate(inputs):
        heads = slice(n * GROUP * HEAD, (n + 1) * GROUP * HEAD)
        grad_out = dot_nt(wo_own[heads, :], branch[:, : width // 2])
        grad_out = grad_out + dot_nt(wo_other[heads, :], branch[:, width // 2 :])
        for h in range(GROUP):
            grad_lanes[:, h * rows : (h + 1) * rows] = grad_out[h * HEAD : (h + 1) * HEAD].astype(bf16)
        ks = [kv[:, :HEAD] for kv in kvs]
        vs = [kv[:, HEAD:] for kv in kvs]
        k_turned = jnp.concatenate([kv[...] for kv in kvs], axis=0).astype(f32).T[:HEAD].astype(bf16)
        k_total, v_total, parts = None, None, []
        for c in range(GROUP // LANE_HEADS):
            span = slice(c * wide, (c + 1) * wide)
            q, mine = queries[0, :, span], grad_lanes[:, span]
            delta = jnp.sum(
                mine.astype(f32) * turned_out[0, :, span].astype(f32), axis=0, keepdims=True
            )
            for d in range(shards):
                score = dot(ks[d], q)
                if d == 0:
                    score = score + bias[...]
                probs = jnp.exp(score - (stats[0, :, span] - far_bias(index[2], d)))
                grad_scores = probs * (dot(vs[d], mine) - delta)
                probs_low[d * rows : (d + 1) * rows, :] = probs.astype(bf16)
                grads_low[d * rows : (d + 1) * rows, :] = grad_scores.astype(bf16)
            u = dot(k_turned, grads_low[...]) * HEAD ** (-0.5)
            parts.append(u * cos - half_rotated(u) * sin)
            k_term = dot_nt(grads_low[...], q)
            v_term = dot_nt(probs_low[...], mine)
            k_total = k_term if k_total is None else k_total + k_term
            v_total = v_term if v_total is None else v_total + v_term
        straight = jnp.concatenate(parts, axis=1).T
        for h in range(GROUP):
            spot = (n * GROUP + h) * HEAD
            grad_q[:, spot : spot + HEAD] = straight[h * rows : (h + 1) * rows].astype(bf16)
        both = jnp.concatenate([k_total, v_total], axis=1)
        spot = slice(n * 2 * HEAD, (n + 1) * 2 * HEAD)
        grad_first[:, spot] = both[:rows, :]
        for d in range(1, shards):
            grad_rest[d - 1, :, spot] = both[d * rows : (d + 1) * rows, :].astype(bf16)


def attention_back_call(index, m, branch, wo_own, wo_other, cosine, sine, groups, before):
    chips, _, wide = groups[0][0].shape
    rows = wide // GROUP
    shards = len(groups[0][3])
    keys = shards * rows
    tokens = chips * rows
    block = pl.BlockSpec((1, HEAD, wide), lambda i, n: (m, 0, 0))
    in_specs = [whole()] * 5
    operands = [branch, wo_own, wo_other, jnp.tile(cosine, (1, LANE_HEADS)), jnp.tile(sine, (1, LANE_HEADS))]
    for queries, turned, stats, kvs in groups:
        in_specs += [block, block, pl.BlockSpec((1, 1, wide), lambda i, n: (m, 0, 0))]
        in_specs += [pl.BlockSpec((rows, 2 * HEAD), lambda i, n: (m, 0))] * shards
        operands += [queries, turned, stats, *kvs]
    aliases = {}
    if before is not None:
        aliases = {1 + len(operands) + n: n for n in range(3)}
        in_specs += [pl.BlockSpec(memory_space=pl.ANY)] * 3
        operands += list(before)
    outs = (
        shape((tokens, PAIR * GROUP * HEAD), bf16),
        shape((tokens, PAIR * 2 * HEAD), f32),
        shape((shards - 1, tokens, PAIR * 2 * HEAD), bf16),
    )
    out_specs = (
        pl.BlockSpec((rows, PAIR * GROUP * HEAD), lambda i, n: (m, 0)),
        pl.BlockSpec((rows, PAIR * 2 * HEAD), lambda i, n: (m, 0)),
        pl.BlockSpec((shards - 1, rows, PAIR * 2 * HEAD), lambda i, n: (0, m, 0)),
    )
    return kernel_call(
        functools.partial(attention_back_body, shards),
        outs,
        in_specs,
        out_specs,
        tuple(operands),
        index=index,
        grid=(1,),
        scratch=(
            VMEM((rows, LANE_HEADS * rows), f32),
            VMEM((keys, LANE_HEADS * rows), bf16),
            VMEM((keys, LANE_HEADS * rows), bf16),
            VMEM((HEAD, wide), bf16),
        ),
        aliases=aliases,
        name="attention_back",
    )


def parts_body(steps, transposed, count, *refs):
    lefts, owns, others = refs[:count], refs[count : 2 * count], refs[2 * count : 3 * count]
    outs = refs[3 * count :]
    rows = outs[0].shape[0]
    step = pl.program_id(0)

    def run(weights):
        total = None
        for left, weight in zip(lefts, weights):
            term = (dot_nt if transposed else dot)(left[...], weight[...])
            total = term if total is None else total + term
        for m, out in enumerate(outs):
            out[...] = total[m * rows : (m + 1) * rows, :].astype(out.dtype)

    @pl.when(step < steps)
    def _():
        run(owns)

    @pl.when(step >= steps)
    def _():
        run(others)


def parts_call(terms, rows, transposed, name):
    tokens = terms[0][0].shape[0]
    half = terms[0][1].shape[0] if transposed else terms[0][1].shape[1]
    tile = 256
    steps = half // tile
    last = steps - 1
    specs = [pl.BlockSpec((tokens, term[0].shape[1]), lambda j: (0, 0)) for term in terms]
    for side in range(2):
        for left, _, _, spot in terms:
            depth = left.shape[1]

            def place(side, spot, j):
                step = jnp.maximum(j - steps, 0) if side else jnp.minimum(j, last)
                return (step, spot) if transposed else (spot, step)

            block = (tile, depth) if transposed else (depth, tile)
            specs.append(pl.BlockSpec(block, functools.partial(place, side, spot)))
    count = tokens // rows
    return kernel_call(
        functools.partial(parts_body, steps, transposed, len(terms)),
        tuple(shape((rows, 2 * half), f32 if m == 0 else bf16) for m in range(count)),
        specs,
        tuple(pl.BlockSpec((rows, tile), lambda j: (0, j)) for _ in range(count)),
        (*(term[0] for term in terms), *(term[1] for term in terms), *(term[2] for term in terms)),
        grid=(2 * steps,),
        name=name,
    )


def gate_body(count, *refs):
    twos = refs[:count]
    gate_own, up_own, gate_other, up_other, act, for_gate, for_up, two_all = refs[count:]
    half = two_all.shape[1] // 2

    @pl.when(pl.program_id(0) == 0)
    def _():
        start = 0
        for two in twos:
            two_all[start : start + two.shape[0], :] = two[...]
            start += two.shape[0]

    own = jnp.concatenate([gate_own[...], up_own[...]], axis=1)
    other = jnp.concatenate([gate_other[...], up_other[...]], axis=1)
    both = dot(two_all[:, :half], own) + dot(two_all[:, half:], other)
    wide = gate_own.shape[1]
    gate, up = both[:, :wide], both[:, wide:]
    sig = 1.0 / (1.0 + jnp.exp(-gate))
    silu = gate * sig
    act[...] = (silu * up).astype(bf16)
    for_gate[...] = (up * sig * (1.0 + gate * (1.0 - sig))).astype(bf16)
    for_up[...] = silu.astype(bf16)


def gate_call(twos, own, other):
    rows, width = twos[0].shape
    tokens = CHIPS * rows
    half = width // 2
    ff = own.shape[1] // 2
    tile = LANES
    steps = ff // tile
    weight = [
        pl.BlockSpec((half, tile), lambda j: (0, j)),
        pl.BlockSpec((half, tile), lambda j: (0, j + steps)),
    ]
    column = pl.BlockSpec((tokens, tile), lambda j: (0, j))
    return kernel_call(
        functools.partial(gate_body, len(twos)),
        tuple(shape((tokens, ff), bf16) for _ in range(3)) + (shape((tokens, width), bf16),),
        [pl.BlockSpec(two.shape, lambda j: (0, 0)) for two in twos] + weight + weight,
        (column, column, column, pl.BlockSpec((tokens, width), lambda j: (0, 0))),
        (*twos, own, own, other, other),
        grid=(steps,),
        name="gate",
    )


def hidden_back_body(g, own, other, for_gate, for_up, grads):
    half = g.shape[1] // 2
    ff = own.shape[0]
    hidden = dot_nt(g[:, :half], own[...]) + dot_nt(g[:, half:], other[...])
    grads[:, :ff] = (hidden * for_gate[...].astype(f32)).astype(bf16)
    grads[:, ff:] = (hidden * for_up[...].astype(f32)).astype(bf16)


def hidden_back_call(g, own, other, for_gate, for_up):
    tokens, width = g.shape
    ff, half = own.shape
    block = tokens // 2
    row = lambda i: (i, 0)
    fixed = lambda i: (0, 0)
    return kernel_call(
        hidden_back_body,
        shape((tokens, 2 * ff), bf16),
        [
            pl.BlockSpec((block, width), row),
            pl.BlockSpec((ff, half), fixed),
            pl.BlockSpec((ff, half), fixed),
            pl.BlockSpec((block, ff), row),
            pl.BlockSpec((block, ff), row),
        ],
        pl.BlockSpec((block, 2 * ff), row),
        (g, own, other, for_gate, for_up),
        grid=(2,),
        name="hidden_back",
    )


def weight_grad_body(per, outputs, adds, left, right, *refs):
    added = [refs[n * outputs : (n + 1) * outputs] for n in range(adds)]
    outs, turned = refs[adds * outputs : -1], refs[-1]
    step = pl.program_id(0)

    @pl.when(step == 0)
    def _():
        turned[...] = left[...].T

    for n in range(outputs):

        @pl.when(step // per == n)
        def _(n=n):
            total = dot(turned[...], right[...])
            for terms in added:
                total = total + terms[n][...].astype(f32)
            outs[n][...] = total.astype(bf16)


def weight_grad(left, left_side, right, place, width, outputs, added, name):
    tokens = left.shape[0]
    rows = left.shape[1] // (1 if left_side is None else 2)
    tile = 256 if width % 256 == 0 else width
    per = width // tile
    first = place * width // tile
    side = left_side or 0

    def spot(n, j):
        return (0, jnp.clip(j - n * per, 0, per - 1))

    tiles = [pl.BlockSpec((rows, tile), functools.partial(spot, n)) for n in range(outputs)]
    return kernel_call(
        functools.partial(weight_grad_body, per, outputs, len(added)),
        tuple(shape((rows, width), bf16) for _ in range(outputs)),
        [
            pl.BlockSpec((tokens, rows), lambda j: (0, side)),
            pl.BlockSpec((tokens, tile), lambda j: (0, first + j)),
        ]
        + tiles * len(added),
        tuple(tiles),
        (left, right, *(term for terms in added for term in terms)),
        grid=(per * outputs,),
        scratch=(VMEM((rows, tokens), bf16),),
        name=name,
    )


def rows_result_body(local, index, *refs):
    pieces, out = refs[:PIECES], refs[PIECES]
    half = local // 2
    shards = out.shape[1] // local
    for m in range(CHIPS):
        for core in range(2):

            @pl.when((pl.program_id(0) == m) & (index[1] == core))
            def _():
                for side in range(2):
                    piece = pieces[2 * m + side]
                    for s in range(shards):
                        spot = s * local + (core ^ side) * half
                        out[:, spot : spot + half] = piece[:, s * half : (s + 1) * half].astype(f32)


def rows_result(index, pieces, local, name):
    cut, half_width = pieces[0].shape
    return kernel_call(
        functools.partial(rows_result_body, local),
        shape((CHIPS * cut, 2 * half_width), f32),
        [pl.BlockSpec((cut, half_width), lambda i, n: (0, 0))] * PIECES,
        pl.BlockSpec((cut, 2 * half_width), lambda i, n: (n[0] ^ i, 0)),
        tuple(pieces),
        index=index,
        grid=(CHIPS,),
        name=name,
    )


def out_result_body(local, base, index, *refs):
    pieces, out = refs[:PIECES], refs[PIECES]
    half = local // 2
    cut = local // CHIPS
    shards = out.shape[1] // local
    for m in range(CHIPS):
        for core in range(2):

            @pl.when((pl.program_id(0) == m) & (index[1] == core))
            def _():
                for side in range(2):
                    piece = pieces[2 * m + side]
                    for s in range(shards):
                        spot = s * local + (core ^ side) * half
                        row, column = (0, s * half) if s * half < 512 else (cut, s * half - 512)
                        column += base
                        out[:, spot : spot + half] = piece[row : row + cut, column : column + half].astype(f32)


def out_result(index, pieces, local, width, base):
    cut = local // CHIPS
    return kernel_call(
        functools.partial(out_result_body, local, base),
        shape((local, width), f32),
        [pl.BlockSpec(pieces[0].shape, lambda i, n: (0, 0))] * PIECES,
        pl.BlockSpec((cut, width), lambda i, n: (n[0] ^ i, 0)),
        tuple(pieces),
        index=index,
        grid=(CHIPS,),
        name="out_result",
    )


def lane_sum(value):
    total = value[:, :LANES]
    for n in range(1, value.shape[1] // LANES):
        total = total + value[:, n * LANES : (n + 1) * LANES]
    return total


def feedforward_result_body(ff_local, cut, index, *refs):
    pieces = refs[:CHIPS]
    gate_weight, up_weight, gain = refs[CHIPS : CHIPS + 3]
    gate_out, up_out, gain_out = refs[-3:]
    shards = gate_weight.shape[1] // ff_local
    width = shards * cut
    for chip in range(CHIPS):

        @pl.when(index[0] == chip)
        def _():
            @pl.loop(0, gate_out.shape[0] // 16)
            def _(n):
                rows = pl.ds(pl.multiple_of(n * 16, 16), 16)
                scale = gain[rows, :1]
                total = jnp.zeros((16, LANES), f32)
                for base, weight, out in ((0, gate_weight, gate_out), (width, up_weight, up_out)):
                    parts = []
                    for s in range(shards):
                        for owner in range(CHIPS):
                            start = base + s * cut
                            parts.append(pieces[owner ^ chip][rows, start : start + cut].astype(f32))
                    wide = jnp.concatenate(parts, axis=1)
                    total = total + lane_sum(wide * weight[rows, :].astype(f32))
                    out[rows, :] = wide * scale
                gain_out[rows, :] = total


def feedforward_result(index, side, pieces, gate_weight, up_weight, gain, ff_local, before):
    local, ff = gate_weight.shape
    half = local // 2
    rows = 64
    steps = half // rows
    row = lambda i, n: ((n[1] ^ side) * steps + i, 0)
    in_specs = [pl.BlockSpec((rows, pieces[0].shape[1]), lambda i, n: (i, 0))] * CHIPS
    in_specs += [pl.BlockSpec((rows, ff), row)] * 2 + [pl.BlockSpec((rows, LANES), row)]
    operands = (*pieces, gate_weight, up_weight, gain)
    aliases = {}
    if before is not None:
        aliases = {1 + len(operands) + n: n for n in range(3)}
        in_specs = in_specs + [pl.BlockSpec(memory_space=pl.ANY)] * 3
        operands = operands + tuple(before)
    return kernel_call(
        functools.partial(feedforward_result_body, ff_local, ff_local // CHIPS),
        (shape((local, ff), f32), shape((local, ff), f32), shape((local, LANES), f32)),
        in_specs,
        (pl.BlockSpec((rows, ff), row), pl.BlockSpec((rows, ff), row), pl.BlockSpec((rows, LANES), row)),
        operands,
        index=index,
        grid=(steps,),
        aliases=aliases,
        name="feedforward_result",
    )


def qkv_result_body(local, group_shards, index, *refs):
    pieces = refs[:PIECES]
    weights, gain = refs[PIECES : PIECES + 3], refs[PIECES + 3]
    outs, gain_out = refs[PIECES + 4 : PIECES + 7], refs[PIECES + 7]
    q_width = GROUP * HEAD
    cut = local // CHIPS
    scale = gain[:, :1]
    for chip in range(CHIPS):
        for side in range(2):

            @pl.when((index[0] == chip) & (pl.program_id(0) == side))
            def _():
                parts, k_parts, v_parts = [], [], []
                for group in range(CHIPS):
                    owner = (group >> 1) + 2 * (group & 1)
                    piece = pieces[2 * (owner ^ chip) + side]
                    for s in range(group_shards):
                        for j in range(CHIPS):
                            start = ((j ^ owner) * group_shards + s) * cut
                            parts.append(piece[:, start : start + cut].astype(f32))
                    k_parts.append(piece[:, q_width : q_width + HEAD].astype(f32))
                    v_parts.append(piece[:, q_width + HEAD : q_width + 2 * HEAD].astype(f32))
                total = jnp.zeros((gain.shape[0], LANES), f32)
                for part, weight, out in zip((parts, k_parts, v_parts), weights, outs):
                    wide = jnp.concatenate(part, axis=1)
                    total = total + lane_sum(wide * weight[...].astype(f32))
                    out[...] = wide * scale
                gain_out[...] = total


def qkv_result(index, pieces, query, key, value, gain):
    local, width = query.shape
    half = local // 2
    group_shards = width // local // CHIPS
    row = lambda i, n: (n[1] ^ i, 0)
    kv_width = key.shape[1]
    return kernel_call(
        functools.partial(qkv_result_body, local, group_shards),
        (
            shape((local, width), f32),
            shape((local, kv_width), f32),
            shape((local, kv_width), f32),
            shape((local, LANES), f32),
        ),
        [pl.BlockSpec(pieces[0].shape, lambda i, n: (0, 0))] * PIECES
        + [
            pl.BlockSpec((half, width), row),
            pl.BlockSpec((half, kv_width), row),
            pl.BlockSpec((half, kv_width), row),
            pl.BlockSpec((half, LANES), row),
        ],
        (
            pl.BlockSpec((half, width), row),
            pl.BlockSpec((half, kv_width), row),
            pl.BlockSpec((half, kv_width), row),
            pl.BlockSpec((half, LANES), row),
        ),
        (*pieces, query, key, value, gain),
        index=index,
        grid=(2,),
        name="qkv_result",
    )


def per_device(
    hidden_in,
    attention_gain,
    query_weight,
    key_weight,
    value_weight,
    output_weight,
    feedforward_gain,
    gate_weight,
    up_weight,
    down_weight,
    out_grad,
):
    rows, width = hidden_in.shape
    shards = lax.axis_size("shard")
    replicas = lax.axis_size("replica")
    place = lax.axis_index("replica")
    depth = lax.axis_index("shard")
    core = place & 1
    chip = (place >> 1) & (CHIPS - 1)
    local = width // shards
    half = local // 2
    ff_local = down_weight.shape[0]
    group_shards = shards // CHIPS
    q_width = GROUP * HEAD
    qkv_width = q_width + 2 * HEAD
    index = jnp.stack([chip, core, depth]).astype(jnp.int32)

    gain_one = jnp.broadcast_to(attention_gain.astype(f32)[:, None], (local, LANES))
    gain_two = jnp.broadcast_to(feedforward_gain.astype(f32)[:, None], (local, LANES))


    at_block, out_block = attention_block(
        index, query_weight, key_weight, value_weight, output_weight, gain_one
    )
    x = own_first(index, (after(hidden_in, at_block),), local)[0]
    xs = [x, swap(x, 2)]
    at_own = lax.all_gather(at_block, "shard", axis=0, tiled=True)
    out_all = lax.all_gather(out_block, "shard", axis=0, tiled=True)
    gu_block = feedforward_block(index, gate_weight, up_weight, after(gain_two, at_block), ff_local)
    gu_own = lax.all_gather(gu_block, "shard", axis=0, tiled=True)
    down_own = lax.all_gather(down_block(index, down_weight, local), "shard", axis=0, tiled=True)
    g = own_first(index, (after(out_grad, x),), local)[0]
    g_blocks = [g, swap(g, 2), swap(g, 4)]
    at_own = after(at_own, gu_block, xs[1], *g_blocks[1:])

    qkv_own = [at_own]
    qkv_own.append(swap(qkv_own[0], 4))
    qkv_other = [swap(qkv_own[0], 1)]
    inverse = rope_base ** (-jnp.arange(0, HEAD, 2, dtype=f32) / HEAD)
    places = (depth * rows + jnp.arange(rows, dtype=jnp.int32)).astype(f32)
    angles = inverse[:, None] * places[None, :]
    angles = jnp.concatenate([angles, angles], axis=0)
    cosine, sine = jnp.cos(angles), jnp.sin(angles)

    def shifted(kv):
        return [kv] + [shift(kv, d) for d in range(1, shards)]

    queries, kv, xhat = qkv_call(xs, qkv_own[0], qkv_other[0], cosine, sine)
    kvs = shifted(kv)
    qkv_own[1] = after(qkv_own[1], *kvs[1:])
    qkv_other.append(swap(qkv_own[1], 1))
    queries_two, kv_two = qkv_call(xhat, qkv_own[1], qkv_other[1], cosine, sine)
    kvs_two = shifted(kv_two)
    groups = [(queries, *attention_call(index, queries, kvs), kvs)]
    groups.append((queries_two, *attention_call(index, queries_two, kvs_two), kvs_two))
    attended = [group[2] for group in groups]
    groups = [(group[0], group[1], group[3], group[4]) for group in groups]

    out_all = after(out_all, qkv_own[1])
    x_place = chip & 1
    low_group = (chip >> 1) == 0
    pair_rows = PAIR * group_shards * half // 2

    def out_for(mask):
        return lax.dynamic_slice_in_dim(out_all, ((chip ^ mask) & 1) * pair_rows, pair_rows, 0)

    out_pieces = [out_for(0)] + [swap(out_for(m), 2 * m) for m in range(1, CHIPS)]
    wo_own = out_rows_call(index, [after(piece, *kvs_two[1:]) for piece in out_pieces])
    wo_other = swap(wo_own, 1)

    mid_terms = [(attended[n], wo_own, wo_other, n) for n in range(PAIR)]
    g_blocks.append(swap(after(g, *out_pieces[1:]), 6))
    mid_out = parts_call(mid_terms, rows, False, "attention_out")
    g_all = jnp.concatenate([after(block, mid_out[0]) for block in g_blocks], axis=0)
    middle, two = middle_call(plane_send(mid_out), after(x, g_all))
    twos = plane_gather_forward(two)

    gu_own = after(gu_own, *twos[1:])
    gu_other = swap(gu_own, 1)
    act, for_gate, for_up, two_all = gate_call(twos, gu_own, gu_other)

    def over_groups(kept):
        if replicas > PIECES:
            groups = [
                [e * PIECES + i for e in range(replicas // PIECES)] for i in range(PIECES)
            ]
            kept = lax.psum(kept, "replica", axis_index_groups=groups)
        return kept

    def reduced(term):
        kept = lax.psum_scatter(term, "shard", scatter_dimension=0, tiled=True)
        return over_groups(kept)

    def plane_pieces(kept):
        mine = plane_gather(kept)
        return mine, [swap(part, 1) for part in mine]

    def mixed(mine, theirs):
        return [part for pair in zip(mine, theirs) for part in pair]

    down_sent = weight_grad(act, None, g_all, 1, width // 2, 1, (), "down_grad_other")
    down_sent = [swap(down_sent[0], 1)]
    down_sent[0] = after(down_sent[0], down_own)
    down_term = weight_grad(act, None, g_all, 0, width // 2, 1, (down_sent,), "down_grad")[0]
    down_kept = reduced(down_term)
    down_other = swap(down_own, 1)

    grads = hidden_back_call(after(g_all, down_term), down_own, down_other, for_gate, for_up)
    grads_wide = grads.shape[1]
    gu_sent = weight_grad(two_all, 1, grads, 0, grads_wide, 1, (), "gate_grad_other")
    gu_sent = [swap(gu_sent[0], 1)]
    gu_term = weight_grad(two_all, 0, grads, 0, grads_wide, 1, (gu_sent,), "gate_grad")[0]
    gu_kept = reduced(gu_term)
    grads_late = after(grads, gu_term)
    e_terms = parts_call([(grads_late, gu_own, gu_other, 0)], rows, True, "feedforward_back")
    e_parts = plane_send(e_terms)
    act_late = after(act, e_terms[0])
    out_terms = parts_call([(act_late, down_own, down_other, 0)], rows, False, "feedforward_out")

    middle_late = after(middle, out_terms[0], down_kept)
    grad_middle, branch = grad_middle_call(e_parts, middle_late, g)
    branches = [branch, swap(branch, 2)]

    def back_block(m, block, before):
        return attention_back_call(index, m, block, wo_own, wo_other, cosine, sine, groups, before)

    before = back_block(0, branch, None)
    out_parts = plane_send(after(out_terms, branches[1], before[1]))
    before = back_block(1, after(branches[1], before[1]), before)
    output = output_call(index, out_parts, middle, local)
    grad_q, grad_first, grad_rest = before
    grad_rest = after(grad_rest, *out_parts[1:3])
    rest = [shift(grad_rest[d - 1], -d) for d in range(1, shards)]

    half_wide = width // 2
    branch_all = jnp.concatenate([after(block, grad_first, *out_parts[1:3]) for block in branches], axis=0)
    both_attended = jnp.concatenate(attended, axis=1)
    wo_sent = weight_grad(both_attended, None, branch_all, 1, half_wide, 1, (), "out_grad_other")
    wo_sent = [after(swap(wo_sent[0], 1), rest[-1])]
    wo_term = weight_grad(both_attended, None, branch_all, 0, half_wide, 1, (wo_sent,), "out_grad")[0]
    wo_terms = out_sends(index, wo_term)
    wo_parts = plane_send(wo_terms)
    wo_wide = out_block_call(index, [after(wo_parts[0], gu_kept), *wo_parts[1:]], shards)
    grad_first = after(grad_first, out_parts[3], wo_terms[0])
    grad_qkv = grad_qkv_call(grad_q, grad_first, rest, cosine, sine)

    def qkv_grad(n, side, added, name):
        return weight_grad(xhat, side, grad_qkv[n], 0, qkv_width, 1, added, name)

    qkv_sent = [swap(qkv_grad(n, 1, (), "qkv_grad_other")[0], 1) for n in (1, 0)]
    back_terms = [(grad_qkv[n], qkv_own[n], qkv_other[n], 0) for n in range(PAIR)]
    qkv_sent[0] = after(qkv_sent[0], *wo_parts[1:3])
    qkv_second = qkv_grad(1, 0, ([qkv_sent[0]],), "qkv_grad")[0]
    qkv_term = qkv_grad(0, 0, ([qkv_sent[1]],), "qkv_grad")[0]
    at_term = jnp.concatenate([qkv_term, qkv_second, wo_wide], axis=1)
    at_kept = reduced(after(at_term, gu_kept))
    back_terms[0] = (after(grad_qkv[0], qkv_term, qkv_second), *back_terms[0][1:])
    back_parts = parts_call(back_terms, rows, True, "qkv_back")
    e_one = plane_send(back_parts)
    gu_mine = plane_gather_forward(gu_kept, back_parts[0])
    gu_mine = gu_mine[:3] + [jnp.concatenate(gu_mine[3:], axis=0)]
    gu_theirs = [swap(after(part, output), 1) for part in gu_mine]
    gu_out = feedforward_result(index, 0, gu_mine, gate_weight, up_weight, gain_two, ff_local, None)
    gu_out = feedforward_result(index, 1, gu_theirs, gate_weight, up_weight, gain_two, ff_local, gu_out)

    grad_input = grad_input_call(index, e_one, x, grad_middle, local)

    second = swap(at_kept[:, qkv_width : 2 * qkv_width], 4)
    first = at_kept[:, :qkv_width].astype(f32) + second.astype(f32)
    at_kept = jnp.concatenate([first.astype(bf16), at_kept[:, 2 * qkv_width :]], axis=1)
    down_mine = plane_gather(after(down_kept, at_kept))
    down_theirs = [swap(part, 1) for part in down_mine]
    down_out = rows_result(index, mixed(down_mine, down_theirs), local, "down_result")
    at_mine = plane_gather(at_kept)
    at_near = [after(piece, gu_out[0], grad_input) for piece in at_mine]
    at_pieces = mixed(at_mine, [swap(piece, 1) for piece in at_near])
    wo_out = out_result(index, at_pieces, local, width, qkv_width)
    q_out, k_out, v_out, gain_one_sums = qkv_result(
        index, at_pieces, query_weight, key_weight, value_weight, gain_one
    )
    return (
        output,
        grad_input,
        jnp.sum(gain_one_sums, axis=1),
        q_out,
        k_out,
        v_out,
        wo_out,
        jnp.sum(gu_out[2], axis=1),
        gu_out[0],
        gu_out[1],
        down_out,
    )


def solution(mesh):
    return jax.shard_map(
        per_device,
        mesh=mesh,
        in_specs=(
            P(("replica", "shard"), None),
            P("shard"),
            P("shard", None),
            P("shard", None),
            P("shard", None),
            P("shard", None),
            P("shard"),
            P("shard", None),
            P("shard", None),
            P("shard", None),
            P(("replica", "shard"), None),
        ),
        out_specs=(
            P(("replica", "shard"), None),
            P(("replica", "shard"), None),
            P("shard"),
            P("shard", None),
            P("shard", None),
            P("shard", None),
            P("shard", None),
            P("shard"),
            P("shard", None),
            P("shard", None),
            P("shard", None),
        ),
        check_vma=False,
    )
```
